32 devices in a mesh: freq: 4 (over y, core), tm: 8 (over z, x).
Axes of the slice: x: 2, y: 2, z: 4, core: 2. Of those that a mesh axis runs over, the one named last changes fastest.
Arguments:
- patches: bfloat16 [12, 832, 256], P('freq', 'tm')
- column_mask: int32 [832], replicated, may hold values from 0 to 1, as said below
- labels: int32 [8, 527], replicated, may hold values 0 or 1
- clip_weights: int32 [8], replicated, may hold values from 1 to 3
- wide_weights: float32 [2, 768, 6144], P(None, 'tm')
- down_weights: float32 [2, 3072, 768], P(None, 'tm'), may hold values from -0.109375 to 0.109375
- embedding: float32 [1504, 768], P(None, 'tm')
- classifier: float32 [768, 527], P('tm'), may hold values from -0.21875 to 0.21875
- vectors: float32 [29, 768], P(None, 'tm')
- class_bias: float32 [527], replicated, may hold values from -3 to 3
- wide_first: float32 [2, 768, 6144], P(None, 'tm'), may hold values from -0.00390625 to 0.00390625
- down_first: float32 [2, 3072, 768], P(None, 'tm'), may hold values from -0.00390625 to 0.00390625
- embedding_first: float32 [1504, 768], P(None, 'tm'), may hold values from -0.00390625 to 0.00390625
- classifier_first: float32 [768, 527], P('tm'), may hold values from -0.00390625 to 0.00390625
- vectors_first: float32 [29, 768], P(None, 'tm'), may hold values from -0.03125 to 0.03125
- bias_first: float32 [527], replicated, may hold values from -0.03125 to 0.03125
- wide_second: float32 [2, 768, 6144], P(None, 'tm'), may hold values from 6.353893e-08 to 2.541557e-07
- down_second: float32 [2, 3072, 768], P(None, 'tm'), may hold values from 6.353893e-08 to 2.541557e-07
- embedding_second: float32 [1504, 768], P(None, 'tm'), may hold values from 6.353893e-08 to 2.541557e-07
- classifier_second: float32 [768, 527], P('tm'), may hold values from 6.353893e-08 to 2.541557e-07
- vectors_second: float32 [29, 768], P(None, 'tm'), may hold values from 4.0664913e-06 to 1.6265965e-05
- bias_second: float32 [527], replicated, may hold values from 4.0664913e-06 to 1.6265965e-05
Outputs:
- wide_new: float32 [2, 768, 6144], P(None, 'tm')
- down_new: float32 [2, 3072, 768], P(None, 'tm')
- embedding_new: float32 [1504, 768], P(None, 'tm')
- classifier_new: float32 [768, 527], P('tm')
- vectors_new: float32 [29, 768], P(None, 'tm')
- bias_new: float32 [527], replicated
- wide_first_new: float32 [2, 768, 6144], P(None, 'tm')
- down_first_new: float32 [2, 3072, 768], P(None, 'tm')
- embedding_first_new: float32 [1504, 768], P(None, 'tm')
- classifier_first_new: float32 [768, 527], P('tm')
- vectors_first_new: float32 [29, 768], P(None, 'tm')
- bias_first_new: float32 [527], replicated
- wide_second_new: float32 [2, 768, 6144], P(None, 'tm')
- down_second_new: float32 [2, 3072, 768], P(None, 'tm')
- embedding_second_new: float32 [1504, 768], P(None, 'tm')
- classifier_second_new: float32 [768, 527], P('tm')
- vectors_second_new: float32 [29, 768], P(None, 'tm')
- bias_second_new: float32 [527], replicated
- wide_copy: bfloat16 [2, 768, 6144], P(None, 'tm')
- down_copy: bfloat16 [2, 3072, 768], P(None, 'tm')
- embedding_copy: bfloat16 [1504, 768], P(None, 'tm')
- classifier_copy: bfloat16 [768, 527], P('tm')
- grad_norm: float32 [], replicated
- loss_sum: float32 [], replicated
- weight_total: float32 [], replicated
The draws below stay inside these ranges and needn't reach their ends.
Inputs may be any that keep to these rules, and one draw needn't show every extreme that they name: `column_mask`: each clip's columns are live for its first columns and dead after them, with 64 to 101 live columns; in every draw some clip has exactly 101.
All inputs are finite; a program needn't handle non-finite values.
Results may differ from the reference program's by a relative error of at most 0.0055.
The reference program's roundings to bfloat16 on the way count: a program that leaves them out, or rounds other values in their place, can miss the bound.
Values may be sent and summed in bfloat16 or wider, within the bound.
A program may use at most 320 MiB of HBM per device.

```python
import math
import jax
import jax.numpy as jnp
from jax import lax

D = 768
HEADS = 12
HDIM = 64
FF = 3072
CLASSES = 527
L = 2
FROWS = 12
HALF = 52
PATCH = 256
LMIN = 64
STEP = 5
CPD = 2
MAXLEN = 101
NGRID = 1248
CLIPS = 8
TCOLS = 832
VROWS = 29
NPARAM = 15738383
N_TM = 8


def draw_patches(key, part):
    key = jax.random.fold_in(key, 1)
    rows = jnp.arange(FROWS, dtype=jnp.float32)[:, None, None] / max(FROWS - 1, 1)
    times = jnp.arange(TCOLS, dtype=jnp.float32)[None, :, None] / max(TCOLS - 1, 1)
    scale = jnp.sqrt((1.0 + 2.0 * rows) * (1.0 + 2.0 * times))
    noise = jax.random.normal(key, (FROWS, TCOLS, PATCH), jnp.float32)
    return (noise * scale + 0.5 * scale).astype(jnp.bfloat16)


def draw_column_mask(key, part):
    key = jax.random.fold_in(key, 2)
    lengths = jax.random.randint(key, (CLIPS,), LMIN, MAXLEN + 1)
    chosen = jax.random.randint(jax.random.fold_in(key, 7), (), 0, CLIPS)
    lengths = jnp.where(jnp.arange(CLIPS) == chosen, MAXLEN, lengths)
    column = jnp.arange(TCOLS)
    device = column // (CPD * HALF)
    clip = device // 2 * CPD + column // HALF % CPD
    place = device % 2 * HALF + column % HALF
    return (place < lengths[clip]).astype(jnp.int32)


def draw_embedding(key, part):
    key = jax.random.fold_in(key, 3)
    noise = jax.random.normal(key, (NGRID + PATCH, D), jnp.float32)
    rows = jnp.arange(NGRID + PATCH)[:, None]
    return jnp.where(rows < NGRID, 0.5, PATCH ** (-0.5)) * noise


def draw_vectors(key, part):
    key = jax.random.fold_in(key, 4)
    noise = jax.random.normal(key, (VROWS, D), jnp.float32)
    rows = jnp.arange(VROWS)[:, None]
    glob = L * 8 + L * (FF // D)
    ramp = 0.6 + 1.2 * jnp.arange(D, dtype=jnp.float32)[None, :] / (D - 1)
    gains = (rows < L * 8) & ((rows % 8 == 0) | (rows % 8 == 2)) | (rows == glob + 3)
    tokens = (rows == glob + 1) | (rows == glob + 2)
    return jnp.where(gains, ramp * (1.0 + 0.1 * noise), jnp.where(tokens, noise, 0.3 * noise))


def draw_wide_weights(key, part):
    key = jax.random.fold_in(key, 5)
    noise = jax.random.normal(key, (L, D, 4 * D + FF), jnp.float32)
    noise = jnp.clip(noise, -6.0, 6.0)
    cols = jnp.arange(4 * D + FF)[None, None, :]
    factor = jnp.where((cols >= 3 * D) & (cols < 4 * D), 3.0, 1.0)
    return noise * factor * D ** (-0.5)


def with_ends(drawn, own_key, smallest, top_value):
    longest = drawn.shape.index(max(drawn.shape))
    spots = []
    for shift in (0, 1):
        where = [jax.random.randint(jax.random.fold_in(own_key, axis), (), 0, length) for axis, length in enumerate(drawn.shape)]
        where[longest] = (where[longest] + shift) % drawn.shape[longest]
        spots.append(tuple(where))
    return drawn.at[spots[0]].set(smallest).at[spots[1]].set(top_value)


def steps_of(stream_key, dims, shards, low, high):
    level, own = 1.0, jax.random.fold_in(stream_key, 6)
    for position, parts in shards:
        heights = jnp.exp(jax.random.uniform(jax.random.fold_in(own, position), (parts,), jnp.float32, low / len(shards), high / len(shards)))
        level = level * jnp.repeat(heights, dims[position] // parts).reshape([-1 if axis == position else 1 for axis in range(len(dims))])
    return level


def bell_draw(own_key, dims, scale, reach, split=(), held_as=jnp.bfloat16):
    entries = jax.random.normal(own_key, dims, jnp.float32) * scale
    if len(split) > 0:
        entries = steps_of(own_key, dims, split, -0.22, 0.18) * entries
    return jnp.clip(entries, min=-reach, max=reach).astype(held_as)


def setup_inputs(seed: int = 0) -> dict:
    key_list = jax.random.split(jax.random.key(seed), 23)
    return {
        "patches": draw_patches(jax.random.fold_in(key_list[22], 71), 0),
        "column_mask": draw_column_mask(jax.random.fold_in(key_list[22], 71), 0),
        "labels": with_ends((jax.random.randint(key_list[2], (CLIPS, CLASSES), 0, 16) < 1).astype(jnp.int32), jax.random.fold_in(key_list[2], 1), 0, 1),
        "clip_weights": with_ends(jax.random.randint(key_list[3], (CLIPS,), 1, 4), jax.random.fold_in(key_list[3], 1), 1, 3).astype(jnp.int32),
        "wide_weights": draw_wide_weights(jax.random.fold_in(key_list[22], 71), 0),
        "down_weights": bell_draw(key_list[5], (L, FF, D), FF ** -0.5, 0.109375, ((1, 8),), jnp.float32),
        "embedding": draw_embedding(jax.random.fold_in(key_list[22], 71), 0),
        "classifier": bell_draw(key_list[7], (D, CLASSES), D ** -0.5, 0.21875, ((0, 8),), jnp.float32),
        "vectors": draw_vectors(jax.random.fold_in(key_list[22], 71), 0),
        "class_bias": bell_draw(key_list[9], (CLASSES,), 0.5, 3.0, (), jnp.float32),
        "wide_first": bell_draw(key_list[10], (L, D, 4 * D + FF), (1.0 / NPARAM ** 0.5), 0.00390625, ((1, 8),), jnp.float32),
        "down_first": bell_draw(key_list[11], (L, FF, D), (1.0 / NPARAM ** 0.5), 0.00390625, ((1, 8),), jnp.float32),
        "embedding_first": bell_draw(key_list[12], (NGRID + PATCH, D), (1.0 / NPARAM ** 0.5), 0.00390625, ((1, 8),), jnp.float32),
        "classifier_first": bell_draw(key_list[13], (D, CLASSES), (1.0 / NPARAM ** 0.5), 0.00390625, ((0, 8),), jnp.float32),
        "vectors_first": bell_draw(key_list[14], (VROWS, D), (8.0 / NPARAM ** 0.5), 0.03125, ((1, 8),), jnp.float32),
        "bias_first": bell_draw(key_list[15], (CLASSES,), (8.0 / NPARAM ** 0.5), 0.03125, (), jnp.float32),
        "wide_second": jnp.clip(jnp.exp(math.log(2.5415570803488663e-07) - 1.3862944 * jax.random.uniform(key_list[16], (L, D, 4 * D + FF), jnp.float32) ** steps_of(key_list[16], (L, D, 4 * D + FF), ((1, 8),), -0.2, 0.2)), 6.353892700872166e-08, 2.5415570803488663e-07),
        "down_second": jnp.clip(jnp.exp(math.log(2.5415570803488663e-07) - 1.3862944 * jax.random.uniform(key_list[17], (L, FF, D), jnp.float32) ** steps_of(key_list[17], (L, FF, D), ((1, 8),), -0.2, 0.2)), 6.353892700872166e-08, 2.5415570803488663e-07),
        "embedding_second": jnp.clip(jnp.exp(math.log(2.5415570803488663e-07) - 1.3862944 * jax.random.uniform(key_list[18], (NGRID + PATCH, D), jnp.float32) ** steps_of(key_list[18], (NGRID + PATCH, D), ((1, 8),), -0.2, 0.2)), 6.353892700872166e-08, 2.5415570803488663e-07),
        "classifier_second": jnp.clip(jnp.exp(math.log(2.5415570803488663e-07) - 1.3862944 * jax.random.uniform(key_list[19], (D, CLASSES), jnp.float32) ** steps_of(key_list[19], (D, CLASSES), ((0, 8),), -0.2, 0.2)), 6.353892700872166e-08, 2.5415570803488663e-07),
        "vectors_second": jnp.clip(jnp.exp(math.log(1.6265965314232744e-05) - 1.3862944 * jax.random.uniform(key_list[20], (VROWS, D), jnp.float32) ** steps_of(key_list[20], (VROWS, D), ((1, 8),), -0.2, 0.2)), 4.066491328558186e-06, 1.6265965314232744e-05),
        "bias_second": jnp.clip(jnp.exp(jax.random.uniform(key_list[21], (CLASSES,), jnp.float32, math.log(4.066491328558186e-06), math.log(1.6265965314232744e-05))), 4.066491328558186e-06, 1.6265965314232744e-05),
    }


HIGHEST = lax.Precision.HIGHEST
DECAY_FIRST = 0.5
DECAY_SECOND = 0.5
LEARN_RATE = 0.03
WEIGHT_DECAY = 0.05
EPSILON = 1e-08

@jax.custom_vjp
def low(v):
    return lax.optimization_barrier(v.astype(jnp.bfloat16)).astype(jnp.float32)

@jax.custom_vjp
def low_back(v):
    return v

def low_keep(v):
    return (low(v), None)

def low_pass(kept, grad):
    return (grad,)

def back_keep(v):
    return (v, None)

def back_low(kept, grad):
    return (low(grad),)
low.defvjp(low_keep, low_pass)
low_back.defvjp(back_keep, back_low)

def normalize(x):
    center = lax.optimization_barrier(jnp.mean(x, -1, keepdims=True))
    shifted = x - center
    return shifted * lax.rsqrt(lax.optimization_barrier(jnp.mean(shifted * shifted, -1, keepdims=True)) + 1e-06)

def product(left, right):
    return jnp.dot(left, right, precision=HIGHEST)

def block(x, wide, downward, rows, up_bias, valid):
    act = low(normalize(x) * rows[0] + rows[1])
    joined = product(act, wide[:, :3 * D])
    query = low_back(low(joined[:, :D] + rows[4]))
    keys = low_back(low(joined[:, D:2 * D]))
    values = low_back(low(joined[:, 2 * D:3 * D] + rows[5]))
    scores = jnp.einsum('qhd,khd->hqk', query.reshape(-1, HEADS, HDIM), keys.reshape(-1, HEADS, HDIM), precision=HIGHEST) * HDIM ** (-0.5)
    scores = jnp.where(valid[None, None, :], low_back(scores), -1e+30)
    top = lax.optimization_barrier(jnp.max(scores, -1, keepdims=True))
    expo = jnp.exp(scores - top)
    probs = low(expo / lax.optimization_barrier(jnp.sum(expo, -1, keepdims=True)))
    mixed = jnp.einsum('hqk,khd->qhd', probs, values.reshape(-1, HEADS, HDIM), precision=HIGHEST).reshape(-1, D)
    mixed = low_back(low(mixed))
    resid = x + low_back(product(mixed, wide[:, 3 * D:4 * D])) + rows[6]
    act_two = low(normalize(resid) * rows[2] + rows[3])
    before = low_back(product(act_two, wide[:, 4 * D:])) + up_bias
    hidden = low(jax.nn.gelu(before, approximate=False))
    return resid + low_back(product(hidden, downward)) + rows[7]

def clip_loss(params, pnorm, valid, flags, weight):
    wide, downward, embed, classw, vec, cbias = params
    wide, downward, embed, classw, vec = (low(wide), low(downward), low(embed), low(classw), low(vec))
    spread_rows = FF // D
    glob = L * 8 + L * spread_rows
    grid = low_back(product(pnorm, embed[NGRID:])) + vec[glob] + embed[:NGRID]
    x = jnp.concatenate([vec[glob + 1:glob + 3], grid], 0)
    for layer in range(L):
        up_bias = vec[L * 8 + layer * spread_rows:L * 8 + (layer + 1) * spread_rows].reshape(FF)
        x = block(x, wide[layer], downward[layer], vec[layer * 8:layer * 8 + 8], up_bias, valid)
    final = normalize(x[:2]) * vec[glob + 3] + vec[glob + 4]
    feature = low(lax.optimization_barrier(jnp.mean(final, 0)))
    logits = low_back(product(feature, classw)) + cbias
    return weight * jnp.sum(jax.nn.softplus(logits) - flags * logits)

def adam(weight, first, second, grad):
    first = DECAY_FIRST * first + (1.0 - DECAY_FIRST) * grad
    second = DECAY_SECOND * second + (1.0 - DECAY_SECOND) * grad * grad
    fix_one = 1.0 - DECAY_FIRST ** STEP
    fix_two = 1.0 - DECAY_SECOND ** STEP
    weight = weight - LEARN_RATE * (first / fix_one / (jnp.sqrt(second / fix_two) + EPSILON) + WEIGHT_DECAY * weight)
    return (weight, first, second)

def reference(patches, column_mask, labels, clip_weights, wide_weights, down_weights, embedding, classifier, vectors, class_bias, wide_first, down_first, embedding_first, classifier_first, vectors_first, bias_first, wide_second, down_second, embedding_second, classifier_second, vectors_second, bias_second):
    pixels = patches.astype(jnp.float32)
    live = column_mask.astype(jnp.float32)[None, :, None]
    count = jnp.sum(column_mask.astype(jnp.float32)) * (FROWS * PATCH)
    center = jnp.sum(pixels * live) / count
    spread = jnp.sum(pixels * pixels * live) / count - center * center
    pnorm = low((pixels - center) * lax.rsqrt(spread + 1e-05))
    pnorm = pnorm.reshape(FROWS, N_TM // 2, 2, CPD, HALF, PATCH).transpose(1, 3, 0, 2, 4, 5).reshape(CLIPS, NGRID, PATCH)
    columns = column_mask.reshape(N_TM // 2, 2, CPD, HALF).transpose(0, 2, 1, 3).reshape(CLIPS, 2 * HALF) > 0
    valid = jnp.concatenate([jnp.ones((CLIPS, 2), bool), jnp.tile(columns, (1, FROWS))], 1)
    weight_total = jnp.sum(clip_weights).astype(jnp.float32)
    flags = labels.astype(jnp.float32)
    weights = clip_weights.astype(jnp.float32)
    params = (wide_weights, down_weights, embedding, classifier, vectors, class_bias)

    def one_clip(carry, index):
        grads, total = carry
        loss, pull = jax.vjp(lambda p: clip_loss(p, pnorm[index], valid[index], flags[index], weights[index]), params)
        grad = pull(jnp.ones_like(loss) / weight_total)[0]
        return ((jax.tree.map(jnp.add, grads, grad), total + loss), None)
    start = (jax.tree.map(jnp.zeros_like, params), jnp.zeros((), jnp.float32))
    (grads, loss_sum), _ = lax.scan(one_clip, start, jnp.arange(CLIPS))
    grad_norm = jnp.sqrt(sum((jnp.sum(g * g) for g in grads)))
    coef = jnp.minimum(1.0, 1.0 / (grad_norm + 1e-06))
    firsts = (wide_first, down_first, embedding_first, classifier_first, vectors_first, bias_first)
    seconds = (wide_second, down_second, embedding_second, classifier_second, vectors_second, bias_second)
    news = [adam(w, m, v, g * coef) for w, m, v, g in zip(params, firsts, seconds, grads)]
    masters = tuple((n[0] for n in news))
    first_new = tuple((n[1] for n in news))
    second_new = tuple((n[2] for n in news))
    return (masters[0], masters[1], masters[2], masters[3], masters[4], masters[5], first_new[0], first_new[1], first_new[2], first_new[3], first_new[4], first_new[5], second_new[0], second_new[1], second_new[2], second_new[3], second_new[4], second_new[5], masters[0].astype(jnp.bfloat16), masters[1].astype(jnp.bfloat16), masters[2].astype(jnp.bfloat16), masters[3].astype(jnp.bfloat16), grad_norm, loss_sum, weight_total)
```

```python
import functools

import jax
import jax.numpy as jnp
from jax import lax
from jax.experimental import pallas as pl
from jax.experimental.pallas import tpu as pltpu
from jax.sharding import PartitionSpec as P

D = 768
HEADS = 12
HDIM = 64
FF = 3072
L = 2
FROWS = 12
HALF = 52
PATCH = 256
STEP = 5
CPD = 2
NGRID = FROWS * 2 * HALF
CLASSES = 527
VROWS = 29
GLOB = L * 8 + L * (FF // D)

TOK = 320
PER = 3
NF = 4

DECAY_FIRST = 0.5
DECAY_SECOND = 0.5
LEARN_RATE = 0.03
WEIGHT_DECAY = 0.05
EPSILON = 1e-08

MESH = pl.DeviceIdType.MESH
BF = jnp.bfloat16
F32 = jnp.float32
VLIM = 60 * 1024 * 1024
VM = pltpu.VMEM


def nn(a, b):
    return lax.dot_general(a, b, (((1,), (0,)), ((), ())), preferred_element_type=F32)


def nt(a, b):
    return lax.dot_general(a, b, (((1,), (1,)), ((), ())), preferred_element_type=F32)


def tn(a, b):
    return lax.dot_general(a, b, (((0,), (0,)), ((), ())), preferred_element_type=F32)


def norm_rows(x):
    center = jnp.mean(x, -1, keepdims=True)
    shifted = x - center
    scale = lax.rsqrt(jnp.mean(shifted * shifted, -1, keepdims=True) + 1e-06)
    return (shifted * scale, scale)


def norm_back(dnorm, normed, scale):
    return scale * (
        dnorm
        - jnp.mean(dnorm, -1, keepdims=True)
        - normed * jnp.mean(dnorm * normed, -1, keepdims=True)
    )


def vspec():
    return pl.BlockSpec(memory_space=VM)


def aspec():
    return pl.BlockSpec(memory_space=pl.ANY)


def place():
    f, t = lax.axis_index("freq"), lax.axis_index("tm")
    return f, t, f // 2, f % 2, t // 2, t % 2


def remote(src, dst, ssem, rsem, dev):
    return pltpu.make_async_remote_copy(
        src_ref=src, dst_ref=dst, send_sem=ssem, recv_sem=rsem, device_id=dev, device_id_type=MESH
    )


def greet_all(times):
    f, t = lax.axis_index("freq"), lax.axis_index("tm")
    n = NF * times
    me = f * times + t
    barrier = pltpu.get_barrier_semaphore()

    def hello(i, carry):
        other = (me + i) % n
        pl.semaphore_signal(
            barrier, inc=1, device_id=(other // times, other % times), device_id_type=MESH
        )
        return carry

    lax.fori_loop(1, n, hello, 0)
    pl.semaphore_wait(barrier, n - 1)


def spread_small(times, small, gathered, ssem, rsem):
    f, t = lax.axis_index("freq"), lax.axis_index("tm")
    n = NF * times
    me = f * times + t

    def send(i, carry):
        other = (me + i) % n
        remote(
            small, gathered.at[me], ssem, rsem, (other // times, other % times)
        ).start()
        return carry

    lax.fori_loop(1, n, send, 0)
    gathered[me] = small[...]


def wait_small(times, gathered, ssem, rsem):
    n = NF * times
    many = gathered.at[pl.ds(0, n - 1)]
    pltpu.make_async_copy(many, many, rsem).wait()
    pltpu.make_async_copy(many, many, ssem).wait()


GROUPS = (("c", 4), ("c", 0), ("c", 1), ("d", 0), ("c", 2), ("c", 3), ("d", 1))
SUBS = tuple((kind, idx, h) for kind, idx in GROUPS for h in (0, 1))


def gather_kernel(
    times, ucol, udown, stats, psend, ocol, odown, sall, precv,
    zs, zr, own, s1, r1, s2, r2, s3, r3, ss, sr, ps, pr,
):
    f, t, y, c, g, x = place()
    count = times // 2
    greet_all(times)
    spread_small(times, stats, sall, ss, sr)
    swap = remote(psend, precv, ps, pr, (f, g * 2 + 1 - x))
    swap.start()
    every = slice(None)

    def source(s):
        kind, idx, h = SUBS[s]
        if kind == "c":
            return ucol.at[idx, y, c, :, pl.ds(h * 384, 384)]
        return udown.at[idx, y, pl.ds(h * 96, 96), pl.ds(pl.multiple_of(c * 384, 128), 384)]

    def view(s, yy, zz, xx):
        kind, idx, h = SUBS[s]
        if kind == "c":
            return ocol.at[idx, yy, c, zz, xx, :, pl.ds(h * 384, 384)]
        return odown.at[
            idx, zz, xx, yy, pl.ds(h * 96, 96), pl.ds(pl.multiple_of(c * 384, 128), 384)
        ]

    def along(s, dz):
        return remote(
            source(s), view(s, y, g, x), zs.at[s, dz - 1], zr.at[s, dz - 1],
            (f, ((g + dz) % count) * 2 + x),
        )

    def keep(s):
        return pltpu.make_async_copy(source(s), view(s, y, g, x), own.at[s])

    over_x = (f, g * 2 + 1 - x)
    over_y = ((1 - y) * 2 + c, t)
    over_c = (y * 2 + 1 - c, t)

    def first(s):
        block = view(s, y, every, x)
        return remote(block, block, s1.at[s], r1.at[s], over_x if s % 2 == 0 else over_y)

    def second(s):
        block = view(s, y, every, every) if s % 2 == 0 else view(s, every, every, x)
        return remote(block, block, s2.at[s], r2.at[s], over_y if s % 2 == 0 else over_x)

    def third(s):
        block = view(s, every, every, every)
        return remote(block, block, s3.at[s], r3.at[s], over_c)

    total = len(SUBS)
    for s in range(total):
        keep(s).start()
        for dz in range(1, count):
            along(s, dz).start()
    for step in range(total + 3):
        if step < total:
            for dz in range(1, count):
                along(step, dz).wait_recv()
            keep(step).wait()
            first(step).start()
        if 0 <= step - 1 < total:
            first(step - 1).wait_recv()
            second(step - 1).start()
        if 0 <= step - 2 < total:
            second(step - 2).wait_recv()
            third(step - 2).start()
        if 0 <= step - 3 < total:
            third(step - 3).wait_recv()
    for s in range(total):
        for dz in range(1, count):
            along(s, dz).wait_send()
        first(s).wait_send()
        second(s).wait_send()
        third(s).wait_send()
    swap.wait()
    wait_small(times, sall, ss, sr)


def gather_weights(times, ucol, udown, stats, psend):
    count = times // 2
    total = len(SUBS)
    dma = pltpu.SemaphoreType.DMA
    return pl.pallas_call(
        functools.partial(gather_kernel, times),
        out_shape=(
            jax.ShapeDtypeStruct((2 * L + 1, 2, 2, count, 2, 96, D), BF),
            jax.ShapeDtypeStruct((L, count, 2, 2, 192, D), BF),
            jax.ShapeDtypeStruct((NF * times, 8, 128), F32),
            jax.ShapeDtypeStruct(psend.shape, BF),
        ),
        in_specs=[vspec()] * 4,
        out_specs=(aspec(), aspec(), vspec(), vspec()),
        scratch_shapes=[
            dma((total, count - 1)), dma((total, count - 1)), dma((total,)),
            dma((total,)), dma((total,)), dma((total,)), dma((total,)), dma((total,)), dma((total,)),
            dma, dma, dma, dma,
        ],
        compiler_params=pltpu.CompilerParams(
            collective_id=1, has_side_effects=True, vmem_limit_bytes=32 * 1024 * 1024
        ),
        name="gather_weights",
    )(ucol, udown, stats, psend)


QROWS = TOK + TOK // 2


def greet_clip():
    f, t = lax.axis_index("freq"), lax.axis_index("tm")
    barrier = pltpu.get_barrier_semaphore()
    for i in range(1, NF):
        pl.semaphore_signal(barrier, inc=1, device_id=((f + i) % NF, t), device_id_type=MESH)
    pl.semaphore_wait(barrier, NF - 1)


def pack_half(v):
    return jnp.concatenate([v[: TOK // 2], v[TOK // 2 :]], 1)


def open_half(v):
    return jnp.concatenate([v[:, :HDIM], v[:, HDIM:]], 0)


def forward_kernel(
    layer, x_ref, rows_ref, upb_ref, mask_ref, wcol, wdown,
    xo_ref, x1_ref, fa_ref, gp_ref, qk_ref,
    wbuf, dbuf, qsend, osend, orecv, kall, vall, acc, wsem, qs, qr, os, orr,
):
    f, t = lax.axis_index("freq"), lax.axis_index("tm")
    loads = [
        pltpu.make_async_copy(wcol.at[2 * layer], wbuf.at[0], wsem.at[0]),
        pltpu.make_async_copy(wcol.at[2 * layer + 1], wbuf.at[1], wsem.at[1]),
        pltpu.make_async_copy(wdown.at[layer], dbuf, wsem.at[2]),
    ]
    for load in loads:
        load.start()
    x = x_ref[...]
    normed, _ = norm_rows(x)
    act = (normed * rows_ref[0:1, :] + rows_ref[1:2, :]).astype(BF)
    fa_ref[0] = act
    greet_clip()
    loads[0].wait()

    def to_clip(j, i):
        other = (f + i) % NF
        return remote(qsend.at[j, other], qk_ref.at[j, f], qs.at[j, i - 1], qr.at[j, i - 1], (other, t))

    def back_clip(j, i):
        other = (f + i) % NF
        return remote(osend.at[j, other], orecv.at[j, f], os.at[j, i - 1], orr.at[j, i - 1], (other, t))

    for j in range(PER):
        cols = slice(256 * j, 256 * (j + 1))
        query = (nn(act, wbuf[0, 0, :, cols]) + rows_ref[4:5, cols]).astype(BF)
        key = nn(act, wbuf[0, 1, :, cols]).astype(BF)
        value = (nn(act, wbuf[0, 2, :, cols]) + rows_ref[5:6, cols]).astype(BF)
        for h in range(NF):
            part = slice(HDIM * h, HDIM * (h + 1))
            qsend[j, h, :TOK] = jnp.concatenate([query[:, part], key[:, part]], 1)
            qsend[j, h, TOK:] = pack_half(value[:, part])
        for i in range(1, NF):
            to_clip(j, i).start()
        qk_ref[j, f] = qsend[j, f]
    mask = mask_ref[...]
    for j in range(PER):
        for i in range(1, NF):
            to_clip(j, i).wait_recv()
        for s in range(NF):
            kall[s * TOK : (s + 1) * TOK] = qk_ref[j, s, :TOK, HDIM:]
            vall[s * TOK : (s + 1) * TOK] = open_half(qk_ref[j, s, TOK:])

        def attend(i, carry):
            s = (f + i) % NF
            halves = []
            for h in range(2):
                lo = h * (TOK // 2)
                q = qk_ref[j, s, lo : lo + TOK // 2, :HDIM]
                scores = nt(q, kall[...]) * (HDIM ** (-0.5)) + mask
                top = jnp.max(scores, -1, keepdims=True)
                expo = jnp.exp(scores - top)
                total = jnp.sum(expo, -1, keepdims=True)
                probs = (expo * (1.0 / total)).astype(BF)
                halves.append(nn(probs, vall[...]).astype(BF))
            osend[j, s] = jnp.concatenate(halves, 1)

            @pl.when(i > 0)
            def _():
                remote(
                    osend.at[j, s], orecv.at[j, f], os.at[j, i - 1], orr.at[j, i - 1], (s, t)
                ).start()

            return carry

        lax.fori_loop(1, NF, attend, 0)
        lax.fori_loop(0, 1, attend, 0)
        orecv[j, f] = osend[j, f]
    for load in loads[1:]:
        load.wait()
    parts = []
    for j in range(PER):
        for i in range(1, NF):
            back_clip(j, i).wait_recv()
        for h in range(NF):
            parts.append(open_half(orecv[j, h]))
    mixed = jnp.concatenate(parts, 1)
    fa_ref[1] = mixed
    resid = x_ref[...] + nn(mixed, wbuf[0, 3]) + rows_ref[6:7, :]
    x1_ref[...] = resid
    normed, _ = norm_rows(resid)
    act = (normed * rows_ref[2:3, :] + rows_ref[3:4, :]).astype(BF)
    fa_ref[2] = act
    acc[...] = resid + rows_ref[7:8, :]

    def mlp(k, carry):
        before = nn(fa_ref[2], wbuf[1, k]) + upb_ref[k]
        lower = 0.5 * (1.0 + lax.erf(before * 0.7071067811865476))
        gp_ref[k] = lower + before * jnp.exp(-0.5 * before * before) * 0.3989422804014327
        hidden = (before * lower).astype(BF)
        fa_ref[3 + k] = hidden
        acc[...] += nn(hidden, dbuf[pl.ds(pl.multiple_of(k * D, D), D)])
        return carry

    lax.fori_loop(0, FF // D, mlp, 0)
    xo_ref[...] = acc[...]
    for j in range(PER):
        for i in range(1, NF):
            to_clip(j, i).wait_send()
            back_clip(j, i).wait_send()


def forward_layer(layer, x, rows, up_bias, mask, wcol, wdown):
    dma = pltpu.SemaphoreType.DMA
    return pl.pallas_call(
        functools.partial(forward_kernel, layer),
        out_shape=(
            jax.ShapeDtypeStruct((TOK, D), F32),
            jax.ShapeDtypeStruct((TOK, D), F32),
            jax.ShapeDtypeStruct((7, TOK, D), BF),
            jax.ShapeDtypeStruct((FF // D, TOK, D), F32),
            jax.ShapeDtypeStruct((PER, NF, QROWS, 128), BF),
        ),
        in_specs=[vspec()] * 4 + [aspec()] * 2,
        out_specs=(vspec(),) * 5,
        scratch_shapes=[
            VM((2, 4, D, D), BF),
            VM((FF, D), BF),
            VM((PER, NF, QROWS, 128), BF),
            VM((PER, NF, TOK // 2, 128), BF),
            VM((PER, NF, TOK // 2, 128), BF),
            VM((NF * TOK, HDIM), BF),
            VM((NF * TOK, HDIM), BF),
            VM((TOK, D), F32),
            dma((3,)),
            dma((PER, NF - 1)), dma((PER, NF - 1)), dma((PER, NF - 1)), dma((PER, NF - 1)),
        ],
        compiler_params=pltpu.CompilerParams(
            collective_id=2 + layer, has_side_effects=True, vmem_limit_bytes=VLIM
        ),
        name="forward_layer",
    )(x, rows, up_bias, mask, wcol, wdown)


def backward_kernel(
    layer, dout_ref, x_ref, x1_ref, gp_ref, qk_ref, rows_ref, mask_ref, wcol, wdown,
    dx_ref, ba_ref, rowg_ref, upg_ref,
    wbuf, dbuf, dsend, drecv, gsend, grecv, kall, vall, dkall, dvall, dqall, acc,
    wsem, ds_, dr_, gs_, gr_,
):
    f, t = lax.axis_index("freq"), lax.axis_index("tm")
    loads = [
        pltpu.make_async_copy(wdown.at[layer], dbuf, wsem.at[0]),
        pltpu.make_async_copy(wcol.at[2 * layer + 1], wbuf.at[1], wsem.at[1]),
        pltpu.make_async_copy(wcol.at[2 * layer], wbuf.at[0], wsem.at[2]),
    ]
    for load in loads:
        load.start()
    dout = dout_ref[...]
    ba_ref[8] = dout.astype(BF)
    rowg_ref[7:8, :] = jnp.sum(dout, 0, keepdims=True)
    acc[...] = jnp.zeros_like(acc)
    greet_clip()
    loads[0].wait()
    loads[1].wait()

    def mlp(k, carry):
        dhidden = nt(ba_ref[8], dbuf[pl.ds(pl.multiple_of(k * D, D), D)])
        dbefore = dhidden * gp_ref[k]
        upg_ref[k] = jnp.sum(dbefore, 0, keepdims=True)
        low = dbefore.astype(BF)
        ba_ref[4 + k] = low
        acc[...] += nt(low, wbuf[1, k])
        return carry

    lax.fori_loop(0, FF // D, mlp, 0)
    normed, scale = norm_rows(x1_ref[...])
    dact = acc[...]
    rowg_ref[2:3, :] = jnp.sum(dact * normed, 0, keepdims=True)
    rowg_ref[3:4, :] = jnp.sum(dact, 0, keepdims=True)
    dresid = dout_ref[...] + norm_back(dact * rows_ref[2:3, :], normed, scale)
    rowg_ref[6:7, :] = jnp.sum(dresid, 0, keepdims=True)
    acc[...] = dresid
    low = dresid.astype(BF)
    ba_ref[3] = low
    loads[2].wait()
    dmixed = nt(low, wbuf[0, 3]).astype(BF)

    def to_clip(j, i):
        other = (f + i) % NF
        return remote(dsend.at[j, other], drecv.at[j, f], ds_.at[j, i - 1], dr_.at[j, i - 1], (other, t))

    def back_clip(j, i):
        other = (f + i) % NF
        return remote(gsend.at[j, other], grecv.at[j, f], gs_.at[j, i - 1], gr_.at[j, i - 1], (other, t))

    for j in range(PER):
        for h in range(NF):
            lo = 256 * j + HDIM * h
            dsend[j, h] = pack_half(dmixed[:, lo : lo + HDIM])
        for i in range(1, NF):
            to_clip(j, i).start()
        drecv[j, f] = dsend[j, f]
    mask = mask_ref[...]
    root = HDIM ** (-0.5)
    for j in range(PER):
        for s in range(NF):
            kall[s * TOK : (s + 1) * TOK] = qk_ref[j, s, :TOK, HDIM:]
            vall[s * TOK : (s + 1) * TOK] = open_half(qk_ref[j, s, TOK:])
        dkall[...] = jnp.zeros_like(dkall)
        dvall[...] = jnp.zeros_like(dvall)
        for i in range(1, NF):
            to_clip(j, i).wait_recv()

        def attend(s, carry):
            q = qk_ref[j, s, :TOK, :HDIM]
            dmix = open_half(drecv[j, s])
            scores = nt(kall[...], q) * root + mask
            top = jnp.max(scores, 0, keepdims=True)
            expo = jnp.exp(scores - top)
            probs = expo * (1.0 / jnp.sum(expo, 0, keepdims=True))
            dprob = nt(vall[...], dmix)
            inner = jnp.sum(probs * dprob, 0, keepdims=True)
            dscore = (probs * (dprob - inner)).astype(BF)
            dvall[...] += nn(probs.astype(BF), dmix)
            dkall[...] += nn(dscore, q)
            dqall[s] = (tn(dscore, kall[...]) * root).astype(BF)
            return carry

        lax.fori_loop(0, NF, attend, 0)
        for s in range(NF):
            span = slice(s * TOK, (s + 1) * TOK)
            gsend[j, s, :TOK] = jnp.concatenate(
                [dqall[s], (dkall[span] * root).astype(BF)], 1
            )
            gsend[j, s, TOK:] = pack_half(dvall[span].astype(BF))
        for i in range(1, NF):
            back_clip(j, i).start()
        grecv[j, f] = gsend[j, f]
    for j in range(PER):
        for i in range(1, NF):
            back_clip(j, i).wait_recv()
        cols = slice(256 * j, 256 * (j + 1))
        ba_ref[0, :, cols] = jnp.concatenate([grecv[j, h, :TOK, :HDIM] for h in range(NF)], 1)
        ba_ref[1, :, cols] = jnp.concatenate([grecv[j, h, :TOK, HDIM:] for h in range(NF)], 1)
        ba_ref[2, :, cols] = jnp.concatenate([open_half(grecv[j, h, TOK:]) for h in range(NF)], 1)
    rowg_ref[4:5, :] = jnp.sum(ba_ref[0].astype(F32), 0, keepdims=True)
    rowg_ref[5:6, :] = jnp.sum(ba_ref[2].astype(F32), 0, keepdims=True)
    dact = nt(ba_ref[0], wbuf[0, 0]) + nt(ba_ref[1], wbuf[0, 1]) + nt(ba_ref[2], wbuf[0, 2])
    normed, scale = norm_rows(x_ref[...])
    rowg_ref[0:1, :] = jnp.sum(dact * normed, 0, keepdims=True)
    rowg_ref[1:2, :] = jnp.sum(dact, 0, keepdims=True)
    dx_ref[...] = acc[...] + norm_back(dact * rows_ref[0:1, :], normed, scale)
    for j in range(PER):
        for i in range(1, NF):
            to_clip(j, i).wait_send()
            back_clip(j, i).wait_send()


def backward_layer(layer, dout, x, x1, gp, qk, rows, mask, wcol, wdown):
    dma = pltpu.SemaphoreType.DMA
    return pl.pallas_call(
        functools.partial(backward_kernel, layer),
        out_shape=(
            jax.ShapeDtypeStruct((TOK, D), F32),
            jax.ShapeDtypeStruct((9, TOK, D), BF),
            jax.ShapeDtypeStruct((8, D), F32),
            jax.ShapeDtypeStruct((FF // D, 1, D), F32),
        ),
        in_specs=[vspec()] * 7 + [aspec()] * 2,
        out_specs=(vspec(),) * 4,
        scratch_shapes=[
            VM((2, 4, D, D), BF),
            VM((FF, D), BF),
            VM((PER, NF, TOK // 2, 128), BF),
            VM((PER, NF, TOK // 2, 128), BF),
            VM((PER, NF, QROWS, 128), BF),
            VM((PER, NF, QROWS, 128), BF),
            VM((NF * TOK, HDIM), BF),
            VM((NF * TOK, HDIM), BF),
            VM((NF * TOK, HDIM), F32),
            VM((NF * TOK, HDIM), F32),
            VM((NF, TOK, HDIM), BF),
            VM((TOK, D), F32),
            dma((3,)),
            dma((PER, NF - 1)), dma((PER, NF - 1)), dma((PER, NF - 1)), dma((PER, NF - 1)),
        ],
        compiler_params=pltpu.CompilerParams(
            collective_id=2 + L + layer, has_side_effects=True, vmem_limit_bytes=VLIM
        ),
        name="backward_layer",
    )(dout, x, x1, gp, qk, rows, mask, wcol, wdown)


RGROUPS = (("d", 1), ("u", 1), ("q", 1), ("d", 0), ("u", 0), ("q", 0), ("m", 0))


def reduce_kernel(
    times, fa0, fa1, ba0, ba1, ma, small,
    gcol, gdown, small_all, square_all, rfa0, rfa1, rba0, rba1, rma,
    lbuf, rbuf, full, low, recv1, mid_own, mid_low, recv2, zlow, zown, zrecv, sq,
    ls, cs, cr, s1, r1, s2, r2, zs, zr, fs, fr, ks, kr, ss, sr, qs, qr,
):
    f, t, y, c, g, x = place()
    count = times // 2
    over_x = (f, g * 2 + 1 - x)
    over_y = ((1 - y) * 2 + c, t)
    over_c = (y * 2 + 1 - c, t)
    total = len(RGROUPS)
    fas, rfas = (fa0, fa1), (rfa0, rfa1)
    bas, rbas = (ba0, ba1), (rba0, rba1)
    greet_all(times)

    def operands(gi, core):
        kind, l = RGROUPS[gi]
        out = []
        if kind == "d":
            for k in range(4):
                out.append((fas[l], rfas[l], 3 + k, None, lbuf, k))
            out.append((bas[l], rbas[l], 8, pl.ds(pl.multiple_of(core * 384, 128), 384), rbuf, 0))
            return out
        for role in range(2):
            yy = y if role == 0 else 1 - y
            if kind == "u":
                if role == 0:
                    out.append((fas[l], rfas[l], 2, None, lbuf, 0))
                out.append((bas[l], rbas[l], 4 + 2 * yy + core, None, rbuf, role))
            elif kind == "q":
                out.append((fas[l], rfas[l], yy * core, None, lbuf, role))
                out.append((bas[l], rbas[l], 2 * yy + core, None, rbuf, role))
            else:
                out.append((ma, rma, 3 * yy, None, lbuf, role))
                out.append((ma, rma, 1 + core + 3 * yy, None, rbuf, role))
        return out

    def swaps(gi):
        kind, l = RGROUPS[gi]
        co = 1 - c
        if kind == "d":
            pairs = [(fas[l], rfas[l], pl.ds(3, 4), None)]
            pairs.append((bas[l], rbas[l], 8, pl.ds(pl.multiple_of(co * 384, 128), 384)))
        elif kind == "u":
            pairs = [(fas[l], rfas[l], 2, None)]
            pairs += [(bas[l], rbas[l], 4 + 2 * yy + co, None) for yy in range(2)]
        elif kind == "q":
            pairs = [(fas[l], rfas[l], pl.ds(0, 2), None)]
            pairs += [(bas[l], rbas[l], 2 * yy + co, None) for yy in range(2)]
        else:
            pairs = [(ma, rma, 3 * yy, None) for yy in range(2)]
            pairs += [(ma, rma, 1 + co + 3 * yy, None) for yy in range(2)]
        out = []
        for n, (src, dst, idx, cols) in enumerate(pairs):
            if cols is None:
                a, b = src.at[idx], dst.at[idx]
            else:
                a, b = src.at[idx, :, cols], dst.at[idx, :, cols]
            out.append(remote(a, b, cs.at[gi, n], cr.at[gi, n], over_c))
        return out

    def loads(gi, received):
        slot = gi % 2
        out = []
        for n, (mine, other, idx, cols, buf, where) in enumerate(operands(gi, c)):
            src = other if received else mine
            rows = pl.ds(TOK, TOK) if received else pl.ds(0, TOK)
            if cols is None:
                a, b = src.at[idx], buf.at[slot, where, rows]
            else:
                a, b = src.at[idx, :, cols], buf.at[slot, where, rows, pl.ds(0, 384)]
            out.append(pltpu.make_async_copy(a, b, ls.at[slot, 1 if received else 0, n]))
        return out

    def step1(gi, h):
        slot = gi % 2
        block = low.at[slot, 0, 1] if h == 0 else low.at[slot, 1, :, 1 - x]
        return remote(
            block, recv1.at[gi, h], s1.at[gi, h], r1.at[gi, h], over_y if h == 0 else over_x
        )

    def step2(gi, h):
        slot = gi % 2
        return remote(
            mid_low.at[slot, h], recv2.at[gi, h], s2.at[gi, h], r2.at[gi, h],
            over_x if h == 0 else over_y,
        )

    def along(gi, dz):
        slot = gi % 2
        return remote(
            zlow.at[slot, (g + dz) % count], zrecv.at[gi, dz - 1], zs.at[gi, dz - 1], zr.at[gi, dz - 1],
            (f, ((g + dz) % count) * 2 + x),
        )

    def result(gi, yy):
        kind, l = RGROUPS[gi]
        if kind == "d":
            return gdown.at[l, yy, :, pl.ds(pl.multiple_of(c * 384, 128), 384)]
        idx = 4 if kind == "m" else 2 * l + (1 if kind == "u" else 0)
        return gcol.at[idx, yy, c]

    def spread_y(gi):
        block = result(gi, y)
        return remote(block, block, fs.at[gi], fr.at[gi], over_y)

    def spread_c(gi):
        block = result(gi, slice(None))
        return remote(block, block, ks.at[gi], kr.at[gi], over_c)

    def compute(gi):
        kind, _ = RGROUPS[gi]
        slot = gi % 2
        if kind == "d":
            def one(z, carry):
                prod = tn(lbuf[slot, z], rbuf[slot, 0, :, :384])
                prod = prod.reshape(2, 2, 2, 96, 384)
                for xx in range(2):
                    for yy in range(2):
                        role = (yy + y) % 2
                        for h in range(2):
                            full[slot, h, role, xx, z] = prod[xx, yy, h]
                            low[slot, h, role, xx, z] = prod[xx, yy, h].astype(BF)
                return carry

            lax.fori_loop(0, count, one, 0)
            return

        def role_loop(role, carry):
            lrole = role * 0 if kind == "u" else role
            for h in range(2):
                prod = tn(lbuf[slot, lrole], rbuf[slot, role, :, h * 384 : (h + 1) * 384])
                prod = prod.reshape(count, 2, 96, 384)
                for xx in range(2):
                    full[slot, h, role, xx] = prod[:, xx]
                    low[slot, h, role, xx] = prod[:, xx].astype(BF)
            return carry

        lax.fori_loop(0, 2, role_loop, 0)

    spread_small(times, small, small_all, ss, sr)
    for gi in range(total):
        for copy in swaps(gi):
            copy.start()
    sq[...] = jnp.zeros_like(sq)

    def begin_loads(gi):
        for copy in loads(gi, False):
            copy.start()
        for copy in swaps(gi):
            copy.wait_recv()
        for copy in loads(gi, True):
            copy.start()

    begin_loads(0)
    for step in range(total + 5):
        gi = step
        if gi < total:
            slot = gi % 2
            for copy in loads(gi, False) + loads(gi, True):
                copy.wait()
            if gi + 1 < total:
                begin_loads(gi + 1)
            if gi >= 2:
                for h in range(2):
                    step1(gi - 2, h).wait_send()
            compute(gi)
            for h in range(2):
                step1(gi, h).start()
        gi = step - 1
        if 0 <= gi < total:
            slot = gi % 2
            if gi >= 2:
                for h in range(2):
                    step2(gi - 2, h).wait_send()
            step1(gi, 0).wait_recv()
            mid_low[slot, 0] = (full[slot, 0, 0, 1 - x] + recv1[gi, 0, 1 - x].astype(F32)).astype(BF)
            step2(gi, 0).start()
            mid_own[slot, 0] = full[slot, 0, 0, x] + recv1[gi, 0, x].astype(F32)
            step1(gi, 1).wait_recv()
            mid_low[slot, 1] = (full[slot, 1, 1, x] + recv1[gi, 1, 1].astype(F32)).astype(BF)
            step2(gi, 1).start()
            mid_own[slot, 1] = full[slot, 1, 0, x] + recv1[gi, 1, 0].astype(F32)
        gi = step - 2
        if 0 <= gi < total:
            slot = gi % 2
            if gi >= 2:
                for dz in range(1, count):
                    along(gi - 2, dz).wait_send()
            for h in range(2):
                step2(gi, h).wait_recv()
                summed = mid_own[slot, h] + recv2[gi, h].astype(F32)
                zlow[slot, :, h] = summed.astype(BF)
                mid_own[slot, h] = summed
            for dz in range(1, count):
                along(gi, dz).start()
            for h in range(2):
                zown[slot, h] = mid_own[slot, h, g]
        gi = step - 3
        if 0 <= gi < total:
            slot = gi % 2
            for dz in range(1, count):
                along(gi, dz).wait_recv()
            for h in range(2):
                value = zown[slot, h]
                for dz in range(1, count):
                    value = value + zrecv[gi, dz - 1, h].astype(F32)
                sq[...] += jnp.sum((value * value).reshape(12, 8, 384), 0)
                kind, l = RGROUPS[gi]
                if kind == "d":
                    spot = pl.ds(pl.multiple_of(c * 384, 128), 384)
                    gdown[l, y, h * 96 : (h + 1) * 96, spot] = value.astype(BF)
                else:
                    idx = 4 if kind == "m" else 2 * l + (1 if kind == "u" else 0)
                    gcol[idx, y, c, :, h * 384 : (h + 1) * 384] = value.astype(BF)
            spread_y(gi).start()
        gi = step - 4
        if 0 <= gi < total:
            spread_y(gi).wait_recv()
            spread_c(gi).start()
        if step == total + 2:
            value = sq[...]
            sq[:, :128] = value[:, :128] + value[:, 128:256] + value[:, 256:]
            part = sq.at[:, pl.ds(0, 128)]
            n = NF * times
            me = f * times + t

            def send(i, carry):
                other = (me + i) % n
                remote(part, square_all.at[me], qs, qr, (other // times, other % times)).start()
                return carry

            lax.fori_loop(1, n, send, 0)
            square_all[me] = sq[:, :128]
    for gi in range(total):
        spread_c(gi).wait_recv()
        for copy in swaps(gi):
            copy.wait_send()
        spread_y(gi).wait_send()
        spread_c(gi).wait_send()
    for gi in range(total - 2, total):
        for h in range(2):
            step1(gi, h).wait_send()
            step2(gi, h).wait_send()
        for dz in range(1, count):
            along(gi, dz).wait_send()
    wait_small(times, small_all, ss, sr)
    wait_small(times, square_all, qs, qr)


def reduce_grads(times, fa, ba, ma, small):
    count = times // 2
    n = NF * times
    total = len(RGROUPS)
    dma = pltpu.SemaphoreType.DMA
    return pl.pallas_call(
        functools.partial(reduce_kernel, times),
        out_shape=(
            jax.ShapeDtypeStruct((2 * L + 1, 2, 2, 96, D), BF),
            jax.ShapeDtypeStruct((L, 2, 192, D), BF),
            jax.ShapeDtypeStruct((n, 8, 128), F32),
            jax.ShapeDtypeStruct((n, 8, 128), F32),
            jax.ShapeDtypeStruct(fa[0].shape, BF),
            jax.ShapeDtypeStruct(fa[1].shape, BF),
            jax.ShapeDtypeStruct(ba[0].shape, BF),
            jax.ShapeDtypeStruct(ba[1].shape, BF),
            jax.ShapeDtypeStruct(ma.shape, BF),
        ),
        in_specs=[aspec()] * 5 + [vspec()],
        out_specs=(vspec(),) * 4 + (aspec(),) * 5,
        scratch_shapes=[
            VM((2, 4, 2 * TOK, D), BF),
            VM((2, 2, 2 * TOK, D), BF),
            VM((2, 2, 2, 2, count, 96, 384), F32),
            VM((2, 2, 2, 2, count, 96, 384), BF),
            VM((total, 2, 2, count, 96, 384), BF),
            VM((2, 2, count, 96, 384), F32),
            VM((2, 2, count, 96, 384), BF),
            VM((total, 2, count, 96, 384), BF),
            VM((2, count, 2, 96, 384), BF),
            VM((2, 2, 96, 384), F32),
            VM((total, count - 1, 2, 96, 384), BF),
            VM((8, 384), F32),
            dma((2, 2, 8)),
            dma((total, 4)), dma((total, 4)),
            dma((total, 2)), dma((total, 2)), dma((total, 2)), dma((total, 2)),
            dma((total, count - 1)), dma((total, count - 1)),
            dma((total,)), dma((total,)), dma((total,)), dma((total,)),
            dma, dma, dma, dma,
        ],
        compiler_params=pltpu.CompilerParams(
            collective_id=2 + 2 * L, has_side_effects=True, vmem_limit_bytes=VLIM
        ),
        name="reduce_grads",
    )(fa[0], fa[1], ba[0], ba[1], ma, small)[:4]


def adam(weight, first, second, grad):
    first = DECAY_FIRST * first + (1.0 - DECAY_FIRST) * grad
    second = DECAY_SECOND * second + (1.0 - DECAY_SECOND) * grad * grad
    fix_one = 1.0 - DECAY_FIRST**STEP
    fix_two = 1.0 - DECAY_SECOND**STEP
    weight = weight - LEARN_RATE * (
        first / fix_one / (jnp.sqrt(second / fix_two) + EPSILON) + WEIGHT_DECAY * weight
    )
    return (weight, first, second)


def pad_to(v, axis, size):
    pads = [(0, 0)] * v.ndim
    pads[axis] = (0, size - v.shape[axis])
    return jnp.pad(v, pads)


def local(
    patches, column_mask, labels, clip_weights, wide_weights, down_weights, embedding, classifier,
    vectors, class_bias, wide_first, down_first, embedding_first, classifier_first, vectors_first,
    bias_first, wide_second, down_second, embedding_second, classifier_second, vectors_second,
    bias_second,
):
    times = lax.axis_size("tm")
    f, t = lax.axis_index("freq"), lax.axis_index("tm")
    half = t % 2
    pair = t // 2
    rows_dev = FROWS // NF
    kernels = D // times == 96
    shard = D // times
    columns = column_mask.reshape(times, CPD, HALF) > 0
    mine_columns = lax.dynamic_index_in_dim(columns, t, 0, keepdims=False)
    raw = patches.reshape(rows_dev, CPD, HALF, PATCH)

    pixels = raw.astype(F32)
    live = mine_columns.astype(F32)[None, :, :, None]
    sums = jnp.stack(
        [
            jnp.sum(pixels * live),
            jnp.sum(pixels * pixels * live),
            jnp.sum(live) * (rows_dev * PATCH),
        ]
    )
    keep_block = lax.dynamic_index_in_dim(raw, half, 1, keepdims=False)
    give_block = lax.dynamic_index_in_dim(raw, 1 - half, 1, keepdims=False)
    give_block = pad_to(give_block.reshape(rows_dev * HALF, PATCH), 0, 160)

    wide_low = wide_weights.astype(BF)
    down_low = down_weights.astype(BF)
    embed_t = pad_to(embedding.astype(BF).T, 1, 2 * D)
    class_vec = jnp.concatenate([classifier.astype(BF), vectors.astype(BF).T], 1)
    class_vec = pad_to(class_vec, 1, D)
    if kernels:
        units = jnp.concatenate(
            [
                wide_low.reshape(L, shard, 2, 4, D).transpose(0, 2, 3, 1, 4).reshape(2 * L, 4, shard, D),
                jnp.stack([embed_t[:, :D], embed_t[:, D:], class_vec, jnp.zeros_like(class_vec)])[None],
            ],
            0,
        ).reshape(2 * L + 1, 2, 2, shard, D)
        wcol, wdown, sall, take_block = gather_weights(
            times, units, down_low.reshape(L, 2, 192, D), jnp.broadcast_to(pad_to(sums, 0, 128), (8, 128)), give_block
        )
        wcol = wcol.reshape(2 * L + 1, 4, D, D)
        wdown = wdown.reshape(L, FF, D)
        embed_all = jnp.concatenate([wcol[4, 0], wcol[4, 1]], 1)
        class_vec_all = wcol[4, 2]
        sums = jnp.sum(sall[:, 0, :3], 0)
    else:
        wide_all = lax.all_gather(wide_low, "tm", axis=1, tiled=True)
        wcol = wide_all.reshape(L, D, 2, 4, D).transpose(0, 2, 3, 1, 4).reshape(2 * L, 4, D, D)
        wdown = lax.all_gather(down_low, "tm", axis=1, tiled=True)
        embed_all = lax.all_gather(embed_t, "tm", axis=0, tiled=True)
        class_vec_all = lax.all_gather(class_vec, "tm", axis=0, tiled=True)
        sums = lax.psum(sums, ("freq", "tm"))
        take_block = lax.ppermute(
            give_block, "tm", [(i, i + 1 - 2 * (i % 2)) for i in range(times)]
        )
    class_all = class_vec_all[:, :CLASSES]
    vec_all = class_vec_all[:, CLASSES : CLASSES + VROWS].T.astype(F32)
    take_block = take_block[: rows_dev * HALF].reshape(rows_dev, HALF, PATCH)
    clip_pixels = jnp.where(
        half == 0,
        jnp.stack([keep_block, take_block], 1),
        jnp.stack([take_block, keep_block], 1),
    ).reshape(rows_dev * 2 * HALF, PATCH)

    center = sums[0] / sums[2]
    mel_scale = lax.rsqrt(sums[1] / sums[2] - center * center + 1e-05)
    pnorm = ((clip_pixels.astype(F32) - center) * mel_scale).astype(BF)
    grid_rows = rows_dev * 2 * HALF
    positions = lax.dynamic_slice(embed_all, (0, f * grid_rows), (D, grid_rows)).T.astype(F32)
    grid = (
        jnp.einsum("rp,dp->rd", pnorm, embed_all[:, NGRID : NGRID + PATCH], preferred_element_type=F32)
        + vec_all[GLOB]
        + positions
    )
    x = jnp.concatenate(
        [grid, vec_all[GLOB + 1 : GLOB + 3], jnp.zeros((TOK - grid_rows - 2, D), F32)], 0
    )

    clip_columns = lax.dynamic_slice(columns, (pair * 2, half, 0), (2, 1, HALF)).reshape(2 * HALF)
    slots = jnp.concatenate(
        [
            jnp.broadcast_to(jnp.tile(clip_columns, rows_dev), (NF, grid_rows)),
            jnp.broadcast_to((jnp.arange(NF) == 0)[:, None], (NF, 2)),
            jnp.zeros((NF, TOK - grid_rows - 2), bool),
        ],
        1,
    ).reshape(NF * TOK)
    mask = jnp.where(slots, 0.0, -1e30).astype(F32)

    saved = []
    fa = []
    for layer in range(L):
        rows = vec_all[layer * 8 : layer * 8 + 8]
        up_bias = vec_all[L * 8 + layer * 4 : L * 8 + layer * 4 + 4].reshape(4, 1, D)
        x_in = x
        x, x1, acts, gp, qk = forward_layer(layer, x, rows, up_bias, mask.reshape(1, -1), wcol, wdown)
        saved.append((x_in, x1, gp, qk))
        fa.append(acts)

    owner = (f == 0).astype(F32)
    special = x[grid_rows : grid_rows + 2]
    normed_end, scale_end = norm_rows(special)
    feature = jnp.mean(normed_end * vec_all[GLOB + 3] + vec_all[GLOB + 4], 0, keepdims=True).astype(BF)
    logits = nn(feature, class_all) + class_bias
    clip = pair * CPD + half
    flags = lax.dynamic_slice_in_dim(labels, clip, 1, 0).astype(F32)
    weight = lax.dynamic_slice_in_dim(clip_weights, clip, 1, 0).astype(F32)[:, None]
    weight_total = jnp.sum(clip_weights).astype(F32)
    loss_part = owner * jnp.sum(weight * (jax.nn.softplus(logits) - flags * logits))
    dlogits = owner * weight * (jax.nn.sigmoid(logits) - flags) / weight_total
    dlogits_low = dlogits.astype(BF)
    dfinal = jnp.broadcast_to(0.5 * nt(dlogits_low, class_all), (2, D))
    dspecial = norm_back(dfinal * vec_all[GLOB + 3], normed_end, scale_end)
    end_rows = jnp.stack([jnp.sum(dfinal * normed_end, 0), jnp.sum(dfinal, 0)])
    dx = jnp.concatenate(
        [jnp.zeros((grid_rows, D), F32), dspecial, jnp.zeros((TOK - grid_rows - 2, D), F32)], 0
    )
    ba = [None] * L
    row_grads = [None] * L
    up_grads = [None] * L
    for layer in reversed(range(L)):
        rows = vec_all[layer * 8 : layer * 8 + 8]
        x_in, x1, gp, qk = saved[layer]
        dx, ba[layer], row_grads[layer], up = backward_layer(
            layer, dx, x_in, x1, gp, qk, rows, mask.reshape(-1, 1), wcol, wdown
        )
        up_grads[layer] = up.reshape(4, D)
    dgrid = dx[:grid_rows]
    grad_vec = jnp.concatenate(
        row_grads + up_grads + [jnp.sum(dgrid, 0, keepdims=True), dx[grid_rows : grid_rows + 2], end_rows], 0
    )

    vec_high = grad_vec.astype(BF)
    vec_low = (grad_vec - vec_high.astype(F32)).astype(BF)
    left = pad_to(jnp.concatenate([feature, vec_high, vec_low], 0), 0, TOK)
    pick = (
        jnp.arange(D)[None, :] == CLASSES + jnp.arange(VROWS)[:, None]
    ).astype(BF)
    right = pad_to(jnp.concatenate([pad_to(dlogits_low, 1, D), pick, pick], 0), 0, TOK)
    spot = jnp.arange(TOK)
    place_pos = (
        (jnp.arange(NGRID)[None, :] == f * grid_rows + spot[:, None]) & (spot[:, None] < grid_rows)
    ).astype(BF)
    grid_right = jnp.concatenate(
        [place_pos, pad_to(pnorm, 0, TOK), jnp.zeros((TOK, 2 * D - NGRID - PATCH), BF)], 1
    )
    dx_low = jnp.where(spot[:, None] < grid_rows, dx, 0.0).astype(BF)
    misc = jnp.stack(
        [dx_low, grid_right[:, :D], grid_right[:, D:], left, right, jnp.zeros((TOK, D), BF)]
    )
    small = jnp.concatenate([dlogits.reshape(-1), loss_part.reshape(1)])
    small = pad_to(small, 0, 1024).reshape(8, 128)
    if kernels:
        gcol, gdown, small_all, square_all = reduce_grads(times, fa, ba, misc, small)
        small = jnp.sum(small_all, 0).reshape(-1)
        square_total = jnp.sum(square_all)
        gcol = gcol.reshape(2 * L + 1, 4, shard, D).astype(F32)
        grad_wide = gcol[: 2 * L].reshape(L, 2, 4, shard, D).transpose(0, 3, 1, 2, 4).reshape(L, shard, 8 * D)
        grad_down = gdown.reshape(L, FF // times, D).astype(F32)
        grad_embed = jnp.concatenate([gcol[4, 0], gcol[4, 1]], 1)
        grad_cv = gcol[4, 2]
    else:
        ein = functools.partial(jnp.einsum, preferred_element_type=F32)
        wides, downs = [], []
        for l in range(L):
            cols = [tn(fa[l][0], ba[l][i]) for i in range(3)]
            cols += [tn(fa[l][1], ba[l][3])]
            cols += [tn(fa[l][2], ba[l][4 + i]) for i in range(4)]
            wides.append(jnp.concatenate(cols, 1))
            downs.append(jnp.concatenate([tn(fa[l][3 + i], ba[l][8]) for i in range(4)], 0))
        grad_wide = lax.psum_scatter(jnp.stack(wides), "tm", scatter_dimension=1, tiled=True)
        grad_down = lax.psum_scatter(jnp.stack(downs), "tm", scatter_dimension=1, tiled=True)
        grad_embed = lax.psum_scatter(
            jnp.concatenate([tn(misc[0], misc[1]), tn(misc[0], misc[2])], 1), "tm", scatter_dimension=0, tiled=True
        )
        grad_cv = lax.psum_scatter(tn(misc[3], misc[4]), "tm", scatter_dimension=0, tiled=True)
        grad_wide, grad_down, grad_embed, grad_cv = lax.psum(
            (grad_wide, grad_down, grad_embed, grad_cv), "freq"
        )
        squares = sum(jnp.sum(v * v) for v in (grad_wide, grad_down, grad_embed, grad_cv))
        square_total, small = lax.psum(
            (jnp.where(f == 0, squares, 0.0), small.reshape(-1)), ("freq", "tm")
        )
    grad_embed = grad_embed[:, : NGRID + PATCH].T
    grad_class = grad_cv[:, :CLASSES]
    grad_vectors = grad_cv[:, CLASSES : CLASSES + VROWS].T
    grad_bias = small[:CLASSES]
    loss_sum = small[CLASSES]
    grad_norm = jnp.sqrt(square_total + jnp.sum(grad_bias * grad_bias))
    coef = jnp.minimum(1.0, 1.0 / (grad_norm + 1e-06))

    params = (wide_weights, down_weights, embedding, classifier, vectors, class_bias)
    firsts = (wide_first, down_first, embedding_first, classifier_first, vectors_first, bias_first)
    seconds = (wide_second, down_second, embedding_second, classifier_second, vectors_second, bias_second)
    grads = (grad_wide, grad_down, grad_embed, grad_class, grad_vectors, grad_bias)
    news = [adam(w, m, v, g * coef) for w, m, v, g in zip(params, firsts, seconds, grads)]
    masters = [n[0] for n in news]
    return (
        *masters,
        *[n[1] for n in news],
        *[n[2] for n in news],
        *[m.astype(BF) for m in masters[:4]],
        grad_norm,
        loss_sum,
        weight_total,
    )


def solution(mesh):
    split = (
        P(None, "tm", None), P(None, "tm", None), P(None, "tm"), P("tm", None), P(None, "tm"), P(),
    )
    return jax.shard_map(
        local,
        mesh=mesh,
        in_specs=(P("freq", "tm", None), P(), P(), P()) + split * 3,
        out_specs=split * 3 + split[:4] + (P(), P(), P()),
        check_vma=False,
    )
```

```python
import functools

import jax
import jax.numpy as jnp
from jax import lax
from jax.experimental import pallas as pl
from jax.experimental.pallas import tpu as pltpu
from jax.sharding import PartitionSpec as P

D = 768
HEADS = 12
HDIM = 64
FF = 3072
L = 2
FROWS = 12
HALF = 52
PATCH = 256
STEP = 5
CPD = 2
NGRID = FROWS * 2 * HALF
CLASSES = 527
VROWS = 29
GLOB = L * 8 + L * (FF // D)

TOK = 320
PER = 3
NF = 4

DECAY_FIRST = 0.5
DECAY_SECOND = 0.5
LEARN_RATE = 0.03
WEIGHT_DECAY = 0.05
EPSILON = 1e-08

MESH = pl.DeviceIdType.MESH
BF = jnp.bfloat16
F32 = jnp.float32
VLIM = 60 * 1024 * 1024
VM = pltpu.VMEM


def nn(a, b):
    return lax.dot_general(a, b, (((1,), (0,)), ((), ())), preferred_element_type=F32)


def nt(a, b):
    return lax.dot_general(a, b, (((1,), (1,)), ((), ())), preferred_element_type=F32)


def tn(a, b):
    return lax.dot_general(a, b, (((0,), (0,)), ((), ())), preferred_element_type=F32)


def norm_rows(x):
    center = jnp.mean(x, -1, keepdims=True)
    shifted = x - center
    scale = lax.rsqrt(jnp.mean(shifted * shifted, -1, keepdims=True) + 1e-06)
    return (shifted * scale, scale)


def norm_back(dnorm, normed, scale):
    return scale * (
        dnorm
        - jnp.mean(dnorm, -1, keepdims=True)
        - normed * jnp.mean(dnorm * normed, -1, keepdims=True)
    )


def vspec():
    return pl.BlockSpec(memory_space=VM)


def aspec():
    return pl.BlockSpec(memory_space=pl.ANY)


def place():
    f, t = lax.axis_index("freq"), lax.axis_index("tm")
    return f, t, f // 2, f % 2, t // 2, t % 2


def remote(src, dst, ssem, rsem, dev):
    return pltpu.make_async_remote_copy(
        src_ref=src, dst_ref=dst, send_sem=ssem, recv_sem=rsem, device_id=dev, device_id_type=MESH
    )


def greet_all(times):
    f, t = lax.axis_index("freq"), lax.axis_index("tm")
    n = NF * times
    me = f * times + t
    barrier = pltpu.get_barrier_semaphore()

    def hello(i, carry):
        other = (me + i) % n
        pl.semaphore_signal(
            barrier, inc=1, device_id=(other // times, other % times), device_id_type=MESH
        )
        return carry

    lax.fori_loop(1, n, hello, 0)
    pl.semaphore_wait(barrier, n - 1)


def spread_small(times, small, gathered, ssem, rsem):
    f, t = lax.axis_index("freq"), lax.axis_index("tm")
    n = NF * times
    me = f * times + t

    def send(i, carry):
        other = (me + i) % n
        remote(
            small, gathered.at[me], ssem, rsem, (other // times, other % times)
        ).start()
        return carry

    lax.fori_loop(1, n, send, 0)
    gathered[me] = small[...]


def wait_small(times, gathered, ssem, rsem):
    n = NF * times
    many = gathered.at[pl.ds(0, n - 1)]
    pltpu.make_async_copy(many, many, rsem).wait()
    pltpu.make_async_copy(many, many, ssem).wait()


QROWS = TOK + TOK // 2
SLOTS = TOK // 2
GRID = FROWS // NF * HALF
EWIDE = 384
EVEC = TOK
ECLS = 352
CMAIN = 512


def greet_clip():
    f, t = lax.axis_index("freq"), lax.axis_index("tm")
    barrier = pltpu.get_barrier_semaphore()
    for i in range(1, NF):
        pl.semaphore_signal(barrier, inc=1, device_id=((f + i) % NF, t), device_id_type=MESH)
    pl.semaphore_wait(barrier, NF - 1)


def pack_half(v):
    return jnp.concatenate([v[: TOK // 2], v[TOK // 2 :]], 1)


def open_half(v):
    return jnp.concatenate([v[:, :HDIM], v[:, HDIM:]], 0)


def exchange_sems():
    dma = pltpu.SemaphoreType.DMA
    return [dma((PER, NF - 1))] * 4


FORWARD_SCRATCH = [
    VM((2, 2, 2, 4, 2, 96, D), BF),
    VM((4, 2, 2, 192, D), BF),
    VM((PER, NF, QROWS, 128), BF),
    VM((PER, NF, TOK // 2, 128), BF),
    VM((NF * TOK, HDIM), BF),
    VM((NF * TOK, HDIM), BF),
    VM((TOK, D), F32),
]


def layer_body(layer, x_ref, vec_ref, mask_ref, outs, scratch, orecv, sems, fetch, tick):
    xo_ref, x1_ref, fa_ref, gp_ref, qk_ref = outs
    wbuf, dbuf, qsend, osend, kall, vall, acc = scratch
    qs, qr, os, orr = sems
    f, t = lax.axis_index("freq"), lax.axis_index("tm")

    def row(i):
        return vec_ref[EVEC + layer * 8 + i : EVEC + layer * 8 + i + 1, :]

    def mat(part, q, cols=slice(None)):
        return wbuf[part, q // 2, q % 2, :, :, :, cols].reshape(D, -1)

    normed, _ = norm_rows(x_ref[...])
    act = (normed * row(0) + row(1)).astype(BF)
    fa_ref[0] = act
    fetch(0)

    def to_clip(j, i):
        other = (f + i) % NF
        return remote(
            qsend.at[j, other], qk_ref.at[j, f], qs.at[j, i - 1], qr.at[j, i - 1], (other, t)
        )

    def back_clip(j, i):
        other = (f + i) % NF
        return remote(
            osend.at[j, other], orecv.at[j, f], os.at[j, i - 1], orr.at[j, i - 1], (other, t)
        )

    for j in range(PER):
        cols = slice(256 * j, 256 * (j + 1))
        query = (nn(act, mat(0, 0, cols)) + row(4)[:, cols]).astype(BF)
        key = nn(act, mat(0, 1, cols)).astype(BF)
        value = (nn(act, mat(0, 2, cols)) + row(5)[:, cols]).astype(BF)
        for h in range(NF):
            part = slice(HDIM * h, HDIM * (h + 1))
            qsend[j, h, :TOK] = jnp.concatenate([query[:, part], key[:, part]], 1)
            qsend[j, h, TOK:] = pack_half(value[:, part])
        for i in range(1, NF):
            to_clip(j, i).start()
        qk_ref[j, f] = qsend[j, f]
    tick()
    mask = mask_ref[...]
    for j in range(PER):
        for i in range(1, NF):
            to_clip(j, i).wait_recv()
        for s in range(NF):
            kall[s * TOK : (s + 1) * TOK] = qk_ref[j, s, :TOK, HDIM:]
            vall[s * TOK : (s + 1) * TOK] = open_half(qk_ref[j, s, TOK:])

        def attend(i, carry):
            s = (f + i) % NF
            halves = []
            for h in range(2):
                lo = h * (TOK // 2)
                q = qk_ref[j, s, lo : lo + TOK // 2, :HDIM]
                scores = nt(q, kall[...]) * (HDIM ** (-0.5)) + mask
                top = jnp.max(scores, -1, keepdims=True)
                expo = jnp.exp(scores - top)
                total = jnp.sum(expo, -1, keepdims=True)
                probs = (expo * (1.0 / total)).astype(BF)
                halves.append(nn(probs, vall[...]).astype(BF))
            osend[j, s] = jnp.concatenate(halves, 1)

            @pl.when(i > 0)
            def _():
                remote(
                    osend.at[j, s], orecv.at[j, f], os.at[j, i - 1], orr.at[j, i - 1], (s, t)
                ).start()

            return carry

        lax.fori_loop(1, NF, attend, 0)
        lax.fori_loop(0, 1, attend, 0)
        orecv[j, f] = osend[j, f]
        tick()
    parts = []
    for j in range(PER):
        for i in range(1, NF):
            back_clip(j, i).wait_recv()
        for h in range(NF):
            parts.append(open_half(orecv[j, h]))
    mixed = jnp.concatenate(parts, 1)
    fa_ref[1] = mixed
    resid = x_ref[...] + nn(mixed, mat(0, 3)) + row(6)
    x1_ref[...] = resid
    normed, _ = norm_rows(resid)
    fa_ref[2] = (normed * row(2) + row(3)).astype(BF)
    acc[...] = resid + row(7)
    fetch(1)
    fetch(2)

    def mlp(k, carry):
        bias = vec_ref[pl.ds(EVEC + L * 8 + layer * 4 + k, 1), :]
        before = nn(fa_ref[2], mat(1, k)) + bias
        lower = 0.5 * (1.0 + lax.erf(before * 0.7071067811865476))
        gp_ref[k] = lower + before * jnp.exp(-0.5 * before * before) * 0.3989422804014327
        hidden = (before * lower).astype(BF)
        fa_ref[3 + k] = hidden
        acc[...] += nn(hidden, dbuf[k].reshape(D, D))
        return carry

    for k in range(0, FF // D, 2):
        lax.fori_loop(k, k + 2, mlp, 0)
        tick()
    xo_ref[...] = acc[...]
    for j in range(PER):
        for i in range(1, NF):
            to_clip(j, i).wait_send()
            back_clip(j, i).wait_send()


def forward_kernel(
    layer, x_ref, vec_ref, mask_ref, wcol, wdown,
    xo_ref, x1_ref, fa_ref, gp_ref, qk_ref,
    wbuf, dbuf, qsend, osend, kall, vall, acc, orecv, wsem, qs, qr, os, orr,
):
    loads = [
        pltpu.make_async_copy(wcol.at[2 * layer], wbuf.at[0], wsem.at[0]),
        pltpu.make_async_copy(wcol.at[2 * layer + 1], wbuf.at[1], wsem.at[1]),
        pltpu.make_async_copy(wdown.at[layer], dbuf, wsem.at[2]),
    ]
    for load in loads:
        load.start()
    greet_clip()
    layer_body(
        layer, x_ref, vec_ref, mask_ref, (xo_ref, x1_ref, fa_ref, gp_ref, qk_ref),
        (wbuf, dbuf, qsend, osend, kall, vall, acc), orecv, (qs, qr, os, orr),
        lambda part: loads[part].wait(), lambda: None,
    )


def forward_layer(layer, x, vec, mask, wcol, wdown):
    return pl.pallas_call(
        functools.partial(forward_kernel, layer),
        out_shape=(
            jax.ShapeDtypeStruct((TOK, D), F32),
            jax.ShapeDtypeStruct((TOK, D), F32),
            jax.ShapeDtypeStruct((7, TOK, D), BF),
            jax.ShapeDtypeStruct((FF // D, TOK, D), F32),
            jax.ShapeDtypeStruct((PER, NF, QROWS, 128), BF),
        ),
        in_specs=[vspec()] * 3 + [aspec()] * 2,
        out_specs=(vspec(),) * 5,
        scratch_shapes=FORWARD_SCRATCH
        + [VM((PER, NF, TOK // 2, 128), BF), pltpu.SemaphoreType.DMA((3,))]
        + exchange_sems(),
        compiler_params=pltpu.CompilerParams(
            collective_id=2 + layer, has_side_effects=True, vmem_limit_bytes=VLIM
        ),
        name="forward_layer",
    )(x, vec, mask, wcol, wdown)


GROUPS = (("c", 0), ("c", 1), ("d", 0), ("c", 2), ("c", 3), ("d", 1))
SUBS = tuple((kind, idx, h) for kind, idx in GROUPS for h in (0, 1))
PATHS = "yzyzyzyyzyzy"
AHEAD = 3


def gather_plan():
    moves = {}
    for s, path in enumerate(PATHS):
        lag = 1 if s < 2 else 2
        times = {"along": s - AHEAD, "first": s}
        times["third"] = s + lag
        if path == "y":
            times["second"] = s + lag
            times["third"] = s + 2 * lag
        times["arrive"] = times["third"] + 1
        for action, when in times.items():
            moves.setdefault(max(when, -1), []).append((s, action))
    plan = [sorted(moves[when]) for when in sorted(moves)]
    ready = {s: n for n, step in enumerate(plan) for s, action in step if action == "arrive"}
    return plan, ready


def gather_steps(count, ucol, udown, ocol, odown, sems):
    zs, zr, own, s1, r1, s2, r2, s3, r3 = sems
    f, t, y, c, g, x = place()
    every = slice(None)

    def source(s):
        kind, idx, h = SUBS[s]
        yy = every if PATHS[s] == "z" else y
        if kind == "c":
            return ucol.at[idx, yy, c, :, pl.ds(h * 384, 384)]
        return udown.at[idx, yy, pl.ds(h * 96, 96), pl.ds(pl.multiple_of(c * 384, 128), 384)]

    def view(s, yy, zz, xx):
        kind, idx, h = SUBS[s]
        if PATHS[s] == "z":
            yy = every
        if kind == "c":
            return ocol.at[idx, yy, c, zz, xx, :, pl.ds(h * 384, 384)]
        return odown.at[
            idx, zz, xx, yy, pl.ds(h * 96, 96), pl.ds(pl.multiple_of(c * 384, 128), 384)
        ]

    def along(s, dz):
        return remote(
            source(s), view(s, y, g, x), zs.at[s, dz - 1], zr.at[s, dz - 1],
            (f, ((g + dz) % count) * 2 + x),
        )

    def keep(s):
        return pltpu.make_async_copy(source(s), view(s, y, g, x), own.at[s])

    def first(s):
        block = view(s, y, every, x)
        return remote(block, block, s1.at[s], r1.at[s], (f, g * 2 + 1 - x))

    def second(s):
        block = view(s, y, every, every)
        return remote(block, block, s2.at[s], r2.at[s], ((1 - y) * 2 + c, t))

    def third(s):
        block = view(s, every, every, every)
        return remote(block, block, s3.at[s], r3.at[s], (y * 2 + 1 - c, t))

    def act(s, action):
        if action == "along":
            keep(s).start()
            for dz in range(1, count):
                along(s, dz).start()
        elif action == "first":
            for dz in range(1, count):
                along(s, dz).wait_recv()
            keep(s).wait()
            first(s).start()
        elif action == "second":
            first(s).wait_recv()
            second(s).start()
        elif action == "third":
            (second if PATHS[s] == "y" else first)(s).wait_recv()
            third(s).start()
        else:
            third(s).wait_recv()

    for step in gather_plan()[0]:
        for s, action in step:
            act(s, action)
        yield
    for s in range(len(SUBS)):
        for dz in range(1, count):
            along(s, dz).wait_send()
        first(s).wait_send()
        if PATHS[s] == "y":
            second(s).wait_send()
        third(s).wait_send()
    yield


def forward_all_kernel(
    times, ucol, udown, uemb, upatch, uclass, stats, pkeep, psend, mask_ref,
    ocol, odown, oclass, vec_out, xs_out, fa_out, gp_out, qk_out, pn_out,
    wbuf, dbuf, qsend, osend, kall, vall, acc, orecv, sall, precv, emb, patches, classes, vec, xs, fa, gp, qk, pn,
    zs, zr, own, s1, r1, s2, r2, s3, r3, es, er, exs, exr, ss, sr, ps, pr, wsem, osem,
    qs0, qr0, os0, or0, qs1, qr1, os1, or1,
):
    f, t, y, c, g, x = place()
    count = times // 2
    over_x = (f, g * 2 + 1 - x)
    greet_all(times)
    spread_small(times, stats, sall, ss, sr)
    swap = remote(psend, precv, ps, pr, over_x)
    swap.start()
    units = ((uemb, emb), (upatch, patches), (uclass, classes))

    def unit_along(n, dz):
        src, dst = units[n]
        return remote(
            src, dst.at[g, x], es.at[n, dz - 1], er.at[n, dz - 1], (f, ((g + dz) % count) * 2 + x)
        )

    def loads(layer, part):
        if part < 2:
            return pltpu.make_async_copy(ocol.at[2 * layer + part], wbuf.at[part], wsem.at[layer, part])
        return pltpu.make_async_copy(odown.at[layer], dbuf, wsem.at[layer, part])

    def unit_over(n):
        block = units[n][1].at[:, x]
        return remote(block, block, exs.at[n], exr.at[n], over_x)

    for n in range(3):
        units[n][1][g, x] = units[n][0][...]
    for n in range(2):
        for dz in range(1, count):
            unit_along(n, dz).start()
    steps = gather_steps(count, ucol, udown, ocol, odown, (zs, zr, own, s1, r1, s2, r2, s3, r3))
    plan, ready = gather_plan()
    last = len(plan) - 1
    done = [-1]

    started, allowed = set(), {(0, part) for part in range(3)}

    def arrived(layer, part):
        group = 3 * layer + part
        return max(ready[2 * group], ready[2 * group + 1])

    def prefetch():
        for layer, part in sorted(allowed - started):
            if done[0] >= arrived(layer, part):
                loads(layer, part).start()
                started.add((layer, part))

    def tick():
        if done[0] < last:
            next(steps)
            done[0] += 1
        prefetch()

    def need(step):
        while done[0] < step:
            tick()

    need(0)
    for n in range(2):
        for dz in range(1, count):
            unit_along(n, dz).wait_recv()
        unit_over(n).start()
    need(1)
    for n in range(2):
        unit_over(n).wait_recv()
    swap.wait_recv()
    wait_small(times, sall, ss, sr)
    sums = jnp.sum(sall[...], 0)
    total, squares, live = sums[0:1, 0:1], sums[0:1, 1:2], sums[0:1, 2:3]
    center = total / live
    mel_scale = lax.rsqrt(squares / live - center * center + 1e-05)
    inside = lax.broadcasted_iota(jnp.int32, (SLOTS, PATCH), 0) < GRID

    def normalized(block):
        return jnp.where(inside, (block[...].astype(F32) - center) * mel_scale, 0.0).astype(BF)

    pn[pl.ds(pl.multiple_of(x * SLOTS, SLOTS), SLOTS)] = normalized(pkeep)
    pn[pl.ds(pl.multiple_of((1 - x) * SLOTS, SLOTS), SLOTS)] = normalized(precv)
    vec[...] = emb[...].reshape(D, EWIDE).astype(F32).T
    patch = patches[...].reshape(D, PATCH)
    bias = vec[EVEC + GLOB : EVEC + GLOB + 1, :]
    spot = lax.broadcasted_iota(jnp.int32, (TOK, D), 0)
    grid_row = jnp.logical_or(spot < GRID, jnp.logical_and(spot >= SLOTS, spot < SLOTS + GRID))
    xs[0] = (nt(pn[...], patch) + vec[:TOK]) + jnp.where(grid_row, bias, 0.0)

    copies = [
        pltpu.make_async_copy(vec, vec_out, osem.at[1]),
        pltpu.make_async_copy(pn, pn_out, osem.at[2]),
    ]
    for copy in copies:
        copy.start()
    sems = ((qs0, qr0, os0, or0), (qs1, qr1, os1, or1))
    for dz in range(1, count):
        unit_along(2, dz).start()
    for layer in range(L):
        if layer == 1:
            for dz in range(1, count):
                unit_along(2, dz).wait_recv()
            unit_over(2).start()

        def fetch(part):
            if part == 1 and layer + 1 < L:
                allowed.add((layer + 1, 0))
            need(arrived(layer, part))
            prefetch()
            loads(layer, part).wait()

        layer_body(
            layer, xs.at[2 * layer], vec, mask_ref,
            (xs.at[2 * layer + 2], xs.at[2 * layer + 1], fa.at[layer], gp.at[layer], qk.at[layer]),
            (wbuf, dbuf, qsend, osend, kall, vall, acc), orecv.at[layer], sems[layer], fetch, tick,
        )
        more = [
            pltpu.make_async_copy(fa.at[layer], fa_out.at[layer], osem.at[3 + 4 * layer]),
            pltpu.make_async_copy(gp.at[layer], gp_out.at[layer], osem.at[4 + 4 * layer]),
            pltpu.make_async_copy(qk.at[layer], qk_out.at[layer], osem.at[5 + 4 * layer]),
        ]
        if layer == 0:
            more.append(pltpu.make_async_copy(xs.at[pl.ds(0, 2)], xs_out.at[pl.ds(0, 2)], osem.at[6]))
        else:
            more.append(pltpu.make_async_copy(xs.at[pl.ds(2, 3)], xs_out.at[pl.ds(2, 3)], osem.at[10]))
        for copy in more:
            copy.start()
        copies += more
        allowed.update((layer + 1, part) for part in (1, 2) if layer + 1 < L)
    need(last)
    next(steps)
    unit_over(2).wait_recv()
    copies.append(pltpu.make_async_copy(classes, oclass, osem.at[0]))
    copies[-1].start()
    for n in range(3):
        for dz in range(1, count):
            unit_along(n, dz).wait_send()
        unit_over(n).wait_send()
    swap.wait_send()
    for copy in copies:
        copy.wait()


def forward_all(times, ucol, udown, uemb, upatch, uclass, stats, pkeep, psend, mask):
    count = times // 2
    total = len(SUBS)
    dma = pltpu.SemaphoreType.DMA
    outs = (
        ((2 * L, 2, 2, count, 2, 96, D), BF),
        ((L, count, 2, 2, 192, D), BF),
        ((count, 2, 96, CMAIN), BF),
        ((EWIDE, D), F32),
        ((2 * L + 1, TOK, D), F32),
        ((L, 7, TOK, D), BF),
        ((L, FF // D, TOK, D), F32),
        ((L, PER, NF, QROWS, 128), BF),
        ((TOK, PATCH), BF),
    )
    return pl.pallas_call(
        functools.partial(forward_all_kernel, times),
        out_shape=tuple(jax.ShapeDtypeStruct(*o) for o in outs),
        in_specs=[vspec()] * 9,
        out_specs=(aspec(),) * len(outs),
        scratch_shapes=FORWARD_SCRATCH
        + [
            VM((L, PER, NF, TOK // 2, 128), BF),
            VM((NF * times, 8, 128), F32),
            VM((SLOTS, PATCH), BF),
            VM((count, 2, 96, EWIDE), BF),
            VM((count, 2, 96, PATCH), BF),
            VM((count, 2, 96, CMAIN), BF),
            VM((EWIDE, D), F32),
            VM((2 * L + 1, TOK, D), F32),
            VM((L, 7, TOK, D), BF),
            VM((L, FF // D, TOK, D), F32),
            VM((L, PER, NF, QROWS, 128), BF),
            VM((TOK, PATCH), BF),
            dma((total, count - 1)), dma((total, count - 1)), dma((total,)),
            dma((total,)), dma((total,)), dma((total,)), dma((total,)), dma((total,)), dma((total,)),
            dma((3, count - 1)), dma((3, count - 1)), dma((3,)), dma((3,)),
            dma, dma, dma, dma, dma((L, 3)), dma((12,)),
        ]
        + exchange_sems() * L,
        compiler_params=pltpu.CompilerParams(
            collective_id=1, has_side_effects=True, vmem_limit_bytes=VLIM
        ),
        name="forward_all",
    )(ucol, udown, uemb, upatch, uclass, stats, pkeep, psend, mask)


BACKWARD_SCRATCH = [
    VM((PER, NF, TOK // 2, 128), BF),
    VM((PER, NF, TOK // 2, 128), BF),
    VM((PER, NF, QROWS, 128), BF),
    VM((PER, NF, QROWS, 128), BF),
    VM((NF * TOK, HDIM), BF),
    VM((NF * TOK, HDIM), BF),
    VM((NF * TOK, HDIM), F32),
    VM((NF * TOK, HDIM), F32),
    VM((NF, TOK, HDIM), BF),
    VM((TOK, D), F32),
]


def backward_body(layer, dcur, er, ba, vec_ref, mask_ref, qk_ref, mats, slope, kept, scratch, sems, at):
    down, up, qkvo = mats
    dsend, drecv, gsend, grecv, kall, vall, dkall, dvall, dqall, acc = scratch
    ds_, dr_, gs_, gr_ = sems
    f, t = lax.axis_index("freq"), lax.axis_index("tm")

    def row(i):
        return vec_ref[EVEC + layer * 8 + i : EVEC + layer * 8 + i + 1, :]

    def note(i, value):
        er[EVEC + i : EVEC + i + 1, :] = jnp.sum(value, 0, keepdims=True)

    ba[8] = dcur[...].astype(BF)
    note(layer * 8 + 7, dcur[...])
    for k in range(FF // D):
        dbefore = nt(ba[8], down(k)) * slope(k)
        note(L * 8 + layer * 4 + k, dbefore)
        ba[4 + k] = dbefore.astype(BF)
        product = nt(ba[4 + k], up(k))
        acc[...] = product if k == 0 else acc[...] + product
        at("mlp%d" % k)
    normed, scale = norm_rows(kept(1))
    dact = acc[...]
    note(layer * 8 + 2, dact * normed)
    note(layer * 8 + 3, dact)
    dcur[...] += norm_back(dact * row(2), normed, scale)
    note(layer * 8 + 6, dcur[...])
    ba[3] = dcur[...].astype(BF)
    at("resid")
    dmixed = nt(ba[3], qkvo(3)).astype(BF)

    def to_clip(j, i):
        other = (f + i) % NF
        return remote(
            dsend.at[j, other], drecv.at[j, f], ds_.at[j, i - 1], dr_.at[j, i - 1], (other, t)
        )

    def back_clip(j, i):
        other = (f + i) % NF
        return remote(
            gsend.at[j, other], grecv.at[j, f], gs_.at[j, i - 1], gr_.at[j, i - 1], (other, t)
        )

    for j in range(PER):
        for h in range(NF):
            lo = 256 * j + HDIM * h
            dsend[j, h] = pack_half(dmixed[:, lo : lo + HDIM])
        for i in range(1, NF):
            to_clip(j, i).start()
        drecv[j, f] = dsend[j, f]
    at("sent")
    mask = mask_ref[...]
    root = HDIM ** (-0.5)
    part = TOK // 2
    for j in range(PER):
        for s in range(NF):
            kall[s * TOK : (s + 1) * TOK] = qk_ref[j, s, :TOK, HDIM:]
            vall[s * TOK : (s + 1) * TOK] = open_half(qk_ref[j, s, TOK:])
        dkall[...] = jnp.zeros_like(dkall)
        dvall[...] = jnp.zeros_like(dvall)
        for i in range(1, NF):
            to_clip(j, i).wait_recv()

        def attend(s, carry):
            q = qk_ref[j, s, :TOK, :HDIM]
            dmix = open_half(drecv[j, s])
            scores = nt(kall[...], q) * root + mask
            top = jnp.max(scores, 0, keepdims=True)
            expo = jnp.exp(scores - top)
            probs = expo * (1.0 / jnp.sum(expo, 0, keepdims=True))
            dprob = nt(vall[...], dmix)
            inner = jnp.sum(probs * dprob, 0, keepdims=True)
            dscore = (probs * (dprob - inner)).astype(BF)
            dvall[...] += nn(probs.astype(BF), dmix)
            dkall[...] += nn(dscore, q)
            dqall[s] = (tn(dscore, kall[...]) * root).astype(BF)
            return carry

        lax.fori_loop(0, NF, attend, 0)
        for s in range(NF):
            span = slice(s * TOK, (s + 1) * TOK)
            gsend[j, s, :TOK] = jnp.concatenate([dqall[s], (dkall[span] * root).astype(BF)], 1)
            gsend[j, s, TOK:] = pack_half(dvall[span].astype(BF))
        for i in range(1, NF):
            back_clip(j, i).start()
        grecv[j, f] = gsend[j, f]
        at("head%d" % j)
    for j in range(PER):
        for i in range(1, NF):
            back_clip(j, i).wait_recv()
        cols = slice(256 * j, 256 * (j + 1))
        ba[0, :, cols] = jnp.concatenate([grecv[j, h, :TOK, :HDIM] for h in range(NF)], 1)
        ba[1, :, cols] = jnp.concatenate([grecv[j, h, :TOK, HDIM:] for h in range(NF)], 1)
        ba[2, :, cols] = jnp.concatenate([open_half(grecv[j, h, TOK:]) for h in range(NF)], 1)
    at("heads")
    note(layer * 8 + 4, ba[0].astype(F32))
    note(layer * 8 + 5, ba[2].astype(F32))
    dact = nt(ba[0], qkvo(0)) + nt(ba[1], qkvo(1)) + nt(ba[2], qkvo(2))
    normed, scale = norm_rows(kept(0))
    note(layer * 8 + 0, dact * normed)
    note(layer * 8 + 1, dact)
    dcur[...] += norm_back(dact * row(0), normed, scale)
    for j in range(PER):
        for i in range(1, NF):
            to_clip(j, i).wait_send()
            back_clip(j, i).wait_send()
    at("done")


def backward_kernel(
    layer, dout_ref, x_ref, x1_ref, gp_ref, qk_ref, vec_ref, mask_ref, wcol, wdown,
    dx_ref, ba_ref, er_ref, wbuf, dbuf, wsem, ds_, dr_, gs_, gr_, *scratch,
):
    loads = [
        pltpu.make_async_copy(wdown.at[layer], dbuf, wsem.at[0]),
        pltpu.make_async_copy(wcol.at[2 * layer + 1], wbuf.at[1], wsem.at[1]),
        pltpu.make_async_copy(wcol.at[2 * layer], wbuf.at[0], wsem.at[2]),
    ]
    for load in loads:
        load.start()
    dx_ref[...] = dout_ref[...]
    er_ref[...] = jnp.zeros_like(er_ref)
    greet_clip()
    for load in loads:
        load.wait()
    backward_body(
        layer, dx_ref, er_ref, ba_ref, vec_ref, mask_ref, qk_ref,
        (lambda k: dbuf[k], lambda k: wbuf[1, k], lambda k: wbuf[0, k]),
        lambda k: gp_ref[k], lambda i: x1_ref[...] if i else x_ref[...],
        scratch, (ds_, dr_, gs_, gr_), lambda point: None,
    )


def backward_layer(layer, dout, x, x1, gp, qk, vec, mask, wcol, wdown):
    return pl.pallas_call(
        functools.partial(backward_kernel, layer),
        out_shape=(
            jax.ShapeDtypeStruct((TOK, D), F32),
            jax.ShapeDtypeStruct((9, TOK, D), BF),
            jax.ShapeDtypeStruct((EWIDE, D), F32),
        ),
        in_specs=[vspec()] * 7 + [aspec()] * 2,
        out_specs=(vspec(),) * 3,
        scratch_shapes=[VM((2, 4, D, D), BF), VM((4, D, D), BF), pltpu.SemaphoreType.DMA((3,))]
        + exchange_sems()
        + BACKWARD_SCRATCH,
        compiler_params=pltpu.CompilerParams(
            collective_id=2 + L + layer, has_side_effects=True, vmem_limit_bytes=VLIM
        ),
        name="backward_layer",
    )(dout, x, x1, gp, qk, vec, mask, wcol, wdown)


RGROUPS = (("d", 1), ("u", 1), ("q", 1), ("d", 0), ("u", 0), ("q", 0))
RFIRST = ("xx", "yx", "xx", "xx", "yx", "xx")
SLOTS_R = 2
PWIDE = (CMAIN, EWIDE + PATCH)
STAGES = 5


def backward_all_kernel(
    times, dout_in, xs_in, gp_in, qk_in, fa_in, vec_ref, mask_ref, pn_ref, head_ref, end_ref, small, wcol, wdown,
    gcol, gdown, gpart, small_all, square_all, rfa,
    *refs,
):
    (
        wbuf, gp, xb, dcur, er, qk, ba, lbuf, rd, ru, rq, full, low, recv1, mid_own, mid_low, recv2,
        zlow, zown, zrecv, psend0, psend1, pown0, pown1, pxr0, pxr1, pzs0, pzs1, pzr0, pzr1, sq,
        wsem, gsem, xsem, qsem, ls, fas, far, bs, br, s1, r1, s2, r2, zs, zr, fs, fr, ks, kr,
        ss, sr, qs, qr, p1, p1r, p2, p2r, p3, p3r, p4, p4r, credit,
        ds_, dr_, gs_, gr_,
    ) = refs[: -len(BACKWARD_SCRATCH)]
    scratch = refs[-len(BACKWARD_SCRATCH) :]
    f, t, y, c, g, x = place()
    count = times // 2
    over_x = (f, g * 2 + 1 - x)
    over_y = ((1 - y) * 2 + c, t)
    over_c = (y * 2 + 1 - c, t)
    total = len(RGROUPS)
    other_core = 1 - c

    def half_cols(core):
        return pl.ds(pl.multiple_of(core * 384, 128), 384)

    def weight(layer, which):
        src = (wdown.at[layer], wcol.at[2 * layer + 1], wcol.at[2 * layer])[which]
        return pltpu.make_async_copy(src, wbuf.at[weight_slot(layer, which)], wsem.at[layer, which])

    def weight_slot(layer, which):
        return (which % 2 + (L - 1 - layer)) % 2

    def slope_load(layer, k):
        return pltpu.make_async_copy(gp_in.at[layer, k], gp.at[k % 2], gsem.at[layer, k])

    def kept_load(layer, i):
        return pltpu.make_async_copy(xs_in.at[2 * layer + i], xb, xsem.at[layer, i])

    def heads_load(layer):
        return pltpu.make_async_copy(qk_in.at[layer], qk, qsem.at[layer])

    first_load = pltpu.make_async_copy(dout_in, dcur, qsem.at[L])
    first_load.start()
    for which in range(2):
        weight(L - 1, which).start()
    for k in range(2):
        slope_load(L - 1, k).start()
    kept_load(L - 1, 1).start()
    heads_load(L - 1).start()
    greet_all(times)
    spread_small(times, small, small_all, ss, sr)

    def forward_swap(layer, n):
        span = pl.ds(3, 4) if n == 0 else pl.ds(0, 3)
        return remote(
            fa_in.at[layer, span], rfa.at[layer, span], fas.at[layer, n], far.at[layer, n], over_c
        )

    for layer in reversed(range(L)):
        for n in range(2):
            forward_swap(layer, n).start()

    def swap(gi, n):
        kind, l = RGROUPS[gi]
        if kind == "d":
            src, dst = ba.at[8, :, half_cols(other_core)], rd.at[l]
        elif kind == "u":
            src, dst = ba.at[4 + 2 * n + other_core], ru.at[l, n]
        else:
            src, dst = ba.at[2 * n + other_core], rq.at[l, n]
        return remote(src, dst, bs.at[gi, n], br.at[gi, n], over_c)

    def swaps(gi):
        return range(1 if RGROUPS[gi][0] == "d" else 2)

    def left_loads(gi):
        kind, l = RGROUPS[gi]
        out = []
        blocks = {"d": (3, 4, 5, 6), "u": (2,), "q": (0, c)}[kind]
        for n, block in enumerate(blocks):
            for m, src in enumerate((fa_in, rfa)):
                out.append(
                    pltpu.make_async_copy(
                        src.at[l, block], lbuf.at[n, pl.ds(m * TOK, TOK)], ls.at[n, m]
                    )
                )
        return out

    def product(left, own, other, cols):
        return tn(lbuf[left, :TOK], own(cols)) + tn(lbuf[left, TOK:], other(cols))

    def store(gi, h, role, xx, where, value):
        if RFIRST[gi][h] == "y":
            keep, index = role == 0, xx
        else:
            keep, index = x == xx, role

        def save_full():
            full[(h, index) + where] = value

        def save_low():
            low[(h, index) + where] = value.astype(BF)

        if isinstance(keep, bool):
            (save_full if keep else save_low)()
        else:
            pl.when(keep)(save_full)
            pl.when(jnp.logical_not(keep))(save_low)

    def compute(gi):
        kind, l = RGROUPS[gi]
        if kind == "d":

            def one(z, carry):
                prod = product(
                    z, lambda _: ba[8, :, half_cols(c)], lambda _: rd[l], None
                ).reshape(2, 2, 2, 96, 384)
                for xx in range(2):
                    for yy in range(2):
                        for h in range(2):
                            store(gi, h, (yy + y) % 2, xx, (z,), prod[xx, yy, h])
                return carry

            lax.fori_loop(0, count, one, 0)
            return
        recv = ru if kind == "u" else rq
        base = 4 if kind == "u" else 0
        for role in range(2):
            yy = y if role == 0 else 1 - y
            left = 0 if kind == "u" else yy
            for h in range(2):
                cols = slice(h * 384, (h + 1) * 384)
                prod = product(
                    left, lambda cols: ba[base + 2 * yy + c, :, cols], lambda cols: recv[l, yy, :, cols], cols
                ).reshape(count, 2, 96, 384)
                for xx in range(2):
                    store(gi, h, role, xx, (), prod[:, xx])

    def step1(gi, h):
        return remote(
            low.at[h], recv1.at[gi % SLOTS_R, h], s1.at[gi, h], r1.at[gi, h],
            over_y if RFIRST[gi][h] == "y" else over_x,
        )

    def step2(gi, h):
        return remote(
            mid_low.at[h], recv2.at[gi % SLOTS_R, h], s2.at[gi, h], r2.at[gi, h],
            over_x if RFIRST[gi][h] == "y" else over_y,
        )

    def along(gi, dz):
        return remote(
            zlow.at[(g + dz) % count], zrecv.at[gi % SLOTS_R, dz - 1], zs.at[gi, dz - 1], zr.at[gi, dz - 1],
            (f, ((g + dz) % count) * 2 + x),
        )

    def result(gi, yy):
        kind, l = RGROUPS[gi]
        if kind == "d":
            return gdown.at[l, yy, :, half_cols(c)]
        return gcol.at[2 * l + (1 if kind == "u" else 0), yy, c]

    def spread_y(gi):
        block = result(gi, y)
        return remote(block, block, fs.at[gi], fr.at[gi], over_y)

    def spread_c(gi):
        block = result(gi, slice(None))
        return remote(block, block, ks.at[gi], kr.at[gi], over_c)

    def advance(gi, stage):
        slot = gi % SLOTS_R
        if stage == 1:
            for h in range(2):
                step1(gi, h).wait_recv()
                step1(gi, h).wait_send()
                keep, send = (x, 1 - x) if RFIRST[gi][h] == "y" else (0, 1)
                mid_low[h] = (full[h, send] + recv1[slot, h, send].astype(F32)).astype(BF)
                step2(gi, h).start()
                mid_own[h] = full[h, keep] + recv1[slot, h, keep].astype(F32)
        elif stage == 2:
            for h in range(2):
                step2(gi, h).wait_recv()
                step2(gi, h).wait_send()
                summed = mid_own[h] + recv2[slot, h].astype(F32)
                zlow[:, h] = summed.astype(BF)
                mid_own[h] = summed
            if gi >= SLOTS_R:
                for dz in range(1, count):
                    pl.semaphore_wait(credit.at[1 + dz], 1)
            for dz in range(1, count):
                along(gi, dz).start()
            for h in range(2):
                zown[h] = mid_own[h, g]
            if gi + SLOTS_R < total:
                pl.semaphore_signal(credit.at[0], inc=1, device_id=over_x, device_id_type=MESH)
                pl.semaphore_signal(credit.at[1], inc=1, device_id=over_y, device_id_type=MESH)
        elif stage == 3:
            for dz in range(1, count):
                along(gi, dz).wait_recv()
                along(gi, dz).wait_send()
            for h in range(2):
                value = zown[h]
                for dz in range(1, count):
                    value = value + zrecv[slot, dz - 1, h].astype(F32)
                sq[...] += jnp.sum((value * value).reshape(12, 8, 3, 128), (0, 2))
                kind, l = RGROUPS[gi]
                if kind == "d":
                    gdown[l, y, h * 96 : (h + 1) * 96, half_cols(c)] = value.astype(BF)
                else:
                    idx = 2 * l + (1 if kind == "u" else 0)
                    gcol[idx, y, c, :, h * 384 : (h + 1) * 384] = value.astype(BF)
            if gi + SLOTS_R < total:
                for dz in range(1, count):
                    pl.semaphore_signal(
                        credit.at[1 + dz], inc=1, device_id=(f, ((g + count - dz) % count) * 2 + x), device_id_type=MESH
                    )
            spread_y(gi).start()
        elif stage == 4:
            spread_y(gi).wait_recv()
            spread_c(gi).start()
        else:
            spread_c(gi).wait_recv()

    psends, powns, pxrs, pzss, pzrs = (psend0, psend1), (pown0, pown1), (pxr0, pxr1), (pzs0, pzs1), (pzr0, pzr1)
    pspans = (slice(0, CMAIN), slice(CMAIN, CMAIN + PWIDE[1]))

    def part_over(n):
        return remote(psends[n], pxrs[n], p1.at[n], p1r.at[n], over_x)

    def part_along(n, dz):
        return remote(
            pzss[n].at[(g + dz) % count], pzrs[n].at[dz - 1], p2.at[n, dz - 1], p2r.at[n, dz - 1],
            (f, ((g + dz) % count) * 2 + x),
        )

    def part_y(n):
        block = gpart.at[n, y, c]
        return remote(block, block, p3.at[n], p3r.at[n], over_y)

    def part_c(n):
        block = gpart.at[n, :, c]
        return remote(block, block, p4.at[n], p4r.at[n], over_c)

    def part_compute(n):
        pieces = []
        if n == 0:
            pieces.append((0, tn(head_ref[0], head_ref[1, :, :CMAIN])))
        else:
            pieces.append((0, er[...].T))
            pieces.append((EWIDE, tn(dcur[...].astype(BF), pn_ref[...])))
        for lo, piece in pieces:
            piece = piece.reshape(count, 2, 96, -1)
            span = slice(lo, lo + piece.shape[-1])
            for xx in range(2):

                @pl.when(x == xx)
                def _():
                    powns[n][:, :, span] = piece[:, xx]
                    psends[n][:, :, span] = piece[:, 1 - xx].astype(BF)

        part_over(n).start()

    def part_advance(n, stage):
        if stage == 1:
            part_over(n).wait_recv()
            summed = powns[n][...] + pxrs[n][...].astype(F32)
            powns[n][...] = summed
            pzss[n][...] = summed.astype(BF)
            for dz in range(1, count):
                part_along(n, dz).start()
        elif stage == 2:
            value = powns[n][g]
            for dz in range(1, count):
                part_along(n, dz).wait_recv()
                value = value + pzrs[n][dz - 1].astype(F32)
            gpart[n, y, c, :, : PWIDE[n]] = value.astype(BF)
            part_y(n).start()
            if n == 1:
                lane = lax.broadcasted_iota(jnp.int32, (96, EWIDE), 1)
                inside = jnp.logical_and(lane % SLOTS < GRID, lane < TOK)
                own = jnp.where(inside, value[:, :EWIDE], 0.0)
                sq[...] += jnp.sum((own * own).reshape(12, 8, 3, 128), (0, 2))
        elif stage == 3:
            part_y(n).wait_recv()
            part_c(n).start()
        else:
            part_c(n).wait_recv()
            value = gpart[n, 0, 0].astype(F32) + gpart[n, 0, 1].astype(F32)
            value = value + gpart[n, 1, 0].astype(F32) + gpart[n, 1, 1].astype(F32)
            value = value[:, : PWIDE[n]]
            if n == 1:
                lane = lax.broadcasted_iota(jnp.int32, value.shape, 1)
                value = jnp.where(lane >= EVEC, value, 0.0)
            value = jnp.where(f == 0, value * value, 0.0)
            sq[...] += jnp.sum(value.reshape(12, 8, PWIDE[n] // 128, 128), (0, 2))

    under_way = []

    def tick():
        for entry in list(under_way):
            entry[2] += 1
            (advance if entry[0] == "group" else part_advance)(entry[1], entry[2])
            if entry[2] == (STAGES if entry[0] == "group" else STAGES - 1):
                under_way.remove(entry)

    def stage_of(kind, n):
        for entry in under_way:
            if entry[0] == kind and entry[1] == n:
                return entry[2]
        return STAGES

    def launch(gi):
        while gi > 0 and stage_of("group", gi - 1) < 1:
            tick()
        l = RGROUPS[gi][1]
        for n in swaps(gi):
            swap(gi, n).wait_recv()
        for copy in left_loads(gi):
            copy.wait()
        if gi >= SLOTS_R:
            while stage_of("group", gi - SLOTS_R) < 2:
                tick()
        compute(gi)
        for n in swaps(gi):
            swap(gi, n).wait_send()
        if gi >= SLOTS_R:
            pl.semaphore_wait(credit.at[0], 1)
            pl.semaphore_wait(credit.at[1], 1)
        for h in range(2):
            step1(gi, h).start()
        under_way.append(["group", gi, 0])
        if gi + 1 < total:
            prepare(gi + 1)

    waited = set()

    def prepare(gi):
        kind, l = RGROUPS[gi]
        for n in ((0,) if kind == "d" else (1,)):
            if (l, n) not in waited:
                waited.add((l, n))
                forward_swap(l, n).wait_recv()
        for copy in left_loads(gi):
            copy.start()

    def launch_part(n):
        part_compute(n)
        under_way.append(["part", n, 0])

    sq[...] = jnp.zeros_like(sq)
    er[...] = jnp.zeros_like(er)
    er[EVEC + GLOB + 3 : EVEC + GLOB + 5, :] = end_ref[...]
    er[ECLS:, :] = tn(head_ref[1, :, CMAIN : CMAIN + EWIDE - ECLS], head_ref[0])
    launch_part(0)
    prepare(0)
    first_load.wait()
    loaded = set()

    for layer in reversed(range(L)):
        base = 3 * (L - 1 - layer)

        def mat(which):
            def read(k):
                if (layer, which) not in loaded:
                    loaded.add((layer, which))
                    weight(layer, which).wait()
                return wbuf[weight_slot(layer, which), k]

            return read

        def slope(k):
            slope_load(layer, k).wait()
            return gp[k % 2]

        def kept(i):
            kept_load(layer, i).wait()
            return xb[...]

        def at(point):
            if point.startswith("mlp"):
                k = int(point[3:])
                if k + 2 < FF // D:
                    slope_load(layer, k + 2).start()
                elif layer > 0:
                    slope_load(layer - 1, k - 2).start()
                if k == 0:
                    swap(base, 0).start()
                if k == 3:
                    for n in swaps(base + 1):
                        swap(base + 1, n).start()
                    weight(layer, 2).start()
                    if layer > 0:
                        weight(layer - 1, 0).start()
                if k % 2:
                    tick()
            elif point == "resid":
                kept_load(layer, 0).start()
                if layer == L - 1:
                    heads_load(layer).wait()
            elif point == "sent":
                if layer < L - 1:
                    heads_load(layer).wait()
                launch(base)
            elif point == "head0":
                tick()
            elif point == "head1":
                launch(base + 1)
            elif point == "head2":
                tick()
                if layer > 0:
                    heads_load(layer - 1).start()
            elif point == "heads":
                for n in swaps(base + 2):
                    swap(base + 2, n).start()
                tick()
            elif point == "done":
                if layer > 0:
                    weight(layer - 1, 1).start()
                    kept_load(layer - 1, 1).start()
                    launch(base + 2)

        backward_body(
            layer, dcur, er, ba, vec_ref, mask_ref, qk, (mat(0), mat(1), mat(2)), slope, kept, scratch,
            (ds_.at[layer], dr_.at[layer], gs_.at[layer], gr_.at[layer]), at,
        )
    dgrid = dcur[...]
    spot = lax.broadcasted_iota(jnp.int32, (TOK, D), 0)
    er[:TOK, :] = dgrid
    inside = jnp.where(spot % SLOTS < GRID, dgrid, 0.0)
    er[EVEC + GLOB : EVEC + GLOB + 1, :] = jnp.sum(inside, 0, keepdims=True)
    er[EVEC + GLOB + 1 : EVEC + GLOB + 3, :] = dgrid[GRID : GRID + 2, :]
    launch_part(1)
    launch(total - 1)
    shared = False
    while under_way:
        tick()
        if not shared and stage_of("group", total - 1) >= 3 and stage_of("part", 1) >= STAGES - 1:
            shared = True
            n = NF * times
            me = f * times + t

            def send(i, carry):
                other = (me + i) % n
                remote(sq, square_all.at[me], qs, qr, (other // times, other % times)).start()
                return carry

            lax.fori_loop(1, n, send, 0)
            square_all[me] = sq[...]
    for layer in range(L):
        for n in range(2):
            forward_swap(layer, n).wait_send()
    for gi in range(total):
        spread_y(gi).wait_send()
        spread_c(gi).wait_send()
    for n in range(2):
        part_over(n).wait_send()
        for dz in range(1, count):
            part_along(n, dz).wait_send()
        part_y(n).wait_send()
        part_c(n).wait_send()
    wait_small(times, small_all, ss, sr)
    wait_small(times, square_all, qs, qr)


def backward_all(times, dout, xs, gp, qk, fa, vec, mask, pnorm, head, end_rows, small, wcol, wdown):
    count = times // 2
    n = NF * times
    total = len(RGROUPS)
    dma = pltpu.SemaphoreType.DMA
    most = max(PWIDE)
    return pl.pallas_call(
        functools.partial(backward_all_kernel, times),
        out_shape=(
            jax.ShapeDtypeStruct((2 * L, 2, 2, 96, D), BF),
            jax.ShapeDtypeStruct((L, 2, 192, D), BF),
            jax.ShapeDtypeStruct((2, 2, 2, 96, most), BF),
            jax.ShapeDtypeStruct((n, 8, 128), F32),
            jax.ShapeDtypeStruct((n, 8, 128), F32),
            jax.ShapeDtypeStruct(fa.shape, BF),
        ),
        in_specs=[aspec()] * 5 + [vspec()] * 6 + [aspec()] * 2,
        out_specs=(vspec(),) * 5 + (aspec(),),
        scratch_shapes=[
            VM((2, 4, D, D), BF),
            VM((2, TOK, D), F32),
            VM((TOK, D), F32),
            VM((TOK, D), F32),
            VM((EWIDE, D), F32),
            VM((PER, NF, QROWS, 128), BF),
            VM((9, TOK, D), BF),
            VM((4, 2 * TOK, D), BF),
            VM((L, TOK, 384), BF),
            VM((L, 2, TOK, D), BF),
            VM((L, 2, TOK, D), BF),
            VM((2, 2, count, 96, 384), F32),
            VM((2, 2, count, 96, 384), BF),
            VM((SLOTS_R, 2, 2, count, 96, 384), BF),
            VM((2, count, 96, 384), F32),
            VM((2, count, 96, 384), BF),
            VM((SLOTS_R, 2, count, 96, 384), BF),
            VM((count, 2, 96, 384), BF),
            VM((2, 96, 384), F32),
            VM((SLOTS_R, count - 1, 2, 96, 384), BF),
            *[VM((count, 96, w), BF) for w in PWIDE],
            *[VM((count, 96, w), F32) for w in PWIDE],
            *[VM((count, 96, w), BF) for w in PWIDE],
            *[VM((count, 96, w), BF) for w in PWIDE],
            *[VM((count - 1, 96, w), BF) for w in PWIDE],
            VM((8, 128), F32),
            dma((L, 3)), dma((L, 4)), dma((L, 2)), dma((L + 1,)), dma((4, 2)),
            dma((L, 2)), dma((L, 2)), dma((total, 2)), dma((total, 2)),
            dma((total, 2)), dma((total, 2)), dma((total, 2)), dma((total, 2)),
            dma((total, count - 1)), dma((total, count - 1)),
            dma((total,)), dma((total,)), dma((total,)), dma((total,)),
            dma, dma, dma, dma,
            dma((2,)), dma((2,)), dma((2, count - 1)), dma((2, count - 1)), dma((2,)), dma((2,)), dma((2,)), dma((2,)),
            pltpu.SemaphoreType.REGULAR((count + 1,)),
            *[dma((L, PER, NF - 1))] * 4,
        ]
        + BACKWARD_SCRATCH,
        compiler_params=pltpu.CompilerParams(
            collective_id=2 + 2 * L, has_side_effects=True, vmem_limit_bytes=63 * 1024 * 1024
        ),
        name="backward_all",
    )(dout, xs, gp, qk, fa, vec, mask, pnorm, head, end_rows, small, wcol, wdown)[:5]


def adam(weight, first, second, grad):
    first = DECAY_FIRST * first + (1.0 - DECAY_FIRST) * grad
    second = DECAY_SECOND * second + (1.0 - DECAY_SECOND) * grad * grad
    fix_one = 1.0 - DECAY_FIRST**STEP
    fix_two = 1.0 - DECAY_SECOND**STEP
    weight = weight - LEARN_RATE * (
        first / fix_one / (jnp.sqrt(second / fix_two) + EPSILON) + WEIGHT_DECAY * weight
    )
    return (weight, first, second)


def pad_to(v, axis, size):
    pads = [(0, 0)] * v.ndim
    pads[axis] = (0, size - v.shape[axis])
    return jnp.pad(v, pads)


def embed_units(embedding, classifier, vectors, f):
    width = embedding.shape[1]
    blocks = embedding[:NGRID].reshape(NF, FROWS // NF, 2, HALF, width)
    block = lax.dynamic_index_in_dim(blocks, f, 0, keepdims=False).transpose(1, 0, 2, 3)
    block = block.reshape(2, GRID, width)
    tokens = jnp.where(f == 0, vectors[GLOB + 1 : GLOB + 3], 0.0)
    tokens = jnp.stack([tokens, jnp.zeros_like(tokens)])
    block = jnp.concatenate([block, tokens, jnp.zeros((2, SLOTS - GRID - 2, width), F32)], 1)
    rest = classifier[:, CMAIN:].T
    unit = jnp.concatenate(
        [
            block.reshape(TOK, width), vectors, jnp.zeros((ECLS - EVEC - VROWS, width), F32),
            pad_to(rest, 0, EWIDE - ECLS),
        ],
        0,
    )
    return unit.T.astype(BF), embedding[NGRID:].T.astype(BF), classifier[:, :CMAIN].astype(BF)


def local(
    patches, column_mask, labels, clip_weights, wide_weights, down_weights, embedding, classifier,
    vectors, class_bias, wide_first, down_first, embedding_first, classifier_first, vectors_first,
    bias_first, wide_second, down_second, embedding_second, classifier_second, vectors_second,
    bias_second,
):
    times = lax.axis_size("tm")
    f, t = lax.axis_index("freq"), lax.axis_index("tm")
    half = t % 2
    pair = t // 2
    rows_dev = FROWS // NF
    kernels = D // times == 96
    shard = D // times
    columns = column_mask.reshape(times, CPD, HALF) > 0
    mine_columns = lax.dynamic_index_in_dim(columns, t, 0, keepdims=False)
    raw = patches.reshape(rows_dev, CPD, HALF, PATCH)

    pixels = raw.astype(F32)
    live = mine_columns.astype(F32)[None, :, :, None]
    sums = jnp.stack(
        [
            jnp.sum(pixels * live),
            jnp.sum(pixels * pixels * live),
            jnp.sum(live) * (rows_dev * PATCH),
        ]
    )
    keep_block, give_block = (
        pad_to(lax.dynamic_index_in_dim(raw, i, 1, keepdims=False).reshape(GRID, PATCH), 0, SLOTS)
        for i in (half, 1 - half)
    )

    wide_low = wide_weights.astype(BF)
    down_low = down_weights.astype(BF)
    unit_embed, unit_patch, unit_class = embed_units(embedding, classifier, vectors, f)

    clip_columns = lax.dynamic_slice(columns, (pair * 2, half, 0), (2, 1, HALF)).reshape(2, HALF)
    slots = jnp.concatenate(
        [
            jnp.broadcast_to(jnp.tile(clip_columns, (1, rows_dev)), (NF, 2, GRID)),
            jnp.broadcast_to(
                ((jnp.arange(NF)[:, None] == 0) & (jnp.arange(2)[None, :] == 0))[:, :, None], (NF, 2, 2)
            ),
            jnp.zeros((NF, 2, SLOTS - GRID - 2), bool),
        ],
        2,
    ).reshape(NF * TOK)
    mask = jnp.where(slots, 0.0, -1e30).astype(F32)

    if kernels:
        units = wide_low.reshape(L, shard, 2, 4, D).transpose(0, 2, 3, 1, 4)
        wcol, wdown, class_main, vec, xs, fa, gp, qk, pnorm = forward_all(
            times, units.reshape(2 * L, 2, 2, shard, D), down_low.reshape(L, 2, 192, D), unit_embed, unit_patch, unit_class,
            jnp.broadcast_to(pad_to(sums, 0, 128), (8, 128)), keep_block, give_block, mask.reshape(1, -1),
        )
        class_main = class_main.reshape(D, CMAIN)
    else:
        wide_all = lax.all_gather(wide_low, "tm", axis=1, tiled=True)
        wcol = wide_all.reshape(L, D, 2, 4, D).transpose(0, 2, 3, 1, 4)
        wcol = wcol.reshape(2 * L, 2, 2, 4, 2, 96, D)
        wdown = lax.all_gather(down_low, "tm", axis=1, tiled=True).reshape(L, 4, 2, 2, 192, D)
        vec = lax.all_gather(unit_embed, "tm", axis=0, tiled=True).T.astype(F32)
        patch = lax.all_gather(unit_patch, "tm", axis=0, tiled=True)
        class_main = lax.all_gather(unit_class, "tm", axis=0, tiled=True)
        sums = lax.psum(sums, ("freq", "tm"))
        take_block = lax.ppermute(
            give_block, "tm", [(i, i + 1 - 2 * (i % 2)) for i in range(times)]
        )
        pixels = jnp.concatenate(
            [jnp.where(half == 0, keep_block, take_block), jnp.where(half == 0, take_block, keep_block)], 0
        )
        center = sums[0] / sums[2]
        mel_scale = lax.rsqrt(sums[1] / sums[2] - center * center + 1e-05)
        inside = (jnp.arange(TOK) % SLOTS < GRID)[:, None]
        pnorm = jnp.where(inside, (pixels.astype(F32) - center) * mel_scale, 0.0).astype(BF)
        x = nt(pnorm, patch) + vec[:TOK] + jnp.where(inside, vec[EVEC + GLOB], 0.0)
        xs, fa, gp, qk = [x], [], [], []
        for layer in range(L):
            x, x1, acts, slopes, heads = forward_layer(layer, x, vec, mask.reshape(1, -1), wcol, wdown)
            xs += [x1, x]
            fa.append(acts)
            gp.append(slopes)
            qk.append(heads)
    wcol = wcol.reshape(2 * L, 4, D, D)
    wdown = wdown.reshape(L, 4, D, D)
    vec_all = vec[EVEC : EVEC + VROWS]
    class_all = jnp.concatenate([class_main, vec[ECLS : ECLS + CLASSES - CMAIN].T.astype(BF)], 1)

    owner = (f == 0).astype(F32)
    special = xs[2 * L][GRID : GRID + 2]
    normed_end, scale_end = norm_rows(special)
    feature = jnp.mean(normed_end * vec_all[GLOB + 3] + vec_all[GLOB + 4], 0, keepdims=True).astype(BF)
    logits = nn(feature, class_all) + class_bias
    clip = pair * CPD + half
    flags = lax.dynamic_slice_in_dim(labels, clip, 1, 0).astype(F32)
    weight = lax.dynamic_slice_in_dim(clip_weights, clip, 1, 0).astype(F32)[:, None]
    weight_total = jnp.sum(clip_weights).astype(F32)
    loss_part = owner * jnp.sum(weight * (jax.nn.softplus(logits) - flags * logits))
    dlogits = owner * weight * (jax.nn.sigmoid(logits) - flags) / weight_total
    dlogits_low = dlogits.astype(BF)
    dfinal = jnp.broadcast_to(0.5 * nt(dlogits_low, class_all), (2, D))
    dspecial = norm_back(dfinal * vec_all[GLOB + 3], normed_end, scale_end)
    end_rows = jnp.stack([jnp.sum(dfinal * normed_end, 0), jnp.sum(dfinal, 0)])
    dx = jnp.concatenate(
        [jnp.zeros((GRID, D), F32), dspecial, jnp.zeros((TOK - GRID - 2, D), F32)], 0
    )
    small = jnp.concatenate([dlogits.reshape(-1), loss_part.reshape(1)])
    small = pad_to(small, 0, 1024).reshape(8, 128)
    if kernels:
        head = jnp.stack([pad_to(feature, 0, 16), pad_to(pad_to(dlogits_low, 1, D), 0, 16)])
        gcol, gdown, gpart, small_all, square_all = backward_all(
            times, dx, xs, gp, qk, fa, vec, mask.reshape(-1, 1), pnorm, head, end_rows, small, wcol, wdown
        )
        small = jnp.sum(small_all, 0).reshape(-1)
        square_total = jnp.sum(square_all)
        gcol = gcol.astype(F32)
        grad_wide = gcol.reshape(L, 2, 4, shard, D).transpose(0, 3, 1, 2, 4).reshape(L, shard, 8 * D)
        grad_down = gdown.reshape(L, FF // times, D).astype(F32)
        gpart = gpart.astype(F32).reshape(2, NF, shard, -1)
        grad_pos = gpart[1, :, :, :TOK].reshape(NF, shard, 2, SLOTS)[:, :, :, :GRID]
        grad_pos = grad_pos.reshape(NF, shard, 2, rows_dev, HALF).transpose(0, 3, 2, 4, 1).reshape(NGRID, shard)
        summed = jnp.sum(gpart, 1)
        grad_embed = jnp.concatenate([grad_pos, summed[1, :, EWIDE : EWIDE + PATCH].T], 0)
        grad_class = jnp.concatenate(
            [summed[0, :, :CMAIN], summed[1, :, ECLS : ECLS + CLASSES - CMAIN]], 1
        )
        grad_vectors = summed[1, :, EVEC : EVEC + VROWS].T
    else:
        ba = [None] * L
        er = jnp.zeros((EWIDE, D), F32)
        for layer in reversed(range(L)):
            dx, ba[layer], rows = backward_layer(
                layer, dx, xs[2 * layer], xs[2 * layer + 1], gp[layer], qk[layer], vec, mask.reshape(-1, 1), wcol, wdown
            )
            er = er + rows
        dgrid = jnp.where(inside, dx, 0.0)
        grad_vectors = er[EVEC : EVEC + GLOB]
        grad_vectors = jnp.concatenate(
            [grad_vectors, jnp.sum(dgrid, 0, keepdims=True), dx[GRID : GRID + 2], end_rows], 0
        )
        wides, downs = [], []
        for l in range(L):
            cols = [tn(fa[l][0], ba[l][i]) for i in range(3)]
            cols += [tn(fa[l][1], ba[l][3])]
            cols += [tn(fa[l][2], ba[l][4 + i]) for i in range(4)]
            wides.append(jnp.concatenate(cols, 1))
            downs.append(jnp.concatenate([tn(fa[l][3 + i], ba[l][8]) for i in range(4)], 0))
        dpos = dgrid.reshape(2, SLOTS, D)[:, :GRID].reshape(2, rows_dev, HALF, D)
        dpos = dpos.transpose(1, 0, 2, 3).reshape(rows_dev * 2 * HALF, D)
        dpos = lax.dynamic_update_slice(jnp.zeros((NGRID, D), F32), dpos, (f * rows_dev * 2 * HALF, 0))
        dembed = jnp.concatenate([dpos, tn(pnorm, dgrid.astype(BF))], 0)
        grads = (
            lax.psum_scatter(jnp.stack(wides), "tm", scatter_dimension=1, tiled=True),
            lax.psum_scatter(jnp.stack(downs), "tm", scatter_dimension=1, tiled=True),
            lax.psum_scatter(dembed, "tm", scatter_dimension=1, tiled=True),
            lax.psum_scatter(tn(feature, dlogits_low), "tm", scatter_dimension=0, tiled=True),
            lax.psum_scatter(grad_vectors, "tm", scatter_dimension=1, tiled=True),
        )
        grads = lax.psum(grads, "freq")
        grad_wide, grad_down, grad_embed, grad_class, grad_vectors = grads
        squares = sum(jnp.sum(v * v) for v in grads)
        square_total, small = lax.psum(
            (jnp.where(f == 0, squares, 0.0), small.reshape(-1)), ("freq", "tm")
        )
    grad_bias = small[:CLASSES]
    loss_sum = small[CLASSES]
    grad_norm = jnp.sqrt(square_total + jnp.sum(grad_bias * grad_bias))
    coef = jnp.minimum(1.0, 1.0 / (grad_norm + 1e-06))

    params = (wide_weights, down_weights, embedding, classifier, vectors, class_bias)
    firsts = (wide_first, down_first, embedding_first, classifier_first, vectors_first, bias_first)
    seconds = (wide_second, down_second, embedding_second, classifier_second, vectors_second, bias_second)
    grads = (grad_wide, grad_down, grad_embed, grad_class, grad_vectors, grad_bias)
    news = [adam(w, m, v, g * coef) for w, m, v, g in zip(params, firsts, seconds, grads)]
    masters = [n[0] for n in news]
    return (
        *masters,
        *[n[1] for n in news],
        *[n[2] for n in news],
        *[m.astype(BF) for m in masters[:4]],
        grad_norm,
        loss_sum,
        weight_total,
    )


def solution(mesh):
    split = (
        P(None, "tm", None), P(None, "tm", None), P(None, "tm"), P("tm", None), P(None, "tm"), P(),
    )
    return jax.shard_map(
        local,
        mesh=mesh,
        in_specs=(P("freq", "tm", None), P(), P(), P()) + split * 3,
        out_specs=split * 3 + split[:4] + (P(), P(), P()),
        check_vma=False,
    )
```

```python
import functools

import jax
import jax.numpy as jnp
from jax import lax
from jax.experimental import pallas as pl
from jax.experimental.pallas import tpu as pltpu
from jax.sharding import PartitionSpec as P

D = 768
HEADS = 12
HDIM = 64
FF = 3072
L = 2
FROWS = 12
HALF = 52
PATCH = 256
STEP = 5
CPD = 2
NGRID = FROWS * 2 * HALF
CLASSES = 527
VROWS = 29
GLOB = L * 8 + L * (FF // D)

TOK = 320
PER = 3
NF = 4

DECAY_FIRST = 0.5
DECAY_SECOND = 0.5
LEARN_RATE = 0.03
WEIGHT_DECAY = 0.05
EPSILON = 1e-08

MESH = pl.DeviceIdType.MESH
BF = jnp.bfloat16
F32 = jnp.float32
VLIM = 60 * 1024 * 1024
VM = pltpu.VMEM


def nn(a, b):
    return lax.dot_general(a, b, (((1,), (0,)), ((), ())), preferred_element_type=F32)


def nt(a, b):
    return lax.dot_general(a, b, (((1,), (1,)), ((), ())), preferred_element_type=F32)


def tn(a, b):
    return lax.dot_general(a, b, (((0,), (0,)), ((), ())), preferred_element_type=F32)


def norm_rows(x):
    center = jnp.mean(x, -1, keepdims=True)
    shifted = x - center
    scale = lax.rsqrt(jnp.mean(shifted * shifted, -1, keepdims=True) + 1e-06)
    return (shifted * scale, scale)


def norm_back(dnorm, normed, scale):
    return scale * (
        dnorm
        - jnp.mean(dnorm, -1, keepdims=True)
        - normed * jnp.mean(dnorm * normed, -1, keepdims=True)
    )


def vspec():
    return pl.BlockSpec(memory_space=VM)


def aspec():
    return pl.BlockSpec(memory_space=pl.ANY)


def place():
    f, t = lax.axis_index("freq"), lax.axis_index("tm")
    return f, t, f // 2, f % 2, t // 2, t % 2


def remote(src, dst, ssem, rsem, dev):
    return pltpu.make_async_remote_copy(
        src_ref=src, dst_ref=dst, send_sem=ssem, recv_sem=rsem, device_id=dev, device_id_type=MESH
    )


def greet_all(times):
    f, t = lax.axis_index("freq"), lax.axis_index("tm")
    n = NF * times
    me = f * times + t
    barrier = pltpu.get_barrier_semaphore()

    def hello(i, carry):
        other = (me + i) % n
        pl.semaphore_signal(
            barrier, inc=1, device_id=(other // times, other % times), device_id_type=MESH
        )
        return carry

    lax.fori_loop(1, n, hello, 0)
    pl.semaphore_wait(barrier, n - 1)


def spread_small(times, small, gathered, ssem, rsem):
    f, t = lax.axis_index("freq"), lax.axis_index("tm")
    n = NF * times
    me = f * times + t

    def send(i, carry):
        other = (me + i) % n
        remote(
            small, gathered.at[me], ssem, rsem, (other // times, other % times)
        ).start()
        return carry

    lax.fori_loop(1, n, send, 0)
    gathered[me] = small[...]


def wait_small(times, gathered, ssem, rsem):
    n = NF * times
    many = gathered.at[pl.ds(0, n - 1)]
    pltpu.make_async_copy(many, many, rsem).wait()
    pltpu.make_async_copy(many, many, ssem).wait()


QROWS = TOK + TOK // 2
SLOTS = TOK // 2
GRID = FROWS // NF * HALF
EWIDE = 384
EVEC = TOK
ECLS = 352
CMAIN = 512


def greet_clip():
    f, t = lax.axis_index("freq"), lax.axis_index("tm")
    barrier = pltpu.get_barrier_semaphore()
    for i in range(1, NF):
        pl.semaphore_signal(barrier, inc=1, device_id=((f + i) % NF, t), device_id_type=MESH)
    pl.semaphore_wait(barrier, NF - 1)


def pack_half(v):
    return jnp.concatenate([v[: TOK // 2], v[TOK // 2 :]], 1)


def open_half(v):
    return jnp.concatenate([v[:, :HDIM], v[:, HDIM:]], 0)


def with_mask(block):
    lane = lax.broadcasted_iota(jnp.int32, block.shape, 1)
    query = jnp.where(lane < HDIM, block.astype(F32) * (HDIM ** (-0.5)), 0.0)
    return jnp.where(lane == HDIM, 1.0, query).astype(BF)


def exchange_sems():
    dma = pltpu.SemaphoreType.DMA
    return [dma((PER, NF - 1))] * 4


FORWARD_SCRATCH = [
    VM((2, 2, 2, 4, 2, 96, D), BF),
    VM((4, 2, 2, 192, D), BF),
    VM((PER, NF, QROWS, 128), BF),
    VM((PER, NF, TOK // 2, 128), BF),
    VM((NF * TOK, 128), BF),
    VM((NF * TOK, HDIM), BF),
    VM((TOK, D), F32),
]


def layer_body(layer, x_ref, vec_ref, outs, scratch, orecv, sems, fetch, tick):
    xo_ref, x1_ref, fa_ref, gp_ref, qk_ref = outs
    wbuf, dbuf, qsend, osend, kall, vall, acc = scratch
    qs, qr, os, orr = sems
    f, t = lax.axis_index("freq"), lax.axis_index("tm")

    def row(i):
        return vec_ref[EVEC + layer * 8 + i : EVEC + layer * 8 + i + 1, :]

    def mat(part, q, cols=slice(None)):
        return wbuf[part, q // 2, q % 2, :, :, :, cols].reshape(D, -1)

    normed, _ = norm_rows(x_ref[...])
    act = (normed * row(0) + row(1)).astype(BF)
    fa_ref[0] = act
    fetch(0)

    def to_clip(j, i):
        other = (f + i) % NF
        return remote(
            qsend.at[j, other], qk_ref.at[j, f], qs.at[j, i - 1], qr.at[j, i - 1], (other, t)
        )

    def back_clip(j, i):
        other = (f + i) % NF
        return remote(
            osend.at[j, other], orecv.at[j, f], os.at[j, i - 1], orr.at[j, i - 1], (other, t)
        )

    for j in range(PER):
        cols = slice(256 * j, 256 * (j + 1))
        query = (nn(act, mat(0, 0, cols)) + row(4)[:, cols]).astype(BF)
        key = nn(act, mat(0, 1, cols)).astype(BF)
        value = (nn(act, mat(0, 2, cols)) + row(5)[:, cols]).astype(BF)
        for h in range(NF):
            part = slice(HDIM * h, HDIM * (h + 1))
            qsend[j, h, :TOK] = jnp.concatenate([query[:, part], key[:, part]], 1)
            qsend[j, h, TOK:] = pack_half(value[:, part])
        for i in range(1, NF):
            to_clip(j, i).start()
        qk_ref[j, f] = qsend[j, f]
    tick()
    for j in range(PER):
        for i in range(1, NF):
            to_clip(j, i).wait_recv()
        for s in range(NF):
            kall[s * TOK : (s + 1) * TOK, :HDIM] = qk_ref[j, s, :TOK, HDIM:]
            vall[s * TOK : (s + 1) * TOK] = open_half(qk_ref[j, s, TOK:])

        def attend(i, carry):
            s = (f + i) % NF
            halves = []
            for h in range(2):
                lo = h * (TOK // 2)
                scores = nt(with_mask(qk_ref[j, s, lo : lo + TOK // 2]), kall[...])
                top = jnp.max(scores, -1, keepdims=True)
                expo = jnp.exp(scores - top)
                total = jnp.sum(expo, -1, keepdims=True)
                probs = (expo * (1.0 / total)).astype(BF)
                halves.append(nn(probs, vall[...]).astype(BF))
            osend[j, s] = jnp.concatenate(halves, 1)

            @pl.when(i > 0)
            def _():
                remote(
                    osend.at[j, s], orecv.at[j, f], os.at[j, i - 1], orr.at[j, i - 1], (s, t)
                ).start()

            return carry

        lax.fori_loop(1, NF, attend, 0)
        lax.fori_loop(0, 1, attend, 0)
        orecv[j, f] = osend[j, f]
        tick()
    parts = []
    for j in range(PER):
        for i in range(1, NF):
            back_clip(j, i).wait_recv()
        for h in range(NF):
            parts.append(open_half(orecv[j, h]))
    mixed = jnp.concatenate(parts, 1)
    fa_ref[1] = mixed
    resid = x_ref[...] + nn(mixed, mat(0, 3)) + row(6)
    x1_ref[...] = resid
    normed, _ = norm_rows(resid)
    fa_ref[2] = (normed * row(2) + row(3)).astype(BF)
    acc[...] = resid + row(7)
    fetch(1)
    fetch(2)

    def mlp(k, carry):
        bias = vec_ref[pl.ds(EVEC + L * 8 + layer * 4 + k, 1), :]
        before = nn(fa_ref[2], mat(1, k)) + bias
        lower = 0.5 * (1.0 + lax.erf(before * 0.7071067811865476))
        gp_ref[k] = lower + before * jnp.exp(-0.5 * before * before) * 0.3989422804014327
        hidden = (before * lower).astype(BF)
        fa_ref[3 + k] = hidden
        acc[...] += nn(hidden, dbuf[k].reshape(D, D))
        return carry

    for k in range(0, FF // D, 2):
        lax.fori_loop(k, k + 2, mlp, 0)
        tick()
    xo_ref[...] = acc[...]
    for j in range(PER):
        for i in range(1, NF):
            to_clip(j, i).wait_send()
            back_clip(j, i).wait_send()


def load_mask(mask, kall):
    def body(sem):
        copy = pltpu.make_async_copy(mask, kall, sem)
        copy.start()
        copy.wait()

    pl.run_scoped(body, pltpu.SemaphoreType.DMA)


def forward_kernel(
    layer, x_ref, vec_ref, mask, wcol, wdown,
    xo_ref, x1_ref, fa_ref, gp_ref, qk_ref,
    wbuf, dbuf, qsend, osend, kall, vall, acc, orecv, wsem, qs, qr, os, orr,
):
    loads = [
        pltpu.make_async_copy(wcol.at[2 * layer], wbuf.at[0], wsem.at[0]),
        pltpu.make_async_copy(wcol.at[2 * layer + 1], wbuf.at[1], wsem.at[1]),
        pltpu.make_async_copy(wdown.at[layer], dbuf, wsem.at[2]),
    ]
    for load in loads:
        load.start()
    load_mask(mask, kall)
    greet_clip()
    layer_body(
        layer, x_ref, vec_ref, (xo_ref, x1_ref, fa_ref, gp_ref, qk_ref),
        (wbuf, dbuf, qsend, osend, kall, vall, acc), orecv, (qs, qr, os, orr),
        lambda part: loads[part].wait(), lambda: None,
    )


def forward_layer(layer, x, vec, mask, wcol, wdown):
    return pl.pallas_call(
        functools.partial(forward_kernel, layer),
        out_shape=(
            jax.ShapeDtypeStruct((TOK, D), F32),
            jax.ShapeDtypeStruct((TOK, D), F32),
            jax.ShapeDtypeStruct((7, TOK, D), BF),
            jax.ShapeDtypeStruct((FF // D, TOK, D), F32),
            jax.ShapeDtypeStruct((PER, NF, QROWS, 128), BF),
        ),
        in_specs=[vspec()] * 2 + [aspec()] * 3,
        out_specs=(vspec(),) * 5,
        scratch_shapes=FORWARD_SCRATCH
        + [VM((PER, NF, TOK // 2, 128), BF), pltpu.SemaphoreType.DMA((3,))]
        + exchange_sems(),
        compiler_params=pltpu.CompilerParams(
            collective_id=2 + layer, has_side_effects=True, vmem_limit_bytes=VLIM
        ),
        name="forward_layer",
    )(x, vec, mask, wcol, wdown)


GROUPS = (("c", 0), ("c", 1), ("d", 0), ("c", 2), ("c", 3), ("d", 1))
SUBS = tuple((kind, idx, h) for kind, idx in GROUPS for h in (0, 1))
PATHS = "yzyzyzyyzyzy"
AHEAD = 3


def gather_plan():
    moves = {}
    for s, path in enumerate(PATHS):
        lag = 1 if s < 2 else 2
        times = {"along": s - AHEAD, "first": s}
        times["third"] = s + lag
        if path == "y":
            times["second"] = s + lag
            times["third"] = s + 2 * lag
        times["arrive"] = times["third"] + 1
        for action, when in times.items():
            moves.setdefault(max(when, -1), []).append((s, action))
    plan = [sorted(moves[when]) for when in sorted(moves)]
    ready = {s: n for n, step in enumerate(plan) for s, action in step if action == "arrive"}
    return plan, ready


def gather_steps(count, ucol, udown, ocol, odown, sems, prepare):
    zs, zr, own, s1, r1, s2, r2, s3, r3 = sems
    f, t, y, c, g, x = place()
    every = slice(None)

    def source(s):
        kind, idx, h = SUBS[s]
        yy = every if PATHS[s] == "z" else y
        if kind == "c":
            return ucol.at[idx, yy, c, :, pl.ds(h * 384, 384)]
        return udown.at[idx, yy, pl.ds(h * 96, 96), pl.ds(pl.multiple_of(c * 384, 128), 384)]

    def view(s, yy, zz, xx):
        kind, idx, h = SUBS[s]
        if PATHS[s] == "z":
            yy = every
        if kind == "c":
            return ocol.at[idx, yy, c, zz, xx, :, pl.ds(h * 384, 384)]
        return odown.at[
            idx, zz, xx, yy, pl.ds(h * 96, 96), pl.ds(pl.multiple_of(c * 384, 128), 384)
        ]

    def along(s, dz):
        return remote(
            source(s), view(s, y, g, x), zs.at[s, dz - 1], zr.at[s, dz - 1],
            (f, ((g + dz) % count) * 2 + x),
        )

    def keep(s):
        return pltpu.make_async_copy(source(s), view(s, y, g, x), own.at[s])

    def first(s):
        block = view(s, y, every, x)
        return remote(block, block, s1.at[s], r1.at[s], (f, g * 2 + 1 - x))

    def second(s):
        block = view(s, y, every, every)
        return remote(block, block, s2.at[s], r2.at[s], ((1 - y) * 2 + c, t))

    def third(s):
        block = view(s, every, every, every)
        return remote(block, block, s3.at[s], r3.at[s], (y * 2 + 1 - c, t))

    def act(s, action):
        if action == "along":
            prepare(s // 2)
            keep(s).start()
            for dz in range(1, count):
                along(s, dz).start()
        elif action == "first":
            for dz in range(1, count):
                along(s, dz).wait_recv()
            keep(s).wait()
            first(s).start()
        elif action == "second":
            first(s).wait_recv()
            second(s).start()
        elif action == "third":
            (second if PATHS[s] == "y" else first)(s).wait_recv()
            third(s).start()
        else:
            third(s).wait_recv()

    for step in gather_plan()[0]:
        for s, action in step:
            act(s, action)
        yield
    for s in range(len(SUBS)):
        for dz in range(1, count):
            along(s, dz).wait_send()
        first(s).wait_send()
        if PATHS[s] == "y":
            second(s).wait_send()
        third(s).wait_send()
    yield


def loss_part(owner, clip, x_ref, vec, classes, labels, clip_weights, class_bias, dout, head, end_rows, small):
    owner = jnp.where(owner, 1.0, 0.0)
    normed, scale = norm_rows(x_ref[GRID : GRID + 2, :])
    gain = vec[EVEC + GLOB + 3 : EVEC + GLOB + 4, :]
    final = normed * gain + vec[EVEC + GLOB + 4 : EVEC + GLOB + 5, :]
    feature = jnp.mean(final, 0, keepdims=True).astype(BF)
    first_row = lax.broadcasted_iota(jnp.int32, (16, D), 0) == 0
    feature = jnp.where(first_row, jnp.broadcast_to(feature.astype(F32), (16, D)), 0.0).astype(BF)
    head[0] = feature
    main = classes[...].reshape(D, CMAIN)
    tail = vec[ECLS:EWIDE, :].astype(BF)
    logits = jnp.concatenate([nn(feature, main), nt(feature, tail), jnp.zeros((16, 224), F32)], 1)[0:1]
    logits = logits + class_bias[...]
    flags = labels[pl.ds(clip, 1), :].astype(F32)
    weights = clip_weights[...].astype(F32)
    weight = jnp.sum(
        jnp.where(lax.broadcasted_iota(jnp.int32, weights.shape, 1) == clip, weights, 0.0), keepdims=True
    )
    total = jnp.sum(weights, keepdims=True)
    lane = lax.broadcasted_iota(jnp.int32, (1, D), 1)
    inside = lane < CLASSES
    soft = jnp.maximum(logits, 0.0) + jnp.log1p(jnp.exp(-jnp.abs(logits)))
    loss = jnp.sum(jnp.where(inside, soft - flags * logits, 0.0), keepdims=True) * weight * owner
    slope = 1.0 / (1.0 + jnp.exp(-logits))
    grads = jnp.where(inside, owner * weight * (slope - flags) / total, 0.0)
    for i in range(8):
        small[i : i + 1, :] = jnp.zeros((1, 128), F32) if i > 5 else (
            grads[:, 128 * i : 128 * (i + 1)]
            + (jnp.where(lane[:, 128 * i : 128 * (i + 1)] == CLASSES, loss, 0.0))
        )
    grads = jnp.where(first_row, jnp.broadcast_to(grads, (16, D)), 0.0).astype(BF)
    head[1] = grads
    dfinal = 0.5 * (nt(grads[:, :CMAIN], main) + nn(grads[:, CMAIN : CMAIN + EWIDE - ECLS], tail))[0:1]
    end_rows[0:1, :] = jnp.sum(dfinal * normed, 0, keepdims=True)
    end_rows[1:2, :] = 2.0 * dfinal
    special = norm_back(jnp.broadcast_to(dfinal * gain, normed.shape), normed, scale)
    dout[...] = jnp.zeros_like(dout)
    dout[GRID : GRID + 2, :] = special


def forward_all_kernel(
    times, wide, down, uemb, upatch, uclass, live, pkeep, psend, labels, clip_weights, class_bias, mask,
    ocol, odown, vec_out, xs_out, fa_out, gp_out, qk_out, pn_out, dout_out, head, end_rows, small,
    wbuf, dbuf, qsend, osend, kall, vall, acc, orecv, sall, precv, emb, patches, classes, vec, xs, fa, gp, qk, pn,
    zs, zr, own, s1, r1, s2, r2, s3, r3, es, er, exs, exr, ss, sr, ps, pr, wsem, osem,
    qs0, qr0, os0, or0, qs1, qr1, os1, or1, ucol, udown, cols_wide, cols_down, stats, dout, psem,
):
    f, t, y, c, g, x = place()
    count = times // 2
    over_x = (f, g * 2 + 1 - x)

    def fetch_master(group):
        kind, idx = GROUPS[group]
        if kind == "c":
            src = wide.at[idx // 2, :, pl.ds(idx % 2 * 4 * D, 4 * D)]
            return pltpu.make_async_copy(src, cols_wide.at[idx], psem.at[group])
        return pltpu.make_async_copy(down.at[idx], cols_down.at[idx], psem.at[group])

    prepared = set()

    def prepare(group):
        if group in prepared:
            return
        prepared.add(group)
        fetch_master(group).wait()
        kind, idx = GROUPS[group]
        for q in range(4):
            if kind == "c":
                ucol[idx, q // 2, q % 2] = cols_wide[idx, :, q * D : (q + 1) * D].astype(BF)
            else:
                udown[idx, q // 2, q % 2 * 96 : q % 2 * 96 + 96] = cols_down[idx, q * 96 : (q + 1) * 96].astype(BF)

    for group in range(len(GROUPS)):
        fetch_master(group).start()
    row = lax.broadcasted_iota(jnp.int32, (8, 128), 1)
    stats[...] = jnp.zeros_like(stats)
    for n, block in enumerate((pkeep, psend)):
        pixel, alive = block[...].astype(F32), live[n]
        masked = pixel * alive
        for lane, value in enumerate((masked, masked * pixel, alive * float(PATCH))):
            stats[...] += jnp.where(row == lane, jnp.sum(value, keepdims=True), 0.0)
    greet_all(times)
    spread_small(times, stats, sall, ss, sr)
    swap = remote(psend, precv, ps, pr, over_x)
    swap.start()
    load_mask(mask, kall)
    units = ((uemb, emb), (upatch, patches), (uclass, classes))

    def unit_along(n, dz):
        src, dst = units[n]
        return remote(
            src, dst.at[g, x], es.at[n, dz - 1], er.at[n, dz - 1], (f, ((g + dz) % count) * 2 + x)
        )

    def loads(layer, part):
        if part < 2:
            return pltpu.make_async_copy(ocol.at[2 * layer + part], wbuf.at[part], wsem.at[layer, part])
        return pltpu.make_async_copy(odown.at[layer], dbuf, wsem.at[layer, part])

    def unit_over(n):
        block = units[n][1].at[:, x]
        return remote(block, block, exs.at[n], exr.at[n], over_x)

    for n in range(3):
        units[n][1][g, x] = units[n][0][...]
    for n in range(2):
        for dz in range(1, count):
            unit_along(n, dz).start()
    steps = gather_steps(count, ucol, udown, ocol, odown, (zs, zr, own, s1, r1, s2, r2, s3, r3), prepare)
    plan, ready = gather_plan()
    last = len(plan) - 1
    done = [-1]

    started, allowed = set(), {(0, part) for part in range(3)}

    def arrived(layer, part):
        group = 3 * layer + part
        return max(ready[2 * group], ready[2 * group + 1])

    def prefetch():
        for layer, part in sorted(allowed - started):
            if done[0] >= arrived(layer, part):
                loads(layer, part).start()
                started.add((layer, part))

    def tick():
        if done[0] < last:
            next(steps)
            done[0] += 1
        prefetch()

    def need(step):
        while done[0] < step:
            tick()

    need(0)
    for n in range(2):
        for dz in range(1, count):
            unit_along(n, dz).wait_recv()
        unit_over(n).start()
    need(1)
    for n in range(2):
        unit_over(n).wait_recv()
    swap.wait_recv()
    wait_small(times, sall, ss, sr)
    sums = jnp.sum(sall[...], 0)
    total, squares, live = sums[0:1, 0:1], sums[0:1, 1:2], sums[0:1, 2:3]
    center = total / live
    mel_scale = lax.rsqrt(squares / live - center * center + 1e-05)
    inside = lax.broadcasted_iota(jnp.int32, (SLOTS, PATCH), 0) < GRID

    def normalized(block):
        return jnp.where(inside, (block[...].astype(F32) - center) * mel_scale, 0.0).astype(BF)

    pn[pl.ds(pl.multiple_of(x * SLOTS, SLOTS), SLOTS)] = normalized(pkeep)
    pn[pl.ds(pl.multiple_of((1 - x) * SLOTS, SLOTS), SLOTS)] = normalized(precv)
    vec[...] = emb[...].reshape(D, EWIDE).astype(F32).T
    patch = patches[...].reshape(D, PATCH)
    bias = vec[EVEC + GLOB : EVEC + GLOB + 1, :]
    spot = lax.broadcasted_iota(jnp.int32, (TOK, D), 0)
    grid_row = jnp.logical_or(spot < GRID, jnp.logical_and(spot >= SLOTS, spot < SLOTS + GRID))
    xs[0] = (nt(pn[...], patch) + vec[:TOK]) + jnp.where(grid_row, bias, 0.0)

    copies = [
        pltpu.make_async_copy(vec, vec_out, osem.at[1]),
        pltpu.make_async_copy(pn, pn_out, osem.at[2]),
    ]
    for copy in copies:
        copy.start()
    sems = ((qs0, qr0, os0, or0), (qs1, qr1, os1, or1))
    for dz in range(1, count):
        unit_along(2, dz).start()
    for layer in range(L):
        if layer == 1:
            for dz in range(1, count):
                unit_along(2, dz).wait_recv()
            unit_over(2).start()

        def fetch(part):
            if part == 1 and layer + 1 < L:
                allowed.add((layer + 1, 0))
            need(arrived(layer, part))
            prefetch()
            loads(layer, part).wait()

        layer_body(
            layer, xs.at[2 * layer], vec,
            (xs.at[2 * layer + 2], xs.at[2 * layer + 1], fa.at[layer], gp.at[layer], qk.at[layer]),
            (wbuf, dbuf, qsend, osend, kall, vall, acc), orecv.at[layer], sems[layer], fetch, tick,
        )
        more = [
            pltpu.make_async_copy(fa.at[layer], fa_out.at[layer], osem.at[3 + 4 * layer]),
            pltpu.make_async_copy(gp.at[layer], gp_out.at[layer], osem.at[4 + 4 * layer]),
            pltpu.make_async_copy(qk.at[layer], qk_out.at[layer], osem.at[5 + 4 * layer]),
        ]
        if layer == 0:
            more.append(pltpu.make_async_copy(xs.at[pl.ds(0, 2)], xs_out.at[pl.ds(0, 2)], osem.at[6]))
        else:
            more.append(pltpu.make_async_copy(xs.at[pl.ds(2, 3)], xs_out.at[pl.ds(2, 3)], osem.at[10]))
        for copy in more:
            copy.start()
        copies += more
        allowed.update((layer + 1, part) for part in (1, 2) if layer + 1 < L)
    unit_over(2).wait_recv()
    loss_part(
        f == 0, g * 2 + x, xs.at[2 * L], vec, classes, labels, clip_weights, class_bias, dout, head, end_rows, small
    )
    copies.append(pltpu.make_async_copy(dout, dout_out, osem.at[0]))
    copies[-1].start()
    need(last)
    next(steps)
    for n in range(3):
        for dz in range(1, count):
            unit_along(n, dz).wait_send()
        unit_over(n).wait_send()
    swap.wait_send()
    for copy in copies:
        copy.wait()


def forward_all(times, wide, down, uemb, upatch, uclass, live, pkeep, psend, labels, clip_weights, class_bias, mask):
    count = times // 2
    total = len(SUBS)
    dma = pltpu.SemaphoreType.DMA
    outs = (
        ((2 * L, 2, 2, count, 2, 96, D), BF),
        ((L, count, 2, 2, 192, D), BF),
        ((EWIDE, D), F32),
        ((2 * L + 1, TOK, D), F32),
        ((L, 7, TOK, D), BF),
        ((L, FF // D, TOK, D), F32),
        ((L, PER, NF, QROWS, 128), BF),
        ((TOK, PATCH), BF),
        ((TOK, D), F32),
        ((2, 16, D), BF),
        ((2, D), F32),
        ((8, 128), F32),
    )
    return pl.pallas_call(
        functools.partial(forward_all_kernel, times),
        out_shape=tuple(jax.ShapeDtypeStruct(*o) for o in outs),
        in_specs=[aspec()] * 2 + [vspec()] * 9 + [aspec()],
        out_specs=(aspec(),) * (len(outs) - 3) + (vspec(),) * 3,
        scratch_shapes=FORWARD_SCRATCH
        + [
            VM((L, PER, NF, TOK // 2, 128), BF),
            VM((NF * times, 8, 128), F32),
            VM((SLOTS, PATCH), BF),
            VM((count, 2, 96, EWIDE), BF),
            VM((count, 2, 96, PATCH), BF),
            VM((count, 2, 96, CMAIN), BF),
            VM((EWIDE, D), F32),
            VM((2 * L + 1, TOK, D), F32),
            VM((L, 7, TOK, D), BF),
            VM((L, FF // D, TOK, D), F32),
            VM((L, PER, NF, QROWS, 128), BF),
            VM((TOK, PATCH), BF),
            dma((total, count - 1)), dma((total, count - 1)), dma((total,)),
            dma((total,)), dma((total,)), dma((total,)), dma((total,)), dma((total,)), dma((total,)),
            dma((3, count - 1)), dma((3, count - 1)), dma((3,)), dma((3,)),
            dma, dma, dma, dma, dma((L, 3)), dma((12,)),
        ]
        + exchange_sems() * L
        + [
            VM((2 * L, 2, 2, 96, D), BF),
            VM((L, 2, 192, D), BF),
            VM((2 * L, 96, 4 * D), F32),
            VM((L, 4 * 96, D), F32),
            VM((8, 128), F32),
            VM((TOK, D), F32),
            dma((len(GROUPS),)),
        ],
        compiler_params=pltpu.CompilerParams(
            collective_id=1, has_side_effects=True, vmem_limit_bytes=VLIM
        ),
        name="forward_all",
    )(wide, down, uemb, upatch, uclass, live, pkeep, psend, labels, clip_weights, class_bias, mask)


BACKWARD_SCRATCH = [
    VM((PER, NF, TOK // 2, 128), BF),
    VM((PER, NF, TOK // 2, 128), BF),
    VM((PER, NF, QROWS, 128), BF),
    VM((PER, NF, QROWS, 128), BF),
    VM((NF * TOK, 128), BF),
    VM((NF * TOK, HDIM), BF),
    VM((NF * TOK, HDIM), F32),
    VM((NF * TOK, HDIM), F32),
    VM((NF, TOK, HDIM), BF),
    VM((TOK, D), F32),
]


def backward_body(layer, dcur, er, ba, vec_ref, qk_ref, mats, slope, kept, scratch, sems, at):
    down, up, qkvo = mats
    dsend, drecv, gsend, grecv, kall, vall, dkall, dvall, dqall, acc = scratch
    ds_, dr_, gs_, gr_ = sems
    f, t = lax.axis_index("freq"), lax.axis_index("tm")

    def row(i):
        return vec_ref[EVEC + layer * 8 + i : EVEC + layer * 8 + i + 1, :]

    def note(i, value):
        er[EVEC + i : EVEC + i + 1, :] = jnp.sum(value, 0, keepdims=True)

    ba[8] = dcur[...].astype(BF)
    note(layer * 8 + 7, dcur[...])
    for k in range(FF // D):
        dbefore = nt(ba[8], down(k)) * slope(k)
        note(L * 8 + layer * 4 + k, dbefore)
        ba[4 + k] = dbefore.astype(BF)
        product = nt(ba[4 + k], up(k))
        acc[...] = product if k == 0 else acc[...] + product
        at("mlp%d" % k)
    normed, scale = norm_rows(kept(1))
    dact = acc[...]
    note(layer * 8 + 2, dact * normed)
    note(layer * 8 + 3, dact)
    dcur[...] += norm_back(dact * row(2), normed, scale)
    note(layer * 8 + 6, dcur[...])
    ba[3] = dcur[...].astype(BF)
    at("resid")
    dmixed = nt(ba[3], qkvo(3)).astype(BF)

    def to_clip(j, i):
        other = (f + i) % NF
        return remote(
            dsend.at[j, other], drecv.at[j, f], ds_.at[j, i - 1], dr_.at[j, i - 1], (other, t)
        )

    def back_clip(j, i):
        other = (f + i) % NF
        return remote(
            gsend.at[j, other], grecv.at[j, f], gs_.at[j, i - 1], gr_.at[j, i - 1], (other, t)
        )

    for j in range(PER):
        for h in range(NF):
            lo = 256 * j + HDIM * h
            dsend[j, h] = pack_half(dmixed[:, lo : lo + HDIM])
        for i in range(1, NF):
            to_clip(j, i).start()
        drecv[j, f] = dsend[j, f]
    at("sent")
    root = HDIM ** (-0.5)
    for j in range(PER):
        for s in range(NF):
            kall[s * TOK : (s + 1) * TOK, :HDIM] = qk_ref[j, s, :TOK, HDIM:]
            vall[s * TOK : (s + 1) * TOK] = open_half(qk_ref[j, s, TOK:])
        dkall[...] = jnp.zeros_like(dkall)
        dvall[...] = jnp.zeros_like(dvall)
        for i in range(1, NF):
            to_clip(j, i).wait_recv()

        def attend(s, carry):
            q = with_mask(qk_ref[j, s, :TOK])
            dmix = open_half(drecv[j, s])
            scores = nt(kall[...], q)
            top = jnp.max(scores, 0, keepdims=True)
            expo = jnp.exp(scores - top)
            probs = expo * (1.0 / jnp.sum(expo, 0, keepdims=True))
            dprob = nt(vall[...], dmix)
            inner = jnp.sum(probs * dprob, 0, keepdims=True)
            dscore = (probs * (dprob - inner)).astype(BF)
            dvall[...] += nn(probs.astype(BF), dmix)
            dkall[...] += nn(dscore, q[:, :HDIM])
            dqall[s] = (tn(dscore, kall[:, :HDIM]) * root).astype(BF)
            return carry

        lax.fori_loop(0, NF, attend, 0)
        for s in range(NF):
            span = slice(s * TOK, (s + 1) * TOK)
            gsend[j, s, :TOK] = jnp.concatenate([dqall[s], dkall[span].astype(BF)], 1)
            gsend[j, s, TOK:] = pack_half(dvall[span].astype(BF))
        for i in range(1, NF):
            back_clip(j, i).start()
        grecv[j, f] = gsend[j, f]
        at("head%d" % j)
    for j in range(PER):
        for i in range(1, NF):
            back_clip(j, i).wait_recv()
        cols = slice(256 * j, 256 * (j + 1))
        ba[0, :, cols] = jnp.concatenate([grecv[j, h, :TOK, :HDIM] for h in range(NF)], 1)
        ba[1, :, cols] = jnp.concatenate([grecv[j, h, :TOK, HDIM:] for h in range(NF)], 1)
        ba[2, :, cols] = jnp.concatenate([open_half(grecv[j, h, TOK:]) for h in range(NF)], 1)
    at("heads")
    note(layer * 8 + 4, ba[0].astype(F32))
    note(layer * 8 + 5, ba[2].astype(F32))
    dact = nt(ba[0], qkvo(0)) + nt(ba[1], qkvo(1)) + nt(ba[2], qkvo(2))
    normed, scale = norm_rows(kept(0))
    note(layer * 8 + 0, dact * normed)
    note(layer * 8 + 1, dact)
    dcur[...] += norm_back(dact * row(0), normed, scale)
    for j in range(PER):
        for i in range(1, NF):
            to_clip(j, i).wait_send()
            back_clip(j, i).wait_send()
    at("done")


def backward_kernel(
    layer, dout_ref, x_ref, x1_ref, gp_ref, qk_ref, vec_ref, mask, wcol, wdown,
    dx_ref, ba_ref, er_ref, wbuf, dbuf, wsem, ds_, dr_, gs_, gr_, *scratch,
):
    loads = [
        pltpu.make_async_copy(wdown.at[layer], dbuf, wsem.at[0]),
        pltpu.make_async_copy(wcol.at[2 * layer + 1], wbuf.at[1], wsem.at[1]),
        pltpu.make_async_copy(wcol.at[2 * layer], wbuf.at[0], wsem.at[2]),
    ]
    for load in loads:
        load.start()
    dx_ref[...] = dout_ref[...]
    er_ref[...] = jnp.zeros_like(er_ref)
    load_mask(mask, scratch[4])
    greet_clip()
    for load in loads:
        load.wait()
    backward_body(
        layer, dx_ref, er_ref, ba_ref, vec_ref, qk_ref,
        (lambda k: dbuf[k], lambda k: wbuf[1, k], lambda k: wbuf[0, k]),
        lambda k: gp_ref[k], lambda i: x1_ref[...] if i else x_ref[...],
        scratch, (ds_, dr_, gs_, gr_), lambda point: None,
    )


def backward_layer(layer, dout, x, x1, gp, qk, vec, mask, wcol, wdown):
    return pl.pallas_call(
        functools.partial(backward_kernel, layer),
        out_shape=(
            jax.ShapeDtypeStruct((TOK, D), F32),
            jax.ShapeDtypeStruct((9, TOK, D), BF),
            jax.ShapeDtypeStruct((EWIDE, D), F32),
        ),
        in_specs=[vspec()] * 6 + [aspec()] * 3,
        out_specs=(vspec(),) * 3,
        scratch_shapes=[VM((2, 4, D, D), BF), VM((4, D, D), BF), pltpu.SemaphoreType.DMA((3,))]
        + exchange_sems()
        + BACKWARD_SCRATCH,
        compiler_params=pltpu.CompilerParams(
            collective_id=2 + L + layer, has_side_effects=True, vmem_limit_bytes=VLIM
        ),
        name="backward_layer",
    )(dout, x, x1, gp, qk, vec, mask, wcol, wdown)


RGROUPS = (("d", 1), ("u", 1), ("q", 1), ("d", 0), ("u", 0), ("q", 0))
RFIRST = ("xx", "yx", "xx", "yx", "yx", "xx")
SLOTS_R = 2
BUFS = 2
PWIDE = (CMAIN, EWIDE + PATCH)
STAGES = 5


def backward_all_kernel(
    times, dout_in, xs_in, gp_in, qk_in, fa_in, vec_ref, mask, pn_ref, head_ref, end_ref, small, wcol, wdown,
    gcol, gdown, gpart, scalars, rfa,
    *refs,
):
    (
        wbuf, gp, xb, dcur, er, qk, ba, lbuf, rd, ru, rq, full, low, recv1, mid_own, mid_low, recv2,
        zlow, zown, zrecv, psend, pown, pxr0, pxr1, pzr0, pzr1, sq,
        wsem, gsem, xsem, qsem, ls, fas, far, bs, br, s1, r1, s2, r2, zs, zr, fs, fr, ks, kr,
        ss, sr, qs, qr, p1, p1r, p2, p2r, p3, p3r, p4, p4r, credit,
        ds_, dr_, gs_, gr_, small_all, square_all,
    ) = refs[: -len(BACKWARD_SCRATCH)]
    scratch = refs[-len(BACKWARD_SCRATCH) :]
    f, t, y, c, g, x = place()
    count = times // 2
    over_x = (f, g * 2 + 1 - x)
    over_y = ((1 - y) * 2 + c, t)
    over_c = (y * 2 + 1 - c, t)
    total = len(RGROUPS)
    other_core = 1 - c

    def half_cols(core):
        return pl.ds(pl.multiple_of(core * 384, 128), 384)

    def weight(layer, which):
        src = (wdown.at[layer], wcol.at[2 * layer + 1], wcol.at[2 * layer])[which]
        return pltpu.make_async_copy(src, wbuf.at[weight_slot(layer, which)], wsem.at[layer, which])

    def weight_slot(layer, which):
        return (which % 2 + (L - 1 - layer)) % 2

    def slope_load(layer, k):
        return pltpu.make_async_copy(gp_in.at[layer, k], gp.at[k % 2], gsem.at[layer, k])

    def kept_load(layer, i):
        return pltpu.make_async_copy(xs_in.at[2 * layer + i], xb, xsem.at[layer, i])

    def heads_load(layer):
        return pltpu.make_async_copy(qk_in.at[layer], qk, qsem.at[layer])

    first_load = pltpu.make_async_copy(dout_in, dcur, qsem.at[L])
    first_load.start()
    for which in range(2):
        weight(L - 1, which).start()
    for k in range(2):
        slope_load(L - 1, k).start()
    kept_load(L - 1, 1).start()
    heads_load(L - 1).start()
    greet_all(times)
    spread_small(times, small, small_all, ss, sr)

    def forward_swap(layer, n):
        span = pl.ds(3, 4) if n == 0 else pl.ds(0, 3)
        return remote(
            fa_in.at[layer, span], rfa.at[layer, span], fas.at[layer, n], far.at[layer, n], over_c
        )

    for layer in reversed(range(L)):
        for n in range(2):
            forward_swap(layer, n).start()

    def swap(gi, n):
        kind, l = RGROUPS[gi]
        if kind == "d":
            src, dst = ba.at[8, :, half_cols(other_core)], rd.at[l]
        elif kind == "u":
            src, dst = ba.at[4 + 2 * n + other_core], ru.at[l, n]
        else:
            src, dst = ba.at[2 * n + other_core], rq.at[l, n]
        return remote(src, dst, bs.at[gi, n], br.at[gi, n], over_c)

    def swaps(gi):
        return range(1 if RGROUPS[gi][0] == "d" else 2)

    def left_loads(gi):
        kind, l = RGROUPS[gi]
        out = []
        blocks = {"d": (3, 4, 5, 6), "u": (2,), "q": (0, c)}[kind]
        for n, block in enumerate(blocks):
            for m, src in enumerate((fa_in, rfa)):
                out.append(
                    pltpu.make_async_copy(
                        src.at[l, block], lbuf.at[n, pl.ds(m * TOK, TOK)], ls.at[n, m]
                    )
                )
        return out

    def product(left, own, other, cols):
        return tn(lbuf[left, :TOK], own(cols)) + tn(lbuf[left, TOK:], other(cols))

    def store(gi, h, role, xx, where, value):
        if RFIRST[gi][h] == "y":
            keep, index = role == 0, xx
        else:
            keep, index = x == xx, role

        def save_full():
            full[(gi % BUFS, h, index) + where] = value

        def save_low():
            low[(gi % BUFS, h, index) + where] = value.astype(BF)

        if isinstance(keep, bool):
            (save_full if keep else save_low)()
        else:
            pl.when(keep)(save_full)
            pl.when(jnp.logical_not(keep))(save_low)

    def compute(gi, h):
        kind, l = RGROUPS[gi]
        if kind == "d":

            def one(z, carry):
                prod = product(
                    z, lambda _: ba[8, :, half_cols(c)], lambda _: rd[l], None
                ).reshape(2, 2, 2, 96, 384)
                for xx in range(2):
                    for yy in range(2):
                        for hh in range(2):
                            store(gi, hh, (yy + y) % 2, xx, (z,), prod[xx, yy, hh])
                return carry

            if h == 0:
                lax.fori_loop(0, count, one, 0)
            return
        recv = ru if kind == "u" else rq
        base = 4 if kind == "u" else 0
        for role in range(2):
            yy = y if role == 0 else 1 - y
            left = 0 if kind == "u" else yy
            prod = product(
                left, lambda cols: ba[base + 2 * yy + c, :, cols], lambda cols: recv[l, yy, :, cols],
                slice(h * 384, (h + 1) * 384),
            ).reshape(count, 2, 96, 384)
            for xx in range(2):
                store(gi, h, role, xx, (), prod[:, xx])

    def step1(gi, h):
        return remote(
            low.at[gi % BUFS, h], recv1.at[gi % SLOTS_R, h], s1.at[gi, h], r1.at[gi, h],
            over_y if RFIRST[gi][h] == "y" else over_x,
        )

    def step2(gi, h):
        return remote(
            mid_low.at[h], recv2.at[gi % SLOTS_R, h], s2.at[gi, h], r2.at[gi, h],
            over_x if RFIRST[gi][h] == "y" else over_y,
        )

    def along(gi, h, dz):
        return remote(
            zlow.at[h, (g + dz) % count], zrecv.at[gi % SLOTS_R, h, dz - 1],
            zs.at[gi, h, dz - 1], zr.at[gi, h, dz - 1], (f, ((g + dz) % count) * 2 + x),
        )

    def result(gi, h, yy):
        kind, l = RGROUPS[gi]
        if kind == "d":
            return gdown.at[l, yy, pl.ds(h * 96, 96), half_cols(c)]
        return gcol.at[2 * l + (1 if kind == "u" else 0), yy, c, :, pl.ds(h * 384, 384)]

    def spread_y(gi, h):
        block = result(gi, h, y)
        return remote(block, block, fs.at[gi, h], fr.at[gi, h], over_y)

    def spread_c(gi, h):
        block = result(gi, h, slice(None))
        return remote(block, block, ks.at[gi, h], kr.at[gi, h], over_c)

    def advance(gi, h, stage):
        slot, buf = gi % SLOTS_R, gi % BUFS
        if stage == 1:
            step1(gi, h).wait_recv()
            step1(gi, h).wait_send()
            keep, send = (x, 1 - x) if RFIRST[gi][h] == "y" else (0, 1)
            mid_low[h] = (full[buf, h, send] + recv1[slot, h, send].astype(F32)).astype(BF)
            step2(gi, h).start()
            mid_own[h] = full[buf, h, keep] + recv1[slot, h, keep].astype(F32)
        elif stage == 2:
            step2(gi, h).wait_recv()
            step2(gi, h).wait_send()
            summed = mid_own[h] + recv2[slot, h].astype(F32)
            zlow[h] = summed.astype(BF)
            mid_own[h] = summed
            for dz in range(1, count):
                if gi >= SLOTS_R:
                    pl.semaphore_wait(credit.at[1 + dz], 1)
                along(gi, h, dz).start()
            zown[h] = mid_own[h, g]
            if gi + SLOTS_R < total:
                pl.semaphore_signal(credit.at[0], inc=1, device_id=over_x, device_id_type=MESH)
                pl.semaphore_signal(credit.at[1], inc=1, device_id=over_y, device_id_type=MESH)
        elif stage == 3:
            value = zown[h]
            for dz in range(1, count):
                along(gi, h, dz).wait_recv()
                along(gi, h, dz).wait_send()
                value = value + zrecv[slot, h, dz - 1].astype(F32)
            sq[...] += jnp.sum((value * value).reshape(12, 8, 3, 128), (0, 2))
            kind, l = RGROUPS[gi]
            if kind == "d":
                gdown[l, y, h * 96 : (h + 1) * 96, half_cols(c)] = value.astype(BF)
            else:
                idx = 2 * l + (1 if kind == "u" else 0)
                gcol[idx, y, c, :, h * 384 : (h + 1) * 384] = value.astype(BF)
            if gi + SLOTS_R < total:
                for dz in range(1, count):
                    back = (f, ((g + count - dz) % count) * 2 + x)
                    pl.semaphore_signal(
                        credit.at[1 + dz], inc=1, device_id=back, device_id_type=MESH
                    )
            spread_y(gi, h).start()
        elif stage == 4:
            spread_y(gi, h).wait_recv()
            spread_c(gi, h).start()
        else:
            spread_c(gi, h).wait_recv()

    pxrs, pzrs = (pxr0, pxr1), (pzr0, pzr1)
    psends = [psend.at[:, :, pl.ds(0, w)] for w in PWIDE]
    powns = [pown.at[:, :, pl.ds(0, w)] for w in PWIDE]

    def part_over(n):
        return remote(psends[n], pxrs[n], p1.at[n], p1r.at[n], over_x)

    def part_along(n, dz):
        return remote(
            psends[n].at[(g + dz) % count], pzrs[n].at[dz - 1], p2.at[n, dz - 1], p2r.at[n, dz - 1],
            (f, ((g + dz) % count) * 2 + x),
        )

    def part_y(n):
        block = gpart.at[n, y, c]
        return remote(block, block, p3.at[n], p3r.at[n], over_y)

    def part_c(n):
        block = gpart.at[n, :, c]
        return remote(block, block, p4.at[n], p4r.at[n], over_c)

    def part_compute(n):
        pieces = []
        if n == 0:
            pieces.append((0, tn(head_ref[0], head_ref[1, :, :CMAIN])))
        else:
            pieces.append((0, er[...].T))
            pieces.append((EWIDE, tn(dcur[...].astype(BF), pn_ref[...])))
        for lo, piece in pieces:
            piece = piece.reshape(count, 2, 96, -1)
            span = slice(lo, lo + piece.shape[-1])
            for xx in range(2):

                @pl.when(x == xx)
                def _():
                    powns[n][:, :, span] = piece[:, xx]
                    psends[n][:, :, span] = piece[:, 1 - xx].astype(BF)

        part_over(n).start()

    def part_advance(n, stage):
        if stage == 1:
            part_over(n).wait_recv()
            summed = powns[n][...] + pxrs[n][...].astype(F32)
            powns[n][...] = summed
            part_over(n).wait_send()
            psends[n][...] = summed.astype(BF)
            for dz in range(1, count):
                part_along(n, dz).start()
        elif stage == 2:
            value = powns[n][g]
            for dz in range(1, count):
                part_along(n, dz).wait_recv()
                part_along(n, dz).wait_send()
                value = value + pzrs[n][dz - 1].astype(F32)
            gpart[n, y, c, :, : PWIDE[n]] = value.astype(BF)
            part_y(n).start()
            if n == 1:
                lane = lax.broadcasted_iota(jnp.int32, (96, EWIDE), 1)
                inside = jnp.logical_and(lane % SLOTS < GRID, lane < TOK)
                own = jnp.where(inside, value[:, :EWIDE], 0.0)
                sq[...] += jnp.sum((own * own).reshape(12, 8, 3, 128), (0, 2))
        elif stage == 3:
            part_y(n).wait_recv()
            part_c(n).start()
        else:
            part_c(n).wait_recv()
            value = gpart[n, 0, 0].astype(F32) + gpart[n, 0, 1].astype(F32)
            value = value + gpart[n, 1, 0].astype(F32) + gpart[n, 1, 1].astype(F32)
            value = value[:, : PWIDE[n]]
            if n == 1:
                lane = lax.broadcasted_iota(jnp.int32, value.shape, 1)
                value = jnp.where(lane >= EVEC, value, 0.0)
            value = jnp.where(f == 0, value * value, 0.0)
            sq[...] += jnp.sum(value.reshape(12, 8, PWIDE[n] // 128, 128), (0, 2))

    under_way = []

    def tick():
        for entry in list(under_way):
            after = entry[3] + 1
            if entry[0] == "group" and after < 3 and stage_of("group", entry[1] - 1, entry[2]) <= after:
                continue
            entry[3] = after
            if entry[0] == "part":
                part_advance(entry[1], entry[3])
            else:
                advance(entry[1], entry[2], entry[3])
            if entry[3] == (STAGES if entry[0] == "group" else STAGES - 1):
                under_way.remove(entry)

    def stage_of(kind, n, h=0):
        for entry in under_way:
            if entry[:3] == [kind, n, h]:
                return entry[3]
        return STAGES

    def launch(gi):
        for n in swaps(gi):
            swap(gi, n).wait_recv()
        for copy in left_loads(gi):
            copy.wait()
        for h in range(2):
            hs = range(2) if RGROUPS[gi][0] == "d" else (h,)
            while any(gi >= BUFS and stage_of("group", gi - BUFS, i) < 1 for i in hs):
                tick()
            while gi >= SLOTS_R and stage_of("group", gi - SLOTS_R, h) < 2:
                tick()
            compute(gi, h)
            if gi >= SLOTS_R:
                pl.semaphore_wait(credit.at[0], 1)
                pl.semaphore_wait(credit.at[1], 1)
            step1(gi, h).start()
            under_way.append(["group", gi, h, 0])
        for n in swaps(gi):
            swap(gi, n).wait_send()
        if gi + 1 < total:
            prepare(gi + 1)

    waited = set()

    def prepare(gi):
        kind, l = RGROUPS[gi]
        for n in ((0,) if kind == "d" else (1,)):
            if (l, n) not in waited:
                waited.add((l, n))
                forward_swap(l, n).wait_recv()
        for copy in left_loads(gi):
            copy.start()

    def launch_part(n):
        part_compute(n)
        under_way.append(["part", n, 0, 0])

    load_mask(mask, scratch[4])
    sq[...] = jnp.zeros_like(sq)
    er[...] = jnp.zeros_like(er)
    er[EVEC + GLOB + 3 : EVEC + GLOB + 5, :] = end_ref[...]
    er[ECLS:, :] = tn(head_ref[1, :, CMAIN : CMAIN + EWIDE - ECLS], head_ref[0])
    launch_part(0)
    prepare(0)
    first_load.wait()
    loaded = set()

    for layer in reversed(range(L)):
        base = 3 * (L - 1 - layer)

        def mat(which):
            def read(k):
                if (layer, which) not in loaded:
                    loaded.add((layer, which))
                    weight(layer, which).wait()
                return wbuf[weight_slot(layer, which), k]

            return read

        def slope(k):
            slope_load(layer, k).wait()
            return gp[k % 2]

        def kept(i):
            kept_load(layer, i).wait()
            return xb[...]

        def at(point):
            if point.startswith("mlp"):
                k = int(point[3:])
                if k + 2 < FF // D:
                    slope_load(layer, k + 2).start()
                elif layer > 0:
                    slope_load(layer - 1, k - 2).start()
                if k == 0:
                    swap(base, 0).start()
                if k == 3:
                    for n in swaps(base + 1):
                        swap(base + 1, n).start()
                    weight(layer, 2).start()
                    if layer > 0:
                        weight(layer - 1, 0).start()
                if k % 2:
                    tick()
            elif point == "resid":
                kept_load(layer, 0).start()
                if layer == L - 1:
                    heads_load(layer).wait()
            elif point == "sent":
                if layer < L - 1:
                    heads_load(layer).wait()
                launch(base)
            elif point == "head0":
                launch(base + 1)
            elif point == "head1":
                tick()
            elif point == "head2":
                tick()
                if layer > 0:
                    heads_load(layer - 1).start()
            elif point == "heads":
                for n in swaps(base + 2):
                    swap(base + 2, n).start()
                tick()
            elif point == "done":
                if layer > 0:
                    weight(layer - 1, 1).start()
                    kept_load(layer - 1, 1).start()
                    launch(base + 2)

        backward_body(
            layer, dcur, er, ba, vec_ref, qk, (mat(0), mat(1), mat(2)), slope, kept, scratch,
            (ds_.at[layer], dr_.at[layer], gs_.at[layer], gr_.at[layer]), at,
        )
    dgrid = dcur[...]
    spot = lax.broadcasted_iota(jnp.int32, (TOK, D), 0)
    er[:TOK, :] = dgrid
    inside = jnp.where(spot % SLOTS < GRID, dgrid, 0.0)
    er[EVEC + GLOB : EVEC + GLOB + 1, :] = jnp.sum(inside, 0, keepdims=True)
    er[EVEC + GLOB + 1 : EVEC + GLOB + 3, :] = dgrid[GRID : GRID + 2, :]
    launch_part(1)
    launch(total - 1)
    shared = False
    while under_way:
        tick()
        if not shared and stage_of("group", total - 1, 1) >= 3 and stage_of("part", 1) >= STAGES - 1:
            shared = True
            n = NF * times
            me = f * times + t

            def send(i, carry):
                other = (me + i) % n
                remote(sq, square_all.at[me], qs, qr, (other // times, other % times)).start()
                return carry

            lax.fori_loop(1, n, send, 0)
            square_all[me] = sq[...]
    for layer in range(L):
        for n in range(2):
            forward_swap(layer, n).wait_send()
    for gi in range(total):
        for h in range(2):
            spread_y(gi, h).wait_send()
            spread_c(gi, h).wait_send()
    for n in range(2):
        part_y(n).wait_send()
        part_c(n).wait_send()
    wait_small(times, small_all, ss, sr)
    wait_small(times, square_all, qs, qr)
    summed = jnp.sum(small_all[...], 0)
    spot = lax.broadcasted_iota(jnp.int32, (8, 128), 0) * 128 + lax.broadcasted_iota(jnp.int32, (8, 128), 1)
    bias = jnp.where(spot < CLASSES, summed, 0.0)
    norm = jnp.sqrt(jnp.sum(jnp.sum(square_all[...], 0) + bias * bias, keepdims=True))
    scalars[0] = summed
    scalars[1] = jnp.broadcast_to(norm, (8, 128))
    scalars[2] = jnp.broadcast_to(jnp.minimum(1.0, 1.0 / (norm + 1e-06)), (8, 128))


def backward_all(times, dout, xs, gp, qk, fa, vec, mask, pnorm, head, end_rows, small, wcol, wdown):
    count = times // 2
    n = NF * times
    total = len(RGROUPS)
    dma = pltpu.SemaphoreType.DMA
    most = max(PWIDE)
    return pl.pallas_call(
        functools.partial(backward_all_kernel, times),
        out_shape=(
            jax.ShapeDtypeStruct((2 * L, 2, 2, 96, D), BF),
            jax.ShapeDtypeStruct((L, 2, 192, D), BF),
            jax.ShapeDtypeStruct((2, 2, 2, 96, most), BF),
            jax.ShapeDtypeStruct((3, 8, 128), F32),
            jax.ShapeDtypeStruct(fa.shape, BF),
        ),
        in_specs=[aspec()] * 5 + [vspec()] + [aspec()] + [vspec()] * 4 + [aspec()] * 2,
        out_specs=(vspec(),) * 4 + (aspec(),),
        scratch_shapes=[
            VM((2, 4, D, D), BF),
            VM((2, TOK, D), F32),
            VM((TOK, D), F32),
            VM((TOK, D), F32),
            VM((EWIDE, D), F32),
            VM((PER, NF, QROWS, 128), BF),
            VM((9, TOK, D), BF),
            VM((4, 2 * TOK, D), BF),
            VM((L, TOK, 384), BF),
            VM((L, 2, TOK, D), BF),
            VM((L, 2, TOK, D), BF),
            VM((BUFS, 2, 2, count, 96, 384), F32),
            VM((BUFS, 2, 2, count, 96, 384), BF),
            VM((SLOTS_R, 2, 2, count, 96, 384), BF),
            VM((2, count, 96, 384), F32),
            VM((2, count, 96, 384), BF),
            VM((SLOTS_R, 2, count, 96, 384), BF),
            VM((2, count, 96, 384), BF),
            VM((2, 96, 384), F32),
            VM((SLOTS_R, 2, count - 1, 96, 384), BF),
            VM((count, 96, most), BF),
            VM((count, 96, most), F32),
            *[VM((count, 96, w), BF) for w in PWIDE],
            *[VM((count - 1, 96, w), BF) for w in PWIDE],
            VM((8, 128), F32),
            dma((L, 3)), dma((L, 4)), dma((L, 2)), dma((L + 1,)), dma((4, 2)),
            dma((L, 2)), dma((L, 2)), dma((total, 2)), dma((total, 2)),
            dma((total, 2)), dma((total, 2)), dma((total, 2)), dma((total, 2)),
            dma((total, 2, count - 1)), dma((total, 2, count - 1)),
            dma((total, 2)), dma((total, 2)), dma((total, 2)), dma((total, 2)),
            dma, dma, dma, dma,
            dma((2,)), dma((2,)), dma((2, count - 1)), dma((2, count - 1)), dma((2,)), dma((2,)), dma((2,)), dma((2,)),
            pltpu.SemaphoreType.REGULAR((count + 1,)),
            *[dma((L, PER, NF - 1))] * 4,
            VM((n, 8, 128), F32),
            VM((n, 8, 128), F32),
        ]
        + BACKWARD_SCRATCH,
        compiler_params=pltpu.CompilerParams(
            collective_id=2 + 2 * L, has_side_effects=True, vmem_limit_bytes=65400 * 1024
        ),
        name="backward_all",
    )(dout, xs, gp, qk, fa, vec, mask, pnorm, head, end_rows, small, wcol, wdown)[:4]


def adam(weight, first, second, grad):
    first = DECAY_FIRST * first + (1.0 - DECAY_FIRST) * grad
    second = DECAY_SECOND * second + (1.0 - DECAY_SECOND) * grad * grad
    fix_one = 1.0 - DECAY_FIRST**STEP
    fix_two = 1.0 - DECAY_SECOND**STEP
    scaled = jnp.sqrt(second * (1.0 / fix_two)) + EPSILON
    weight = weight * (1.0 - LEARN_RATE * WEIGHT_DECAY) - (LEARN_RATE / fix_one) * first / scaled
    return (weight, first, second)


PIECES = 2
WIDE_STEPS = L * 8 // PIECES
DOWN_STEPS = L * 4 // PIECES


def update_kernel(*refs):
    scalars, gcol, gdown, gpart = refs[:4]
    ins, outs, gemb = refs[4:19], refs[19:38], refs[38]
    step = pl.program_id(0)
    coef = scalars[2, 0:1, 0:1]

    def apply(which, grad, at=...):
        new = adam(*(ins[which + 5 * i][at] for i in range(3)), grad * coef)
        for i in range(3):
            outs[which + 5 * i][at] = new[i]
        if which < 4:
            outs[15 + which][at] = new[0].astype(BF)

    @pl.when(step < WIDE_STEPS)
    def _():
        for p in range(PIECES):
            apply(0, gcol[0, p].astype(F32), (0, slice(None), slice(p * D, (p + 1) * D)))

    @pl.when(step >= WIDE_STEPS)
    def _():
        apply(1, gdown[0].astype(F32), (0,))

    @pl.when(step == 0)
    def _():
        main = sum(gpart[0, i, :, :CMAIN].astype(F32) for i in range(NF))
        rest = sum(gpart[1, i, :, EVEC:].astype(F32) for i in range(NF))
        per = FROWS // NF
        for i in range(NF):
            block = gpart[1, i].astype(F32)
            for h in range(2):
                for r in range(per):
                    to = (i * per + r) * 2 * HALF + h * HALF
                    gemb[:, to : to + HALF] = block[:, h * SLOTS + r * HALF : h * SLOTS + (r + 1) * HALF]
        gemb[:, NGRID:] = rest[:, EWIDE - EVEC :]
        apply(2, gemb[...])
        tail = rest[:, ECLS - EVEC : ECLS - EVEC + CLASSES - CMAIN]
        apply(3, jnp.concatenate([main, tail], 1))
        turned = rest[:, : 128].T
        apply(4, turned[:VROWS])


def update(scalars, gcol, gdown, gpart, params, firsts, seconds):
    shard = gcol.shape[2]
    per_wide, per_down = 8 // PIECES, 4 // PIECES

    def wide(step):
        step = jnp.minimum(step, WIDE_STEPS - 1)
        return (step // per_wide, 0, step % per_wide)

    def wide_grad(step):
        step = jnp.minimum(step, WIDE_STEPS - 1)
        return (step // per_wide, step % per_wide, 0, 0)

    def down(step):
        step = jnp.maximum(step - WIDE_STEPS, 0)
        return (step // per_down, step % per_down, 0)

    params, firsts, seconds = (
        [v[0], v[1], v[2].T, v[3], v[4]] for v in (params, firsts, seconds)
    )
    down_block = pl.BlockSpec((1, PIECES * shard, D), down)
    specs = [pl.BlockSpec((1, shard, PIECES * D), wide), down_block] + [vspec()] * 3
    shapes = [jax.ShapeDtypeStruct(v.shape, F32) for v in params] * 3
    shapes += [jax.ShapeDtypeStruct(v.shape, BF) for v in params[:4]]
    news = pl.pallas_call(
        update_kernel,
        grid=(WIDE_STEPS + DOWN_STEPS,),
        out_shape=shapes,
        in_specs=[vspec(), pl.BlockSpec((1, PIECES, shard, D), wide_grad), down_block, vspec()] + specs * 3,
        out_specs=specs * 3 + specs[:4],
        scratch_shapes=[VM((shard, NGRID + PATCH), F32)],
        compiler_params=pltpu.CompilerParams(vmem_limit_bytes=48 * 1024 * 1024),
        name="update",
    )(scalars, gcol, gdown, gpart, *params, *firsts, *seconds)
    return [v.T if i % 5 == 2 else v for i, v in enumerate(news)]


def pad_to(v, axis, size):
    pads = [(0, 0)] * v.ndim
    pads[axis] = (0, size - v.shape[axis])
    return jnp.pad(v, pads)


def embed_units(embedding, classifier, vectors, f):
    width = embedding.shape[1]
    blocks = embedding[:NGRID].reshape(NF, FROWS // NF, 2, HALF, width)
    block = lax.dynamic_index_in_dim(blocks, f, 0, keepdims=False).transpose(1, 0, 2, 3)
    block = block.reshape(2, GRID, width)
    tokens = jnp.where(f == 0, vectors[GLOB + 1 : GLOB + 3], 0.0)
    tokens = jnp.stack([tokens, jnp.zeros_like(tokens)])
    block = jnp.concatenate([block, tokens, jnp.zeros((2, SLOTS - GRID - 2, width), F32)], 1)
    rest = classifier[:, CMAIN:].T
    unit = jnp.concatenate(
        [
            block.reshape(TOK, width), vectors, jnp.zeros((ECLS - EVEC - VROWS, width), F32),
            pad_to(rest, 0, EWIDE - ECLS),
        ],
        0,
    )
    return unit.T.astype(BF), embedding[NGRID:].T.astype(BF), classifier[:, :CMAIN].astype(BF)


def local(
    patches, column_mask, labels, clip_weights, wide_weights, down_weights, embedding, classifier,
    vectors, class_bias, wide_first, down_first, embedding_first, classifier_first, vectors_first,
    bias_first, wide_second, down_second, embedding_second, classifier_second, vectors_second,
    bias_second,
):
    times = lax.axis_size("tm")
    f, t = lax.axis_index("freq"), lax.axis_index("tm")
    half = t % 2
    pair = t // 2
    rows_dev = FROWS // NF
    kernels = D // times == 96
    shard = D // times
    columns = column_mask.reshape(times, CPD, HALF) > 0
    mine_columns = lax.dynamic_index_in_dim(columns, t, 0, keepdims=False)
    raw = patches.reshape(rows_dev, CPD, HALF, PATCH)

    keep_block, give_block = (
        pad_to(lax.dynamic_index_in_dim(raw, i, 1, keepdims=False).reshape(GRID, PATCH), 0, SLOTS)
        for i in (half, 1 - half)
    )

    live = jnp.stack([pad_to(jnp.tile(mine_columns[i], rows_dev), 0, SLOTS) for i in range(2)])
    live = jnp.where(half == 0, live, live[::-1]).astype(F32)[:, :, None]
    unit_embed, unit_patch, unit_class = embed_units(embedding, classifier, vectors, f)

    clip_columns = lax.dynamic_slice(columns, (pair * 2, half, 0), (2, 1, HALF)).reshape(2, HALF)
    slots = jnp.concatenate(
        [
            jnp.broadcast_to(jnp.tile(clip_columns, (1, rows_dev)), (NF, 2, GRID)),
            jnp.broadcast_to(
                ((jnp.arange(NF)[:, None] == 0) & (jnp.arange(2)[None, :] == 0))[:, :, None], (NF, 2, 2)
            ),
            jnp.zeros((NF, 2, SLOTS - GRID - 2), bool),
        ],
        2,
    ).reshape(NF * TOK)
    mask = jnp.where(slots[:, None] | (jnp.arange(128) != HDIM)[None, :], 0.0, -1e30).astype(BF)

    weight_total = jnp.sum(clip_weights).astype(F32)
    if kernels:
        wcol, wdown, vec, xs, fa, gp, qk, pnorm, dx, head, end_rows, small = forward_all(
            times, wide_weights, down_weights, unit_embed, unit_patch, unit_class, live, keep_block, give_block,
            pad_to(labels, 1, D), clip_weights[None], pad_to(class_bias[None], 1, D), mask,
        )
    else:
        wide_all = lax.all_gather(wide_weights.astype(BF), "tm", axis=1, tiled=True)
        wcol = wide_all.reshape(L, D, 2, 4, D).transpose(0, 2, 3, 1, 4)
        wcol = wcol.reshape(2 * L, 2, 2, 4, 2, 96, D)
        wdown = lax.all_gather(down_weights.astype(BF), "tm", axis=1, tiled=True)
        wdown = wdown.reshape(L, 4, 2, 2, 192, D)
        vec = lax.all_gather(unit_embed, "tm", axis=0, tiled=True).T.astype(F32)
        patch = lax.all_gather(unit_patch, "tm", axis=0, tiled=True)
        class_main = lax.all_gather(unit_class, "tm", axis=0, tiled=True)
        pixels = jnp.stack([keep_block, give_block]).astype(F32)
        sums = jnp.stack(
            [jnp.sum(pixels * live), jnp.sum(pixels * pixels * live), jnp.sum(live) * PATCH]
        )
        sums = lax.psum(sums, ("freq", "tm"))
        take_block = lax.ppermute(
            give_block, "tm", [(i, i + 1 - 2 * (i % 2)) for i in range(times)]
        )
        pixels = jnp.concatenate(
            [jnp.where(half == 0, keep_block, take_block), jnp.where(half == 0, take_block, keep_block)], 0
        )
        center = sums[0] / sums[2]
        mel_scale = lax.rsqrt(sums[1] / sums[2] - center * center + 1e-05)
        inside = (jnp.arange(TOK) % SLOTS < GRID)[:, None]
        pnorm = jnp.where(inside, (pixels.astype(F32) - center) * mel_scale, 0.0).astype(BF)
        x = nt(pnorm, patch) + vec[:TOK] + jnp.where(inside, vec[EVEC + GLOB], 0.0)
        xs, fa, gp, qk = [x], [], [], []
        for layer in range(L):
            x, x1, acts, slopes, heads = forward_layer(layer, x, vec, mask, wcol, wdown)
            xs += [x1, x]
            fa.append(acts)
            gp.append(slopes)
            qk.append(heads)
    wcol = wcol.reshape(2 * L, 4, D, D)
    wdown = wdown.reshape(L, 4, D, D)
    if not kernels:
        vec_all = vec[EVEC : EVEC + VROWS]
        class_all = jnp.concatenate([class_main, vec[ECLS : ECLS + CLASSES - CMAIN].T.astype(BF)], 1)

        owner = (f == 0).astype(F32)
        special = xs[2 * L][GRID : GRID + 2]
        normed_end, scale_end = norm_rows(special)
        feature = jnp.mean(normed_end * vec_all[GLOB + 3] + vec_all[GLOB + 4], 0, keepdims=True).astype(BF)
        logits = nn(feature, class_all) + class_bias
        clip = pair * CPD + half
        flags = lax.dynamic_slice_in_dim(labels, clip, 1, 0).astype(F32)
        weight = lax.dynamic_slice_in_dim(clip_weights, clip, 1, 0).astype(F32)[:, None]
        loss_part = owner * jnp.sum(weight * (jax.nn.softplus(logits) - flags * logits))
        dlogits = owner * weight * (jax.nn.sigmoid(logits) - flags) / weight_total
        dlogits_low = dlogits.astype(BF)
        dfinal = jnp.broadcast_to(0.5 * nt(dlogits_low, class_all), (2, D))
        dspecial = norm_back(dfinal * vec_all[GLOB + 3], normed_end, scale_end)
        end_rows = jnp.stack([jnp.sum(dfinal * normed_end, 0), jnp.sum(dfinal, 0)])
        dx = jnp.concatenate(
            [jnp.zeros((GRID, D), F32), dspecial, jnp.zeros((TOK - GRID - 2, D), F32)], 0
        )
        small = jnp.concatenate([dlogits.reshape(-1), loss_part.reshape(1)])
        small = pad_to(small, 0, 1024).reshape(8, 128)
    if kernels:
        gcol, gdown, gpart, scalars = backward_all(
            times, dx, xs, gp, qk, fa, vec, mask, pnorm, head, end_rows, small, wcol, wdown
        )
        small = scalars[0].reshape(-1)
        grad_norm, coef = scalars[1, 0, 0], scalars[2, 0, 0]
        params = (wide_weights, down_weights, embedding, classifier, vectors)
        firsts = (wide_first, down_first, embedding_first, classifier_first, vectors_first)
        seconds = (wide_second, down_second, embedding_second, classifier_second, vectors_second)
        news = update(
            scalars, gcol.reshape(L, 8, shard, D), gdown.reshape(L, FF // times, D),
            gpart.reshape(2, NF, shard, -1), params, firsts, seconds,
        )
        bias = adam(class_bias, bias_first, bias_second, small[:CLASSES] * coef)
        return (
            *news[:5], bias[0], *news[5:10], bias[1], *news[10:15], bias[2], *news[15:],
            grad_norm, small[CLASSES], weight_total,
        )
    else:
        ba = [None] * L
        er = jnp.zeros((EWIDE, D), F32)
        for layer in reversed(range(L)):
            dx, ba[layer], rows = backward_layer(
                layer, dx, xs[2 * layer], xs[2 * layer + 1], gp[layer], qk[layer], vec, mask, wcol, wdown
            )
            er = er + rows
        dgrid = jnp.where(inside, dx, 0.0)
        grad_vectors = er[EVEC : EVEC + GLOB]
        grad_vectors = jnp.concatenate(
            [grad_vectors, jnp.sum(dgrid, 0, keepdims=True), dx[GRID : GRID + 2], end_rows], 0
        )
        wides, downs = [], []
        for l in range(L):
            cols = [tn(fa[l][0], ba[l][i]) for i in range(3)]
            cols += [tn(fa[l][1], ba[l][3])]
            cols += [tn(fa[l][2], ba[l][4 + i]) for i in range(4)]
            wides.append(jnp.concatenate(cols, 1))
            downs.append(jnp.concatenate([tn(fa[l][3 + i], ba[l][8]) for i in range(4)], 0))
        dpos = dgrid.reshape(2, SLOTS, D)[:, :GRID].reshape(2, rows_dev, HALF, D)
        dpos = dpos.transpose(1, 0, 2, 3).reshape(rows_dev * 2 * HALF, D)
        dpos = lax.dynamic_update_slice(jnp.zeros((NGRID, D), F32), dpos, (f * rows_dev * 2 * HALF, 0))
        dembed = jnp.concatenate([dpos, tn(pnorm, dgrid.astype(BF))], 0)
        grads = (
            lax.psum_scatter(jnp.stack(wides), "tm", scatter_dimension=1, tiled=True),
            lax.psum_scatter(jnp.stack(downs), "tm", scatter_dimension=1, tiled=True),
            lax.psum_scatter(dembed, "tm", scatter_dimension=1, tiled=True),
            lax.psum_scatter(tn(feature, dlogits_low), "tm", scatter_dimension=0, tiled=True),
            lax.psum_scatter(grad_vectors, "tm", scatter_dimension=1, tiled=True),
        )
        grads = lax.psum(grads, "freq")
        grad_wide, grad_down, grad_embed, grad_class, grad_vectors = grads
        squares = sum(jnp.sum(v * v) for v in grads)
        square_total, small = lax.psum(
            (jnp.where(f == 0, squares, 0.0), small.reshape(-1)), ("freq", "tm")
        )
    grad_bias = small[:CLASSES]
    loss_sum = small[CLASSES]
    grad_norm = jnp.sqrt(square_total + jnp.sum(grad_bias * grad_bias))
    coef = jnp.minimum(1.0, 1.0 / (grad_norm + 1e-06))

    params = (wide_weights, down_weights, embedding, classifier, vectors, class_bias)
    firsts = (wide_first, down_first, embedding_first, classifier_first, vectors_first, bias_first)
    seconds = (wide_second, down_second, embedding_second, classifier_second, vectors_second, bias_second)
    grads = (grad_wide, grad_down, grad_embed, grad_class, grad_vectors, grad_bias)
    news = [adam(w, m, v, g * coef) for w, m, v, g in zip(params, firsts, seconds, grads)]
    masters = [n[0] for n in news]
    return (
        *masters,
        *[n[1] for n in news],
        *[n[2] for n in news],
        *[m.astype(BF) for m in masters[:4]],
        grad_norm,
        loss_sum,
        weight_total,
    )


def solution(mesh):
    split = (
        P(None, "tm", None), P(None, "tm", None), P(None, "tm"), P("tm", None), P(None, "tm"), P(),
    )
    return jax.shard_map(
        local,
        mesh=mesh,
        in_specs=(P("freq", "tm", None), P(), P(), P()) + split * 3,
        out_specs=split * 3 + split[:4] + (P(), P(), P()),
        check_vma=False,
    )
```

```python
import functools

import jax
import jax.numpy as jnp
from jax import lax
from jax.experimental import pallas as pl
from jax.experimental.pallas import tpu as pltpu
from jax.sharding import PartitionSpec as P

D = 768
HEADS = 12
HDIM = 64
FF = 3072
L = 2
FROWS = 12
HALF = 52
PATCH = 256
STEP = 5
CPD = 2
NGRID = FROWS * 2 * HALF
CLASSES = 527
VROWS = 29
GLOB = L * 8 + L * (FF // D)

TOK = 320
PER = 3
NF = 4

DECAY_FIRST = 0.5
DECAY_SECOND = 0.5
LEARN_RATE = 0.03
WEIGHT_DECAY = 0.05
EPSILON = 1e-08

MESH = pl.DeviceIdType.MESH
BF = jnp.bfloat16
F32 = jnp.float32
VLIM = 60 * 1024 * 1024
VM = pltpu.VMEM


def nn(a, b):
    return lax.dot_general(a, b, (((1,), (0,)), ((), ())), preferred_element_type=F32)


def nt(a, b):
    return lax.dot_general(a, b, (((1,), (1,)), ((), ())), preferred_element_type=F32)


def tn(a, b):
    return lax.dot_general(a, b, (((0,), (0,)), ((), ())), preferred_element_type=F32)


def norm_rows(x):
    center = jnp.mean(x, -1, keepdims=True)
    shifted = x - center
    scale = lax.rsqrt(jnp.mean(shifted * shifted, -1, keepdims=True) + 1e-06)
    return (shifted * scale, scale)


def norm_back(dnorm, normed, scale):
    return scale * (
        dnorm
        - jnp.mean(dnorm, -1, keepdims=True)
        - normed * jnp.mean(dnorm * normed, -1, keepdims=True)
    )


def vspec():
    return pl.BlockSpec(memory_space=VM)


def aspec():
    return pl.BlockSpec(memory_space=pl.ANY)


def place():
    f, t = lax.axis_index("freq"), lax.axis_index("tm")
    return f, t, f // 2, f % 2, t // 2, t % 2


def remote(src, dst, ssem, rsem, dev):
    return pltpu.make_async_remote_copy(
        src_ref=src, dst_ref=dst, send_sem=ssem, recv_sem=rsem, device_id=dev, device_id_type=MESH
    )


def greet_all(times):
    f, t = lax.axis_index("freq"), lax.axis_index("tm")
    n = NF * times
    me = f * times + t
    barrier = pltpu.get_barrier_semaphore()

    def hello(i, carry):
        other = (me + i) % n
        pl.semaphore_signal(
            barrier, inc=1, device_id=(other // times, other % times), device_id_type=MESH
        )
        return carry

    lax.fori_loop(1, n, hello, 0)
    pl.semaphore_wait(barrier, n - 1)


def spread_small(times, small, gathered, ssem, rsem):
    f, t = lax.axis_index("freq"), lax.axis_index("tm")
    n = NF * times
    me = f * times + t

    def send(i, carry):
        other = (me + i) % n
        remote(
            small, gathered.at[me], ssem, rsem, (other // times, other % times)
        ).start()
        return carry

    lax.fori_loop(1, n, send, 0)
    gathered[me] = small[...]


def wait_small(times, gathered, ssem, rsem):
    n = NF * times
    many = gathered.at[pl.ds(0, n - 1)]
    pltpu.make_async_copy(many, many, rsem).wait()
    pltpu.make_async_copy(many, many, ssem).wait()


QROWS = TOK + TOK // 2
SLOTS = TOK // 2
GRID = FROWS // NF * HALF
EWIDE = 384
EVEC = TOK
ECLS = 352
CMAIN = 512


def greet_clip():
    f, t = lax.axis_index("freq"), lax.axis_index("tm")
    barrier = pltpu.get_barrier_semaphore()
    for i in range(1, NF):
        pl.semaphore_signal(barrier, inc=1, device_id=((f + i) % NF, t), device_id_type=MESH)
    pl.semaphore_wait(barrier, NF - 1)


def pack_half(v):
    return jnp.concatenate([v[: TOK // 2], v[TOK // 2 :]], 1)


def open_half(v):
    return jnp.concatenate([v[:, :HDIM], v[:, HDIM:]], 0)


def with_mask(block):
    lane = lax.broadcasted_iota(jnp.int32, block.shape, 1)
    query = jnp.where(lane < HDIM, block.astype(F32) * (HDIM ** (-0.5)), 0.0)
    return jnp.where(lane == HDIM, 1.0, query).astype(BF)


def exchange_sems():
    dma = pltpu.SemaphoreType.DMA
    return [dma((PER, NF - 1))] * 4


FORWARD_SCRATCH = [
    VM((2, 2, 2, 4, 2, 96, D), BF),
    VM((4, 2, 2, 192, D), BF),
    VM((PER, NF, QROWS, 128), BF),
    VM((PER, NF, TOK // 2, 128), BF),
    VM((NF * TOK, 128), BF),
    VM((NF * TOK, HDIM), BF),
    VM((TOK, D), F32),
]


def layer_body(layer, x_ref, vec_ref, outs, scratch, orecv, sems, fetch, tick):
    xo_ref, x1_ref, fa_ref, gp_ref, qk_ref = outs
    wbuf, dbuf, qsend, osend, kall, vall, acc = scratch
    qs, qr, os, orr = sems
    f, t = lax.axis_index("freq"), lax.axis_index("tm")

    def row(i):
        return vec_ref[EVEC + layer * 8 + i : EVEC + layer * 8 + i + 1, :]

    def mat(part, q, cols=slice(None)):
        return wbuf[part, q // 2, q % 2, :, :, :, cols].reshape(D, -1)

    normed, _ = norm_rows(x_ref[...])
    act = (normed * row(0) + row(1)).astype(BF)
    fa_ref[0] = act
    fetch(0)

    def to_clip(j, i):
        other = (f + i) % NF
        return remote(
            qsend.at[j, other], qk_ref.at[j, f], qs.at[j, i - 1], qr.at[j, i - 1], (other, t)
        )

    def back_clip(j, i):
        other = (f + i) % NF
        return remote(
            osend.at[j, other], orecv.at[j, f], os.at[j, i - 1], orr.at[j, i - 1], (other, t)
        )

    for j in range(PER):
        cols = slice(256 * j, 256 * (j + 1))
        query = (nn(act, mat(0, 0, cols)) + row(4)[:, cols]).astype(BF)
        key = nn(act, mat(0, 1, cols)).astype(BF)
        value = (nn(act, mat(0, 2, cols)) + row(5)[:, cols]).astype(BF)
        for h in range(NF):
            part = slice(HDIM * h, HDIM * (h + 1))
            qsend[j, h, :TOK] = jnp.concatenate([query[:, part], key[:, part]], 1)
            qsend[j, h, TOK:] = pack_half(value[:, part])
        for i in range(1, NF):
            to_clip(j, i).start()
        qk_ref[j, f] = qsend[j, f]
    tick()
    for j in range(PER):
        for i in range(1, NF):
            to_clip(j, i).wait_recv()
        for s in range(NF):
            kall[s * TOK : (s + 1) * TOK, :HDIM] = qk_ref[j, s, :TOK, HDIM:]
            vall[s * TOK : (s + 1) * TOK] = open_half(qk_ref[j, s, TOK:])

        def attend(i, carry):
            s = (f + i) % NF
            halves = []
            for h in range(2):
                lo = h * (TOK // 2)
                scores = nt(with_mask(qk_ref[j, s, lo : lo + TOK // 2]), kall[...])
                top = jnp.max(scores, -1, keepdims=True)
                expo = jnp.exp(scores - top)
                total = jnp.sum(expo, -1, keepdims=True)
                probs = (expo * (1.0 / total)).astype(BF)
                halves.append(nn(probs, vall[...]).astype(BF))
            osend[j, s] = jnp.concatenate(halves, 1)

            @pl.when(i > 0)
            def _():
                remote(
                    osend.at[j, s], orecv.at[j, f], os.at[j, i - 1], orr.at[j, i - 1], (s, t)
                ).start()

            return carry

        lax.fori_loop(1, NF, attend, 0)
        lax.fori_loop(0, 1, attend, 0)
        orecv[j, f] = osend[j, f]
        tick()
    parts = []
    for j in range(PER):
        for i in range(1, NF):
            back_clip(j, i).wait_recv()
        for h in range(NF):
            parts.append(open_half(orecv[j, h]))
    mixed = jnp.concatenate(parts, 1)
    fa_ref[1] = mixed
    resid = x_ref[...] + nn(mixed, mat(0, 3)) + row(6)
    x1_ref[...] = resid
    normed, _ = norm_rows(resid)
    fa_ref[2] = (normed * row(2) + row(3)).astype(BF)
    acc[...] = resid + row(7)
    fetch(1)
    fetch(2)

    def mlp(k, carry):
        bias = vec_ref[pl.ds(EVEC + L * 8 + layer * 4 + k, 1), :]
        before = nn(fa_ref[2], mat(1, k)) + bias
        lower = 0.5 * (1.0 + lax.erf(before * 0.7071067811865476))
        gp_ref[k] = lower + before * jnp.exp(-0.5 * before * before) * 0.3989422804014327
        hidden = (before * lower).astype(BF)
        fa_ref[3 + k] = hidden
        acc[...] += nn(hidden, dbuf[k].reshape(D, D))
        return carry

    for k in range(0, FF // D, 2):
        lax.fori_loop(k, k + 2, mlp, 0)
        tick()
    xo_ref[...] = acc[...]
    for j in range(PER):
        for i in range(1, NF):
            to_clip(j, i).wait_send()
            back_clip(j, i).wait_send()


def load_mask(mask, kall):
    def body(sem):
        copy = pltpu.make_async_copy(mask, kall, sem)
        copy.start()
        copy.wait()

    pl.run_scoped(body, pltpu.SemaphoreType.DMA)


def forward_kernel(
    layer, x_ref, vec_ref, mask, wcol, wdown,
    xo_ref, x1_ref, fa_ref, gp_ref, qk_ref,
    wbuf, dbuf, qsend, osend, kall, vall, acc, orecv, wsem, qs, qr, os, orr,
):
    loads = [
        pltpu.make_async_copy(wcol.at[2 * layer], wbuf.at[0], wsem.at[0]),
        pltpu.make_async_copy(wcol.at[2 * layer + 1], wbuf.at[1], wsem.at[1]),
        pltpu.make_async_copy(wdown.at[layer], dbuf, wsem.at[2]),
    ]
    for load in loads:
        load.start()
    load_mask(mask, kall)
    greet_clip()
    layer_body(
        layer, x_ref, vec_ref, (xo_ref, x1_ref, fa_ref, gp_ref, qk_ref),
        (wbuf, dbuf, qsend, osend, kall, vall, acc), orecv, (qs, qr, os, orr),
        lambda part: loads[part].wait(), lambda: None,
    )


def forward_layer(layer, x, vec, mask, wcol, wdown):
    return pl.pallas_call(
        functools.partial(forward_kernel, layer),
        out_shape=(
            jax.ShapeDtypeStruct((TOK, D), F32),
            jax.ShapeDtypeStruct((TOK, D), F32),
            jax.ShapeDtypeStruct((7, TOK, D), BF),
            jax.ShapeDtypeStruct((FF // D, TOK, D), F32),
            jax.ShapeDtypeStruct((PER, NF, QROWS, 128), BF),
        ),
        in_specs=[vspec()] * 2 + [aspec()] * 3,
        out_specs=(vspec(),) * 5,
        scratch_shapes=FORWARD_SCRATCH
        + [VM((PER, NF, TOK // 2, 128), BF), pltpu.SemaphoreType.DMA((3,))]
        + exchange_sems(),
        compiler_params=pltpu.CompilerParams(
            collective_id=2 + layer, has_side_effects=True, vmem_limit_bytes=VLIM
        ),
        name="forward_layer",
    )(x, vec, mask, wcol, wdown)


GROUPS = (("c", 0), ("c", 1), ("d", 0), ("c", 2), ("c", 3), ("d", 1))
SUBS = tuple((kind, idx, h) for kind, idx in GROUPS for h in (0, 1))
PATHS = "yzyzyzyyzyzy"
AHEAD = 3


def gather_plan():
    moves = {}
    for s, path in enumerate(PATHS):
        lag = 1 if s < 2 else 2
        times = {"along": s - AHEAD, "first": s}
        times["third"] = s + lag
        if path == "y":
            times["second"] = s + lag
            times["third"] = s + 2 * lag
        times["arrive"] = times["third"] + 1
        for action, when in times.items():
            moves.setdefault(max(when, -1), []).append((s, action))
    plan = [sorted(moves[when]) for when in sorted(moves)]
    ready = {s: n for n, step in enumerate(plan) for s, action in step if action == "arrive"}
    return plan, ready


def gather_steps(count, ucol, udown, ocol, odown, sems, prepare):
    zs, zr, own, s1, r1, s2, r2, s3, r3 = sems
    f, t, y, c, g, x = place()
    every = slice(None)

    def source(s):
        kind, idx, h = SUBS[s]
        yy = every if PATHS[s] == "z" else y
        if kind == "c":
            return ucol.at[idx, yy, c, :, pl.ds(h * 384, 384)]
        return udown.at[idx, yy, pl.ds(h * 96, 96), pl.ds(pl.multiple_of(c * 384, 128), 384)]

    def view(s, yy, zz, xx):
        kind, idx, h = SUBS[s]
        if PATHS[s] == "z":
            yy = every
        if kind == "c":
            return ocol.at[idx, yy, c, zz, xx, :, pl.ds(h * 384, 384)]
        return odown.at[
            idx, zz, xx, yy, pl.ds(h * 96, 96), pl.ds(pl.multiple_of(c * 384, 128), 384)
        ]

    def along(s, dz):
        return remote(
            source(s), view(s, y, g, x), zs.at[s, dz - 1], zr.at[s, dz - 1],
            (f, ((g + dz) % count) * 2 + x),
        )

    def keep(s):
        return pltpu.make_async_copy(source(s), view(s, y, g, x), own.at[s])

    def first(s):
        block = view(s, y, every, x)
        return remote(block, block, s1.at[s], r1.at[s], (f, g * 2 + 1 - x))

    def second(s):
        block = view(s, y, every, every)
        return remote(block, block, s2.at[s], r2.at[s], ((1 - y) * 2 + c, t))

    def third(s):
        block = view(s, every, every, every)
        return remote(block, block, s3.at[s], r3.at[s], (y * 2 + 1 - c, t))

    def act(s, action):
        if action == "along":
            prepare(s // 2)
            keep(s).start()
            for dz in range(1, count):
                along(s, dz).start()
        elif action == "first":
            for dz in range(1, count):
                along(s, dz).wait_recv()
            keep(s).wait()
            first(s).start()
        elif action == "second":
            first(s).wait_recv()
            second(s).start()
        elif action == "third":
            (second if PATHS[s] == "y" else first)(s).wait_recv()
            third(s).start()
        else:
            third(s).wait_recv()

    for step in gather_plan()[0]:
        for s, action in step:
            act(s, action)
        yield
    for s in range(len(SUBS)):
        for dz in range(1, count):
            along(s, dz).wait_send()
        first(s).wait_send()
        if PATHS[s] == "y":
            second(s).wait_send()
        third(s).wait_send()
    yield


def loss_part(owner, clip, x_ref, vec, classes, labels, clip_weights, class_bias, dout, head, end_rows, small):
    owner = jnp.where(owner, 1.0, 0.0)
    normed, scale = norm_rows(x_ref[GRID : GRID + 2, :])
    gain = vec[EVEC + GLOB + 3 : EVEC + GLOB + 4, :]
    final = normed * gain + vec[EVEC + GLOB + 4 : EVEC + GLOB + 5, :]
    feature = jnp.mean(final, 0, keepdims=True).astype(BF)
    first_row = lax.broadcasted_iota(jnp.int32, (16, D), 0) == 0
    feature = jnp.where(first_row, jnp.broadcast_to(feature.astype(F32), (16, D)), 0.0).astype(BF)
    head[0] = feature
    main = classes[...].reshape(D, CMAIN)
    tail = vec[ECLS:EWIDE, :].astype(BF)
    logits = jnp.concatenate([nn(feature, main), nt(feature, tail), jnp.zeros((16, 224), F32)], 1)[0:1]
    logits = logits + class_bias[...]
    flags = labels[pl.ds(clip, 1), :].astype(F32)
    weights = clip_weights[...].astype(F32)
    weight = jnp.sum(
        jnp.where(lax.broadcasted_iota(jnp.int32, weights.shape, 1) == clip, weights, 0.0), keepdims=True
    )
    total = jnp.sum(weights, keepdims=True)
    lane = lax.broadcasted_iota(jnp.int32, (1, D), 1)
    inside = lane < CLASSES
    soft = jnp.maximum(logits, 0.0) + jnp.log1p(jnp.exp(-jnp.abs(logits)))
    loss = jnp.sum(jnp.where(inside, soft - flags * logits, 0.0), keepdims=True) * weight * owner
    slope = 1.0 / (1.0 + jnp.exp(-logits))
    grads = jnp.where(inside, owner * weight * (slope - flags) / total, 0.0)
    for i in range(8):
        small[i : i + 1, :] = jnp.zeros((1, 128), F32) if i > 5 else (
            grads[:, 128 * i : 128 * (i + 1)]
            + (jnp.where(lane[:, 128 * i : 128 * (i + 1)] == CLASSES, loss, 0.0))
        )
    grads = jnp.where(first_row, jnp.broadcast_to(grads, (16, D)), 0.0).astype(BF)
    head[1] = grads
    dfinal = 0.5 * (nt(grads[:, :CMAIN], main) + nn(grads[:, CMAIN : CMAIN + EWIDE - ECLS], tail))[0:1]
    end_rows[0:1, :] = jnp.sum(dfinal * normed, 0, keepdims=True)
    end_rows[1:2, :] = 2.0 * dfinal
    special = norm_back(jnp.broadcast_to(dfinal * gain, normed.shape), normed, scale)
    dout[...] = jnp.zeros_like(dout)
    dout[GRID : GRID + 2, :] = special


def forward_all_kernel(
    times, wide, down, uemb, upatch, uclass, live, pkeep, psend, labels, clip_weights, class_bias, mask,
    ocol, odown, vec_out, xs_out, fa_out, gp_out, qk_out, pn_out, dout_out, head, end_rows, small,
    wbuf, dbuf, qsend, osend, kall, vall, acc, orecv, sall, precv, emb, patches, classes, vec, xs, fa, gp, qk, pn,
    zs, zr, own, s1, r1, s2, r2, s3, r3, es, er, exs, exr, ss, sr, ps, pr, wsem, osem,
    qs0, qr0, os0, or0, qs1, qr1, os1, or1, ucol, udown, cols_wide, cols_down, stats, dout, psem,
):
    f, t, y, c, g, x = place()
    count = times // 2
    over_x = (f, g * 2 + 1 - x)

    def fetch_master(group):
        kind, idx = GROUPS[group]
        if kind == "c":
            src = wide.at[idx // 2, :, pl.ds(idx % 2 * 4 * D, 4 * D)]
            return pltpu.make_async_copy(src, cols_wide.at[idx], psem.at[group])
        return pltpu.make_async_copy(down.at[idx], cols_down.at[idx], psem.at[group])

    prepared = set()

    def prepare(group):
        if group in prepared:
            return
        prepared.add(group)
        fetch_master(group).wait()
        kind, idx = GROUPS[group]
        for q in range(4):
            if kind == "c":
                ucol[idx, q // 2, q % 2] = cols_wide[idx, :, q * D : (q + 1) * D].astype(BF)
            else:
                udown[idx, q // 2, q % 2 * 96 : q % 2 * 96 + 96] = cols_down[idx, q * 96 : (q + 1) * 96].astype(BF)

    for group in range(len(GROUPS)):
        fetch_master(group).start()
    row = lax.broadcasted_iota(jnp.int32, (8, 128), 1)
    stats[...] = jnp.zeros_like(stats)
    for n, block in enumerate((pkeep, psend)):
        pixel, alive = block[...].astype(F32), live[n]
        masked = pixel * alive
        for lane, value in enumerate((masked, masked * pixel, alive * float(PATCH))):
            stats[...] += jnp.where(row == lane, jnp.sum(value, keepdims=True), 0.0)
    greet_all(times)
    spread_small(times, stats, sall, ss, sr)
    swap = remote(psend, precv, ps, pr, over_x)
    swap.start()
    load_mask(mask, kall)
    units = ((uemb, emb), (upatch, patches), (uclass, classes))

    def unit_along(n, dz):
        src, dst = units[n]
        return remote(
            src, dst.at[g, x], es.at[n, dz - 1], er.at[n, dz - 1], (f, ((g + dz) % count) * 2 + x)
        )

    def loads(layer, part):
        if part < 2:
            return pltpu.make_async_copy(ocol.at[2 * layer + part], wbuf.at[part], wsem.at[layer, part])
        return pltpu.make_async_copy(odown.at[layer], dbuf, wsem.at[layer, part])

    def unit_over(n):
        block = units[n][1].at[:, x]
        return remote(block, block, exs.at[n], exr.at[n], over_x)

    for n in range(3):
        units[n][1][g, x] = units[n][0][...]
    for n in range(2):
        for dz in range(1, count):
            unit_along(n, dz).start()
    steps = gather_steps(count, ucol, udown, ocol, odown, (zs, zr, own, s1, r1, s2, r2, s3, r3), prepare)
    plan, ready = gather_plan()
    last = len(plan) - 1
    done = [-1]

    started, allowed = set(), {(0, part) for part in range(3)}

    def arrived(layer, part):
        group = 3 * layer + part
        return max(ready[2 * group], ready[2 * group + 1])

    def prefetch():
        for layer, part in sorted(allowed - started):
            if done[0] >= arrived(layer, part):
                loads(layer, part).start()
                started.add((layer, part))

    def tick():
        if done[0] < last:
            next(steps)
            done[0] += 1
        prefetch()

    def need(step):
        while done[0] < step:
            tick()

    need(0)
    for n in range(2):
        for dz in range(1, count):
            unit_along(n, dz).wait_recv()
        unit_over(n).start()
    need(1)
    for n in range(2):
        unit_over(n).wait_recv()
    swap.wait_recv()
    wait_small(times, sall, ss, sr)
    sums = jnp.sum(sall[...], 0)
    total, squares, live = sums[0:1, 0:1], sums[0:1, 1:2], sums[0:1, 2:3]
    center = total / live
    mel_scale = lax.rsqrt(squares / live - center * center + 1e-05)
    inside = lax.broadcasted_iota(jnp.int32, (SLOTS, PATCH), 0) < GRID

    def normalized(block):
        return jnp.where(inside, (block[...].astype(F32) - center) * mel_scale, 0.0).astype(BF)

    pn[pl.ds(pl.multiple_of(x * SLOTS, SLOTS), SLOTS)] = normalized(pkeep)
    pn[pl.ds(pl.multiple_of((1 - x) * SLOTS, SLOTS), SLOTS)] = normalized(precv)
    vec[...] = emb[...].reshape(D, EWIDE).astype(F32).T
    patch = patches[...].reshape(D, PATCH)
    bias = vec[EVEC + GLOB : EVEC + GLOB + 1, :]
    spot = lax.broadcasted_iota(jnp.int32, (TOK, D), 0)
    grid_row = jnp.logical_or(spot < GRID, jnp.logical_and(spot >= SLOTS, spot < SLOTS + GRID))
    xs[0] = (nt(pn[...], patch) + vec[:TOK]) + jnp.where(grid_row, bias, 0.0)

    copies = [
        pltpu.make_async_copy(vec, vec_out, osem.at[1]),
        pltpu.make_async_copy(pn, pn_out, osem.at[2]),
    ]
    for copy in copies:
        copy.start()
    sems = ((qs0, qr0, os0, or0), (qs1, qr1, os1, or1))
    for dz in range(1, count):
        unit_along(2, dz).start()
    for layer in range(L):
        if layer == 1:
            for dz in range(1, count):
                unit_along(2, dz).wait_recv()
            unit_over(2).start()

        def fetch(part):
            if part == 1 and layer + 1 < L:
                allowed.add((layer + 1, 0))
            need(arrived(layer, part))
            prefetch()
            loads(layer, part).wait()

        layer_body(
            layer, xs.at[2 * layer], vec,
            (xs.at[2 * layer + 2], xs.at[2 * layer + 1], fa.at[layer], gp.at[layer], qk.at[layer]),
            (wbuf, dbuf, qsend, osend, kall, vall, acc), orecv.at[layer], sems[layer], fetch, tick,
        )
        more = [
            pltpu.make_async_copy(fa.at[layer], fa_out.at[layer], osem.at[3 + 4 * layer]),
            pltpu.make_async_copy(gp.at[layer], gp_out.at[layer], osem.at[4 + 4 * layer]),
            pltpu.make_async_copy(qk.at[layer], qk_out.at[layer], osem.at[5 + 4 * layer]),
        ]
        if layer == 0:
            more.append(pltpu.make_async_copy(xs.at[pl.ds(0, 2)], xs_out.at[pl.ds(0, 2)], osem.at[6]))
        else:
            more.append(pltpu.make_async_copy(xs.at[pl.ds(2, 3)], xs_out.at[pl.ds(2, 3)], osem.at[10]))
        for copy in more:
            copy.start()
        copies += more
        allowed.update((layer + 1, part) for part in (1, 2) if layer + 1 < L)
    unit_over(2).wait_recv()
    loss_part(
        f == 0, g * 2 + x, xs.at[2 * L], vec, classes, labels, clip_weights, class_bias, dout, head, end_rows, small
    )
    copies.append(pltpu.make_async_copy(dout, dout_out, osem.at[0]))
    copies[-1].start()
    need(last)
    next(steps)
    for n in range(3):
        for dz in range(1, count):
            unit_along(n, dz).wait_send()
        unit_over(n).wait_send()
    swap.wait_send()
    for copy in copies:
        copy.wait()


def forward_all(times, wide, down, uemb, upatch, uclass, live, pkeep, psend, labels, clip_weights, class_bias, mask):
    count = times // 2
    total = len(SUBS)
    dma = pltpu.SemaphoreType.DMA
    outs = (
        ((2 * L, 2, 2, count, 2, 96, D), BF),
        ((L, count, 2, 2, 192, D), BF),
        ((EWIDE, D), F32),
        ((2 * L + 1, TOK, D), F32),
        ((L, 7, TOK, D), BF),
        ((L, FF // D, TOK, D), F32),
        ((L, PER, NF, QROWS, 128), BF),
        ((TOK, PATCH), BF),
        ((TOK, D), F32),
        ((2, 16, D), BF),
        ((2, D), F32),
        ((8, 128), F32),
    )
    return pl.pallas_call(
        functools.partial(forward_all_kernel, times),
        out_shape=tuple(jax.ShapeDtypeStruct(*o) for o in outs),
        in_specs=[aspec()] * 2 + [vspec()] * 9 + [aspec()],
        out_specs=(aspec(),) * (len(outs) - 3) + (vspec(),) * 3,
        scratch_shapes=FORWARD_SCRATCH
        + [
            VM((L, PER, NF, TOK // 2, 128), BF),
            VM((NF * times, 8, 128), F32),
            VM((SLOTS, PATCH), BF),
            VM((count, 2, 96, EWIDE), BF),
            VM((count, 2, 96, PATCH), BF),
            VM((count, 2, 96, CMAIN), BF),
            VM((EWIDE, D), F32),
            VM((2 * L + 1, TOK, D), F32),
            VM((L, 7, TOK, D), BF),
            VM((L, FF // D, TOK, D), F32),
            VM((L, PER, NF, QROWS, 128), BF),
            VM((TOK, PATCH), BF),
            dma((total, count - 1)), dma((total, count - 1)), dma((total,)),
            dma((total,)), dma((total,)), dma((total,)), dma((total,)), dma((total,)), dma((total,)),
            dma((3, count - 1)), dma((3, count - 1)), dma((3,)), dma((3,)),
            dma, dma, dma, dma, dma((L, 3)), dma((12,)),
        ]
        + exchange_sems() * L
        + [
            VM((2 * L, 2, 2, 96, D), BF),
            VM((L, 2, 192, D), BF),
            VM((2 * L, 96, 4 * D), F32),
            VM((L, 4 * 96, D), F32),
            VM((8, 128), F32),
            VM((TOK, D), F32),
            dma((len(GROUPS),)),
        ],
        compiler_params=pltpu.CompilerParams(
            collective_id=1, has_side_effects=True, vmem_limit_bytes=VLIM
        ),
        name="forward_all",
    )(wide, down, uemb, upatch, uclass, live, pkeep, psend, labels, clip_weights, class_bias, mask)


BACKWARD_SCRATCH = [
    VM((PER, NF, TOK // 2, 128), BF),
    VM((PER, NF, TOK // 2, 128), BF),
    VM((PER, NF, QROWS, 128), BF),
    VM((PER, NF, QROWS, 128), BF),
    VM((NF * TOK, 128), BF),
    VM((NF * TOK, HDIM), BF),
    VM((NF * TOK, HDIM), F32),
    VM((NF * TOK, HDIM), F32),
    VM((NF, TOK, HDIM), BF),
    VM((TOK, D), F32),
]


def backward_body(layer, dcur, er, ba, vec_ref, qk_ref, mats, slope, kept, scratch, sems, at):
    down, up, qkvo = mats
    dsend, drecv, gsend, grecv, kall, vall, dkall, dvall, dqall, acc = scratch
    ds_, dr_, gs_, gr_ = sems
    f, t = lax.axis_index("freq"), lax.axis_index("tm")

    def row(i):
        return vec_ref[EVEC + layer * 8 + i : EVEC + layer * 8 + i + 1, :]

    def note(i, value):
        er[EVEC + i : EVEC + i + 1, :] = jnp.sum(value, 0, keepdims=True)

    ba[8] = dcur[...].astype(BF)
    note(layer * 8 + 7, dcur[...])
    for k in range(FF // D):
        dbefore = nt(ba[8], down(k)) * slope(k)
        note(L * 8 + layer * 4 + k, dbefore)
        ba[4 + k] = dbefore.astype(BF)
        product = nt(ba[4 + k], up(k))
        acc[...] = product if k == 0 else acc[...] + product
        at("mlp%d" % k)
    normed, scale = norm_rows(kept(1))
    dact = acc[...]
    note(layer * 8 + 2, dact * normed)
    note(layer * 8 + 3, dact)
    dcur[...] += norm_back(dact * row(2), normed, scale)
    note(layer * 8 + 6, dcur[...])
    ba[3] = dcur[...].astype(BF)
    at("resid")
    dmixed = nt(ba[3], qkvo(3)).astype(BF)

    def to_clip(j, i):
        other = (f + i) % NF
        return remote(
            dsend.at[j, other], drecv.at[j, f], ds_.at[j, i - 1], dr_.at[j, i - 1], (other, t)
        )

    def back_clip(j, i):
        other = (f + i) % NF
        return remote(
            gsend.at[j, other], grecv.at[j, f], gs_.at[j, i - 1], gr_.at[j, i - 1], (other, t)
        )

    for j in range(PER):
        for h in range(NF):
            lo = 256 * j + HDIM * h
            dsend[j, h] = pack_half(dmixed[:, lo : lo + HDIM])
        for i in range(1, NF):
            to_clip(j, i).start()
        drecv[j, f] = dsend[j, f]
    at("sent")
    root = HDIM ** (-0.5)
    for j in range(PER):
        for s in range(NF):
            kall[s * TOK : (s + 1) * TOK, :HDIM] = qk_ref[j, s, :TOK, HDIM:]
            vall[s * TOK : (s + 1) * TOK] = open_half(qk_ref[j, s, TOK:])
        dkall[...] = jnp.zeros_like(dkall)
        dvall[...] = jnp.zeros_like(dvall)
        for i in range(1, NF):
            to_clip(j, i).wait_recv()

        def attend(s):
            q = with_mask(qk_ref[j, s, :TOK])
            dmix = open_half(drecv[j, s])
            scores = nt(kall[...], q)
            top = jnp.max(scores, 0, keepdims=True)
            expo = jnp.exp(scores - top)
            probs = expo * (1.0 / jnp.sum(expo, 0, keepdims=True))
            dprob = nt(vall[...], dmix)
            inner = jnp.sum(probs * dprob, 0, keepdims=True)
            dscore = (probs * (dprob - inner)).astype(BF)
            dvall[...] += nn(probs.astype(BF), dmix)
            dkall[...] += nn(dscore, q[:, :HDIM])
            dqall[s] = (tn(dscore, kall[:, :HDIM]) * root).astype(BF)

        for s in range(NF):
            attend(s)
            if s < NF - 1:
                at("head%d%d" % (j, s))
        for s in range(NF):
            span = slice(s * TOK, (s + 1) * TOK)
            gsend[j, s, :TOK] = jnp.concatenate([dqall[s], dkall[span].astype(BF)], 1)
            gsend[j, s, TOK:] = pack_half(dvall[span].astype(BF))
        for i in range(1, NF):
            back_clip(j, i).start()
        grecv[j, f] = gsend[j, f]
        at("head%d%d" % (j, NF - 1))
    for j in range(PER):
        for i in range(1, NF):
            back_clip(j, i).wait_recv()
        cols = slice(256 * j, 256 * (j + 1))
        ba[0, :, cols] = jnp.concatenate([grecv[j, h, :TOK, :HDIM] for h in range(NF)], 1)
        ba[1, :, cols] = jnp.concatenate([grecv[j, h, :TOK, HDIM:] for h in range(NF)], 1)
        ba[2, :, cols] = jnp.concatenate([open_half(grecv[j, h, TOK:]) for h in range(NF)], 1)
    at("heads")
    note(layer * 8 + 4, ba[0].astype(F32))
    note(layer * 8 + 5, ba[2].astype(F32))
    dact = nt(ba[0], qkvo(0)) + nt(ba[1], qkvo(1)) + nt(ba[2], qkvo(2))
    normed, scale = norm_rows(kept(0))
    note(layer * 8 + 0, dact * normed)
    note(layer * 8 + 1, dact)
    dcur[...] += norm_back(dact * row(0), normed, scale)
    for j in range(PER):
        for i in range(1, NF):
            to_clip(j, i).wait_send()
            back_clip(j, i).wait_send()
    at("done")


def backward_kernel(
    layer, dout_ref, x_ref, x1_ref, gp_ref, qk_ref, vec_ref, mask, wcol, wdown,
    dx_ref, ba_ref, er_ref, wbuf, dbuf, wsem, ds_, dr_, gs_, gr_, *scratch,
):
    loads = [
        pltpu.make_async_copy(wdown.at[layer], dbuf, wsem.at[0]),
        pltpu.make_async_copy(wcol.at[2 * layer + 1], wbuf.at[1], wsem.at[1]),
        pltpu.make_async_copy(wcol.at[2 * layer], wbuf.at[0], wsem.at[2]),
    ]
    for load in loads:
        load.start()
    dx_ref[...] = dout_ref[...]
    er_ref[...] = jnp.zeros_like(er_ref)
    load_mask(mask, scratch[4])
    greet_clip()
    for load in loads:
        load.wait()
    backward_body(
        layer, dx_ref, er_ref, ba_ref, vec_ref, qk_ref,
        (lambda k: dbuf[k], lambda k: wbuf[1, k], lambda k: wbuf[0, k]),
        lambda k: gp_ref[k], lambda i: x1_ref[...] if i else x_ref[...],
        scratch, (ds_, dr_, gs_, gr_), lambda point: None,
    )


def backward_layer(layer, dout, x, x1, gp, qk, vec, mask, wcol, wdown):
    return pl.pallas_call(
        functools.partial(backward_kernel, layer),
        out_shape=(
            jax.ShapeDtypeStruct((TOK, D), F32),
            jax.ShapeDtypeStruct((9, TOK, D), BF),
            jax.ShapeDtypeStruct((EWIDE, D), F32),
        ),
        in_specs=[vspec()] * 6 + [aspec()] * 3,
        out_specs=(vspec(),) * 3,
        scratch_shapes=[VM((2, 4, D, D), BF), VM((4, D, D), BF), pltpu.SemaphoreType.DMA((3,))]
        + exchange_sems()
        + BACKWARD_SCRATCH,
        compiler_params=pltpu.CompilerParams(
            collective_id=2 + L + layer, has_side_effects=True, vmem_limit_bytes=VLIM
        ),
        name="backward_layer",
    )(dout, x, x1, gp, qk, vec, mask, wcol, wdown)


RGROUPS = (("d", 1), ("u", 1), ("q", 1), ("d", 0), ("u", 0), ("q", 0))
ROUTES = ("zz", "xz", "zy", "yz", "xz", "yy")
ORDER = {
    (1, "mlp1"): (0,),
    (1, "mlp3"): (200,),
    (1, "head00"): (1,),
    (1, "head01"): (200, 100,),
    (1, "head03"): (200,),
    (1, "head10"): (10, 200,),
    (1, "head13"): (101,),
    (1, "head20"): (100,),
    (1, "head22"): (11,),
    (1, "head23"): (100,),
    (1, "heads"): (100, 101, 110,),
    (1, "done"): (100, 101, 20, 111, 21,),
    (0, "mlp0"): (110,),
    (0, "mlp1"): (101,),
    (0, "mlp2"): (101,),
    (0, "sent"): (111,),
    (0, "head00"): (110, 120, 121, 30, 111, 31, 110,),
    (0, "head02"): (110,),
    (0, "head03"): (121,),
    (0, "head12"): (120,),
    (0, "head13"): (130,),
    (0, "head20"): (111,),
    (0, "head21"): (121, 131, 111,),
    (0, "head23"): (120, 40, 130,),
    (0, "heads"): (120, 121, 131, 41, 140, 120,),
    (0, "done"): (121, 130, 131, 50,),
    "end": (140, 130, 131, 130, 131, 141, 51, 140, 150, 210, 141, 150, 151, 140, 210, 141, 140, 210, 151, 141, 150, 210, 141, 150, 150, 151, 151, 151,),
}
SLOTS_R = 2
BUFS = 1
PWIDE = (CMAIN, EWIDE + PATCH)
STAGES = 5


def backward_all_kernel(
    times, dout_in, xs_in, gp_in, qk_in, fa_in, vec_ref, mask, pn_ref, head_ref, end_ref, small, wcol, wdown,
    gcol, gdown, gpart, scalars, rfa,
    *refs,
):
    (
        wbuf, gp, xb, dcur, er, qk, ba, lbuf, rd, ru, rq, full, low, recv1, mid_own, mid_low, recv2,
        zlow, zown, zrecv, psend, pown, pxr0, pxr1, pzr0, pzr1, sq,
        wsem, gsem, xsem, qsem, ls, fas, far, bs, br, s1, r1, s2, r2, zs, zr, fs, fr, ks, kr,
        ss, sr, qs, qr, p1, p1r, p2, p2r, p3, p3r, p4, p4r, credit,
        ds_, dr_, gs_, gr_, small_all, square_all,
    ) = refs[: -len(BACKWARD_SCRATCH)]
    scratch = refs[-len(BACKWARD_SCRATCH) :]
    f, t, y, c, g, x = place()
    count = times // 2
    over_x = (f, g * 2 + 1 - x)
    over_y = ((1 - y) * 2 + c, t)
    over_c = (y * 2 + 1 - c, t)
    total = len(RGROUPS)
    other_core = 1 - c

    def half_cols(core):
        return pl.ds(pl.multiple_of(core * 384, 128), 384)

    def weight(layer, which):
        src = (wdown.at[layer], wcol.at[2 * layer + 1], wcol.at[2 * layer])[which]
        return pltpu.make_async_copy(src, wbuf.at[weight_slot(layer, which)], wsem.at[layer, which])

    def weight_slot(layer, which):
        return (which % 2 + (L - 1 - layer)) % 2

    def slope_load(layer, k):
        return pltpu.make_async_copy(gp_in.at[layer, k], gp.at[k % 2], gsem.at[layer, k])

    def kept_load(layer, i):
        return pltpu.make_async_copy(xs_in.at[2 * layer + i], xb, xsem.at[layer, i])

    def heads_load(layer):
        return pltpu.make_async_copy(qk_in.at[layer], qk, qsem.at[layer])

    first_load = pltpu.make_async_copy(dout_in, dcur, qsem.at[L])
    first_load.start()
    for which in range(2):
        weight(L - 1, which).start()
    for k in range(2):
        slope_load(L - 1, k).start()
    kept_load(L - 1, 1).start()
    heads_load(L - 1).start()
    greet_all(times)
    spread_small(times, small, small_all, ss, sr)

    def forward_swap(layer, n):
        span = pl.ds(3, 4) if n == 0 else pl.ds(0, 3)
        return remote(
            fa_in.at[layer, span], rfa.at[layer, span], fas.at[layer, n], far.at[layer, n], over_c
        )

    for layer in reversed(range(L)):
        for n in range(2):
            forward_swap(layer, n).start()

    def swap(gi, n):
        kind, l = RGROUPS[gi]
        if kind == "d":
            src, dst = ba.at[8, :, half_cols(other_core)], rd.at[l]
        elif kind == "u":
            src, dst = ba.at[4 + 2 * n + other_core], ru.at[l, n]
        else:
            src, dst = ba.at[2 * n + other_core], rq.at[l, n]
        return remote(src, dst, bs.at[gi, n], br.at[gi, n], over_c)

    def swaps(gi):
        return range(1 if RGROUPS[gi][0] == "d" else 2)

    def left_loads(gi):
        kind, l = RGROUPS[gi]
        out = []
        blocks = {"d": (3, 4, 5, 6), "u": (2,), "q": (0, c)}[kind]
        for n, block in enumerate(blocks):
            for m, src in enumerate((fa_in, rfa)):
                out.append(
                    pltpu.make_async_copy(
                        src.at[l, block], lbuf.at[n, pl.ds(m * TOK, TOK)], ls.at[n, m]
                    )
                )
        return out

    def product(left, own, other, cols):
        return tn(lbuf[left, :TOK], own(cols)) + tn(lbuf[left, TOK:], other(cols))

    def store(gi, h, role, xx, where, value):
        if ROUTES[gi][h] == "y":
            keep, index = role == 0, xx
        else:
            keep, index = x == xx, role

        def save_full():
            full[(gi % BUFS, h, index) + where] = value

        def save_low():
            low[(gi % BUFS, h, index) + where] = value.astype(BF)

        if isinstance(keep, bool):
            (save_full if keep else save_low)()
        else:
            pl.when(keep)(save_full)
            pl.when(jnp.logical_not(keep))(save_low)

    def compute(gi, h):
        kind, l = RGROUPS[gi]
        if kind == "d":

            def one(z, carry):
                prod = product(
                    z, lambda _: ba[8, :, half_cols(c)], lambda _: rd[l], None
                ).reshape(2, 2, 2, 96, 384)
                for xx in range(2):
                    for yy in range(2):
                        for hh in range(2):
                            store(gi, hh, (yy + y) % 2, xx, (z,), prod[xx, yy, hh])
                return carry

            if h == 0:
                lax.fori_loop(0, count, one, 0)
            return
        recv = ru if kind == "u" else rq
        base = 4 if kind == "u" else 0
        for role in range(2):
            yy = y if role == 0 else 1 - y
            left = 0 if kind == "u" else yy
            prod = product(
                left, lambda cols: ba[base + 2 * yy + c, :, cols], lambda cols: recv[l, yy, :, cols],
                slice(h * 384, (h + 1) * 384),
            ).reshape(count, 2, 96, 384)
            for xx in range(2):
                store(gi, h, role, xx, (), prod[:, xx])

    def step1(gi, h):
        return remote(
            low.at[gi % BUFS, h], recv1.at[gi % SLOTS_R, h], s1.at[gi, h], r1.at[gi, h],
            over_y if ROUTES[gi][h] == "y" else over_x,
        )

    def step2(gi, h):
        if ROUTES[gi][h] == "z":
            src, dst = zlow.at[h, 0], recv2.at[gi % SLOTS_R, h, count - 1]
        else:
            src, dst = mid_low.at[h], recv2.at[gi % SLOTS_R, h]
        return remote(
            src, dst, s2.at[gi, h], r2.at[gi, h], over_x if ROUTES[gi][h] == "y" else over_y
        )

    def along(gi, h, dz, role=0):
        to = (g + dz) % count
        slot = gi % SLOTS_R
        if ROUTES[gi][h] != "z":
            src, dst = zlow.at[h, to], zrecv.at[slot, h, dz - 1]
        elif role == 0:
            src, dst = mid_low.at[h, to], zrecv.at[slot, h, dz - 1]
        else:
            src, dst = zlow.at[h, to], recv2.at[slot, h, dz - 1]
        return remote(src, dst, zs.at[gi, h, role, dz - 1], zr.at[gi, h, role, dz - 1], (f, to * 2 + x))

    def result(gi, h, yy):
        kind, l = RGROUPS[gi]
        if kind == "d":
            return gdown.at[l, yy, pl.ds(h * 96, 96), half_cols(c)]
        return gcol.at[2 * l + (1 if kind == "u" else 0), yy, c, :, pl.ds(h * 384, 384)]

    def spread_y(gi, h):
        block = result(gi, h, y)
        return remote(block, block, fs.at[gi, h], fr.at[gi, h], over_y)

    def spread_c(gi, h):
        block = result(gi, h, slice(None))
        return remote(block, block, ks.at[gi, h], kr.at[gi, h], over_c)

    def wait_along(gi, h):
        for role in range(2 if ROUTES[gi][h] == "z" else 1):
            for dz in range(1, count):
                along(gi, h, dz, role).wait_recv()
                along(gi, h, dz, role).wait_send()

    def start_along(gi, h):
        for dz in range(1, count):
            if gi >= SLOTS_R:
                pl.semaphore_wait(credit.at[1 + dz], 1)
            for role in range(2 if ROUTES[gi][h] == "z" else 1):
                along(gi, h, dz, role).start()

    def advance(gi, h, stage):
        slot, buf = gi % SLOTS_R, gi % BUFS
        twice = ROUTES[gi][h] == "z"
        if stage == 1:
            step1(gi, h).wait_recv()
            step1(gi, h).wait_send()
            if twice:
                summed = full[buf, h, 0] + recv1[slot, h, 0].astype(F32)
                mid_low[h] = summed.astype(BF)
                mid_own[h] = summed
                summed = full[buf, h, 1] + recv1[slot, h, 1].astype(F32)
                zlow[h] = summed.astype(BF)
                start_along(gi, h)
                full[buf, h, 1] = summed
                zown[h] = full[buf, h, 1, g]
                return
            keep, send = (x, 1 - x) if ROUTES[gi][h] == "y" else (0, 1)
            mid_low[h] = (full[buf, h, send] + recv1[slot, h, send].astype(F32)).astype(BF)
            step2(gi, h).start()
            mid_own[h] = full[buf, h, keep] + recv1[slot, h, keep].astype(F32)
        elif stage == 2:
            if twice:
                wait_along(gi, h)
                value = zown[h]
                for dz in range(1, count):
                    value = value + recv2[slot, h, dz - 1].astype(F32)
                zlow[h, 0] = value.astype(BF)
                step2(gi, h).start()
                value = mid_own[h, g]
                for dz in range(1, count):
                    value = value + zrecv[slot, h, dz - 1].astype(F32)
                zown[h] = value
                return
            step2(gi, h).wait_recv()
            step2(gi, h).wait_send()
            summed = mid_own[h] + recv2[slot, h].astype(F32)
            zlow[h] = summed.astype(BF)
            start_along(gi, h)
            mid_own[h] = summed
            zown[h] = mid_own[h, g]
        elif stage == 3:
            value = zown[h]
            if twice:
                step2(gi, h).wait_recv()
                step2(gi, h).wait_send()
                value = value + recv2[slot, h, count - 1].astype(F32)
            else:
                wait_along(gi, h)
                for dz in range(1, count):
                    value = value + zrecv[slot, h, dz - 1].astype(F32)
            sq[...] += jnp.sum((value * value).reshape(12, 8, 3, 128), (0, 2))
            kind, l = RGROUPS[gi]
            if kind == "d":
                gdown[l, y, h * 96 : (h + 1) * 96, half_cols(c)] = value.astype(BF)
            else:
                idx = 2 * l + (1 if kind == "u" else 0)
                gcol[idx, y, c, :, h * 384 : (h + 1) * 384] = value.astype(BF)
            spread_y(gi, h).start()
            if gi + SLOTS_R < total:
                pl.semaphore_signal(credit.at[0], inc=1, device_id=over_x, device_id_type=MESH)
                pl.semaphore_signal(credit.at[1], inc=1, device_id=over_y, device_id_type=MESH)
                for dz in range(1, count):
                    back = (f, ((g + count - dz) % count) * 2 + x)
                    pl.semaphore_signal(
                        credit.at[1 + dz], inc=1, device_id=back, device_id_type=MESH
                    )
        elif stage == 4:
            spread_y(gi, h).wait_recv()
            spread_c(gi, h).start()
        else:
            spread_c(gi, h).wait_recv()

    pxrs, pzrs = (pxr0, pxr1), (pzr0, pzr1)
    psends = [psend.at[:, :, pl.ds(0, w)] for w in PWIDE]
    powns = [pown.at[:, :, pl.ds(0, w)] for w in PWIDE]

    def part_over(n):
        return remote(psends[n], pxrs[n], p1.at[n], p1r.at[n], over_x)

    def part_along(n, dz):
        return remote(
            psends[n].at[(g + dz) % count], pzrs[n].at[dz - 1], p2.at[n, dz - 1], p2r.at[n, dz - 1],
            (f, ((g + dz) % count) * 2 + x),
        )

    def part_y(n):
        block = gpart.at[n, y, c]
        return remote(block, block, p3.at[n], p3r.at[n], over_y)

    def part_c(n):
        block = gpart.at[n, :, c]
        return remote(block, block, p4.at[n], p4r.at[n], over_c)

    def part_compute(n):
        pieces = []
        if n == 0:
            pieces.append((0, tn(head_ref[0], head_ref[1, :, :CMAIN])))
        else:
            pieces.append((0, er[...].T))
            pieces.append((EWIDE, tn(dcur[...].astype(BF), pn_ref[...])))
        for lo, piece in pieces:
            piece = piece.reshape(count, 2, 96, -1)
            span = slice(lo, lo + piece.shape[-1])
            for xx in range(2):

                @pl.when(x == xx)
                def _():
                    powns[n][:, :, span] = piece[:, xx]
                    psends[n][:, :, span] = piece[:, 1 - xx].astype(BF)

        part_over(n).start()

    def part_advance(n, stage):
        if stage == 1:
            part_over(n).wait_recv()
            summed = powns[n][...] + pxrs[n][...].astype(F32)
            powns[n][...] = summed
            part_over(n).wait_send()
            psends[n][...] = summed.astype(BF)
            for dz in range(1, count):
                part_along(n, dz).start()
        elif stage == 2:
            value = powns[n][g]
            for dz in range(1, count):
                part_along(n, dz).wait_recv()
                part_along(n, dz).wait_send()
                value = value + pzrs[n][dz - 1].astype(F32)
            gpart[n, y, c, :, : PWIDE[n]] = value.astype(BF)
            part_y(n).start()
            if n == 1:
                lane = lax.broadcasted_iota(jnp.int32, (96, EWIDE), 1)
                inside = jnp.logical_and(lane % SLOTS < GRID, lane < TOK)
                own = jnp.where(inside, value[:, :EWIDE], 0.0)
                sq[...] += jnp.sum((own * own).reshape(12, 8, 3, 128), (0, 2))
        elif stage == 3:
            part_y(n).wait_recv()
            part_c(n).start()
        else:
            part_c(n).wait_recv()
            value = gpart[n, 0, 0].astype(F32) + gpart[n, 0, 1].astype(F32)
            value = value + gpart[n, 1, 0].astype(F32) + gpart[n, 1, 1].astype(F32)
            value = value[:, : PWIDE[n]]
            if n == 1:
                lane = lax.broadcasted_iota(jnp.int32, value.shape, 1)
                value = jnp.where(lane >= EVEC, value, 0.0)
            value = jnp.where(f == 0, value * value, 0.0)
            sq[...] += jnp.sum(value.reshape(12, 8, PWIDE[n] // 128, 128), (0, 2))

    stages = {}

    def launch(gi, h):
        if h == 0:
            for n in swaps(gi):
                swap(gi, n).wait_recv()
            for copy in left_loads(gi):
                copy.wait()
        compute(gi, h)
        if gi >= SLOTS_R:
            pl.semaphore_wait(credit.at[0], 1)
            pl.semaphore_wait(credit.at[1], 1)
        step1(gi, h).start()
        stages[gi, h] = 0
        if h == 1:
            for n in swaps(gi):
                swap(gi, n).wait_send()
            if gi + 1 < total:
                prepare(gi + 1)

    def perform(op):
        what, gi, h = op // 100, op // 10 % 10, op % 10
        if what == 0:
            launch(gi, h)
            return
        stages[gi, h if what == 1 else 2] += 1
        if what == 1:
            advance(gi, h, stages[gi, h])
        else:
            part_advance(gi, stages[gi, 2])

    waited = set()

    def prepare(gi):
        kind, l = RGROUPS[gi]
        for n in ((0,) if kind == "d" else (1,)):
            if (l, n) not in waited:
                waited.add((l, n))
                forward_swap(l, n).wait_recv()
        for copy in left_loads(gi):
            copy.start()

    def launch_part(n):
        part_compute(n)
        stages[n, 2] = 0

    load_mask(mask, scratch[4])
    sq[...] = jnp.zeros_like(sq)
    er[...] = jnp.zeros_like(er)
    er[EVEC + GLOB + 3 : EVEC + GLOB + 5, :] = end_ref[...]
    er[ECLS:, :] = tn(head_ref[1, :, CMAIN : CMAIN + EWIDE - ECLS], head_ref[0])
    launch_part(0)
    prepare(0)
    first_load.wait()
    loaded = set()

    for layer in reversed(range(L)):
        base = 3 * (L - 1 - layer)

        def mat(which):
            def read(k):
                if (layer, which) not in loaded:
                    loaded.add((layer, which))
                    weight(layer, which).wait()
                return wbuf[weight_slot(layer, which), k]

            return read

        def slope(k):
            slope_load(layer, k).wait()
            return gp[k % 2]

        def kept(i):
            kept_load(layer, i).wait()
            return xb[...]

        def at(point):
            if point.startswith("mlp"):
                k = int(point[3:])
                if k + 2 < FF // D:
                    slope_load(layer, k + 2).start()
                elif layer > 0:
                    slope_load(layer - 1, k - 2).start()
                if k == 0:
                    swap(base, 0).start()
                if k == 3:
                    for n in swaps(base + 1):
                        swap(base + 1, n).start()
                    weight(layer, 2).start()
                    if layer > 0:
                        weight(layer - 1, 0).start()
            elif point == "resid":
                kept_load(layer, 0).start()
                if layer == L - 1:
                    heads_load(layer).wait()
            elif point == "sent":
                if layer < L - 1:
                    heads_load(layer).wait()
            elif point == "head%d%d" % (PER - 1, NF - 1):
                if layer > 0:
                    heads_load(layer - 1).start()
            elif point == "heads":
                for n in swaps(base + 2):
                    swap(base + 2, n).start()
            elif point == "done":
                if layer > 0:
                    weight(layer - 1, 1).start()
                    kept_load(layer - 1, 1).start()
            for op in ORDER.get((layer, point), ()):
                perform(op)

        backward_body(
            layer, dcur, er, ba, vec_ref, qk, (mat(0), mat(1), mat(2)), slope, kept, scratch,
            (ds_.at[layer], dr_.at[layer], gs_.at[layer], gr_.at[layer]), at,
        )
    dgrid = dcur[...]
    spot = lax.broadcasted_iota(jnp.int32, (TOK, D), 0)
    er[:TOK, :] = dgrid
    inside = jnp.where(spot % SLOTS < GRID, dgrid, 0.0)
    er[EVEC + GLOB : EVEC + GLOB + 1, :] = jnp.sum(inside, 0, keepdims=True)
    er[EVEC + GLOB + 1 : EVEC + GLOB + 3, :] = dgrid[GRID : GRID + 2, :]
    launch_part(1)
    shared = False
    for op in ORDER["end"]:
        perform(op)
        summed = all(stages.get((gi, h), 0) >= 3 for gi in range(total) for h in range(2))
        if not shared and summed and stages[0, 2] == stages[1, 2] == STAGES - 1:
            shared = True
            n = NF * times
            me = f * times + t

            def send(i, carry):
                other = (me + i) % n
                remote(sq, square_all.at[me], qs, qr, (other // times, other % times)).start()
                return carry

            lax.fori_loop(1, n, send, 0)
            square_all[me] = sq[...]
    if not shared or any(stages[gi, h] < STAGES for gi in range(total) for h in range(2)):
        raise ValueError("incomplete order")
    for layer in range(L):
        for n in range(2):
            forward_swap(layer, n).wait_send()
    for gi in range(total):
        for h in range(2):
            spread_y(gi, h).wait_send()
            spread_c(gi, h).wait_send()
    for n in range(2):
        part_y(n).wait_send()
        part_c(n).wait_send()
    wait_small(times, small_all, ss, sr)
    wait_small(times, square_all, qs, qr)
    summed = jnp.sum(small_all[...], 0)
    spot = lax.broadcasted_iota(jnp.int32, (8, 128), 0) * 128 + lax.broadcasted_iota(jnp.int32, (8, 128), 1)
    bias = jnp.where(spot < CLASSES, summed, 0.0)
    norm = jnp.sqrt(jnp.sum(jnp.sum(square_all[...], 0) + bias * bias, keepdims=True))
    scalars[0] = summed
    scalars[1] = jnp.broadcast_to(norm, (8, 128))
    scalars[2] = jnp.broadcast_to(jnp.minimum(1.0, 1.0 / (norm + 1e-06)), (8, 128))


def backward_all(times, dout, xs, gp, qk, fa, vec, mask, pnorm, head, end_rows, small, wcol, wdown):
    count = times // 2
    n = NF * times
    total = len(RGROUPS)
    dma = pltpu.SemaphoreType.DMA
    most = max(PWIDE)
    return pl.pallas_call(
        functools.partial(backward_all_kernel, times),
        out_shape=(
            jax.ShapeDtypeStruct((2 * L, 2, 2, 96, D), BF),
            jax.ShapeDtypeStruct((L, 2, 192, D), BF),
            jax.ShapeDtypeStruct((2, 2, 2, 96, most), BF),
            jax.ShapeDtypeStruct((3, 8, 128), F32),
            jax.ShapeDtypeStruct(fa.shape, BF),
        ),
        in_specs=[aspec()] * 5 + [vspec()] + [aspec()] + [vspec()] * 4 + [aspec()] * 2,
        out_specs=(vspec(),) * 4 + (aspec(),),
        scratch_shapes=[
            VM((2, 4, D, D), BF),
            VM((2, TOK, D), F32),
            VM((TOK, D), F32),
            VM((TOK, D), F32),
            VM((EWIDE, D), F32),
            VM((PER, NF, QROWS, 128), BF),
            VM((9, TOK, D), BF),
            VM((4, 2 * TOK, D), BF),
            VM((L, TOK, 384), BF),
            VM((L, 2, TOK, D), BF),
            VM((L, 2, TOK, D), BF),
            VM((BUFS, 2, 2, count, 96, 384), F32),
            VM((BUFS, 2, 2, count, 96, 384), BF),
            VM((SLOTS_R, 2, 2, count, 96, 384), BF),
            VM((2, count, 96, 384), F32),
            VM((2, count, 96, 384), BF),
            VM((SLOTS_R, 2, count, 96, 384), BF),
            VM((2, count, 96, 384), BF),
            VM((2, 96, 384), F32),
            VM((SLOTS_R, 2, count - 1, 96, 384), BF),
            VM((count, 96, most), BF),
            VM((count, 96, most), F32),
            *[VM((count, 96, w), BF) for w in PWIDE],
            *[VM((count - 1, 96, w), BF) for w in PWIDE],
            VM((8, 128), F32),
            dma((L, 3)), dma((L, 4)), dma((L, 2)), dma((L + 1,)), dma((4, 2)),
            dma((L, 2)), dma((L, 2)), dma((total, 2)), dma((total, 2)),
            dma((total, 2)), dma((total, 2)), dma((total, 2)), dma((total, 2)),
            dma((total, 2, 2, count - 1)), dma((total, 2, 2, count - 1)),
            dma((total, 2)), dma((total, 2)), dma((total, 2)), dma((total, 2)),
            dma, dma, dma, dma,
            dma((2,)), dma((2,)), dma((2, count - 1)), dma((2, count - 1)), dma((2,)), dma((2,)), dma((2,)), dma((2,)),
            pltpu.SemaphoreType.REGULAR((count + 1,)),
            *[dma((L, PER, NF - 1))] * 4,
            VM((n, 8, 128), F32),
            VM((n, 8, 128), F32),
        ]
        + BACKWARD_SCRATCH,
        compiler_params=pltpu.CompilerParams(
            collective_id=2 + 2 * L, has_side_effects=True, vmem_limit_bytes=65400 * 1024
        ),
        name="backward_all",
    )(dout, xs, gp, qk, fa, vec, mask, pnorm, head, end_rows, small, wcol, wdown)[:4]


def adam(weight, first, second, grad):
    first = DECAY_FIRST * first + (1.0 - DECAY_FIRST) * grad
    second = DECAY_SECOND * second + (1.0 - DECAY_SECOND) * grad * grad
    fix_one = 1.0 - DECAY_FIRST**STEP
    fix_two = 1.0 - DECAY_SECOND**STEP
    scaled = jnp.sqrt(second * (1.0 / fix_two)) + EPSILON
    weight = weight * (1.0 - LEARN_RATE * WEIGHT_DECAY) - (LEARN_RATE / fix_one) * first / scaled
    return (weight, first, second)


PIECES = 2
WIDE_STEPS = L * 8 // PIECES
DOWN_STEPS = L * 4 // PIECES


def update_kernel(*refs):
    scalars, gcol, gdown, gpart = refs[:4]
    ins, outs, gemb = refs[4:19], refs[19:38], refs[38]
    step = pl.program_id(0)
    coef = scalars[2, 0:1, 0:1]

    def apply(which, grad, at=...):
        new = adam(*(ins[which + 5 * i][at] for i in range(3)), grad * coef)
        for i in range(3):
            outs[which + 5 * i][at] = new[i]
        if which < 4:
            outs[15 + which][at] = new[0].astype(BF)

    @pl.when(step < WIDE_STEPS)
    def _():
        for p in range(PIECES):
            apply(0, gcol[0, p].astype(F32), (0, slice(None), slice(p * D, (p + 1) * D)))

    @pl.when(step >= WIDE_STEPS)
    def _():
        apply(1, gdown[0].astype(F32), (0,))

    @pl.when(step == 0)
    def _():
        main = sum(gpart[0, i, :, :CMAIN].astype(F32) for i in range(NF))
        rest = sum(gpart[1, i, :, EVEC:].astype(F32) for i in range(NF))
        per = FROWS // NF
        for i in range(NF):
            block = gpart[1, i].astype(F32)
            for h in range(2):
                for r in range(per):
                    to = (i * per + r) * 2 * HALF + h * HALF
                    gemb[:, to : to + HALF] = block[:, h * SLOTS + r * HALF : h * SLOTS + (r + 1) * HALF]
        gemb[:, NGRID:] = rest[:, EWIDE - EVEC :]
        apply(2, gemb[...])
        tail = rest[:, ECLS - EVEC : ECLS - EVEC + CLASSES - CMAIN]
        apply(3, jnp.concatenate([main, tail], 1))
        turned = rest[:, : 128].T
        apply(4, turned[:VROWS])


def update(scalars, gcol, gdown, gpart, params, firsts, seconds):
    shard = gcol.shape[2]
    per_wide, per_down = 8 // PIECES, 4 // PIECES

    def wide(step):
        step = jnp.minimum(step, WIDE_STEPS - 1)
        return (step // per_wide, 0, step % per_wide)

    def wide_grad(step):
        step = jnp.minimum(step, WIDE_STEPS - 1)
        return (step // per_wide, step % per_wide, 0, 0)

    def down(step):
        step = jnp.maximum(step - WIDE_STEPS, 0)
        return (step // per_down, step % per_down, 0)

    params, firsts, seconds = (
        [v[0], v[1], v[2].T, v[3], v[4]] for v in (params, firsts, seconds)
    )
    down_block = pl.BlockSpec((1, PIECES * shard, D), down)
    specs = [pl.BlockSpec((1, shard, PIECES * D), wide), down_block] + [vspec()] * 3
    shapes = [jax.ShapeDtypeStruct(v.shape, F32) for v in params] * 3
    shapes += [jax.ShapeDtypeStruct(v.shape, BF) for v in params[:4]]
    news = pl.pallas_call(
        update_kernel,
        grid=(WIDE_STEPS + DOWN_STEPS,),
        out_shape=shapes,
        in_specs=[vspec(), pl.BlockSpec((1, PIECES, shard, D), wide_grad), down_block, vspec()] + specs * 3,
        out_specs=specs * 3 + specs[:4],
        scratch_shapes=[VM((shard, NGRID + PATCH), F32)],
        compiler_params=pltpu.CompilerParams(vmem_limit_bytes=48 * 1024 * 1024),
        name="update",
    )(scalars, gcol, gdown, gpart, *params, *firsts, *seconds)
    return [v.T if i % 5 == 2 else v for i, v in enumerate(news)]


def pad_to(v, axis, size):
    pads = [(0, 0)] * v.ndim
    pads[axis] = (0, size - v.shape[axis])
    return jnp.pad(v, pads)


def embed_units(embedding, classifier, vectors, f):
    width = embedding.shape[1]
    blocks = embedding[:NGRID].reshape(NF, FROWS // NF, 2, HALF, width)
    block = lax.dynamic_index_in_dim(blocks, f, 0, keepdims=False).transpose(1, 0, 2, 3)
    block = block.reshape(2, GRID, width)
    tokens = jnp.where(f == 0, vectors[GLOB + 1 : GLOB + 3], 0.0)
    tokens = jnp.stack([tokens, jnp.zeros_like(tokens)])
    block = jnp.concatenate([block, tokens, jnp.zeros((2, SLOTS - GRID - 2, width), F32)], 1)
    rest = classifier[:, CMAIN:].T
    unit = jnp.concatenate(
        [
            block.reshape(TOK, width), vectors, jnp.zeros((ECLS - EVEC - VROWS, width), F32),
            pad_to(rest, 0, EWIDE - ECLS),
        ],
        0,
    )
    return unit.T.astype(BF), embedding[NGRID:].T.astype(BF), classifier[:, :CMAIN].astype(BF)


def local(
    patches, column_mask, labels, clip_weights, wide_weights, down_weights, embedding, classifier,
    vectors, class_bias, wide_first, down_first, embedding_first, classifier_first, vectors_first,
    bias_first, wide_second, down_second, embedding_second, classifier_second, vectors_second,
    bias_second,
):
    times = lax.axis_size("tm")
    f, t = lax.axis_index("freq"), lax.axis_index("tm")
    half = t % 2
    pair = t // 2
    rows_dev = FROWS // NF
    kernels = D // times == 96
    shard = D // times
    columns = column_mask.reshape(times, CPD, HALF) > 0
    mine_columns = lax.dynamic_index_in_dim(columns, t, 0, keepdims=False)
    raw = patches.reshape(rows_dev, CPD, HALF, PATCH)

    keep_block, give_block = (
        pad_to(lax.dynamic_index_in_dim(raw, i, 1, keepdims=False).reshape(GRID, PATCH), 0, SLOTS)
        for i in (half, 1 - half)
    )

    live = jnp.stack([pad_to(jnp.tile(mine_columns[i], rows_dev), 0, SLOTS) for i in range(2)])
    live = jnp.where(half == 0, live, live[::-1]).astype(F32)[:, :, None]
    unit_embed, unit_patch, unit_class = embed_units(embedding, classifier, vectors, f)

    clip_columns = lax.dynamic_slice(columns, (pair * 2, half, 0), (2, 1, HALF)).reshape(2, HALF)
    slots = jnp.concatenate(
        [
            jnp.broadcast_to(jnp.tile(clip_columns, (1, rows_dev)), (NF, 2, GRID)),
            jnp.broadcast_to(
                ((jnp.arange(NF)[:, None] == 0) & (jnp.arange(2)[None, :] == 0))[:, :, None], (NF, 2, 2)
            ),
            jnp.zeros((NF, 2, SLOTS - GRID - 2), bool),
        ],
        2,
    ).reshape(NF * TOK)
    mask = jnp.where(slots[:, None] | (jnp.arange(128) != HDIM)[None, :], 0.0, -1e30).astype(BF)

    weight_total = jnp.sum(clip_weights).astype(F32)
    if kernels:
        wcol, wdown, vec, xs, fa, gp, qk, pnorm, dx, head, end_rows, small = forward_all(
            times, wide_weights, down_weights, unit_embed, unit_patch, unit_class, live, keep_block, give_block,
            pad_to(labels, 1, D), clip_weights[None], pad_to(class_bias[None], 1, D), mask,
        )
    else:
        wide_all = lax.all_gather(wide_weights.astype(BF), "tm", axis=1, tiled=True)
        wcol = wide_all.reshape(L, D, 2, 4, D).transpose(0, 2, 3, 1, 4)
        wcol = wcol.reshape(2 * L, 2, 2, 4, 2, 96, D)
        wdown = lax.all_gather(down_weights.astype(BF), "tm", axis=1, tiled=True)
        wdown = wdown.reshape(L, 4, 2, 2, 192, D)
        vec = lax.all_gather(unit_embed, "tm", axis=0, tiled=True).T.astype(F32)
        patch = lax.all_gather(unit_patch, "tm", axis=0, tiled=True)
        class_main = lax.all_gather(unit_class, "tm", axis=0, tiled=True)
        pixels = jnp.stack([keep_block, give_block]).astype(F32)
        sums = jnp.stack(
            [jnp.sum(pixels * live), jnp.sum(pixels * pixels * live), jnp.sum(live) * PATCH]
        )
        sums = lax.psum(sums, ("freq", "tm"))
        take_block = lax.ppermute(
            give_block, "tm", [(i, i + 1 - 2 * (i % 2)) for i in range(times)]
        )
        pixels = jnp.concatenate(
            [jnp.where(half == 0, keep_block, take_block), jnp.where(half == 0, take_block, keep_block)], 0
        )
        center = sums[0] / sums[2]
        mel_scale = lax.rsqrt(sums[1] / sums[2] - center * center + 1e-05)
        inside = (jnp.arange(TOK) % SLOTS < GRID)[:, None]
        pnorm = jnp.where(inside, (pixels.astype(F32) - center) * mel_scale, 0.0).astype(BF)
        x = nt(pnorm, patch) + vec[:TOK] + jnp.where(inside, vec[EVEC + GLOB], 0.0)
        xs, fa, gp, qk = [x], [], [], []
        for layer in range(L):
            x, x1, acts, slopes, heads = forward_layer(layer, x, vec, mask, wcol, wdown)
            xs += [x1, x]
            fa.append(acts)
            gp.append(slopes)
            qk.append(heads)
    wcol = wcol.reshape(2 * L, 4, D, D)
    wdown = wdown.reshape(L, 4, D, D)
    if not kernels:
        vec_all = vec[EVEC : EVEC + VROWS]
        class_all = jnp.concatenate([class_main, vec[ECLS : ECLS + CLASSES - CMAIN].T.astype(BF)], 1)

        owner = (f == 0).astype(F32)
        special = xs[2 * L][GRID : GRID + 2]
        normed_end, scale_end = norm_rows(special)
        feature = jnp.mean(normed_end * vec_all[GLOB + 3] + vec_all[GLOB + 4], 0, keepdims=True).astype(BF)
        logits = nn(feature, class_all) + class_bias
        clip = pair * CPD + half
        flags = lax.dynamic_slice_in_dim(labels, clip, 1, 0).astype(F32)
        weight = lax.dynamic_slice_in_dim(clip_weights, clip, 1, 0).astype(F32)[:, None]
        loss_part = owner * jnp.sum(weight * (jax.nn.softplus(logits) - flags * logits))
        dlogits = owner * weight * (jax.nn.sigmoid(logits) - flags) / weight_total
        dlogits_low = dlogits.astype(BF)
        dfinal = jnp.broadcast_to(0.5 * nt(dlogits_low, class_all), (2, D))
        dspecial = norm_back(dfinal * vec_all[GLOB + 3], normed_end, scale_end)
        end_rows = jnp.stack([jnp.sum(dfinal * normed_end, 0), jnp.sum(dfinal, 0)])
        dx = jnp.concatenate(
            [jnp.zeros((GRID, D), F32), dspecial, jnp.zeros((TOK - GRID - 2, D), F32)], 0
        )
        small = jnp.concatenate([dlogits.reshape(-1), loss_part.reshape(1)])
        small = pad_to(small, 0, 1024).reshape(8, 128)
    if kernels:
        gcol, gdown, gpart, scalars = backward_all(
            times, dx, xs, gp, qk, fa, vec, mask, pnorm, head, end_rows, small, wcol, wdown
        )
        small = scalars[0].reshape(-1)
        grad_norm, coef = scalars[1, 0, 0], scalars[2, 0, 0]
        params = (wide_weights, down_weights, embedding, classifier, vectors)
        firsts = (wide_first, down_first, embedding_first, classifier_first, vectors_first)
        seconds = (wide_second, down_second, embedding_second, classifier_second, vectors_second)
        news = update(
            scalars, gcol.reshape(L, 8, shard, D), gdown.reshape(L, FF // times, D),
            gpart.reshape(2, NF, shard, -1), params, firsts, seconds,
        )
        bias = adam(class_bias, bias_first, bias_second, small[:CLASSES] * coef)
        return (
            *news[:5], bias[0], *news[5:10], bias[1], *news[10:15], bias[2], *news[15:],
            grad_norm, small[CLASSES], weight_total,
        )
    else:
        ba = [None] * L
        er = jnp.zeros((EWIDE, D), F32)
        for layer in reversed(range(L)):
            dx, ba[layer], rows = backward_layer(
                layer, dx, xs[2 * layer], xs[2 * layer + 1], gp[layer], qk[layer], vec, mask, wcol, wdown
            )
            er = er + rows
        dgrid = jnp.where(inside, dx, 0.0)
        grad_vectors = er[EVEC : EVEC + GLOB]
        grad_vectors = jnp.concatenate(
            [grad_vectors, jnp.sum(dgrid, 0, keepdims=True), dx[GRID : GRID + 2], end_rows], 0
        )
        wides, downs = [], []
        for l in range(L):
            cols = [tn(fa[l][0], ba[l][i]) for i in range(3)]
            cols += [tn(fa[l][1], ba[l][3])]
            cols += [tn(fa[l][2], ba[l][4 + i]) for i in range(4)]
            wides.append(jnp.concatenate(cols, 1))
            downs.append(jnp.concatenate([tn(fa[l][3 + i], ba[l][8]) for i in range(4)], 0))
        dpos = dgrid.reshape(2, SLOTS, D)[:, :GRID].reshape(2, rows_dev, HALF, D)
        dpos = dpos.transpose(1, 0, 2, 3).reshape(rows_dev * 2 * HALF, D)
        dpos = lax.dynamic_update_slice(jnp.zeros((NGRID, D), F32), dpos, (f * rows_dev * 2 * HALF, 0))
        dembed = jnp.concatenate([dpos, tn(pnorm, dgrid.astype(BF))], 0)
        grads = (
            lax.psum_scatter(jnp.stack(wides), "tm", scatter_dimension=1, tiled=True),
            lax.psum_scatter(jnp.stack(downs), "tm", scatter_dimension=1, tiled=True),
            lax.psum_scatter(dembed, "tm", scatter_dimension=1, tiled=True),
            lax.psum_scatter(tn(feature, dlogits_low), "tm", scatter_dimension=0, tiled=True),
            lax.psum_scatter(grad_vectors, "tm", scatter_dimension=1, tiled=True),
        )
        grads = lax.psum(grads, "freq")
        grad_wide, grad_down, grad_embed, grad_class, grad_vectors = grads
        squares = sum(jnp.sum(v * v) for v in grads)
        square_total, small = lax.psum(
            (jnp.where(f == 0, squares, 0.0), small.reshape(-1)), ("freq", "tm")
        )
    grad_bias = small[:CLASSES]
    loss_sum = small[CLASSES]
    grad_norm = jnp.sqrt(square_total + jnp.sum(grad_bias * grad_bias))
    coef = jnp.minimum(1.0, 1.0 / (grad_norm + 1e-06))

    params = (wide_weights, down_weights, embedding, classifier, vectors, class_bias)
    firsts = (wide_first, down_first, embedding_first, classifier_first, vectors_first, bias_first)
    seconds = (wide_second, down_second, embedding_second, classifier_second, vectors_second, bias_second)
    grads = (grad_wide, grad_down, grad_embed, grad_class, grad_vectors, grad_bias)
    news = [adam(w, m, v, g * coef) for w, m, v, g in zip(params, firsts, seconds, grads)]
    masters = [n[0] for n in news]
    return (
        *masters,
        *[n[1] for n in news],
        *[n[2] for n in news],
        *[m.astype(BF) for m in masters[:4]],
        grad_norm,
        loss_sum,
        weight_total,
    )


def solution(mesh):
    split = (
        P(None, "tm", None), P(None, "tm", None), P(None, "tm"), P("tm", None), P(None, "tm"), P(),
    )
    return jax.shard_map(
        local,
        mesh=mesh,
        in_specs=(P("freq", "tm", None), P(), P(), P()) + split * 3,
        out_specs=split * 3 + split[:4] + (P(), P(), P()),
        check_vma=False,
    )
```

```python
import functools

import jax
import jax.numpy as jnp
from jax import lax
from jax.experimental import pallas as pl
from jax.experimental.pallas import tpu as pltpu
from jax.sharding import PartitionSpec as P

D = 768
HEADS = 12
HDIM = 64
FF = 3072
L = 2
FROWS = 12
HALF = 52
PATCH = 256
STEP = 5
CPD = 2
NGRID = FROWS * 2 * HALF
CLASSES = 527
VROWS = 29
GLOB = L * 8 + L * (FF // D)

TOK = 320
PER = 3
NF = 4

DECAY_FIRST = 0.5
DECAY_SECOND = 0.5
LEARN_RATE = 0.03
WEIGHT_DECAY = 0.05
EPSILON = 1e-08

MESH = pl.DeviceIdType.MESH
BF = jnp.bfloat16
F32 = jnp.float32
VLIM = 60 * 1024 * 1024
VM = pltpu.VMEM


def nn(a, b):
    return lax.dot_general(a, b, (((1,), (0,)), ((), ())), preferred_element_type=F32)


def nt(a, b):
    return lax.dot_general(a, b, (((1,), (1,)), ((), ())), preferred_element_type=F32)


def tn(a, b):
    return lax.dot_general(a, b, (((0,), (0,)), ((), ())), preferred_element_type=F32)


def norm_rows(x):
    center = jnp.mean(x, -1, keepdims=True)
    shifted = x - center
    scale = lax.rsqrt(jnp.mean(shifted * shifted, -1, keepdims=True) + 1e-06)
    return (shifted * scale, scale)


def norm_back(dnorm, normed, scale):
    return scale * (
        dnorm
        - jnp.mean(dnorm, -1, keepdims=True)
        - normed * jnp.mean(dnorm * normed, -1, keepdims=True)
    )


def vspec():
    return pl.BlockSpec(memory_space=VM)


def aspec():
    return pl.BlockSpec(memory_space=pl.ANY)


def place():
    f, t = lax.axis_index("freq"), lax.axis_index("tm")
    return f, t, f // 2, f % 2, t // 2, t % 2


def remote(src, dst, ssem, rsem, dev):
    return pltpu.make_async_remote_copy(
        src_ref=src, dst_ref=dst, send_sem=ssem, recv_sem=rsem, device_id=dev, device_id_type=MESH
    )


def greet_all(times):
    f, t = lax.axis_index("freq"), lax.axis_index("tm")
    n = NF * times
    me = f * times + t
    barrier = pltpu.get_barrier_semaphore()

    def hello(i, carry):
        other = (me + i) % n
        pl.semaphore_signal(
            barrier, inc=1, device_id=(other // times, other % times), device_id_type=MESH
        )
        return carry

    lax.fori_loop(1, n, hello, 0)
    pl.semaphore_wait(barrier, n - 1)


def spread_small(times, small, gathered, ssem, rsem):
    f, t = lax.axis_index("freq"), lax.axis_index("tm")
    n = NF * times
    me = f * times + t

    def send(i, carry):
        other = (me + i) % n
        remote(
            small, gathered.at[me], ssem, rsem, (other // times, other % times)
        ).start()
        return carry

    lax.fori_loop(1, n, send, 0)
    gathered[me] = small[...]


def wait_small(times, gathered, ssem, rsem):
    n = NF * times
    many = gathered.at[pl.ds(0, n - 1)]
    pltpu.make_async_copy(many, many, rsem).wait()
    pltpu.make_async_copy(many, many, ssem).wait()


QROWS = TOK + TOK // 2
SLOTS = TOK // 2
GRID = FROWS // NF * HALF
EWIDE = 384
EVEC = TOK
ECLS = 352
CMAIN = 512


def greet_clip():
    f, t = lax.axis_index("freq"), lax.axis_index("tm")
    barrier = pltpu.get_barrier_semaphore()
    for i in range(1, NF):
        pl.semaphore_signal(barrier, inc=1, device_id=((f + i) % NF, t), device_id_type=MESH)
    pl.semaphore_wait(barrier, NF - 1)


def pack_half(v):
    return jnp.concatenate([v[: TOK // 2], v[TOK // 2 :]], 1)


def open_half(v):
    return jnp.concatenate([v[:, :HDIM], v[:, HDIM:]], 0)


def with_mask(block):
    lane = lax.broadcasted_iota(jnp.int32, block.shape, 1)
    query = jnp.where(lane < HDIM, block.astype(F32) * (HDIM ** (-0.5)), 0.0)
    return jnp.where(lane == HDIM, 1.0, query).astype(BF)


def exchange_sems():
    dma = pltpu.SemaphoreType.DMA
    return [dma((PER, NF - 1))] * 4


FORWARD_SCRATCH = [
    VM((2, 2, 2, 4, 2, 96, D), BF),
    VM((4, 2, 2, 192, D), BF),
    VM((PER, NF, QROWS, 128), BF),
    VM((PER, NF, TOK // 2, 128), BF),
    VM((NF * TOK, 128), BF),
    VM((NF * TOK, HDIM), BF),
    VM((TOK, D), F32),
]


def layer_body(layer, x_ref, vec_ref, outs, scratch, orecv, sems, fetch, at):
    xo_ref, x1_ref, fa_ref, gp_ref, qk_ref = outs
    wbuf, dbuf, qsend, osend, kall, vall, acc = scratch
    qs, qr, os, orr = sems
    f, t = lax.axis_index("freq"), lax.axis_index("tm")

    def row(i):
        return vec_ref[EVEC + layer * 8 + i : EVEC + layer * 8 + i + 1, :]

    def mat(part, q, cols=slice(None)):
        return wbuf[part, q // 2, q % 2, :, :, :, cols].reshape(D, -1)

    normed, _ = norm_rows(x_ref[...])
    act = (normed * row(0) + row(1)).astype(BF)
    fa_ref[0] = act
    fetch(0)

    def to_clip(j, i):
        other = (f + i) % NF
        return remote(
            qsend.at[j, other], qk_ref.at[j, f], qs.at[j, i - 1], qr.at[j, i - 1], (other, t)
        )

    def back_clip(j, i):
        other = (f + i) % NF
        return remote(
            osend.at[j, other], orecv.at[j, f], os.at[j, i - 1], orr.at[j, i - 1], (other, t)
        )

    for j in range(PER):
        cols = slice(256 * j, 256 * (j + 1))
        query = (nn(act, mat(0, 0, cols)) + row(4)[:, cols]).astype(BF)
        key = nn(act, mat(0, 1, cols)).astype(BF)
        value = (nn(act, mat(0, 2, cols)) + row(5)[:, cols]).astype(BF)
        for h in range(NF):
            part = slice(HDIM * h, HDIM * (h + 1))
            qsend[j, h, :TOK] = jnp.concatenate([query[:, part], key[:, part]], 1)
            qsend[j, h, TOK:] = pack_half(value[:, part])
        for i in range(1, NF):
            to_clip(j, i).start()
        qk_ref[j, f] = qsend[j, f]
        at("qkv%d" % j)
    for j in range(PER):
        for i in range(1, NF):
            to_clip(j, i).wait_recv()
        for s in range(NF):
            kall[s * TOK : (s + 1) * TOK, :HDIM] = qk_ref[j, s, :TOK, HDIM:]
            vall[s * TOK : (s + 1) * TOK] = open_half(qk_ref[j, s, TOK:])

        def attend(i, carry):
            s = (f + i) % NF
            to = i % NF
            halves = []
            for h in range(2):
                lo = h * (TOK // 2)
                scores = nt(with_mask(qk_ref[j, s, lo : lo + TOK // 2]), kall[...])
                top = jnp.max(scores, -1, keepdims=True)
                expo = jnp.exp(scores - top)
                total = jnp.sum(expo, -1, keepdims=True)
                probs = (expo * (1.0 / total)).astype(BF)
                halves.append(nn(probs, vall[...]).astype(BF))
            osend[j, s] = jnp.concatenate(halves, 1)

            @pl.when(to > 0)
            def _():
                remote(
                    osend.at[j, s], orecv.at[j, f], os.at[j, to - 1], orr.at[j, to - 1], (s, t)
                ).start()

            return carry

        lax.fori_loop(1, 3, attend, 0)
        at("head%d1" % j)
        lax.fori_loop(3, 5, attend, 0)
        orecv[j, f] = osend[j, f]
        at("head%d3" % j)
    parts = []
    for j in range(PER):
        for i in range(1, NF):
            back_clip(j, i).wait_recv()
        for h in range(NF):
            parts.append(open_half(orecv[j, h]))
    mixed = jnp.concatenate(parts, 1)
    fa_ref[1] = mixed
    resid = x_ref[...] + nn(mixed, mat(0, 3)) + row(6)
    x1_ref[...] = resid
    normed, _ = norm_rows(resid)
    fa_ref[2] = (normed * row(2) + row(3)).astype(BF)
    acc[...] = resid + row(7)
    at("resid")
    fetch(1)

    def up(k, carry):
        bias = vec_ref[pl.ds(EVEC + L * 8 + layer * 4 + k, 1), :]
        before = nn(fa_ref[2], mat(1, k)) + bias
        lower = 0.5 * (1.0 + lax.erf(before * 0.7071067811865476))
        gp_ref[k] = lower + before * jnp.exp(-0.5 * before * before) * 0.3989422804014327
        hidden = (before * lower).astype(BF)
        fa_ref[3 + k] = hidden
        return carry

    def down(k, carry):
        acc[...] += nn(fa_ref[3 + k], dbuf[k].reshape(D, D))
        return carry

    for k in range(0, FF // D, 2):
        lax.fori_loop(k, k + 2, up, 0)
        at("up%d" % (k + 1))
    fetch(2)
    for k in range(0, FF // D, 2):
        lax.fori_loop(k, k + 2, down, 0)
        at("down%d" % (k + 1))
    xo_ref[...] = acc[...]
    for j in range(PER):
        for i in range(1, NF):
            to_clip(j, i).wait_send()
            back_clip(j, i).wait_send()


def load_mask(mask, kall):
    def body(sem):
        copy = pltpu.make_async_copy(mask, kall, sem)
        copy.start()
        copy.wait()

    pl.run_scoped(body, pltpu.SemaphoreType.DMA)


def forward_kernel(
    layer, x_ref, vec_ref, mask, wcol, wdown,
    xo_ref, x1_ref, fa_ref, gp_ref, qk_ref,
    wbuf, dbuf, qsend, osend, kall, vall, acc, orecv, wsem, qs, qr, os, orr,
):
    loads = [
        pltpu.make_async_copy(wcol.at[2 * layer], wbuf.at[0], wsem.at[0]),
        pltpu.make_async_copy(wcol.at[2 * layer + 1], wbuf.at[1], wsem.at[1]),
        pltpu.make_async_copy(wdown.at[layer], dbuf, wsem.at[2]),
    ]
    for load in loads:
        load.start()
    load_mask(mask, kall)
    greet_clip()
    layer_body(
        layer, x_ref, vec_ref, (xo_ref, x1_ref, fa_ref, gp_ref, qk_ref),
        (wbuf, dbuf, qsend, osend, kall, vall, acc), orecv, (qs, qr, os, orr),
        lambda part: loads[part].wait(), lambda point: None,
    )


def forward_layer(layer, x, vec, mask, wcol, wdown):
    return pl.pallas_call(
        functools.partial(forward_kernel, layer),
        out_shape=(
            jax.ShapeDtypeStruct((TOK, D), F32),
            jax.ShapeDtypeStruct((TOK, D), F32),
            jax.ShapeDtypeStruct((7, TOK, D), BF),
            jax.ShapeDtypeStruct((FF // D, TOK, D), F32),
            jax.ShapeDtypeStruct((PER, NF, QROWS, 128), BF),
        ),
        in_specs=[vspec()] * 2 + [aspec()] * 3,
        out_specs=(vspec(),) * 5,
        scratch_shapes=FORWARD_SCRATCH
        + [VM((PER, NF, TOK // 2, 128), BF), pltpu.SemaphoreType.DMA((3,))]
        + exchange_sems(),
        compiler_params=pltpu.CompilerParams(
            collective_id=2 + layer, has_side_effects=True, vmem_limit_bytes=VLIM
        ),
        name="forward_layer",
    )(x, vec, mask, wcol, wdown)


GROUPS = (("c", 0), ("c", 1), ("d", 0), ("c", 2), ("c", 3), ("d", 1))
SUBS = tuple((kind, idx, h) for kind, idx in GROUPS for h in (0, 1))
PATHS = "xyxzxzxzzzzz"
FLOW = {
    ("begin",): (0, 1,),
    ("units",): (2, 3,),
    ("arrived",): (100,),
    ("x0",): (4, 101,),
    ("fetch", 0, 0,): (100, 102, 101, 5, 102, 103, 100, 6, 104, 101, 100, 101,),
    (0, "qkv0",): (7, 102,),
    (0, "qkv1",): (103,),
    (0, "head01",): (8, 102, 103, 104, 105,),
    (0, "head03",): (106,),
    (0, "head11",): (9,),
    (0, "head21",): (105, 107,),
    (0, "head23",): (10, 104, 106, 105,),
    (0, "resid",): (104, 108,),
    (0, "up1",): (11, 107,),
    (0, "up3",): (106,),
    (0, "down1",): (107, 109,),
    ("fetch", 1, 0,): (106, 108,),
    (1, "qkv1",): (108,),
    (1, "head01",): (109, 110,),
    (1, "head11",): (109, 111,),
    (1, "head13",): (110,),
    (1, "head23",): (110,),
    (1, "resid",): (111,),
    (1, "up3",): (111,),
}


def gather_parts(count, ucol, udown, ocol, odown, sems, prepare):
    zs, zr, own, s1, r1, s2, r2, s3, r3 = sems
    f, t, y, c, g, x = place()
    every = slice(None)
    over_x, over_y, over_c = (f, g * 2 + 1 - x), ((1 - y) * 2 + c, t), (y * 2 + 1 - c, t)

    def source(s):
        kind, idx, h = SUBS[s]
        yy = every if PATHS[s] == "z" else y
        if kind == "c":
            return ucol.at[idx, yy, c, :, pl.ds(h * 384, 384)]
        return udown.at[idx, yy, pl.ds(h * 96, 96), pl.ds(pl.multiple_of(c * 384, 128), 384)]

    def view(s, yy, zz, xx):
        kind, idx, h = SUBS[s]
        if PATHS[s] == "z":
            yy = every
        if kind == "c":
            return ocol.at[idx, yy, c, zz, xx, :, pl.ds(h * 384, 384)]
        return odown.at[
            idx, zz, xx, yy, pl.ds(h * 96, 96), pl.ds(pl.multiple_of(c * 384, 128), 384)
        ]

    def along(s, dz):
        return remote(
            source(s), view(s, y, g, x), zs.at[s, dz - 1], zr.at[s, dz - 1],
            (f, ((g + dz) % count) * 2 + x),
        )

    def keep(s):
        return pltpu.make_async_copy(source(s), view(s, y, g, x), own.at[s])

    def leg(s, n):
        if n == legs(s):
            block = view(s, every, every, every)
            return remote(block, block, s3.at[s], r3.at[s], over_c)
        if n == 1:
            block = view(s, y, every, x)
            return remote(block, block, s1.at[s], r1.at[s], over_y if PATHS[s] == "y" else over_x)
        block = view(s, y, every, every) if PATHS[s] == "x" else view(s, every, every, x)
        return remote(block, block, s2.at[s], r2.at[s], over_y if PATHS[s] == "x" else over_x)

    def legs(s):
        return 2 if PATHS[s] == "z" else 3

    def piece(s, zz, src=None):
        block = view(s, y, zz, x)
        return remote(
            block if src is None else src, block, s1.at[s], r1.at[s], over_y if PATHS[s] == "y" else over_x
        )

    stage = {}

    def begin(s):
        prepare(s // 2)
        keep(s).start()
        for dz in range(1, count):
            along(s, dz).start()
        piece(s, g, source(s)).start()
        stage[s] = 0

    def advance(s):
        if stage[s] == 0:
            for dz in range(1, count):
                along(s, dz).wait_recv()
                piece(s, (g + count - dz) % count).start()
            keep(s).wait()
        else:
            leg(s, stage[s]).wait_recv()
        stage[s] += 1
        if 1 < stage[s] <= legs(s):
            leg(s, stage[s]).start()

    def arrived(s):
        return stage.get(s, 0) > legs(s)

    def finish():
        for s in range(len(SUBS)):
            for dz in range(1, count):
                along(s, dz).wait_send()
            for n in range(1, legs(s) + 1):
                leg(s, n).wait_send()

    return begin, advance, arrived, finish


def loss_part(owner, clip, x_ref, vec, classes, labels, clip_weights, class_bias, dout, head, end_rows, small):
    owner = jnp.where(owner, 1.0, 0.0)
    normed, scale = norm_rows(x_ref[GRID : GRID + 2, :])
    gain = vec[EVEC + GLOB + 3 : EVEC + GLOB + 4, :]
    final = normed * gain + vec[EVEC + GLOB + 4 : EVEC + GLOB + 5, :]
    feature = jnp.mean(final, 0, keepdims=True).astype(BF)
    first_row = lax.broadcasted_iota(jnp.int32, (16, D), 0) == 0
    feature = jnp.where(first_row, jnp.broadcast_to(feature.astype(F32), (16, D)), 0.0).astype(BF)
    head[0] = feature
    main = classes[...].reshape(D, CMAIN)
    tail = vec[ECLS:EWIDE, :].astype(BF)
    logits = jnp.concatenate([nn(feature, main), nt(feature, tail), jnp.zeros((16, 224), F32)], 1)[0:1]
    logits = logits + class_bias[...]
    flags = labels[pl.ds(clip, 1), :].astype(F32)
    weights = clip_weights[...].astype(F32)
    weight = jnp.sum(
        jnp.where(lax.broadcasted_iota(jnp.int32, weights.shape, 1) == clip, weights, 0.0), keepdims=True
    )
    total = jnp.sum(weights, keepdims=True)
    lane = lax.broadcasted_iota(jnp.int32, (1, D), 1)
    inside = lane < CLASSES
    soft = jnp.maximum(logits, 0.0) + jnp.log1p(jnp.exp(-jnp.abs(logits)))
    loss = jnp.sum(jnp.where(inside, soft - flags * logits, 0.0), keepdims=True) * weight * owner
    slope = 1.0 / (1.0 + jnp.exp(-logits))
    grads = jnp.where(inside, owner * weight * (slope - flags) / total, 0.0)
    for i in range(8):
        small[i : i + 1, :] = jnp.zeros((1, 128), F32) if i > 5 else (
            grads[:, 128 * i : 128 * (i + 1)]
            + (jnp.where(lane[:, 128 * i : 128 * (i + 1)] == CLASSES, loss, 0.0))
        )
    grads = jnp.where(first_row, jnp.broadcast_to(grads, (16, D)), 0.0).astype(BF)
    head[1] = grads
    dfinal = 0.5 * (nt(grads[:, :CMAIN], main) + nn(grads[:, CMAIN : CMAIN + EWIDE - ECLS], tail))[0:1]
    end_rows[0:1, :] = jnp.sum(dfinal * normed, 0, keepdims=True)
    end_rows[1:2, :] = 2.0 * dfinal
    special = norm_back(jnp.broadcast_to(dfinal * gain, normed.shape), normed, scale)
    dout[...] = jnp.zeros_like(dout)
    dout[GRID : GRID + 2, :] = special


def forward_all_kernel(
    times, wide, down, uemb, upatch, uclass, live, pkeep, psend, labels, clip_weights, class_bias, mask,
    ocol, odown, vec_out, xs_out, fa_out, gp_out, qk_out, pn_out, dout_out, head, end_rows, small,
    wbuf, dbuf, qsend, osend, kall, vall, acc, orecv, sall, precv, emb, patches, classes, vec, xs, fa, gp, qk, pn,
    zs, zr, own, s1, r1, s2, r2, s3, r3, es, er, exs, exr, ss, sr, ps, pr, wsem, osem,
    qs0, qr0, os0, or0, qs1, qr1, os1, or1, ucol, udown, cols_wide, cols_down, stats, dout, psem,
):
    f, t, y, c, g, x = place()
    count = times // 2
    over_x = (f, g * 2 + 1 - x)

    def fetch_master(group):
        kind, idx = GROUPS[group]
        if kind == "c":
            src = wide.at[idx // 2, :, pl.ds(idx % 2 * 4 * D, 4 * D)]
            return pltpu.make_async_copy(src, cols_wide.at[idx], psem.at[group])
        return pltpu.make_async_copy(down.at[idx], cols_down.at[idx], psem.at[group])

    prepared = set()

    def prepare(group):
        if group in prepared:
            return
        prepared.add(group)
        fetch_master(group).wait()
        kind, idx = GROUPS[group]
        for q in range(4):
            if kind == "c":
                ucol[idx, q // 2, q % 2] = cols_wide[idx, :, q * D : (q + 1) * D].astype(BF)
            else:
                udown[idx, q // 2, q % 2 * 96 : q % 2 * 96 + 96] = cols_down[idx, q * 96 : (q + 1) * 96].astype(BF)

    for group in range(len(GROUPS)):
        fetch_master(group).start()
    row = lax.broadcasted_iota(jnp.int32, (8, 128), 1)
    stats[...] = jnp.zeros_like(stats)
    for n, block in enumerate((pkeep, psend)):
        pixel, alive = block[...].astype(F32), live[n]
        masked = pixel * alive
        for lane, value in enumerate((masked, masked * pixel, alive * float(PATCH))):
            stats[...] += jnp.where(row == lane, jnp.sum(value, keepdims=True), 0.0)
    greet_all(times)
    spread_small(times, stats, sall, ss, sr)
    swap = remote(psend, precv, ps, pr, over_x)
    swap.start()
    load_mask(mask, kall)
    units = ((uemb, emb), (upatch, patches), (uclass, classes))

    def unit_along(n, dz):
        src, dst = units[n]
        return remote(
            src, dst.at[g, x], es.at[n, dz - 1], er.at[n, dz - 1], (f, ((g + dz) % count) * 2 + x)
        )

    def loads(layer, part):
        if part < 2:
            return pltpu.make_async_copy(ocol.at[2 * layer + part], wbuf.at[part], wsem.at[layer, part])
        return pltpu.make_async_copy(odown.at[layer], dbuf, wsem.at[layer, part])

    def unit_over(n):
        block = units[n][1].at[:, x]
        return remote(block, block, exs.at[n], exr.at[n], over_x)

    def unit_piece(n, zz):
        block = units[n][1].at[zz, x]
        return remote(block, block, exs.at[n], exr.at[n], over_x)

    def unit_pieces(n):
        for dz in range(1, count):
            unit_along(n, dz).wait_recv()
            unit_piece(n, (g + count - dz) % count).start()

    for n in range(3):
        units[n][1][g, x] = units[n][0][...]
    for n in range(2):
        for dz in range(1, count):
            unit_along(n, dz).start()
        unit_piece(n, g).start()
    begin, advance, arrived, finish = gather_parts(
        count, ucol, udown, ocol, odown, (zs, zr, own, s1, r1, s2, r2, s3, r3), prepare
    )
    started, allowed = set(), {(0, part) for part in range(3)}

    def prefetch():
        for layer, part in sorted(allowed - started):
            first = 2 * (3 * layer + part)
            if arrived(first) and arrived(first + 1):
                loads(layer, part).start()
                started.add((layer, part))

    def at(*point):
        for op in FLOW.get(point, ()):
            (begin if op < 100 else advance)(op % 100)
        prefetch()

    at("begin")
    for n in range(2):
        unit_pieces(n)
    at("units")
    for n in range(2):
        unit_over(n).wait_recv()
    at("arrived")
    swap.wait_recv()
    wait_small(times, sall, ss, sr)
    sums = jnp.sum(sall[...], 0)
    total, squares, live = sums[0:1, 0:1], sums[0:1, 1:2], sums[0:1, 2:3]
    center = total / live
    mel_scale = lax.rsqrt(squares / live - center * center + 1e-05)
    inside = lax.broadcasted_iota(jnp.int32, (SLOTS, PATCH), 0) < GRID

    def normalized(block):
        return jnp.where(inside, (block[...].astype(F32) - center) * mel_scale, 0.0).astype(BF)

    pn[pl.ds(pl.multiple_of(x * SLOTS, SLOTS), SLOTS)] = normalized(pkeep)
    pn[pl.ds(pl.multiple_of((1 - x) * SLOTS, SLOTS), SLOTS)] = normalized(precv)
    vec[...] = emb[...].reshape(D, EWIDE).astype(F32).T
    patch = patches[...].reshape(D, PATCH)
    bias = vec[EVEC + GLOB : EVEC + GLOB + 1, :]
    spot = lax.broadcasted_iota(jnp.int32, (TOK, D), 0)
    grid_row = jnp.logical_or(spot < GRID, jnp.logical_and(spot >= SLOTS, spot < SLOTS + GRID))
    xs[0] = (nt(pn[...], patch) + vec[:TOK]) + jnp.where(grid_row, bias, 0.0)

    copies = [
        pltpu.make_async_copy(vec, vec_out, osem.at[1]),
        pltpu.make_async_copy(pn, pn_out, osem.at[2]),
    ]
    for copy in copies:
        copy.start()
    sems = ((qs0, qr0, os0, or0), (qs1, qr1, os1, or1))
    at("x0")

    @pl.when(f == 0)
    def _():
        for dz in range(1, count):
            unit_along(2, dz).start()

    def classes_over():
        @pl.when(f == 0)
        def _():
            for dz in range(1, count):
                unit_along(2, dz).wait_recv()
            unit_over(2).start()

    def during(layer, point):
        at(layer, point)
        if (layer, point) == (L - 1, "head23"):
            classes_over()
        if point == "up3":
            more = [
                pltpu.make_async_copy(src.at[layer], dst.at[layer], osem.at[3 + 4 * layer + n])
                for n, (src, dst) in enumerate(((fa, fa_out), (gp, gp_out), (qk, qk_out)))
            ]
            span = pl.ds(2 * layer + (1 if layer else 0), 1 if layer else 2)
            more.append(pltpu.make_async_copy(xs.at[span], xs_out.at[span], osem.at[6 if layer == 0 else 12]))
            for copy in more:
                copy.start()
            copies.extend(more)

    for layer in range(L):

        def fetch(part):
            if part == 1 and layer + 1 < L:
                allowed.add((layer + 1, 0))
            at("fetch", layer, part)
            loads(layer, part).wait()

        layer_body(
            layer, xs.at[2 * layer], vec,
            (xs.at[2 * layer + 2], xs.at[2 * layer + 1], fa.at[layer], gp.at[layer], qk.at[layer]),
            (wbuf, dbuf, qsend, osend, kall, vall, acc), orecv.at[layer], sems[layer], fetch,
            functools.partial(during, layer),
        )
        copies.append(pltpu.make_async_copy(xs.at[2 * layer + 2], xs_out.at[2 * layer + 2], osem.at[10 + layer]))
        copies[-1].start()
        allowed.update((layer + 1, part) for part in (1, 2) if layer + 1 < L)

    @pl.when(f == 0)
    def _():
        unit_over(2).wait_recv()

    @pl.when(f != 0)
    def _():
        classes[...] = jnp.zeros_like(classes)

    loss_part(
        f == 0, g * 2 + x, xs.at[2 * L], vec, classes, labels, clip_weights, class_bias, dout, head, end_rows, small
    )
    copies.append(pltpu.make_async_copy(dout, dout_out, osem.at[0]))
    copies[-1].start()
    finish()
    for n in range(2):
        for dz in range(1, count):
            unit_along(n, dz).wait_send()
        unit_over(n).wait_send()

    @pl.when(f == 0)
    def _():
        for dz in range(1, count):
            unit_along(2, dz).wait_send()
        unit_over(2).wait_send()

    swap.wait_send()
    for copy in copies:
        copy.wait()


def forward_all(times, wide, down, uemb, upatch, uclass, live, pkeep, psend, labels, clip_weights, class_bias, mask):
    count = times // 2
    total = len(SUBS)
    dma = pltpu.SemaphoreType.DMA
    outs = (
        ((2 * L, 2, 2, count, 2, 96, D), BF),
        ((L, count, 2, 2, 192, D), BF),
        ((EWIDE, D), F32),
        ((2 * L + 1, TOK, D), F32),
        ((L, 7, TOK, D), BF),
        ((L, FF // D, TOK, D), F32),
        ((L, PER, NF, QROWS, 128), BF),
        ((TOK, PATCH), BF),
        ((TOK, D), F32),
        ((2, 16, D), BF),
        ((2, D), F32),
        ((8, 128), F32),
    )
    return pl.pallas_call(
        functools.partial(forward_all_kernel, times),
        out_shape=tuple(jax.ShapeDtypeStruct(*o) for o in outs),
        in_specs=[aspec()] * 2 + [vspec()] * 9 + [aspec()],
        out_specs=(aspec(),) * (len(outs) - 3) + (vspec(),) * 3,
        scratch_shapes=FORWARD_SCRATCH
        + [
            VM((L, PER, NF, TOK // 2, 128), BF),
            VM((NF * times, 8, 128), F32),
            VM((SLOTS, PATCH), BF),
            VM((count, 2, 96, EWIDE), BF),
            VM((count, 2, 96, PATCH), BF),
            VM((count, 2, 96, CMAIN), BF),
            VM((EWIDE, D), F32),
            VM((2 * L + 1, TOK, D), F32),
            VM((L, 7, TOK, D), BF),
            VM((L, FF // D, TOK, D), F32),
            VM((L, PER, NF, QROWS, 128), BF),
            VM((TOK, PATCH), BF),
            dma((total, count - 1)), dma((total, count - 1)), dma((total,)),
            dma((total,)), dma((total,)), dma((total,)), dma((total,)), dma((total,)), dma((total,)),
            dma((3, count - 1)), dma((3, count - 1)), dma((3,)), dma((3,)),
            dma, dma, dma, dma, dma((L, 3)), dma((13,)),
        ]
        + exchange_sems() * L
        + [
            VM((2 * L, 2, 2, 96, D), BF),
            VM((L, 2, 192, D), BF),
            VM((2 * L, 96, 4 * D), F32),
            VM((L, 4 * 96, D), F32),
            VM((8, 128), F32),
            VM((TOK, D), F32),
            dma((len(GROUPS),)),
        ],
        compiler_params=pltpu.CompilerParams(
            collective_id=1, has_side_effects=True, vmem_limit_bytes=VLIM
        ),
        name="forward_all",
    )(wide, down, uemb, upatch, uclass, live, pkeep, psend, labels, clip_weights, class_bias, mask)


BACKWARD_SCRATCH = [
    VM((PER, NF, TOK // 2, 128), BF),
    VM((PER, NF, TOK // 2, 128), BF),
    VM((PER, NF, QROWS, 128), BF),
    VM((PER, NF, QROWS, 128), BF),
    VM((NF * TOK, 128), BF),
    VM((NF * TOK, HDIM), BF),
    VM((NF * TOK, HDIM), F32),
    VM((NF * TOK, HDIM), F32),
    VM((NF, TOK, HDIM), BF),
    VM((TOK, D), F32),
]


def backward_body(layer, dcur, er, ba, vec_ref, qk_ref, mats, slope, kept, scratch, sems, at):
    down, up, qkvo = mats
    dsend, drecv, gsend, grecv, kall, vall, dkall, dvall, dqall, acc = scratch
    ds_, dr_, gs_, gr_ = sems
    f, t = lax.axis_index("freq"), lax.axis_index("tm")

    def row(i):
        return vec_ref[EVEC + layer * 8 + i : EVEC + layer * 8 + i + 1, :]

    def note(i, value):
        er[EVEC + i : EVEC + i + 1, :] = jnp.sum(value, 0, keepdims=True)

    ba[8] = dcur[...].astype(BF)
    note(layer * 8 + 7, dcur[...])
    for k in range(FF // D):
        dbefore = nt(ba[8], down(k)) * slope(k)
        note(L * 8 + layer * 4 + k, dbefore)
        ba[4 + k] = dbefore.astype(BF)
        product = nt(ba[4 + k], up(k))
        acc[...] = product if k == 0 else acc[...] + product
        at("mlp%d" % k)
    normed, scale = norm_rows(kept(1))
    dact = acc[...]
    note(layer * 8 + 2, dact * normed)
    note(layer * 8 + 3, dact)
    dcur[...] += norm_back(dact * row(2), normed, scale)
    note(layer * 8 + 6, dcur[...])
    ba[3] = dcur[...].astype(BF)
    at("resid")
    dmixed = nt(ba[3], qkvo(3)).astype(BF)

    def to_clip(j, i):
        other = (f + i) % NF
        return remote(
            dsend.at[j, other], drecv.at[j, f], ds_.at[j, i - 1], dr_.at[j, i - 1], (other, t)
        )

    def back_clip(j, i):
        other = (f + i) % NF
        return remote(
            gsend.at[j, other], grecv.at[j, f], gs_.at[j, i - 1], gr_.at[j, i - 1], (other, t)
        )

    for j in range(PER):
        for h in range(NF):
            lo = 256 * j + HDIM * h
            dsend[j, h] = pack_half(dmixed[:, lo : lo + HDIM])
        for i in range(1, NF):
            to_clip(j, i).start()
        drecv[j, f] = dsend[j, f]
    at("sent")
    root = HDIM ** (-0.5)
    for j in range(PER):
        for s in range(NF):
            kall[s * TOK : (s + 1) * TOK, :HDIM] = qk_ref[j, s, :TOK, HDIM:]
            vall[s * TOK : (s + 1) * TOK] = open_half(qk_ref[j, s, TOK:])
        dkall[...] = jnp.zeros_like(dkall)
        dvall[...] = jnp.zeros_like(dvall)
        for i in range(1, NF):
            to_clip(j, i).wait_recv()

        def attend(s):
            q = with_mask(qk_ref[j, s, :TOK])
            dmix = open_half(drecv[j, s])
            scores = nt(kall[...], q)
            top = jnp.max(scores, 0, keepdims=True)
            expo = jnp.exp(scores - top)
            probs = expo * (1.0 / jnp.sum(expo, 0, keepdims=True))
            dprob = nt(vall[...], dmix)
            inner = jnp.sum(probs * dprob, 0, keepdims=True)
            dscore = (probs * (dprob - inner)).astype(BF)
            dvall[...] += nn(probs.astype(BF), dmix)
            dkall[...] += nn(dscore, q[:, :HDIM])
            dqall[s] = (tn(dscore, kall[:, :HDIM]) * root).astype(BF)

        for s in range(NF):
            attend(s)
            if s < NF - 1:
                at("head%d%d" % (j, s))
        for s in range(NF):
            span = slice(s * TOK, (s + 1) * TOK)
            gsend[j, s, :TOK] = jnp.concatenate([dqall[s], dkall[span].astype(BF)], 1)
            gsend[j, s, TOK:] = pack_half(dvall[span].astype(BF))
        for i in range(1, NF):
            back_clip(j, i).start()
        grecv[j, f] = gsend[j, f]
        at("head%d%d" % (j, NF - 1))
    for j in range(PER):
        for i in range(1, NF):
            back_clip(j, i).wait_recv()
        cols = slice(256 * j, 256 * (j + 1))
        ba[0, :, cols] = jnp.concatenate([grecv[j, h, :TOK, :HDIM] for h in range(NF)], 1)
        ba[1, :, cols] = jnp.concatenate([grecv[j, h, :TOK, HDIM:] for h in range(NF)], 1)
        ba[2, :, cols] = jnp.concatenate([open_half(grecv[j, h, TOK:]) for h in range(NF)], 1)
    at("heads")
    note(layer * 8 + 4, ba[0].astype(F32))
    note(layer * 8 + 5, ba[2].astype(F32))
    dact = nt(ba[0], qkvo(0)) + nt(ba[1], qkvo(1)) + nt(ba[2], qkvo(2))
    normed, scale = norm_rows(kept(0))
    note(layer * 8 + 0, dact * normed)
    note(layer * 8 + 1, dact)
    dcur[...] += norm_back(dact * row(0), normed, scale)
    for j in range(PER):
        for i in range(1, NF):
            to_clip(j, i).wait_send()
            back_clip(j, i).wait_send()
    at("done")


def backward_kernel(
    layer, dout_ref, x_ref, x1_ref, gp_ref, qk_ref, vec_ref, mask, wcol, wdown,
    dx_ref, ba_ref, er_ref, wbuf, dbuf, wsem, ds_, dr_, gs_, gr_, *scratch,
):
    loads = [
        pltpu.make_async_copy(wdown.at[layer], dbuf, wsem.at[0]),
        pltpu.make_async_copy(wcol.at[2 * layer + 1], wbuf.at[1], wsem.at[1]),
        pltpu.make_async_copy(wcol.at[2 * layer], wbuf.at[0], wsem.at[2]),
    ]
    for load in loads:
        load.start()
    dx_ref[...] = dout_ref[...]
    er_ref[...] = jnp.zeros_like(er_ref)
    load_mask(mask, scratch[4])
    greet_clip()
    for load in loads:
        load.wait()
    backward_body(
        layer, dx_ref, er_ref, ba_ref, vec_ref, qk_ref,
        (lambda k: dbuf[k], lambda k: wbuf[1, k], lambda k: wbuf[0, k]),
        lambda k: gp_ref[k], lambda i: x1_ref[...] if i else x_ref[...],
        scratch, (ds_, dr_, gs_, gr_), lambda point: None,
    )


def backward_layer(layer, dout, x, x1, gp, qk, vec, mask, wcol, wdown):
    return pl.pallas_call(
        functools.partial(backward_kernel, layer),
        out_shape=(
            jax.ShapeDtypeStruct((TOK, D), F32),
            jax.ShapeDtypeStruct((9, TOK, D), BF),
            jax.ShapeDtypeStruct((EWIDE, D), F32),
        ),
        in_specs=[vspec()] * 6 + [aspec()] * 3,
        out_specs=(vspec(),) * 3,
        scratch_shapes=[VM((2, 4, D, D), BF), VM((4, D, D), BF), pltpu.SemaphoreType.DMA((3,))]
        + exchange_sems()
        + BACKWARD_SCRATCH,
        compiler_params=pltpu.CompilerParams(
            collective_id=2 + L + layer, has_side_effects=True, vmem_limit_bytes=VLIM
        ),
        name="backward_layer",
    )(dout, x, x1, gp, qk, vec, mask, wcol, wdown)


RGROUPS = (("d", 1), ("u", 1), ("q", 1), ("d", 0), ("u", 0), ("q", 0))
ROUTES = ("zz", "xz", "zy", "yz", "xz", "yy")
ORDER = {
    (1, "mlp1"): (0,),
    (1, "mlp3"): (200,),
    (1, "head00"): (1,),
    (1, "head01"): (200, 100,),
    (1, "head03"): (200,),
    (1, "head10"): (10, 200,),
    (1, "head13"): (101,),
    (1, "head20"): (100,),
    (1, "head22"): (11,),
    (1, "head23"): (100,),
    (1, "heads"): (100, 101, 110,),
    (1, "done"): (100, 101, 20, 111, 21,),
    (0, "mlp0"): (110,),
    (0, "mlp1"): (101,),
    (0, "mlp2"): (101,),
    (0, "sent"): (111,),
    (0, "head00"): (110, 120, 121, 30, 111, 31, 110,),
    (0, "head02"): (110,),
    (0, "head03"): (121,),
    (0, "head12"): (120,),
    (0, "head13"): (130,),
    (0, "head20"): (111,),
    (0, "head21"): (121, 131, 111,),
    (0, "head23"): (120, 40, 130,),
    (0, "heads"): (120, 121, 131, 41, 140, 120,),
    (0, "done"): (121, 130, 131, 50,),
    "end": (140, 130, 131, 130, 131, 141, 51, 140, 150, 210, 141, 150, 151, 140, 210, 141, 140, 210, 151, 141, 150, 210, 141, 150, 150, 151, 151, 151,),
}
SLOTS_R = 2
BUFS = 1
PWIDE = (CMAIN, EWIDE + PATCH)
STAGES = 5


def backward_all_kernel(
    times, dout_in, xs_in, gp_in, qk_in, fa_in, vec_ref, mask, pn_ref, head_ref, end_ref, small, wcol, wdown,
    gcol, gdown, gpart, scalars, rfa,
    *refs,
):
    (
        wbuf, gp, xb, dcur, er, qk, ba, lbuf, rd, ru, rq, full, low, recv1, mid_own, mid_low, recv2,
        zlow, zown, zrecv, psend, pown, pxr0, pxr1, pzr0, pzr1, sq,
        wsem, gsem, xsem, qsem, ls, fas, far, bs, br, s1, r1, s2, r2, zs, zr, fs, fr, ks, kr,
        ss, sr, qs, qr, p1, p1r, p2, p2r, p3, p3r, p4, p4r, credit,
        ds_, dr_, gs_, gr_, small_all, square_all,
    ) = refs[: -len(BACKWARD_SCRATCH)]
    scratch = refs[-len(BACKWARD_SCRATCH) :]
    f, t, y, c, g, x = place()
    count = times // 2
    over_x = (f, g * 2 + 1 - x)
    over_y = ((1 - y) * 2 + c, t)
    over_c = (y * 2 + 1 - c, t)
    total = len(RGROUPS)
    other_core = 1 - c

    def half_cols(core):
        return pl.ds(pl.multiple_of(core * 384, 128), 384)

    def weight(layer, which):
        src = (wdown.at[layer], wcol.at[2 * layer + 1], wcol.at[2 * layer])[which]
        return pltpu.make_async_copy(src, wbuf.at[weight_slot(layer, which)], wsem.at[layer, which])

    def weight_slot(layer, which):
        return (which % 2 + (L - 1 - layer)) % 2

    def slope_load(layer, k):
        return pltpu.make_async_copy(gp_in.at[layer, k], gp.at[k % 2], gsem.at[layer, k])

    def kept_load(layer, i):
        return pltpu.make_async_copy(xs_in.at[2 * layer + i], xb, xsem.at[layer, i])

    def heads_load(layer):
        return pltpu.make_async_copy(qk_in.at[layer], qk, qsem.at[layer])

    first_load = pltpu.make_async_copy(dout_in, dcur, qsem.at[L])
    first_load.start()
    for which in range(2):
        weight(L - 1, which).start()
    for k in range(2):
        slope_load(L - 1, k).start()
    kept_load(L - 1, 1).start()
    heads_load(L - 1).start()
    greet_all(times)
    spread_small(times, small, small_all, ss, sr)

    def forward_swap(layer, n):
        span = pl.ds(3, 4) if n == 0 else pl.ds(0, 3)
        return remote(
            fa_in.at[layer, span], rfa.at[layer, span], fas.at[layer, n], far.at[layer, n], over_c
        )

    for layer in reversed(range(L)):
        for n in range(2):
            forward_swap(layer, n).start()

    def swap(gi, n):
        kind, l = RGROUPS[gi]
        if kind == "d":
            src, dst = ba.at[8, :, half_cols(other_core)], rd.at[l]
        elif kind == "u":
            src, dst = ba.at[4 + 2 * n + other_core], ru.at[l, n]
        else:
            src, dst = ba.at[2 * n + other_core], rq.at[l, n]
        return remote(src, dst, bs.at[gi, n], br.at[gi, n], over_c)

    def swaps(gi):
        return range(1 if RGROUPS[gi][0] == "d" else 2)

    def left_loads(gi):
        kind, l = RGROUPS[gi]
        out = []
        blocks = {"d": (3, 4, 5, 6), "u": (2,), "q": (0, c)}[kind]
        for n, block in enumerate(blocks):
            for m, src in enumerate((fa_in, rfa)):
                out.append(
                    pltpu.make_async_copy(
                        src.at[l, block], lbuf.at[n, pl.ds(m * TOK, TOK)], ls.at[n, m]
                    )
                )
        return out

    def product(left, own, other, cols):
        return tn(lbuf[left, :TOK], own(cols)) + tn(lbuf[left, TOK:], other(cols))

    def store(gi, h, role, xx, where, value):
        if ROUTES[gi][h] == "y":
            keep, index = role == 0, xx
        else:
            keep, index = x == xx, role

        def save_full():
            full[(gi % BUFS, h, index) + where] = value

        def save_low():
            low[(gi % BUFS, h, index) + where] = value.astype(BF)

        if isinstance(keep, bool):
            (save_full if keep else save_low)()
        else:
            pl.when(keep)(save_full)
            pl.when(jnp.logical_not(keep))(save_low)

    def compute(gi, h):
        kind, l = RGROUPS[gi]
        if kind == "d":

            def one(z, carry):
                prod = product(
                    z, lambda _: ba[8, :, half_cols(c)], lambda _: rd[l], None
                ).reshape(2, 2, 2, 96, 384)
                for xx in range(2):
                    for yy in range(2):
                        for hh in range(2):
                            store(gi, hh, (yy + y) % 2, xx, (z,), prod[xx, yy, hh])
                return carry

            if h == 0:
                lax.fori_loop(0, count, one, 0)
            return
        recv = ru if kind == "u" else rq
        base = 4 if kind == "u" else 0
        for role in range(2):
            yy = y if role == 0 else 1 - y
            left = 0 if kind == "u" else yy
            prod = product(
                left, lambda cols: ba[base + 2 * yy + c, :, cols], lambda cols: recv[l, yy, :, cols],
                slice(h * 384, (h + 1) * 384),
            ).reshape(count, 2, 96, 384)
            for xx in range(2):
                store(gi, h, role, xx, (), prod[:, xx])

    def step1(gi, h):
        return remote(
            low.at[gi % BUFS, h], recv1.at[gi % SLOTS_R, h], s1.at[gi, h], r1.at[gi, h],
            over_y if ROUTES[gi][h] == "y" else over_x,
        )

    def step2(gi, h):
        if ROUTES[gi][h] == "z":
            src, dst = zlow.at[h, 0], recv2.at[gi % SLOTS_R, h, count - 1]
        else:
            src, dst = mid_low.at[h], recv2.at[gi % SLOTS_R, h]
        return remote(
            src, dst, s2.at[gi, h], r2.at[gi, h], over_x if ROUTES[gi][h] == "y" else over_y
        )

    def along(gi, h, dz, role=0):
        to = (g + dz) % count
        slot = gi % SLOTS_R
        if ROUTES[gi][h] != "z":
            src, dst = zlow.at[h, to], zrecv.at[slot, h, dz - 1]
        elif role == 0:
            src, dst = mid_low.at[h, to], zrecv.at[slot, h, dz - 1]
        else:
            src, dst = zlow.at[h, to], recv2.at[slot, h, dz - 1]
        return remote(src, dst, zs.at[gi, h, role, dz - 1], zr.at[gi, h, role, dz - 1], (f, to * 2 + x))

    def result(gi, h, yy):
        kind, l = RGROUPS[gi]
        if kind == "d":
            return gdown.at[l, yy, pl.ds(h * 96, 96), half_cols(c)]
        return gcol.at[2 * l + (1 if kind == "u" else 0), yy, c, :, pl.ds(h * 384, 384)]

    def spread_y(gi, h):
        block = result(gi, h, y)
        return remote(block, block, fs.at[gi, h], fr.at[gi, h], over_y)

    def spread_c(gi, h):
        block = result(gi, h, slice(None))
        return remote(block, block, ks.at[gi, h], kr.at[gi, h], over_c)

    def wait_along(gi, h):
        for role in range(2 if ROUTES[gi][h] == "z" else 1):
            for dz in range(1, count):
                along(gi, h, dz, role).wait_recv()
                along(gi, h, dz, role).wait_send()

    def start_along(gi, h):
        for dz in range(1, count):
            if gi >= SLOTS_R:
                pl.semaphore_wait(credit.at[1 + dz], 1)
            for role in range(2 if ROUTES[gi][h] == "z" else 1):
                along(gi, h, dz, role).start()

    def advance(gi, h, stage):
        slot, buf = gi % SLOTS_R, gi % BUFS
        twice = ROUTES[gi][h] == "z"
        if stage == 1:
            step1(gi, h).wait_recv()
            step1(gi, h).wait_send()
            if twice:
                summed = full[buf, h, 0] + recv1[slot, h, 0].astype(F32)
                mid_low[h] = summed.astype(BF)
                mid_own[h] = summed
                summed = full[buf, h, 1] + recv1[slot, h, 1].astype(F32)
                zlow[h] = summed.astype(BF)
                start_along(gi, h)
                full[buf, h, 1] = summed
                zown[h] = full[buf, h, 1, g]
                return
            keep, send = (x, 1 - x) if ROUTES[gi][h] == "y" else (0, 1)
            mid_low[h] = (full[buf, h, send] + recv1[slot, h, send].astype(F32)).astype(BF)
            step2(gi, h).start()
            mid_own[h] = full[buf, h, keep] + recv1[slot, h, keep].astype(F32)
        elif stage == 2:
            if twice:
                wait_along(gi, h)
                value = zown[h]
                for dz in range(1, count):
                    value = value + recv2[slot, h, dz - 1].astype(F32)
                zlow[h, 0] = value.astype(BF)
                step2(gi, h).start()
                value = mid_own[h, g]
                for dz in range(1, count):
                    value = value + zrecv[slot, h, dz - 1].astype(F32)
                zown[h] = value
                return
            step2(gi, h).wait_recv()
            step2(gi, h).wait_send()
            summed = mid_own[h] + recv2[slot, h].astype(F32)
            zlow[h] = summed.astype(BF)
            start_along(gi, h)
            mid_own[h] = summed
            zown[h] = mid_own[h, g]
        elif stage == 3:
            value = zown[h]
            if twice:
                step2(gi, h).wait_recv()
                step2(gi, h).wait_send()
                value = value + recv2[slot, h, count - 1].astype(F32)
            else:
                wait_along(gi, h)
                for dz in range(1, count):
                    value = value + zrecv[slot, h, dz - 1].astype(F32)
            sq[...] += jnp.sum((value * value).reshape(12, 8, 3, 128), (0, 2))
            kind, l = RGROUPS[gi]
            if kind == "d":
                gdown[l, y, h * 96 : (h + 1) * 96, half_cols(c)] = value.astype(BF)
            else:
                idx = 2 * l + (1 if kind == "u" else 0)
                gcol[idx, y, c, :, h * 384 : (h + 1) * 384] = value.astype(BF)
            spread_y(gi, h).start()
            if gi + SLOTS_R < total:
                pl.semaphore_signal(credit.at[0], inc=1, device_id=over_x, device_id_type=MESH)
                pl.semaphore_signal(credit.at[1], inc=1, device_id=over_y, device_id_type=MESH)
                for dz in range(1, count):
                    back = (f, ((g + count - dz) % count) * 2 + x)
                    pl.semaphore_signal(
                        credit.at[1 + dz], inc=1, device_id=back, device_id_type=MESH
                    )
        elif stage == 4:
            spread_y(gi, h).wait_recv()
            spread_c(gi, h).start()
        else:
            spread_c(gi, h).wait_recv()

    pxrs, pzrs = (pxr0, pxr1), (pzr0, pzr1)
    psends = [psend.at[:, :, pl.ds(0, w)] for w in PWIDE]
    powns = [pown.at[:, :, pl.ds(0, w)] for w in PWIDE]

    def part_over(n):
        return remote(psends[n], pxrs[n], p1.at[n], p1r.at[n], over_x)

    def part_along(n, dz):
        return remote(
            psends[n].at[(g + dz) % count], pzrs[n].at[dz - 1], p2.at[n, dz - 1], p2r.at[n, dz - 1],
            (f, ((g + dz) % count) * 2 + x),
        )

    def part_y(n):
        block = gpart.at[n, y, c]
        return remote(block, block, p3.at[n], p3r.at[n], over_y)

    def part_c(n):
        block = gpart.at[n, :, c]
        return remote(block, block, p4.at[n], p4r.at[n], over_c)

    def part_compute(n):
        pieces = []
        if n == 0:
            pieces.append((0, tn(head_ref[0], head_ref[1, :, :CMAIN])))
        else:
            pieces.append((0, er[...].T))
            pieces.append((EWIDE, tn(dcur[...].astype(BF), pn_ref[...])))
        for lo, piece in pieces:
            piece = piece.reshape(count, 2, 96, -1)
            span = slice(lo, lo + piece.shape[-1])
            for xx in range(2):

                @pl.when(x == xx)
                def _():
                    powns[n][:, :, span] = piece[:, xx]
                    psends[n][:, :, span] = piece[:, 1 - xx].astype(BF)

        part_over(n).start()

    def part_advance(n, stage):
        if stage == 1:
            part_over(n).wait_recv()
            summed = powns[n][...] + pxrs[n][...].astype(F32)
            powns[n][...] = summed
            part_over(n).wait_send()
            psends[n][...] = summed.astype(BF)
            for dz in range(1, count):
                part_along(n, dz).start()
        elif stage == 2:
            value = powns[n][g]
            for dz in range(1, count):
                part_along(n, dz).wait_recv()
                part_along(n, dz).wait_send()
                value = value + pzrs[n][dz - 1].astype(F32)
            gpart[n, y, c, :, : PWIDE[n]] = value.astype(BF)
            part_y(n).start()
            if n == 1:
                lane = lax.broadcasted_iota(jnp.int32, (96, EWIDE), 1)
                inside = jnp.logical_and(lane % SLOTS < GRID, lane < TOK)
                own = jnp.where(inside, value[:, :EWIDE], 0.0)
                sq[...] += jnp.sum((own * own).reshape(12, 8, 3, 128), (0, 2))
        elif stage == 3:
            part_y(n).wait_recv()
            part_c(n).start()
        else:
            part_c(n).wait_recv()
            value = gpart[n, 0, 0].astype(F32) + gpart[n, 0, 1].astype(F32)
            value = value + gpart[n, 1, 0].astype(F32) + gpart[n, 1, 1].astype(F32)
            value = value[:, : PWIDE[n]]
            if n == 1:
                lane = lax.broadcasted_iota(jnp.int32, value.shape, 1)
                value = jnp.where(lane >= EVEC, value, 0.0)
            value = jnp.where(f == 0, value * value, 0.0)
            sq[...] += jnp.sum(value.reshape(12, 8, PWIDE[n] // 128, 128), (0, 2))

    stages = {}

    def launch(gi, h):
        if h == 0:
            for n in swaps(gi):
                swap(gi, n).wait_recv()
            for copy in left_loads(gi):
                copy.wait()
        compute(gi, h)
        if gi >= SLOTS_R:
            pl.semaphore_wait(credit.at[0], 1)
            pl.semaphore_wait(credit.at[1], 1)
        step1(gi, h).start()
        stages[gi, h] = 0
        if h == 1:
            for n in swaps(gi):
                swap(gi, n).wait_send()
            if gi + 1 < total:
                prepare(gi + 1)

    def perform(op):
        what, gi, h = op // 100, op // 10 % 10, op % 10
        if what == 0:
            launch(gi, h)
            return
        stages[gi, h if what == 1 else 2] += 1
        if what == 1:
            advance(gi, h, stages[gi, h])
        else:
            part_advance(gi, stages[gi, 2])

    waited = set()

    def prepare(gi):
        kind, l = RGROUPS[gi]
        for n in ((0,) if kind == "d" else (1,)):
            if (l, n) not in waited:
                waited.add((l, n))
                forward_swap(l, n).wait_recv()
        for copy in left_loads(gi):
            copy.start()

    def launch_part(n):
        part_compute(n)
        stages[n, 2] = 0

    load_mask(mask, scratch[4])
    sq[...] = jnp.zeros_like(sq)
    er[...] = jnp.zeros_like(er)
    er[EVEC + GLOB + 3 : EVEC + GLOB + 5, :] = end_ref[...]
    er[ECLS:, :] = tn(head_ref[1, :, CMAIN : CMAIN + EWIDE - ECLS], head_ref[0])
    launch_part(0)
    prepare(0)
    first_load.wait()
    loaded = set()

    for layer in reversed(range(L)):
        base = 3 * (L - 1 - layer)

        def mat(which):
            def read(k):
                if (layer, which) not in loaded:
                    loaded.add((layer, which))
                    weight(layer, which).wait()
                return wbuf[weight_slot(layer, which), k]

            return read

        def slope(k):
            slope_load(layer, k).wait()
            return gp[k % 2]

        def kept(i):
            kept_load(layer, i).wait()
            return xb[...]

        def at(point):
            if point.startswith("mlp"):
                k = int(point[3:])
                if k + 2 < FF // D:
                    slope_load(layer, k + 2).start()
                elif layer > 0:
                    slope_load(layer - 1, k - 2).start()
                if k == 0:
                    swap(base, 0).start()
                if k == 3:
                    for n in swaps(base + 1):
                        swap(base + 1, n).start()
                    weight(layer, 2).start()
                    if layer > 0:
                        weight(layer - 1, 0).start()
            elif point == "resid":
                kept_load(layer, 0).start()
                if layer == L - 1:
                    heads_load(layer).wait()
            elif point == "sent":
                if layer < L - 1:
                    heads_load(layer).wait()
            elif point == "head%d%d" % (PER - 1, NF - 1):
                if layer > 0:
                    heads_load(layer - 1).start()
            elif point == "heads":
                for n in swaps(base + 2):
                    swap(base + 2, n).start()
            elif point == "done":
                if layer > 0:
                    weight(layer - 1, 1).start()
                    kept_load(layer - 1, 1).start()
            for op in ORDER.get((layer, point), ()):
                perform(op)

        backward_body(
            layer, dcur, er, ba, vec_ref, qk, (mat(0), mat(1), mat(2)), slope, kept, scratch,
            (ds_.at[layer], dr_.at[layer], gs_.at[layer], gr_.at[layer]), at,
        )
    dgrid = dcur[...]
    spot = lax.broadcasted_iota(jnp.int32, (TOK, D), 0)
    er[:TOK, :] = dgrid
    inside = jnp.where(spot % SLOTS < GRID, dgrid, 0.0)
    er[EVEC + GLOB : EVEC + GLOB + 1, :] = jnp.sum(inside, 0, keepdims=True)
    er[EVEC + GLOB + 1 : EVEC + GLOB + 3, :] = dgrid[GRID : GRID + 2, :]
    launch_part(1)
    shared = False
    for op in ORDER["end"]:
        perform(op)
        summed = all(stages.get((gi, h), 0) >= 3 for gi in range(total) for h in range(2))
        if not shared and summed and stages[0, 2] == stages[1, 2] == STAGES - 1:
            shared = True
            n = NF * times
            me = f * times + t

            def send(i, carry):
                other = (me + i) % n
                remote(sq, square_all.at[me], qs, qr, (other // times, other % times)).start()
                return carry

            lax.fori_loop(1, n, send, 0)
            square_all[me] = sq[...]
    if not shared or any(stages[gi, h] < STAGES for gi in range(total) for h in range(2)):
        raise ValueError("incomplete order")
    for layer in range(L):
        for n in range(2):
            forward_swap(layer, n).wait_send()
    for gi in range(total):
        for h in range(2):
            spread_y(gi, h).wait_send()
            spread_c(gi, h).wait_send()
    for n in range(2):
        part_y(n).wait_send()
        part_c(n).wait_send()
    wait_small(times, small_all, ss, sr)
    wait_small(times, square_all, qs, qr)
    summed = jnp.sum(small_all[...], 0)
    spot = lax.broadcasted_iota(jnp.int32, (8, 128), 0) * 128 + lax.broadcasted_iota(jnp.int32, (8, 128), 1)
    bias = jnp.where(spot < CLASSES, summed, 0.0)
    norm = jnp.sqrt(jnp.sum(jnp.sum(square_all[...], 0) + bias * bias, keepdims=True))
    scalars[0] = summed
    scalars[1] = jnp.broadcast_to(norm, (8, 128))
    scalars[2] = jnp.broadcast_to(jnp.minimum(1.0, 1.0 / (norm + 1e-06)), (8, 128))


def backward_all(times, dout, xs, gp, qk, fa, vec, mask, pnorm, head, end_rows, small, wcol, wdown):
    count = times // 2
    n = NF * times
    total = len(RGROUPS)
    dma = pltpu.SemaphoreType.DMA
    most = max(PWIDE)
    return pl.pallas_call(
        functools.partial(backward_all_kernel, times),
        out_shape=(
            jax.ShapeDtypeStruct((2 * L, 2, 2, 96, D), BF),
            jax.ShapeDtypeStruct((L, 2, 192, D), BF),
            jax.ShapeDtypeStruct((2, 2, 2, 96, most), BF),
            jax.ShapeDtypeStruct((3, 8, 128), F32),
            jax.ShapeDtypeStruct(fa.shape, BF),
        ),
        in_specs=[aspec()] * 5 + [vspec()] + [aspec()] + [vspec()] * 4 + [aspec()] * 2,
        out_specs=(vspec(),) * 4 + (aspec(),),
        scratch_shapes=[
            VM((2, 4, D, D), BF),
            VM((2, TOK, D), F32),
            VM((TOK, D), F32),
            VM((TOK, D), F32),
            VM((EWIDE, D), F32),
            VM((PER, NF, QROWS, 128), BF),
            VM((9, TOK, D), BF),
            VM((4, 2 * TOK, D), BF),
            VM((L, TOK, 384), BF),
            VM((L, 2, TOK, D), BF),
            VM((L, 2, TOK, D), BF),
            VM((BUFS, 2, 2, count, 96, 384), F32),
            VM((BUFS, 2, 2, count, 96, 384), BF),
            VM((SLOTS_R, 2, 2, count, 96, 384), BF),
            VM((2, count, 96, 384), F32),
            VM((2, count, 96, 384), BF),
            VM((SLOTS_R, 2, count, 96, 384), BF),
            VM((2, count, 96, 384), BF),
            VM((2, 96, 384), F32),
            VM((SLOTS_R, 2, count - 1, 96, 384), BF),
            VM((count, 96, most), BF),
            VM((count, 96, most), F32),
            *[VM((count, 96, w), BF) for w in PWIDE],
            *[VM((count - 1, 96, w), BF) for w in PWIDE],
            VM((8, 128), F32),
            dma((L, 3)), dma((L, 4)), dma((L, 2)), dma((L + 1,)), dma((4, 2)),
            dma((L, 2)), dma((L, 2)), dma((total, 2)), dma((total, 2)),
            dma((total, 2)), dma((total, 2)), dma((total, 2)), dma((total, 2)),
            dma((total, 2, 2, count - 1)), dma((total, 2, 2, count - 1)),
            dma((total, 2)), dma((total, 2)), dma((total, 2)), dma((total, 2)),
            dma, dma, dma, dma,
            dma((2,)), dma((2,)), dma((2, count - 1)), dma((2, count - 1)), dma((2,)), dma((2,)), dma((2,)), dma((2,)),
            pltpu.SemaphoreType.REGULAR((count + 1,)),
            *[dma((L, PER, NF - 1))] * 4,
            VM((n, 8, 128), F32),
            VM((n, 8, 128), F32),
        ]
        + BACKWARD_SCRATCH,
        compiler_params=pltpu.CompilerParams(
            collective_id=2 + 2 * L, has_side_effects=True, vmem_limit_bytes=65400 * 1024
        ),
        name="backward_all",
    )(dout, xs, gp, qk, fa, vec, mask, pnorm, head, end_rows, small, wcol, wdown)[:4]


def adam(weight, first, second, grad):
    first = DECAY_FIRST * first + (1.0 - DECAY_FIRST) * grad
    second = DECAY_SECOND * second + (1.0 - DECAY_SECOND) * grad * grad
    fix_one = 1.0 - DECAY_FIRST**STEP
    fix_two = 1.0 - DECAY_SECOND**STEP
    scaled = jnp.sqrt(second * (1.0 / fix_two)) + EPSILON
    weight = weight * (1.0 - LEARN_RATE * WEIGHT_DECAY) - (LEARN_RATE / fix_one) * first / scaled
    return (weight, first, second)


PIECES = 4
WIDE_STEPS = L * 8 // PIECES
DOWN_STEPS = L * 4 // PIECES


def update_kernel(*refs):
    scalars, gcol, gdown, gpart = refs[:4]
    ins, outs, gemb = refs[4:19], refs[19:38], refs[38]
    step = pl.program_id(0)
    coef = scalars[2, 0:1, 0:1]

    def apply(which, grad, at=...):
        new = adam(*(ins[which + 5 * i][at] for i in range(3)), grad * coef)
        for i in range(3):
            outs[which + 5 * i][at] = new[i]
        if which < 4:
            outs[15 + which][at] = new[0].astype(BF)

    @pl.when(step < WIDE_STEPS)
    def _():
        for p in range(PIECES):
            apply(0, gcol[0, p].astype(F32), (0, slice(None), slice(p * D, (p + 1) * D)))

    @pl.when(step >= WIDE_STEPS)
    def _():
        apply(1, gdown[0].astype(F32), (0,))

    @pl.when(step == 0)
    def _():
        main = sum(gpart[0, i, :, :CMAIN].astype(F32) for i in range(NF))
        rest = sum(gpart[1, i, :, EVEC:].astype(F32) for i in range(NF))
        per = FROWS // NF
        for i in range(NF):
            block = gpart[1, i].astype(F32)
            for h in range(2):
                for r in range(per):
                    to = (i * per + r) * 2 * HALF + h * HALF
                    gemb[:, to : to + HALF] = block[:, h * SLOTS + r * HALF : h * SLOTS + (r + 1) * HALF]
        gemb[:, NGRID:] = rest[:, EWIDE - EVEC :]
        apply(2, gemb[...])
        tail = rest[:, ECLS - EVEC : ECLS - EVEC + CLASSES - CMAIN]
        apply(3, jnp.concatenate([main, tail], 1))
        turned = rest[:, : 128].T
        apply(4, turned[:VROWS])


def update(scalars, gcol, gdown, gpart, params, firsts, seconds):
    shard = gcol.shape[2]
    per_wide, per_down = 8 // PIECES, 4 // PIECES

    def wide(step):
        step = jnp.minimum(step, WIDE_STEPS - 1)
        return (step // per_wide, 0, step % per_wide)

    def wide_grad(step):
        step = jnp.minimum(step, WIDE_STEPS - 1)
        return (step // per_wide, step % per_wide, 0, 0)

    def down(step):
        step = jnp.maximum(step - WIDE_STEPS, 0)
        return (step // per_down, step % per_down, 0)

    params, firsts, seconds = (
        [v[0], v[1], v[2].T, v[3], v[4]] for v in (params, firsts, seconds)
    )
    down_block = pl.BlockSpec((1, PIECES * shard, D), down)

    def whole(v):
        return pl.BlockSpec(v.shape, lambda step: (0,) * len(v.shape))

    specs = [pl.BlockSpec((1, shard, PIECES * D), wide), down_block] + [whole(v) for v in params[2:]]
    shapes = [jax.ShapeDtypeStruct(v.shape, F32) for v in params] * 3
    shapes += [jax.ShapeDtypeStruct(v.shape, BF) for v in params[:4]]
    news = pl.pallas_call(
        update_kernel,
        grid=(WIDE_STEPS + DOWN_STEPS,),
        out_shape=shapes,
        in_specs=[whole(scalars), pl.BlockSpec((1, PIECES, shard, D), wide_grad), down_block, whole(gpart)]
        + specs * 3,
        out_specs=specs * 3 + specs[:4],
        scratch_shapes=[VM((shard, NGRID + PATCH), F32)],
        compiler_params=pltpu.CompilerParams(vmem_limit_bytes=48 * 1024 * 1024),
        name="update",
    )(scalars, gcol, gdown, gpart, *params, *firsts, *seconds)
    return [v.T if i % 5 == 2 else v for i, v in enumerate(news)]


def pad_to(v, axis, size):
    pads = [(0, 0)] * v.ndim
    pads[axis] = (0, size - v.shape[axis])
    return jnp.pad(v, pads)


def embed_units(embedding, classifier, vectors, f):
    width = embedding.shape[1]
    blocks = embedding[:NGRID].reshape(NF, FROWS // NF, 2, HALF, width)
    block = lax.dynamic_index_in_dim(blocks, f, 0, keepdims=False).transpose(1, 0, 2, 3)
    block = block.reshape(2, GRID, width)
    tokens = jnp.where(f == 0, vectors[GLOB + 1 : GLOB + 3], 0.0)
    tokens = jnp.stack([tokens, jnp.zeros_like(tokens)])
    block = jnp.concatenate([block, tokens, jnp.zeros((2, SLOTS - GRID - 2, width), F32)], 1)
    rest = classifier[:, CMAIN:].T
    unit = jnp.concatenate(
        [
            block.reshape(TOK, width), vectors, jnp.zeros((ECLS - EVEC - VROWS, width), F32),
            pad_to(rest, 0, EWIDE - ECLS),
        ],
        0,
    )
    return unit.T.astype(BF), embedding[NGRID:].T.astype(BF), classifier[:, :CMAIN].astype(BF)


def local(
    patches, column_mask, labels, clip_weights, wide_weights, down_weights, embedding, classifier,
    vectors, class_bias, wide_first, down_first, embedding_first, classifier_first, vectors_first,
    bias_first, wide_second, down_second, embedding_second, classifier_second, vectors_second,
    bias_second,
):
    times = lax.axis_size("tm")
    f, t = lax.axis_index("freq"), lax.axis_index("tm")
    half = t % 2
    pair = t // 2
    rows_dev = FROWS // NF
    kernels = D // times == 96
    shard = D // times
    columns = column_mask.reshape(times, CPD, HALF) > 0
    mine_columns = lax.dynamic_index_in_dim(columns, t, 0, keepdims=False)
    raw = patches.reshape(rows_dev, CPD, HALF, PATCH)

    keep_block, give_block = (
        pad_to(lax.dynamic_index_in_dim(raw, i, 1, keepdims=False).reshape(GRID, PATCH), 0, SLOTS)
        for i in (half, 1 - half)
    )

    live = jnp.stack([pad_to(jnp.tile(mine_columns[i], rows_dev), 0, SLOTS) for i in range(2)])
    live = jnp.where(half == 0, live, live[::-1]).astype(F32)[:, :, None]
    unit_embed, unit_patch, unit_class = embed_units(embedding, classifier, vectors, f)

    clip_columns = lax.dynamic_slice(columns, (pair * 2, half, 0), (2, 1, HALF)).reshape(2, HALF)
    slots = jnp.concatenate(
        [
            jnp.broadcast_to(jnp.tile(clip_columns, (1, rows_dev)), (NF, 2, GRID)),
            jnp.broadcast_to(
                ((jnp.arange(NF)[:, None] == 0) & (jnp.arange(2)[None, :] == 0))[:, :, None], (NF, 2, 2)
            ),
            jnp.zeros((NF, 2, SLOTS - GRID - 2), bool),
        ],
        2,
    ).reshape(NF * TOK)
    mask = jnp.where(slots[:, None] | (jnp.arange(128) != HDIM)[None, :], 0.0, -1e30).astype(BF)

    weight_total = jnp.sum(clip_weights).astype(F32)
    if kernels:
        wcol, wdown, vec, xs, fa, gp, qk, pnorm, dx, head, end_rows, small = forward_all(
            times, wide_weights, down_weights, unit_embed, unit_patch, unit_class, live, keep_block, give_block,
            pad_to(labels, 1, D), clip_weights[None], pad_to(class_bias[None], 1, D), mask,
        )
    else:
        wide_all = lax.all_gather(wide_weights.astype(BF), "tm", axis=1, tiled=True)
        wcol = wide_all.reshape(L, D, 2, 4, D).transpose(0, 2, 3, 1, 4)
        wcol = wcol.reshape(2 * L, 2, 2, 4, 2, 96, D)
        wdown = lax.all_gather(down_weights.astype(BF), "tm", axis=1, tiled=True)
        wdown = wdown.reshape(L, 4, 2, 2, 192, D)
        vec = lax.all_gather(unit_embed, "tm", axis=0, tiled=True).T.astype(F32)
        patch = lax.all_gather(unit_patch, "tm", axis=0, tiled=True)
        class_main = lax.all_gather(unit_class, "tm", axis=0, tiled=True)
        pixels = jnp.stack([keep_block, give_block]).astype(F32)
        sums = jnp.stack(
            [jnp.sum(pixels * live), jnp.sum(pixels * pixels * live), jnp.sum(live) * PATCH]
        )
        sums = lax.psum(sums, ("freq", "tm"))
        take_block = lax.ppermute(
            give_block, "tm", [(i, i + 1 - 2 * (i % 2)) for i in range(times)]
        )
        pixels = jnp.concatenate(
            [jnp.where(half == 0, keep_block, take_block), jnp.where(half == 0, take_block, keep_block)], 0
        )
        center = sums[0] / sums[2]
        mel_scale = lax.rsqrt(sums[1] / sums[2] - center * center + 1e-05)
        inside = (jnp.arange(TOK) % SLOTS < GRID)[:, None]
        pnorm = jnp.where(inside, (pixels.astype(F32) - center) * mel_scale, 0.0).astype(BF)
        x = nt(pnorm, patch) + vec[:TOK] + jnp.where(inside, vec[EVEC + GLOB], 0.0)
        xs, fa, gp, qk = [x], [], [], []
        for layer in range(L):
            x, x1, acts, slopes, heads = forward_layer(layer, x, vec, mask, wcol, wdown)
            xs += [x1, x]
            fa.append(acts)
            gp.append(slopes)
            qk.append(heads)
    wcol = wcol.reshape(2 * L, 4, D, D)
    wdown = wdown.reshape(L, 4, D, D)
    if not kernels:
        vec_all = vec[EVEC : EVEC + VROWS]
        class_all = jnp.concatenate([class_main, vec[ECLS : ECLS + CLASSES - CMAIN].T.astype(BF)], 1)

        owner = (f == 0).astype(F32)
        special = xs[2 * L][GRID : GRID + 2]
        normed_end, scale_end = norm_rows(special)
        feature = jnp.mean(normed_end * vec_all[GLOB + 3] + vec_all[GLOB + 4], 0, keepdims=True).astype(BF)
        logits = nn(feature, class_all) + class_bias
        clip = pair * CPD + half
        flags = lax.dynamic_slice_in_dim(labels, clip, 1, 0).astype(F32)
        weight = lax.dynamic_slice_in_dim(clip_weights, clip, 1, 0).astype(F32)[:, None]
        loss_part = owner * jnp.sum(weight * (jax.nn.softplus(logits) - flags * logits))
        dlogits = owner * weight * (jax.nn.sigmoid(logits) - flags) / weight_total
        dlogits_low = dlogits.astype(BF)
        dfinal = jnp.broadcast_to(0.5 * nt(dlogits_low, class_all), (2, D))
        dspecial = norm_back(dfinal * vec_all[GLOB + 3], normed_end, scale_end)
        end_rows = jnp.stack([jnp.sum(dfinal * normed_end, 0), jnp.sum(dfinal, 0)])
        dx = jnp.concatenate(
            [jnp.zeros((GRID, D), F32), dspecial, jnp.zeros((TOK - GRID - 2, D), F32)], 0
        )
        small = jnp.concatenate([dlogits.reshape(-1), loss_part.reshape(1)])
        small = pad_to(small, 0, 1024).reshape(8, 128)
    if kernels:
        gcol, gdown, gpart, scalars = backward_all(
            times, dx, xs, gp, qk, fa, vec, mask, pnorm, head, end_rows, small, wcol, wdown
        )
        small = scalars[0].reshape(-1)
        grad_norm, coef = scalars[1, 0, 0], scalars[2, 0, 0]
        params = (wide_weights, down_weights, embedding, classifier, vectors)
        firsts = (wide_first, down_first, embedding_first, classifier_first, vectors_first)
        seconds = (wide_second, down_second, embedding_second, classifier_second, vectors_second)
        news = update(
            scalars, gcol.reshape(L, 8, shard, D), gdown.reshape(L, FF // times, D),
            gpart.reshape(2, NF, shard, -1), params, firsts, seconds,
        )
        bias = adam(class_bias, bias_first, bias_second, small[:CLASSES] * coef)
        return (
            *news[:5], bias[0], *news[5:10], bias[1], *news[10:15], bias[2], *news[15:],
            grad_norm, small[CLASSES], weight_total,
        )
    else:
        ba = [None] * L
        er = jnp.zeros((EWIDE, D), F32)
        for layer in reversed(range(L)):
            dx, ba[layer], rows = backward_layer(
                layer, dx, xs[2 * layer], xs[2 * layer + 1], gp[layer], qk[layer], vec, mask, wcol, wdown
            )
            er = er + rows
        dgrid = jnp.where(inside, dx, 0.0)
        grad_vectors = er[EVEC : EVEC + GLOB]
        grad_vectors = jnp.concatenate(
            [grad_vectors, jnp.sum(dgrid, 0, keepdims=True), dx[GRID : GRID + 2], end_rows], 0
        )
        wides, downs = [], []
        for l in range(L):
            cols = [tn(fa[l][0], ba[l][i]) for i in range(3)]
            cols += [tn(fa[l][1], ba[l][3])]
            cols += [tn(fa[l][2], ba[l][4 + i]) for i in range(4)]
            wides.append(jnp.concatenate(cols, 1))
            downs.append(jnp.concatenate([tn(fa[l][3 + i], ba[l][8]) for i in range(4)], 0))
        dpos = dgrid.reshape(2, SLOTS, D)[:, :GRID].reshape(2, rows_dev, HALF, D)
        dpos = dpos.transpose(1, 0, 2, 3).reshape(rows_dev * 2 * HALF, D)
        dpos = lax.dynamic_update_slice(jnp.zeros((NGRID, D), F32), dpos, (f * rows_dev * 2 * HALF, 0))
        dembed = jnp.concatenate([dpos, tn(pnorm, dgrid.astype(BF))], 0)
        grads = (
            lax.psum_scatter(jnp.stack(wides), "tm", scatter_dimension=1, tiled=True),
            lax.psum_scatter(jnp.stack(downs), "tm", scatter_dimension=1, tiled=True),
            lax.psum_scatter(dembed, "tm", scatter_dimension=1, tiled=True),
            lax.psum_scatter(tn(feature, dlogits_low), "tm", scatter_dimension=0, tiled=True),
            lax.psum_scatter(grad_vectors, "tm", scatter_dimension=1, tiled=True),
        )
        grads = lax.psum(grads, "freq")
        grad_wide, grad_down, grad_embed, grad_class, grad_vectors = grads
        squares = sum(jnp.sum(v * v) for v in grads)
        square_total, small = lax.psum(
            (jnp.where(f == 0, squares, 0.0), small.reshape(-1)), ("freq", "tm")
        )
    grad_bias = small[:CLASSES]
    loss_sum = small[CLASSES]
    grad_norm = jnp.sqrt(square_total + jnp.sum(grad_bias * grad_bias))
    coef = jnp.minimum(1.0, 1.0 / (grad_norm + 1e-06))

    params = (wide_weights, down_weights, embedding, classifier, vectors, class_bias)
    firsts = (wide_first, down_first, embedding_first, classifier_first, vectors_first, bias_first)
    seconds = (wide_second, down_second, embedding_second, classifier_second, vectors_second, bias_second)
    grads = (grad_wide, grad_down, grad_embed, grad_class, grad_vectors, grad_bias)
    news = [adam(w, m, v, g * coef) for w, m, v, g in zip(params, firsts, seconds, grads)]
    masters = [n[0] for n in news]
    return (
        *masters,
        *[n[1] for n in news],
        *[n[2] for n in news],
        *[m.astype(BF) for m in masters[:4]],
        grad_norm,
        loss_sum,
        weight_total,
    )


def solution(mesh):
    split = (
        P(None, "tm", None), P(None, "tm", None), P(None, "tm"), P("tm", None), P(None, "tm"), P(),
    )
    return jax.shard_map(
        local,
        mesh=mesh,
        in_specs=(P("freq", "tm", None), P(), P(), P()) + split * 3,
        out_specs=split * 3 + split[:4] + (P(), P(), P()),
        check_vma=False,
    )
```

```python
import functools

import jax
import jax.numpy as jnp
from jax import lax
from jax.experimental import pallas as pl
from jax.experimental.pallas import tpu as pltpu
from jax.sharding import PartitionSpec as P

D = 768
HEADS = 12
HDIM = 64
FF = 3072
L = 2
FROWS = 12
HALF = 52
PATCH = 256
STEP = 5
CPD = 2
NGRID = FROWS * 2 * HALF
CLASSES = 527
VROWS = 29
GLOB = L * 8 + L * (FF // D)

TOK = 320
PER = 3
NF = 4

DECAY_FIRST = 0.5
DECAY_SECOND = 0.5
LEARN_RATE = 0.03
WEIGHT_DECAY = 0.05
EPSILON = 1e-08

MESH = pl.DeviceIdType.MESH
BF = jnp.bfloat16
F32 = jnp.float32
VLIM = 60 * 1024 * 1024
VM = pltpu.VMEM


def nn(a, b):
    return lax.dot_general(a, b, (((1,), (0,)), ((), ())), preferred_element_type=F32)


def nt(a, b):
    return lax.dot_general(a, b, (((1,), (1,)), ((), ())), preferred_element_type=F32)


def tn(a, b):
    return lax.dot_general(a, b, (((0,), (0,)), ((), ())), preferred_element_type=F32)


def norm_rows(x):
    center = jnp.mean(x, -1, keepdims=True)
    shifted = x - center
    scale = lax.rsqrt(jnp.mean(shifted * shifted, -1, keepdims=True) + 1e-06)
    return (shifted * scale, scale)


def norm_back(dnorm, normed, scale):
    return scale * (
        dnorm
        - jnp.mean(dnorm, -1, keepdims=True)
        - normed * jnp.mean(dnorm * normed, -1, keepdims=True)
    )


def vspec():
    return pl.BlockSpec(memory_space=VM)


def aspec():
    return pl.BlockSpec(memory_space=pl.ANY)


def place():
    f, t = lax.axis_index("freq"), lax.axis_index("tm")
    return f, t, f // 2, f % 2, t // 2, t % 2


def remote(src, dst, ssem, rsem, dev):
    return pltpu.make_async_remote_copy(
        src_ref=src, dst_ref=dst, send_sem=ssem, recv_sem=rsem, device_id=dev, device_id_type=MESH
    )


def greet_all(times):
    f, t = lax.axis_index("freq"), lax.axis_index("tm")
    n = NF * times
    me = f * times + t
    barrier = pltpu.get_barrier_semaphore()

    def hello(i, carry):
        other = (me + i) % n
        pl.semaphore_signal(
            barrier, inc=1, device_id=(other // times, other % times), device_id_type=MESH
        )
        return carry

    lax.fori_loop(1, n, hello, 0)
    pl.semaphore_wait(barrier, n - 1)


def spread_small(times, small, gathered, ssem, rsem):
    f, t = lax.axis_index("freq"), lax.axis_index("tm")
    n = NF * times
    me = f * times + t

    def send(i, carry):
        other = (me + i) % n
        remote(
            small, gathered.at[me], ssem, rsem, (other // times, other % times)
        ).start()
        return carry

    lax.fori_loop(1, n, send, 0)
    gathered[me] = small[...]


def wait_small(times, gathered, ssem, rsem):
    n = NF * times
    many = gathered.at[pl.ds(0, n - 1)]
    pltpu.make_async_copy(many, many, rsem).wait()
    pltpu.make_async_copy(many, many, ssem).wait()


QROWS = TOK + TOK // 2
SLOTS = TOK // 2
GRID = FROWS // NF * HALF
EWIDE = 384
EVEC = TOK
ECLS = 352
CMAIN = 512


def greet_clip():
    f, t = lax.axis_index("freq"), lax.axis_index("tm")
    barrier = pltpu.get_barrier_semaphore()
    for i in range(1, NF):
        pl.semaphore_signal(barrier, inc=1, device_id=((f + i) % NF, t), device_id_type=MESH)
    pl.semaphore_wait(barrier, NF - 1)


def pack_half(v):
    return jnp.concatenate([v[: TOK // 2], v[TOK // 2 :]], 1)


def open_half(v):
    return jnp.concatenate([v[:, :HDIM], v[:, HDIM:]], 0)


def with_mask(block):
    lane = lax.broadcasted_iota(jnp.int32, block.shape, 1)
    query = jnp.where(lane < HDIM, block.astype(F32) * (HDIM ** (-0.5)), 0.0)
    return jnp.where(lane == HDIM, 1.0, query).astype(BF)


def exchange_sems():
    dma = pltpu.SemaphoreType.DMA
    return [dma((PER, NF - 1))] * 4


FORWARD_SCRATCH = [
    VM((2, 2, 2, 4, 2, 96, D), BF),
    VM((4, 2, 2, 192, D), BF),
    VM((PER, NF, QROWS, 128), BF),
    VM((PER, NF, TOK // 2, 128), BF),
    VM((NF * TOK, 128), BF),
    VM((NF * TOK, HDIM), BF),
    VM((TOK, D), F32),
]


def layer_body(layer, x_ref, vec_ref, outs, scratch, orecv, sems, fetch, at):
    xo_ref, x1_ref, fa_ref, gp_ref, qk_ref = outs
    wbuf, dbuf, qsend, osend, kall, vall, acc = scratch
    qs, qr, os, orr = sems
    f, t = lax.axis_index("freq"), lax.axis_index("tm")

    def row(i):
        return vec_ref[EVEC + layer * 8 + i : EVEC + layer * 8 + i + 1, :]

    def mat(part, q, cols=slice(None)):
        return wbuf[part, q // 2, q % 2, :, :, :, cols].reshape(D, -1)

    normed, _ = norm_rows(x_ref[...])
    act = (normed * row(0) + row(1)).astype(BF)
    fa_ref[0] = act
    fetch(0)

    def to_clip(j, i):
        other = (f + i) % NF
        return remote(
            qsend.at[j, other], qk_ref.at[j, f], qs.at[j, i - 1], qr.at[j, i - 1], (other, t)
        )

    def back_clip(j, i):
        other = (f + i) % NF
        return remote(
            osend.at[j, other], orecv.at[j, f], os.at[j, i - 1], orr.at[j, i - 1], (other, t)
        )

    for j in range(PER):
        cols = slice(256 * j, 256 * (j + 1))
        query = (nn(act, mat(0, 0, cols)) + row(4)[:, cols]).astype(BF)
        key = nn(act, mat(0, 1, cols)).astype(BF)
        value = (nn(act, mat(0, 2, cols)) + row(5)[:, cols]).astype(BF)
        for h in range(NF):
            part = slice(HDIM * h, HDIM * (h + 1))
            qsend[j, h, :TOK] = jnp.concatenate([query[:, part], key[:, part]], 1)
            qsend[j, h, TOK:] = pack_half(value[:, part])
        for i in range(1, NF):
            to_clip(j, i).start()
        qk_ref[j, f] = qsend[j, f]
        at("qkv%d" % j)
    for j in range(PER):
        for i in range(1, NF):
            to_clip(j, i).wait_recv()
        for s in range(NF):
            kall[s * TOK : (s + 1) * TOK, :HDIM] = qk_ref[j, s, :TOK, HDIM:]
            vall[s * TOK : (s + 1) * TOK] = open_half(qk_ref[j, s, TOK:])

        def attend(i, carry):
            s = (f + i) % NF
            to = i % NF
            halves = []
            for h in range(2):
                lo = h * (TOK // 2)
                scores = nt(with_mask(qk_ref[j, s, lo : lo + TOK // 2]), kall[...])
                top = jnp.max(scores, -1, keepdims=True)
                expo = jnp.exp(scores - top)
                total = jnp.sum(expo, -1, keepdims=True)
                probs = (expo * (1.0 / total)).astype(BF)
                halves.append(nn(probs, vall[...]).astype(BF))
            osend[j, s] = jnp.concatenate(halves, 1)

            @pl.when(to > 0)
            def _():
                remote(
                    osend.at[j, s], orecv.at[j, f], os.at[j, to - 1], orr.at[j, to - 1], (s, t)
                ).start()

            return carry

        lax.fori_loop(1, 3, attend, 0)
        at("head%d1" % j)
        lax.fori_loop(3, 5, attend, 0)
        orecv[j, f] = osend[j, f]
        at("head%d3" % j)
    parts = []
    for j in range(PER):
        for i in range(1, NF):
            back_clip(j, i).wait_recv()
        for h in range(NF):
            parts.append(open_half(orecv[j, h]))
    mixed = jnp.concatenate(parts, 1)
    fa_ref[1] = mixed
    resid = x_ref[...] + nn(mixed, mat(0, 3)) + row(6)
    x1_ref[...] = resid
    normed, _ = norm_rows(resid)
    fa_ref[2] = (normed * row(2) + row(3)).astype(BF)
    acc[...] = resid + row(7)
    at("resid")
    fetch(1)

    def up(k, carry):
        bias = vec_ref[pl.ds(EVEC + L * 8 + layer * 4 + k, 1), :]
        before = nn(fa_ref[2], mat(1, k)) + bias
        lower = 0.5 * (1.0 + lax.erf(before * 0.7071067811865476))
        gp_ref[k] = lower + before * jnp.exp(-0.5 * before * before) * 0.3989422804014327
        hidden = (before * lower).astype(BF)
        fa_ref[3 + k] = hidden
        return carry

    def down(k, carry):
        acc[...] += nn(fa_ref[3 + k], dbuf[k].reshape(D, D))
        return carry

    for k in range(0, FF // D, 2):
        lax.fori_loop(k, k + 2, up, 0)
        at("up%d" % (k + 1))
    fetch(2)
    for k in range(0, FF // D, 2):
        lax.fori_loop(k, k + 2, down, 0)
        at("down%d" % (k + 1))
    xo_ref[...] = acc[...]
    for j in range(PER):
        for i in range(1, NF):
            to_clip(j, i).wait_send()
            back_clip(j, i).wait_send()


def load_mask(mask, kall):
    def body(sem):
        copy = pltpu.make_async_copy(mask, kall, sem)
        copy.start()
        copy.wait()

    pl.run_scoped(body, pltpu.SemaphoreType.DMA)


def forward_kernel(
    layer, x_ref, vec_ref, mask, wcol, wdown,
    xo_ref, x1_ref, fa_ref, gp_ref, qk_ref,
    wbuf, dbuf, qsend, osend, kall, vall, acc, orecv, wsem, qs, qr, os, orr,
):
    loads = [
        pltpu.make_async_copy(wcol.at[2 * layer], wbuf.at[0], wsem.at[0]),
        pltpu.make_async_copy(wcol.at[2 * layer + 1], wbuf.at[1], wsem.at[1]),
        pltpu.make_async_copy(wdown.at[layer], dbuf, wsem.at[2]),
    ]
    for load in loads:
        load.start()
    load_mask(mask, kall)
    greet_clip()
    layer_body(
        layer, x_ref, vec_ref, (xo_ref, x1_ref, fa_ref, gp_ref, qk_ref),
        (wbuf, dbuf, qsend, osend, kall, vall, acc), orecv, (qs, qr, os, orr),
        lambda part: loads[part].wait(), lambda point: None,
    )


def forward_layer(layer, x, vec, mask, wcol, wdown):
    return pl.pallas_call(
        functools.partial(forward_kernel, layer),
        out_shape=(
            jax.ShapeDtypeStruct((TOK, D), F32),
            jax.ShapeDtypeStruct((TOK, D), F32),
            jax.ShapeDtypeStruct((7, TOK, D), BF),
            jax.ShapeDtypeStruct((FF // D, TOK, D), F32),
            jax.ShapeDtypeStruct((PER, NF, QROWS, 128), BF),
        ),
        in_specs=[vspec()] * 2 + [aspec()] * 3,
        out_specs=(vspec(),) * 5,
        scratch_shapes=FORWARD_SCRATCH
        + [VM((PER, NF, TOK // 2, 128), BF), pltpu.SemaphoreType.DMA((3,))]
        + exchange_sems(),
        compiler_params=pltpu.CompilerParams(
            collective_id=2 + layer, has_side_effects=True, vmem_limit_bytes=VLIM
        ),
        name="forward_layer",
    )(x, vec, mask, wcol, wdown)


GROUPS = (("c", 0), ("c", 1), ("d", 0), ("c", 2), ("c", 3), ("d", 1))
SUBS = tuple((kind, idx, h) for kind, idx in GROUPS for h in (0, 1))
PATHS = "xyxzxzxzzzzz"
FLOW = {
    ("begin",): (0, 1,),
    ("units",): (2, 3,),
    ("arrived",): (100,),
    ("x0",): (4, 101,),
    ("fetch", 0, 0,): (100, 102, 101, 5, 102, 103, 100, 6, 104, 101, 100, 101,),
    (0, "qkv0",): (7, 102,),
    (0, "qkv1",): (103,),
    (0, "head01",): (8, 102, 103, 104, 105,),
    (0, "head03",): (106,),
    (0, "head11",): (9,),
    (0, "head21",): (105, 107,),
    (0, "head23",): (10, 104, 106, 105,),
    (0, "resid",): (104, 108,),
    (0, "up1",): (11, 107,),
    (0, "up3",): (106,),
    (0, "down1",): (107, 109,),
    ("fetch", 1, 0,): (106, 108,),
    (1, "qkv1",): (108,),
    (1, "head01",): (109, 110,),
    (1, "head11",): (109, 111,),
    (1, "head13",): (110,),
    (1, "head23",): (110,),
    (1, "resid",): (111,),
    (1, "up3",): (111,),
}


def gather_parts(count, ucol, udown, ocol, odown, sems, prepare):
    zs, zr, own, s1, r1, s2, r2, s3, r3 = sems
    f, t, y, c, g, x = place()
    every = slice(None)
    over_x, over_y, over_c = (f, g * 2 + 1 - x), ((1 - y) * 2 + c, t), (y * 2 + 1 - c, t)

    def source(s):
        kind, idx, h = SUBS[s]
        yy = every if PATHS[s] == "z" else y
        if kind == "c":
            return ucol.at[idx, yy, c, :, pl.ds(h * 384, 384)]
        return udown.at[idx, yy, pl.ds(h * 96, 96), pl.ds(pl.multiple_of(c * 384, 128), 384)]

    def view(s, yy, zz, xx):
        kind, idx, h = SUBS[s]
        if PATHS[s] == "z":
            yy = every
        if kind == "c":
            return ocol.at[idx, yy, c, zz, xx, :, pl.ds(h * 384, 384)]
        return odown.at[
            idx, zz, xx, yy, pl.ds(h * 96, 96), pl.ds(pl.multiple_of(c * 384, 128), 384)
        ]

    def along(s, dz):
        return remote(
            source(s), view(s, y, g, x), zs.at[s, dz - 1], zr.at[s, dz - 1],
            (f, ((g + dz) % count) * 2 + x),
        )

    def keep(s):
        return pltpu.make_async_copy(source(s), view(s, y, g, x), own.at[s])

    def leg(s, n):
        if n == legs(s):
            block = view(s, every, every, every)
            return remote(block, block, s3.at[s], r3.at[s], over_c)
        if n == 1:
            block = view(s, y, every, x)
            return remote(block, block, s1.at[s], r1.at[s], over_y if PATHS[s] == "y" else over_x)
        block = view(s, y, every, every) if PATHS[s] == "x" else view(s, every, every, x)
        return remote(block, block, s2.at[s], r2.at[s], over_y if PATHS[s] == "x" else over_x)

    def legs(s):
        return 2 if PATHS[s] == "z" else 3

    def piece(s, zz, src=None):
        block = view(s, y, zz, x)
        return remote(
            block if src is None else src, block, s1.at[s], r1.at[s], over_y if PATHS[s] == "y" else over_x
        )

    stage = {}

    def begin(s):
        prepare(s // 2)
        keep(s).start()
        for dz in range(1, count):
            along(s, dz).start()
        piece(s, g, source(s)).start()
        stage[s] = 0

    def advance(s):
        if stage[s] == 0:
            for dz in range(1, count):
                along(s, dz).wait_recv()
                piece(s, (g + count - dz) % count).start()
            keep(s).wait()
        else:
            leg(s, stage[s]).wait_recv()
        stage[s] += 1
        if 1 < stage[s] <= legs(s):
            leg(s, stage[s]).start()

    def arrived(s):
        return stage.get(s, 0) > legs(s)

    def finish():
        for s in range(len(SUBS)):
            for dz in range(1, count):
                along(s, dz).wait_send()
            for n in range(1, legs(s) + 1):
                leg(s, n).wait_send()

    return begin, advance, arrived, finish


def loss_part(owner, clip, x_ref, vec, classes, labels, clip_weights, class_bias, dout, head, end_rows, small):
    owner = jnp.where(owner, 1.0, 0.0)
    normed, scale = norm_rows(x_ref[GRID : GRID + 2, :])
    gain = vec[EVEC + GLOB + 3 : EVEC + GLOB + 4, :]
    final = normed * gain + vec[EVEC + GLOB + 4 : EVEC + GLOB + 5, :]
    feature = jnp.mean(final, 0, keepdims=True).astype(BF)
    first_row = lax.broadcasted_iota(jnp.int32, (16, D), 0) == 0
    feature = jnp.where(first_row, jnp.broadcast_to(feature.astype(F32), (16, D)), 0.0).astype(BF)
    head[0] = feature
    main = classes[...].reshape(D, CMAIN)
    tail = vec[ECLS:EWIDE, :].astype(BF)
    logits = jnp.concatenate([nn(feature, main), nt(feature, tail), jnp.zeros((16, 224), F32)], 1)[0:1]
    logits = logits + class_bias[...]
    flags = labels[pl.ds(clip, 1), :].astype(F32)
    weights = clip_weights[...].astype(F32)
    weight = jnp.sum(
        jnp.where(lax.broadcasted_iota(jnp.int32, weights.shape, 1) == clip, weights, 0.0), keepdims=True
    )
    total = jnp.sum(weights, keepdims=True)
    lane = lax.broadcasted_iota(jnp.int32, (1, D), 1)
    inside = lane < CLASSES
    soft = jnp.maximum(logits, 0.0) + jnp.log1p(jnp.exp(-jnp.abs(logits)))
    loss = jnp.sum(jnp.where(inside, soft - flags * logits, 0.0), keepdims=True) * weight * owner
    slope = 1.0 / (1.0 + jnp.exp(-logits))
    grads = jnp.where(inside, owner * weight * (slope - flags) / total, 0.0)
    for i in range(8):
        small[i : i + 1, :] = jnp.zeros((1, 128), F32) if i > 5 else (
            grads[:, 128 * i : 128 * (i + 1)]
            + (jnp.where(lane[:, 128 * i : 128 * (i + 1)] == CLASSES, loss, 0.0))
        )
    grads = jnp.where(first_row, jnp.broadcast_to(grads, (16, D)), 0.0).astype(BF)
    head[1] = grads
    dfinal = 0.5 * (nt(grads[:, :CMAIN], main) + nn(grads[:, CMAIN : CMAIN + EWIDE - ECLS], tail))[0:1]
    end_rows[0:1, :] = jnp.sum(dfinal * normed, 0, keepdims=True)
    end_rows[1:2, :] = 2.0 * dfinal
    special = norm_back(jnp.broadcast_to(dfinal * gain, normed.shape), normed, scale)
    dout[...] = jnp.zeros_like(dout)
    dout[GRID : GRID + 2, :] = special


def forward_all_kernel(
    times, wide, down, uemb, upatch, uclass, live, pkeep, psend, labels, clip_weights, class_bias, mask,
    ocol, odown, vec_out, xs_out, fa_out, gp_out, qk_out, pn_out, dout_out, head, end_rows, small,
    wbuf, dbuf, qsend, osend, kall, vall, acc, orecv, sall, precv, emb, patches, classes, vec, xs, fa, gp, qk, pn,
    zs, zr, own, s1, r1, s2, r2, s3, r3, es, er, exs, exr, ss, sr, ps, pr, wsem, osem,
    qs0, qr0, os0, or0, qs1, qr1, os1, or1, ucol, udown, cols_wide, cols_down, stats, dout, psem,
):
    f, t, y, c, g, x = place()
    count = times // 2
    over_x = (f, g * 2 + 1 - x)

    def fetch_master(group):
        kind, idx = GROUPS[group]
        if kind == "c":
            src = wide.at[idx // 2, :, pl.ds(idx % 2 * 4 * D, 4 * D)]
            return pltpu.make_async_copy(src, cols_wide.at[idx], psem.at[group])
        return pltpu.make_async_copy(down.at[idx], cols_down.at[idx], psem.at[group])

    prepared = set()

    def prepare(group):
        if group in prepared:
            return
        prepared.add(group)
        fetch_master(group).wait()
        kind, idx = GROUPS[group]
        for q in range(4):
            if kind == "c":
                ucol[idx, q // 2, q % 2] = cols_wide[idx, :, q * D : (q + 1) * D].astype(BF)
            else:
                udown[idx, q // 2, q % 2 * 96 : q % 2 * 96 + 96] = cols_down[idx, q * 96 : (q + 1) * 96].astype(BF)

    for group in range(len(GROUPS)):
        fetch_master(group).start()
    row = lax.broadcasted_iota(jnp.int32, (8, 128), 1)
    stats[...] = jnp.zeros_like(stats)
    for n, block in enumerate((pkeep, psend)):
        pixel, alive = block[...].astype(F32), live[n]
        masked = pixel * alive
        for lane, value in enumerate((masked, masked * pixel, alive * float(PATCH))):
            stats[...] += jnp.where(row == lane, jnp.sum(value, keepdims=True), 0.0)
    greet_all(times)
    spread_small(times, stats, sall, ss, sr)
    swap = remote(psend, precv, ps, pr, over_x)
    swap.start()
    load_mask(mask, kall)
    units = ((uemb, emb), (upatch, patches), (uclass, classes))

    def unit_along(n, dz):
        src, dst = units[n]
        return remote(
            src, dst.at[g, x], es.at[n, dz - 1], er.at[n, dz - 1], (f, ((g + dz) % count) * 2 + x)
        )

    def loads(layer, part):
        if part < 2:
            return pltpu.make_async_copy(ocol.at[2 * layer + part], wbuf.at[part], wsem.at[layer, part])
        return pltpu.make_async_copy(odown.at[layer], dbuf, wsem.at[layer, part])

    def unit_over(n):
        block = units[n][1].at[:, x]
        return remote(block, block, exs.at[n], exr.at[n], over_x)

    def unit_piece(n, zz):
        block = units[n][1].at[zz, x]
        return remote(block, block, exs.at[n], exr.at[n], over_x)

    def unit_pieces(n):
        for dz in range(1, count):
            unit_along(n, dz).wait_recv()
            unit_piece(n, (g + count - dz) % count).start()

    for n in range(3):
        units[n][1][g, x] = units[n][0][...]
    for n in range(2):
        for dz in range(1, count):
            unit_along(n, dz).start()
        unit_piece(n, g).start()
    begin, advance, arrived, finish = gather_parts(
        count, ucol, udown, ocol, odown, (zs, zr, own, s1, r1, s2, r2, s3, r3), prepare
    )
    started, allowed = set(), {(0, part) for part in range(3)}

    def prefetch():
        for layer, part in sorted(allowed - started):
            first = 2 * (3 * layer + part)
            if arrived(first) and arrived(first + 1):
                loads(layer, part).start()
                started.add((layer, part))

    def at(*point):
        for op in FLOW.get(point, ()):
            (begin if op < 100 else advance)(op % 100)
        prefetch()

    at("begin")
    for n in range(2):
        unit_pieces(n)
    at("units")
    for n in range(2):
        unit_over(n).wait_recv()
    at("arrived")
    swap.wait_recv()
    wait_small(times, sall, ss, sr)
    sums = jnp.sum(sall[...], 0)
    total, squares, live = sums[0:1, 0:1], sums[0:1, 1:2], sums[0:1, 2:3]
    center = total / live
    mel_scale = lax.rsqrt(squares / live - center * center + 1e-05)
    inside = lax.broadcasted_iota(jnp.int32, (SLOTS, PATCH), 0) < GRID

    def normalized(block):
        return jnp.where(inside, (block[...].astype(F32) - center) * mel_scale, 0.0).astype(BF)

    pn[pl.ds(pl.multiple_of(x * SLOTS, SLOTS), SLOTS)] = normalized(pkeep)
    pn[pl.ds(pl.multiple_of((1 - x) * SLOTS, SLOTS), SLOTS)] = normalized(precv)
    vec[...] = emb[...].reshape(D, EWIDE).astype(F32).T
    patch = patches[...].reshape(D, PATCH)
    bias = vec[EVEC + GLOB : EVEC + GLOB + 1, :]
    spot = lax.broadcasted_iota(jnp.int32, (TOK, D), 0)
    grid_row = jnp.logical_or(spot < GRID, jnp.logical_and(spot >= SLOTS, spot < SLOTS + GRID))
    xs[0] = (nt(pn[...], patch) + vec[:TOK]) + jnp.where(grid_row, bias, 0.0)

    copies = [
        pltpu.make_async_copy(vec, vec_out, osem.at[1]),
        pltpu.make_async_copy(pn, pn_out, osem.at[2]),
    ]
    for copy in copies:
        copy.start()
    sems = ((qs0, qr0, os0, or0), (qs1, qr1, os1, or1))
    at("x0")

    @pl.when(f == 0)
    def _():
        for dz in range(1, count):
            unit_along(2, dz).start()

    def classes_over():
        @pl.when(f == 0)
        def _():
            for dz in range(1, count):
                unit_along(2, dz).wait_recv()
            unit_over(2).start()

    def during(layer, point):
        at(layer, point)
        if (layer, point) == (L - 1, "head23"):
            classes_over()
        if point == "up3":
            more = [
                pltpu.make_async_copy(src.at[layer], dst.at[layer], osem.at[3 + 4 * layer + n])
                for n, (src, dst) in enumerate(((fa, fa_out), (gp, gp_out), (qk, qk_out)))
            ]
            span = pl.ds(2 * layer + (1 if layer else 0), 1 if layer else 2)
            more.append(pltpu.make_async_copy(xs.at[span], xs_out.at[span], osem.at[6 if layer == 0 else 12]))
            for copy in more:
                copy.start()
            copies.extend(more)

    for layer in range(L):

        def fetch(part):
            if part == 1 and layer + 1 < L:
                allowed.add((layer + 1, 0))
            at("fetch", layer, part)
            loads(layer, part).wait()

        layer_body(
            layer, xs.at[2 * layer], vec,
            (xs.at[2 * layer + 2], xs.at[2 * layer + 1], fa.at[layer], gp.at[layer], qk.at[layer]),
            (wbuf, dbuf, qsend, osend, kall, vall, acc), orecv.at[layer], sems[layer], fetch,
            functools.partial(during, layer),
        )
        copies.append(pltpu.make_async_copy(xs.at[2 * layer + 2], xs_out.at[2 * layer + 2], osem.at[10 + layer]))
        copies[-1].start()
        allowed.update((layer + 1, part) for part in (1, 2) if layer + 1 < L)

    @pl.when(f == 0)
    def _():
        unit_over(2).wait_recv()

    @pl.when(f != 0)
    def _():
        classes[...] = jnp.zeros_like(classes)

    loss_part(
        f == 0, g * 2 + x, xs.at[2 * L], vec, classes, labels, clip_weights, class_bias, dout, head, end_rows, small
    )
    copies.append(pltpu.make_async_copy(dout, dout_out, osem.at[0]))
    copies[-1].start()
    finish()
    for n in range(2):
        for dz in range(1, count):
            unit_along(n, dz).wait_send()
        unit_over(n).wait_send()

    @pl.when(f == 0)
    def _():
        for dz in range(1, count):
            unit_along(2, dz).wait_send()
        unit_over(2).wait_send()

    swap.wait_send()
    for copy in copies:
        copy.wait()


def forward_all(times, wide, down, uemb, upatch, uclass, live, pkeep, psend, labels, clip_weights, class_bias, mask):
    count = times // 2
    total = len(SUBS)
    dma = pltpu.SemaphoreType.DMA
    outs = (
        ((2 * L, 2, 2, count, 2, 96, D), BF),
        ((L, count, 2, 2, 192, D), BF),
        ((EWIDE, D), F32),
        ((2 * L + 1, TOK, D), F32),
        ((L, 7, TOK, D), BF),
        ((L, FF // D, TOK, D), F32),
        ((L, PER, NF, QROWS, 128), BF),
        ((TOK, PATCH), BF),
        ((TOK, D), F32),
        ((2, 16, D), BF),
        ((2, D), F32),
        ((8, 128), F32),
    )
    return pl.pallas_call(
        functools.partial(forward_all_kernel, times),
        out_shape=tuple(jax.ShapeDtypeStruct(*o) for o in outs),
        in_specs=[aspec()] * 2 + [vspec()] * 9 + [aspec()],
        out_specs=(aspec(),) * (len(outs) - 3) + (vspec(),) * 3,
        scratch_shapes=FORWARD_SCRATCH
        + [
            VM((L, PER, NF, TOK // 2, 128), BF),
            VM((NF * times, 8, 128), F32),
            VM((SLOTS, PATCH), BF),
            VM((count, 2, 96, EWIDE), BF),
            VM((count, 2, 96, PATCH), BF),
            VM((count, 2, 96, CMAIN), BF),
            VM((EWIDE, D), F32),
            VM((2 * L + 1, TOK, D), F32),
            VM((L, 7, TOK, D), BF),
            VM((L, FF // D, TOK, D), F32),
            VM((L, PER, NF, QROWS, 128), BF),
            VM((TOK, PATCH), BF),
            dma((total, count - 1)), dma((total, count - 1)), dma((total,)),
            dma((total,)), dma((total,)), dma((total,)), dma((total,)), dma((total,)), dma((total,)),
            dma((3, count - 1)), dma((3, count - 1)), dma((3,)), dma((3,)),
            dma, dma, dma, dma, dma((L, 3)), dma((13,)),
        ]
        + exchange_sems() * L
        + [
            VM((2 * L, 2, 2, 96, D), BF),
            VM((L, 2, 192, D), BF),
            VM((2 * L, 96, 4 * D), F32),
            VM((L, 4 * 96, D), F32),
            VM((8, 128), F32),
            VM((TOK, D), F32),
            dma((len(GROUPS),)),
        ],
        compiler_params=pltpu.CompilerParams(
            collective_id=1, has_side_effects=True, vmem_limit_bytes=VLIM
        ),
        name="forward_all",
    )(wide, down, uemb, upatch, uclass, live, pkeep, psend, labels, clip_weights, class_bias, mask)


BACKWARD_SCRATCH = [
    VM((PER, NF, TOK // 2, 128), BF),
    VM((PER, NF, TOK // 2, 128), BF),
    VM((PER, NF, QROWS, 128), BF),
    VM((PER, NF, QROWS, 128), BF),
    VM((NF * TOK, 128), BF),
    VM((NF * TOK, HDIM), BF),
    VM((NF * TOK, HDIM), F32),
    VM((NF * TOK, HDIM), F32),
    VM((NF, TOK, HDIM), BF),
    VM((TOK, D), F32),
]


def backward_body(layer, dcur, er, ba, vec_ref, qk_ref, mats, slope, kept, scratch, sems, at):
    down, up, qkvo = mats
    dsend, drecv, gsend, grecv, kall, vall, dkall, dvall, dqall, acc = scratch
    ds_, dr_, gs_, gr_ = sems
    f, t = lax.axis_index("freq"), lax.axis_index("tm")

    def row(i):
        return vec_ref[EVEC + layer * 8 + i : EVEC + layer * 8 + i + 1, :]

    def note(i, value):
        er[EVEC + i : EVEC + i + 1, :] = jnp.sum(value, 0, keepdims=True)

    ba[8] = dcur[...].astype(BF)
    note(layer * 8 + 7, dcur[...])
    for k in range(FF // D):
        dbefore = nt(ba[8], down(k)) * slope(k)
        note(L * 8 + layer * 4 + k, dbefore)
        ba[4 + k] = dbefore.astype(BF)
        product = nt(ba[4 + k], up(k))
        acc[...] = product if k == 0 else acc[...] + product
        at("mlp%d" % k)
    normed, scale = norm_rows(kept(1))
    dact = acc[...]
    note(layer * 8 + 2, dact * normed)
    note(layer * 8 + 3, dact)
    dcur[...] += norm_back(dact * row(2), normed, scale)
    note(layer * 8 + 6, dcur[...])
    ba[3] = dcur[...].astype(BF)
    at("resid")
    dmixed = nt(ba[3], qkvo(3)).astype(BF)

    def to_clip(j, i):
        other = (f + i) % NF
        return remote(
            dsend.at[j, other], drecv.at[j, f], ds_.at[j, i - 1], dr_.at[j, i - 1], (other, t)
        )

    def back_clip(j, i):
        other = (f + i) % NF
        return remote(
            gsend.at[j, other], grecv.at[j, f], gs_.at[j, i - 1], gr_.at[j, i - 1], (other, t)
        )

    for j in range(PER):
        for h in range(NF):
            lo = 256 * j + HDIM * h
            dsend[j, h] = pack_half(dmixed[:, lo : lo + HDIM])
        for i in range(1, NF):
            to_clip(j, i).start()
        drecv[j, f] = dsend[j, f]
    at("sent")
    root = HDIM ** (-0.5)
    for j in range(PER):
        for s in range(NF):
            kall[s * TOK : (s + 1) * TOK, :HDIM] = qk_ref[j, s, :TOK, HDIM:]
            vall[s * TOK : (s + 1) * TOK] = open_half(qk_ref[j, s, TOK:])
        dkall[...] = jnp.zeros_like(dkall)
        dvall[...] = jnp.zeros_like(dvall)
        for i in range(1, NF):
            to_clip(j, i).wait_recv()

        def attend(s):
            q = with_mask(qk_ref[j, s, :TOK])
            dmix = open_half(drecv[j, s])
            scores = nt(kall[...], q)
            top = jnp.max(scores, 0, keepdims=True)
            expo = jnp.exp(scores - top)
            probs = expo * (1.0 / jnp.sum(expo, 0, keepdims=True))
            dprob = nt(vall[...], dmix)
            inner = jnp.sum(probs * dprob, 0, keepdims=True)
            dscore = (probs * (dprob - inner)).astype(BF)
            dvall[...] += nn(probs.astype(BF), dmix)
            dkall[...] += nn(dscore, q[:, :HDIM])
            dqall[s] = (tn(dscore, kall[:, :HDIM]) * root).astype(BF)

        for s in range(NF):
            attend(s)
            if s < NF - 1:
                at("head%d%d" % (j, s))
        for s in range(NF):
            span = slice(s * TOK, (s + 1) * TOK)
            gsend[j, s, :TOK] = jnp.concatenate([dqall[s], dkall[span].astype(BF)], 1)
            gsend[j, s, TOK:] = pack_half(dvall[span].astype(BF))
        for i in range(1, NF):
            back_clip(j, i).start()
        grecv[j, f] = gsend[j, f]
        at("head%d%d" % (j, NF - 1))
    for j in range(PER):
        for i in range(1, NF):
            back_clip(j, i).wait_recv()
        cols = slice(256 * j, 256 * (j + 1))
        ba[0, :, cols] = jnp.concatenate([grecv[j, h, :TOK, :HDIM] for h in range(NF)], 1)
        ba[1, :, cols] = jnp.concatenate([grecv[j, h, :TOK, HDIM:] for h in range(NF)], 1)
        ba[2, :, cols] = jnp.concatenate([open_half(grecv[j, h, TOK:]) for h in range(NF)], 1)
    at("heads")
    note(layer * 8 + 4, ba[0].astype(F32))
    note(layer * 8 + 5, ba[2].astype(F32))
    dact = nt(ba[0], qkvo(0)) + nt(ba[1], qkvo(1)) + nt(ba[2], qkvo(2))
    normed, scale = norm_rows(kept(0))
    note(layer * 8 + 0, dact * normed)
    note(layer * 8 + 1, dact)
    dcur[...] += norm_back(dact * row(0), normed, scale)
    for j in range(PER):
        for i in range(1, NF):
            to_clip(j, i).wait_send()
            back_clip(j, i).wait_send()
    at("done")


def backward_kernel(
    layer, dout_ref, x_ref, x1_ref, gp_ref, qk_ref, vec_ref, mask, wcol, wdown,
    dx_ref, ba_ref, er_ref, wbuf, dbuf, wsem, ds_, dr_, gs_, gr_, *scratch,
):
    loads = [
        pltpu.make_async_copy(wdown.at[layer], dbuf, wsem.at[0]),
        pltpu.make_async_copy(wcol.at[2 * layer + 1], wbuf.at[1], wsem.at[1]),
        pltpu.make_async_copy(wcol.at[2 * layer], wbuf.at[0], wsem.at[2]),
    ]
    for load in loads:
        load.start()
    dx_ref[...] = dout_ref[...]
    er_ref[...] = jnp.zeros_like(er_ref)
    load_mask(mask, scratch[4])
    greet_clip()
    for load in loads:
        load.wait()
    backward_body(
        layer, dx_ref, er_ref, ba_ref, vec_ref, qk_ref,
        (lambda k: dbuf[k], lambda k: wbuf[1, k], lambda k: wbuf[0, k]),
        lambda k: gp_ref[k], lambda i: x1_ref[...] if i else x_ref[...],
        scratch, (ds_, dr_, gs_, gr_), lambda point: None,
    )


def backward_layer(layer, dout, x, x1, gp, qk, vec, mask, wcol, wdown):
    return pl.pallas_call(
        functools.partial(backward_kernel, layer),
        out_shape=(
            jax.ShapeDtypeStruct((TOK, D), F32),
            jax.ShapeDtypeStruct((9, TOK, D), BF),
            jax.ShapeDtypeStruct((EWIDE, D), F32),
        ),
        in_specs=[vspec()] * 6 + [aspec()] * 3,
        out_specs=(vspec(),) * 3,
        scratch_shapes=[VM((2, 4, D, D), BF), VM((4, D, D), BF), pltpu.SemaphoreType.DMA((3,))]
        + exchange_sems()
        + BACKWARD_SCRATCH,
        compiler_params=pltpu.CompilerParams(
            collective_id=2 + L + layer, has_side_effects=True, vmem_limit_bytes=VLIM
        ),
        name="backward_layer",
    )(dout, x, x1, gp, qk, vec, mask, wcol, wdown)


RGROUPS = (("d", 1), ("u", 1), ("q", 1), ("d", 0), ("u", 0), ("q", 0))
ROUTES = ("xz", "zz", "zy", "yz", "zz", "yy")
ORDER = {
    (1, "mlp1"): (0,),
    (1, "mlp2"): (200,),
    (1, "mlp3"): (1,),
    (1, "head00"): (200, 100,),
    (1, "head01"): (10, 200,),
    (1, "head02"): (200,),
    (1, "head10"): (100,),
    (1, "head11"): (101, 11,),
    (1, "head13"): (100,),
    (1, "head22"): (110,),
    (1, "head23"): (100,),
    (1, "heads"): (100, 101,),
    (1, "done"): (101, 111, 20, 110, 21, 101,),
    (0, "mlp0"): (101, 110,),
    (0, "resid"): (111, 120,),
    (0, "sent"): (110, 121, 30, 110, 111, 31,),
    (0, "head02"): (121,),
    (0, "head03"): (120,),
    (0, "head12"): (121, 130,),
    (0, "head13"): (111, 131,),
    (0, "head20"): (111,),
    (0, "head21"): (120, 130, 40, 121,),
    (0, "head22"): (121,),
    (0, "head23"): (41,),
    (0, "heads"): (120, 131, 130, 140,),
    (0, "done"): (120, 130, 131, 50,),
    "end": (130, 131, 131, 141, 51, 140, 150, 210, 141, 151, 140, 150, 141, 210, 140, 141, 140, 151, 141, 210, 150, 210, 150, 150, 151, 151, 151,),
}
SLOTS_R = 2
BUFS = 1
PWIDE = (CMAIN, EWIDE + PATCH)
STAGES = 5


def backward_all_kernel(
    times, dout_in, xs_in, gp_in, qk_in, fa_in, vec_ref, mask, pn_ref, head_ref, end_ref, small, wcol, wdown,
    gcol, gdown, gpart, scalars, rfa,
    *refs,
):
    (
        wbuf, gp, xb, dcur, er, qk, ba, lbuf, rd, ru, rq, full, low, recv1, mid_own, mid_low, recv2,
        zlow, zown, zrecv, psend, pown, pxr0, pxr1, pzr0, pzr1, sq,
        wsem, gsem, xsem, qsem, ls, fas, far, bs, br, s1, r1, s2, r2, zs, zr, fs, fr, ks, kr,
        ss, sr, qs, qr, p1, p1r, p2, p2r, p3, p3r, p4, p4r, credit,
        ds_, dr_, gs_, gr_, small_all, square_all,
    ) = refs[: -len(BACKWARD_SCRATCH)]
    scratch = refs[-len(BACKWARD_SCRATCH) :]
    f, t, y, c, g, x = place()
    count = times // 2
    over_x = (f, g * 2 + 1 - x)
    over_y = ((1 - y) * 2 + c, t)
    over_c = (y * 2 + 1 - c, t)
    total = len(RGROUPS)
    other_core = 1 - c

    def half_cols(core):
        return pl.ds(pl.multiple_of(core * 384, 128), 384)

    def weight(layer, which):
        src = (wdown.at[layer], wcol.at[2 * layer + 1], wcol.at[2 * layer])[which]
        return pltpu.make_async_copy(src, wbuf.at[weight_slot(layer, which)], wsem.at[layer, which])

    def weight_slot(layer, which):
        return (which % 2 + (L - 1 - layer)) % 2

    def slope_load(layer, k):
        return pltpu.make_async_copy(gp_in.at[layer, k], gp.at[k % 2], gsem.at[layer, k])

    def kept_load(layer, i):
        return pltpu.make_async_copy(xs_in.at[2 * layer + i], xb, xsem.at[layer, i])

    def heads_load(layer):
        return pltpu.make_async_copy(qk_in.at[layer], qk, qsem.at[layer])

    first_load = pltpu.make_async_copy(dout_in, dcur, qsem.at[L])
    first_load.start()
    for which in range(2):
        weight(L - 1, which).start()
    for k in range(2):
        slope_load(L - 1, k).start()
    kept_load(L - 1, 1).start()
    heads_load(L - 1).start()
    greet_all(times)
    spread_small(times, small, small_all, ss, sr)

    def forward_swap(layer, n):
        span = pl.ds(3, 4) if n == 0 else pl.ds(0, 3)
        return remote(
            fa_in.at[layer, span], rfa.at[layer, span], fas.at[layer, n], far.at[layer, n], over_c
        )

    for layer in reversed(range(L)):
        for n in range(2):
            forward_swap(layer, n).start()

    def swap(gi, n):
        kind, l = RGROUPS[gi]
        if kind == "d":
            src, dst = ba.at[8, :, half_cols(other_core)], rd.at[l]
        elif kind == "u":
            src, dst = ba.at[4 + 2 * n + other_core], ru.at[l, n]
        else:
            src, dst = ba.at[2 * n + other_core], rq.at[l, n]
        return remote(src, dst, bs.at[gi, n], br.at[gi, n], over_c)

    def swaps(gi):
        return range(1 if RGROUPS[gi][0] == "d" else 2)

    def left_loads(gi):
        kind, l = RGROUPS[gi]
        out = []
        blocks = {"d": (3, 4, 5, 6), "u": (2,), "q": (0, c)}[kind]
        for n, block in enumerate(blocks):
            for m, src in enumerate((fa_in, rfa)):
                out.append(
                    pltpu.make_async_copy(
                        src.at[l, block], lbuf.at[n, pl.ds(m * TOK, TOK)], ls.at[n, m]
                    )
                )
        return out

    def product(left, own, other, cols):
        return tn(lbuf[left, :TOK], own(cols)) + tn(lbuf[left, TOK:], other(cols))

    def store(gi, h, role, xx, where, value):
        if ROUTES[gi][h] == "y":
            keep, index = role == 0, xx
        else:
            keep, index = x == xx, role

        def save_full():
            full[(gi % BUFS, h, index) + where] = value

        def save_low():
            low[(gi % BUFS, h, index) + where] = value.astype(BF)

        if isinstance(keep, bool):
            (save_full if keep else save_low)()
        else:
            pl.when(keep)(save_full)
            pl.when(jnp.logical_not(keep))(save_low)

    def compute(gi, h):
        kind, l = RGROUPS[gi]
        if kind == "d":

            def one(z, carry):
                prod = product(
                    z, lambda _: ba[8, :, half_cols(c)], lambda _: rd[l], None
                ).reshape(2, 2, 2, 96, 384)
                for xx in range(2):
                    for yy in range(2):
                        for hh in range(2):
                            store(gi, hh, (yy + y) % 2, xx, (z,), prod[xx, yy, hh])
                return carry

            if h == 0:
                lax.fori_loop(0, count, one, 0)
            return
        recv = ru if kind == "u" else rq
        base = 4 if kind == "u" else 0
        for role in range(2):
            yy = y if role == 0 else 1 - y
            left = 0 if kind == "u" else yy
            prod = product(
                left, lambda cols: ba[base + 2 * yy + c, :, cols], lambda cols: recv[l, yy, :, cols],
                slice(h * 384, (h + 1) * 384),
            ).reshape(count, 2, 96, 384)
            for xx in range(2):
                store(gi, h, role, xx, (), prod[:, xx])

    def step1(gi, h):
        return remote(
            low.at[gi % BUFS, h], recv1.at[gi % SLOTS_R, h], s1.at[gi, h], r1.at[gi, h],
            over_y if ROUTES[gi][h] == "y" else over_x,
        )

    def step2(gi, h):
        if ROUTES[gi][h] == "z":
            src, dst = zlow.at[h, 0], recv2.at[gi % SLOTS_R, h, count - 1]
        else:
            src, dst = mid_low.at[h], recv2.at[gi % SLOTS_R, h]
        return remote(
            src, dst, s2.at[gi, h], r2.at[gi, h], over_x if ROUTES[gi][h] == "y" else over_y
        )

    def along(gi, h, dz, role=0):
        to = (g + dz) % count
        slot = gi % SLOTS_R
        if ROUTES[gi][h] != "z":
            src, dst = zlow.at[h, to], zrecv.at[slot, h, dz - 1]
        elif role == 0:
            src, dst = mid_low.at[h, to], zrecv.at[slot, h, dz - 1]
        else:
            src, dst = zlow.at[h, to], recv2.at[slot, h, dz - 1]
        return remote(src, dst, zs.at[gi, h, role, dz - 1], zr.at[gi, h, role, dz - 1], (f, to * 2 + x))

    def result(gi, h, yy):
        kind, l = RGROUPS[gi]
        if kind == "d":
            return gdown.at[l, yy, pl.ds(h * 96, 96), half_cols(c)]
        return gcol.at[2 * l + (1 if kind == "u" else 0), yy, c, :, pl.ds(h * 384, 384)]

    def spread_y(gi, h):
        block = result(gi, h, y)
        return remote(block, block, fs.at[gi, h], fr.at[gi, h], over_y)

    def spread_c(gi, h):
        block = result(gi, h, slice(None))
        return remote(block, block, ks.at[gi, h], kr.at[gi, h], over_c)

    def wait_along(gi, h):
        for role in range(2 if ROUTES[gi][h] == "z" else 1):
            for dz in range(1, count):
                along(gi, h, dz, role).wait_recv()
                along(gi, h, dz, role).wait_send()

    def start_along(gi, h):
        for dz in range(1, count):
            if gi >= SLOTS_R:
                pl.semaphore_wait(credit.at[1 + dz], 1)
            for role in range(2 if ROUTES[gi][h] == "z" else 1):
                along(gi, h, dz, role).start()

    def advance(gi, h, stage):
        slot, buf = gi % SLOTS_R, gi % BUFS
        twice = ROUTES[gi][h] == "z"
        if stage == 1:
            step1(gi, h).wait_recv()
            step1(gi, h).wait_send()
            if twice:
                summed = full[buf, h, 0] + recv1[slot, h, 0].astype(F32)
                mid_low[h] = summed.astype(BF)
                mid_own[h] = summed
                summed = full[buf, h, 1] + recv1[slot, h, 1].astype(F32)
                zlow[h] = summed.astype(BF)
                start_along(gi, h)
                full[buf, h, 1] = summed
                zown[h] = full[buf, h, 1, g]
                return
            keep, send = (x, 1 - x) if ROUTES[gi][h] == "y" else (0, 1)
            mid_low[h] = (full[buf, h, send] + recv1[slot, h, send].astype(F32)).astype(BF)
            step2(gi, h).start()
            mid_own[h] = full[buf, h, keep] + recv1[slot, h, keep].astype(F32)
        elif stage == 2:
            if twice:
                wait_along(gi, h)
                value = zown[h]
                for dz in range(1, count):
                    value = value + recv2[slot, h, dz - 1].astype(F32)
                zlow[h, 0] = value.astype(BF)
                step2(gi, h).start()
                value = mid_own[h, g]
                for dz in range(1, count):
                    value = value + zrecv[slot, h, dz - 1].astype(F32)
                zown[h] = value
                return
            step2(gi, h).wait_recv()
            step2(gi, h).wait_send()
            summed = mid_own[h] + recv2[slot, h].astype(F32)
            zlow[h] = summed.astype(BF)
            start_along(gi, h)
            mid_own[h] = summed
            zown[h] = mid_own[h, g]
        elif stage == 3:
            value = zown[h]
            if twice:
                step2(gi, h).wait_recv()
                step2(gi, h).wait_send()
                value = value + recv2[slot, h, count - 1].astype(F32)
            else:
                wait_along(gi, h)
                for dz in range(1, count):
                    value = value + zrecv[slot, h, dz - 1].astype(F32)
            sq[...] += jnp.sum((value * value).reshape(12, 8, 3, 128), (0, 2))
            kind, l = RGROUPS[gi]
            if kind == "d":
                gdown[l, y, h * 96 : (h + 1) * 96, half_cols(c)] = value.astype(BF)
            else:
                idx = 2 * l + (1 if kind == "u" else 0)
                gcol[idx, y, c, :, h * 384 : (h + 1) * 384] = value.astype(BF)
            spread_y(gi, h).start()
            if gi + SLOTS_R < total:
                pl.semaphore_signal(credit.at[0], inc=1, device_id=over_x, device_id_type=MESH)
                pl.semaphore_signal(credit.at[1], inc=1, device_id=over_y, device_id_type=MESH)
                for dz in range(1, count):
                    back = (f, ((g + count - dz) % count) * 2 + x)
                    pl.semaphore_signal(
                        credit.at[1 + dz], inc=1, device_id=back, device_id_type=MESH
                    )
        elif stage == 4:
            spread_y(gi, h).wait_recv()
            spread_c(gi, h).start()
        else:
            spread_c(gi, h).wait_recv()

    pxrs, pzrs = (pxr0, pxr1), (pzr0, pzr1)
    psends = [psend.at[:, :, pl.ds(0, w)] for w in PWIDE]
    powns = [pown.at[:, :, pl.ds(0, w)] for w in PWIDE]

    def part_over(n):
        return remote(psends[n], pxrs[n], p1.at[n], p1r.at[n], over_x)

    def part_along(n, dz):
        return remote(
            psends[n].at[(g + dz) % count], pzrs[n].at[dz - 1], p2.at[n, dz - 1], p2r.at[n, dz - 1],
            (f, ((g + dz) % count) * 2 + x),
        )

    def part_y(n):
        block = gpart.at[n, y, c]
        return remote(block, block, p3.at[n], p3r.at[n], over_y)

    def part_c(n):
        block = gpart.at[n, :, c]
        return remote(block, block, p4.at[n], p4r.at[n], over_c)

    def part_compute(n):
        pieces = []
        if n == 0:
            pieces.append((0, tn(head_ref[0], head_ref[1, :, :CMAIN])))
        else:
            pieces.append((0, er[...].T))
            pieces.append((EWIDE, tn(dcur[...].astype(BF), pn_ref[...])))
        for lo, piece in pieces:
            piece = piece.reshape(count, 2, 96, -1)
            span = slice(lo, lo + piece.shape[-1])
            for xx in range(2):

                @pl.when(x == xx)
                def _():
                    powns[n][:, :, span] = piece[:, xx]
                    psends[n][:, :, span] = piece[:, 1 - xx].astype(BF)

        part_over(n).start()

    def part_advance(n, stage):
        if stage == 1:
            part_over(n).wait_recv()
            summed = powns[n][...] + pxrs[n][...].astype(F32)
            powns[n][...] = summed
            part_over(n).wait_send()
            psends[n][...] = summed.astype(BF)
            for dz in range(1, count):
                part_along(n, dz).start()
        elif stage == 2:
            value = powns[n][g]
            for dz in range(1, count):
                part_along(n, dz).wait_recv()
                part_along(n, dz).wait_send()
                value = value + pzrs[n][dz - 1].astype(F32)
            gpart[n, y, c, :, : PWIDE[n]] = value.astype(BF)
            part_y(n).start()
            if n == 1:
                lane = lax.broadcasted_iota(jnp.int32, (96, EWIDE), 1)
                inside = jnp.logical_and(lane % SLOTS < GRID, lane < TOK)
                own = jnp.where(inside, value[:, :EWIDE], 0.0)
                sq[...] += jnp.sum((own * own).reshape(12, 8, 3, 128), (0, 2))
        elif stage == 3:
            part_y(n).wait_recv()
            part_c(n).start()
        else:
            part_c(n).wait_recv()
            value = gpart[n, 0, 0].astype(F32) + gpart[n, 0, 1].astype(F32)
            value = value + gpart[n, 1, 0].astype(F32) + gpart[n, 1, 1].astype(F32)
            value = value[:, : PWIDE[n]]
            if n == 1:
                lane = lax.broadcasted_iota(jnp.int32, value.shape, 1)
                value = jnp.where(lane >= EVEC, value, 0.0)
            value = jnp.where(f == 0, value * value, 0.0)
            sq[...] += jnp.sum(value.reshape(12, 8, PWIDE[n] // 128, 128), (0, 2))

    stages = {}

    def launch(gi, h):
        if h == 0:
            for n in swaps(gi):
                swap(gi, n).wait_recv()
            for copy in left_loads(gi):
                copy.wait()
        compute(gi, h)
        if gi >= SLOTS_R:
            pl.semaphore_wait(credit.at[0], 1)
            pl.semaphore_wait(credit.at[1], 1)
        step1(gi, h).start()
        stages[gi, h] = 0
        if h == 1:
            for n in swaps(gi):
                swap(gi, n).wait_send()
            if gi + 1 < total:
                prepare(gi + 1)

    def perform(op):
        what, gi, h = op // 100, op // 10 % 10, op % 10
        if what == 0:
            launch(gi, h)
            return
        stages[gi, h if what == 1 else 2] += 1
        if what == 1:
            advance(gi, h, stages[gi, h])
        else:
            part_advance(gi, stages[gi, 2])

    waited = set()

    def prepare(gi):
        kind, l = RGROUPS[gi]
        for n in ((0,) if kind == "d" else (1,)):
            if (l, n) not in waited:
                waited.add((l, n))
                forward_swap(l, n).wait_recv()
        for copy in left_loads(gi):
            copy.start()

    def launch_part(n):
        part_compute(n)
        stages[n, 2] = 0

    load_mask(mask, scratch[4])
    sq[...] = jnp.zeros_like(sq)
    er[...] = jnp.zeros_like(er)
    er[EVEC + GLOB + 3 : EVEC + GLOB + 5, :] = end_ref[...]
    er[ECLS:, :] = tn(head_ref[1, :, CMAIN : CMAIN + EWIDE - ECLS], head_ref[0])
    launch_part(0)
    prepare(0)
    first_load.wait()
    loaded = set()

    for layer in reversed(range(L)):
        base = 3 * (L - 1 - layer)

        def mat(which):
            def read(k):
                if (layer, which) not in loaded:
                    loaded.add((layer, which))
                    weight(layer, which).wait()
                return wbuf[weight_slot(layer, which), k]

            return read

        def slope(k):
            slope_load(layer, k).wait()
            return gp[k % 2]

        def kept(i):
            kept_load(layer, i).wait()
            return xb[...]

        def at(point):
            if point.startswith("mlp"):
                k = int(point[3:])
                if k + 2 < FF // D:
                    slope_load(layer, k + 2).start()
                elif layer > 0:
                    slope_load(layer - 1, k - 2).start()
                if k == 0:
                    swap(base, 0).start()
                if k == 3:
                    for n in swaps(base + 1):
                        swap(base + 1, n).start()
                    weight(layer, 2).start()
                    if layer > 0:
                        weight(layer - 1, 0).start()
            elif point == "resid":
                kept_load(layer, 0).start()
                if layer == L - 1:
                    heads_load(layer).wait()
            elif point == "sent":
                if layer < L - 1:
                    heads_load(layer).wait()
            elif point == "head%d%d" % (PER - 1, NF - 1):
                if layer > 0:
                    heads_load(layer - 1).start()
            elif point == "heads":
                for n in swaps(base + 2):
                    swap(base + 2, n).start()
            elif point == "done":
                if layer > 0:
                    weight(layer - 1, 1).start()
                    kept_load(layer - 1, 1).start()
            for op in ORDER.get((layer, point), ()):
                perform(op)

        backward_body(
            layer, dcur, er, ba, vec_ref, qk, (mat(0), mat(1), mat(2)), slope, kept, scratch,
            (ds_.at[layer], dr_.at[layer], gs_.at[layer], gr_.at[layer]), at,
        )
    dgrid = dcur[...]
    spot = lax.broadcasted_iota(jnp.int32, (TOK, D), 0)
    er[:TOK, :] = dgrid
    inside = jnp.where(spot % SLOTS < GRID, dgrid, 0.0)
    er[EVEC + GLOB : EVEC + GLOB + 1, :] = jnp.sum(inside, 0, keepdims=True)
    er[EVEC + GLOB + 1 : EVEC + GLOB + 3, :] = dgrid[GRID : GRID + 2, :]
    launch_part(1)
    shared = False
    for op in ORDER["end"]:
        perform(op)
        summed = all(stages.get((gi, h), 0) >= 3 for gi in range(total) for h in range(2))
        if not shared and summed and stages[0, 2] == stages[1, 2] == STAGES - 1:
            shared = True
            n = NF * times
            me = f * times + t

            def send(i, carry):
                other = (me + i) % n
                remote(sq, square_all.at[me], qs, qr, (other // times, other % times)).start()
                return carry

            lax.fori_loop(1, n, send, 0)
            square_all[me] = sq[...]
    if not shared or any(stages[gi, h] < STAGES for gi in range(total) for h in range(2)):
        raise ValueError("incomplete order")
    for layer in range(L):
        for n in range(2):
            forward_swap(layer, n).wait_send()
    for gi in range(total):
        for h in range(2):
            spread_y(gi, h).wait_send()
            spread_c(gi, h).wait_send()
    for n in range(2):
        part_y(n).wait_send()
        part_c(n).wait_send()
    wait_small(times, small_all, ss, sr)
    wait_small(times, square_all, qs, qr)
    summed = jnp.sum(small_all[...], 0)
    spot = lax.broadcasted_iota(jnp.int32, (8, 128), 0) * 128 + lax.broadcasted_iota(jnp.int32, (8, 128), 1)
    bias = jnp.where(spot < CLASSES, summed, 0.0)
    norm = jnp.sqrt(jnp.sum(jnp.sum(square_all[...], 0) + bias * bias, keepdims=True))
    scalars[0] = summed
    scalars[1] = jnp.broadcast_to(norm, (8, 128))
    scalars[2] = jnp.broadcast_to(jnp.minimum(1.0, 1.0 / (norm + 1e-06)), (8, 128))


def backward_all(times, dout, xs, gp, qk, fa, vec, mask, pnorm, head, end_rows, small, wcol, wdown):
    count = times // 2
    n = NF * times
    total = len(RGROUPS)
    dma = pltpu.SemaphoreType.DMA
    most = max(PWIDE)
    return pl.pallas_call(
        functools.partial(backward_all_kernel, times),
        out_shape=(
            jax.ShapeDtypeStruct((2 * L, 2, 2, 96, D), BF),
            jax.ShapeDtypeStruct((L, 2, 192, D), BF),
            jax.ShapeDtypeStruct((2, 2, 2, 96, most), BF),
            jax.ShapeDtypeStruct((3, 8, 128), F32),
            jax.ShapeDtypeStruct(fa.shape, BF),
        ),
        in_specs=[aspec()] * 5 + [vspec()] + [aspec()] + [vspec()] * 4 + [aspec()] * 2,
        out_specs=(vspec(),) * 4 + (aspec(),),
        scratch_shapes=[
            VM((2, 4, D, D), BF),
            VM((2, TOK, D), F32),
            VM((TOK, D), F32),
            VM((TOK, D), F32),
            VM((EWIDE, D), F32),
            VM((PER, NF, QROWS, 128), BF),
            VM((9, TOK, D), BF),
            VM((4, 2 * TOK, D), BF),
            VM((L, TOK, 384), BF),
            VM((L, 2, TOK, D), BF),
            VM((L, 2, TOK, D), BF),
            VM((BUFS, 2, 2, count, 96, 384), F32),
            VM((BUFS, 2, 2, count, 96, 384), BF),
            VM((SLOTS_R, 2, 2, count, 96, 384), BF),
            VM((2, count, 96, 384), F32),
            VM((2, count, 96, 384), BF),
            VM((SLOTS_R, 2, count, 96, 384), BF),
            VM((2, count, 96, 384), BF),
            VM((2, 96, 384), F32),
            VM((SLOTS_R, 2, count - 1, 96, 384), BF),
            VM((count, 96, most), BF),
            VM((count, 96, most), F32),
            *[VM((count, 96, w), BF) for w in PWIDE],
            *[VM((count - 1, 96, w), BF) for w in PWIDE],
            VM((8, 128), F32),
            dma((L, 3)), dma((L, 4)), dma((L, 2)), dma((L + 1,)), dma((4, 2)),
            dma((L, 2)), dma((L, 2)), dma((total, 2)), dma((total, 2)),
            dma((total, 2)), dma((total, 2)), dma((total, 2)), dma((total, 2)),
            dma((total, 2, 2, count - 1)), dma((total, 2, 2, count - 1)),
            dma((total, 2)), dma((total, 2)), dma((total, 2)), dma((total, 2)),
            dma, dma, dma, dma,
            dma((2,)), dma((2,)), dma((2, count - 1)), dma((2, count - 1)), dma((2,)), dma((2,)), dma((2,)), dma((2,)),
            pltpu.SemaphoreType.REGULAR((count + 1,)),
            *[dma((L, PER, NF - 1))] * 4,
            VM((n, 8, 128), F32),
            VM((n, 8, 128), F32),
        ]
        + BACKWARD_SCRATCH,
        compiler_params=pltpu.CompilerParams(
            collective_id=2 + 2 * L, has_side_effects=True, vmem_limit_bytes=65400 * 1024
        ),
        name="backward_all",
    )(dout, xs, gp, qk, fa, vec, mask, pnorm, head, end_rows, small, wcol, wdown)[:4]


def adam(weight, first, second, grad):
    first = DECAY_FIRST * first + (1.0 - DECAY_FIRST) * grad
    second = DECAY_SECOND * second + (1.0 - DECAY_SECOND) * grad * grad
    fix_one = 1.0 - DECAY_FIRST**STEP
    fix_two = 1.0 - DECAY_SECOND**STEP
    scaled = jnp.sqrt(second * (1.0 / fix_two)) + EPSILON
    weight = weight * (1.0 - LEARN_RATE * WEIGHT_DECAY) - (LEARN_RATE / fix_one) * first / scaled
    return (weight, first, second)


PIECES = 4
WIDE_STEPS = L * 8 // PIECES
DOWN_STEPS = L * 4 // PIECES


def update_kernel(*refs):
    scalars, gcol, gdown, gpart = refs[:4]
    ins, outs, gemb = refs[4:19], refs[19:38], refs[38]
    step = pl.program_id(0)
    coef = scalars[2, 0:1, 0:1]

    def apply(which, grad, at=...):
        new = adam(*(ins[which + 5 * i][at] for i in range(3)), grad * coef)
        for i in range(3):
            outs[which + 5 * i][at] = new[i]
        if which < 4:
            outs[15 + which][at] = new[0].astype(BF)

    @pl.when(step < WIDE_STEPS)
    def _():
        for p in range(PIECES):
            apply(0, gcol[0, p].astype(F32), (0, slice(None), slice(p * D, (p + 1) * D)))

    @pl.when(step >= WIDE_STEPS)
    def _():
        apply(1, gdown[0].astype(F32), (0,))

    @pl.when(step == 0)
    def _():
        main = sum(gpart[0, i, :, :CMAIN].astype(F32) for i in range(NF))
        rest = sum(gpart[1, i, :, EVEC:].astype(F32) for i in range(NF))
        per = FROWS // NF
        for i in range(NF):
            block = gpart[1, i].astype(F32)
            for h in range(2):
                for r in range(per):
                    to = (i * per + r) * 2 * HALF + h * HALF
                    gemb[:, to : to + HALF] = block[:, h * SLOTS + r * HALF : h * SLOTS + (r + 1) * HALF]
        gemb[:, NGRID:] = rest[:, EWIDE - EVEC :]
        apply(2, gemb[...])
        tail = rest[:, ECLS - EVEC : ECLS - EVEC + CLASSES - CMAIN]
        apply(3, jnp.concatenate([main, tail], 1))
        turned = rest[:, : 128].T
        apply(4, turned[:VROWS])


def update(scalars, gcol, gdown, gpart, params, firsts, seconds):
    shard = gcol.shape[2]
    per_wide, per_down = 8 // PIECES, 4 // PIECES

    def wide(step):
        step = jnp.minimum(step, WIDE_STEPS - 1)
        return (step // per_wide, 0, step % per_wide)

    def wide_grad(step):
        step = jnp.minimum(step, WIDE_STEPS - 1)
        return (step // per_wide, step % per_wide, 0, 0)

    def down(step):
        step = jnp.maximum(step - WIDE_STEPS, 0)
        return (step // per_down, step % per_down, 0)

    params, firsts, seconds = (
        [v[0], v[1], v[2].T, v[3], v[4]] for v in (params, firsts, seconds)
    )
    down_block = pl.BlockSpec((1, PIECES * shard, D), down)

    def whole(v):
        return pl.BlockSpec(v.shape, lambda step: (0,) * len(v.shape))

    specs = [pl.BlockSpec((1, shard, PIECES * D), wide), down_block] + [whole(v) for v in params[2:]]
    shapes = [jax.ShapeDtypeStruct(v.shape, F32) for v in params] * 3
    shapes += [jax.ShapeDtypeStruct(v.shape, BF) for v in params[:4]]
    news = pl.pallas_call(
        update_kernel,
        grid=(WIDE_STEPS + DOWN_STEPS,),
        out_shape=shapes,
        in_specs=[whole(scalars), pl.BlockSpec((1, PIECES, shard, D), wide_grad), down_block, whole(gpart)]
        + specs * 3,
        out_specs=specs * 3 + specs[:4],
        scratch_shapes=[VM((shard, NGRID + PATCH), F32)],
        compiler_params=pltpu.CompilerParams(vmem_limit_bytes=48 * 1024 * 1024),
        name="update",
    )(scalars, gcol, gdown, gpart, *params, *firsts, *seconds)
    return [v.T if i % 5 == 2 else v for i, v in enumerate(news)]


def pad_to(v, axis, size):
    pads = [(0, 0)] * v.ndim
    pads[axis] = (0, size - v.shape[axis])
    return jnp.pad(v, pads)


def embed_units(embedding, classifier, vectors, f):
    width = embedding.shape[1]
    blocks = embedding[:NGRID].reshape(NF, FROWS // NF, 2, HALF, width)
    block = lax.dynamic_index_in_dim(blocks, f, 0, keepdims=False).transpose(1, 0, 2, 3)
    block = block.reshape(2, GRID, width)
    tokens = jnp.where(f == 0, vectors[GLOB + 1 : GLOB + 3], 0.0)
    tokens = jnp.stack([tokens, jnp.zeros_like(tokens)])
    block = jnp.concatenate([block, tokens, jnp.zeros((2, SLOTS - GRID - 2, width), F32)], 1)
    rest = classifier[:, CMAIN:].T
    unit = jnp.concatenate(
        [
            block.reshape(TOK, width), vectors, jnp.zeros((ECLS - EVEC - VROWS, width), F32),
            pad_to(rest, 0, EWIDE - ECLS),
        ],
        0,
    )
    return unit.T.astype(BF), embedding[NGRID:].T.astype(BF), classifier[:, :CMAIN].astype(BF)


def local(
    patches, column_mask, labels, clip_weights, wide_weights, down_weights, embedding, classifier,
    vectors, class_bias, wide_first, down_first, embedding_first, classifier_first, vectors_first,
    bias_first, wide_second, down_second, embedding_second, classifier_second, vectors_second,
    bias_second,
):
    times = lax.axis_size("tm")
    f, t = lax.axis_index("freq"), lax.axis_index("tm")
    half = t % 2
    pair = t // 2
    rows_dev = FROWS // NF
    kernels = D // times == 96
    shard = D // times
    columns = column_mask.reshape(times, CPD, HALF) > 0
    mine_columns = lax.dynamic_index_in_dim(columns, t, 0, keepdims=False)
    raw = patches.reshape(rows_dev, CPD, HALF, PATCH)

    keep_block, give_block = (
        pad_to(lax.dynamic_index_in_dim(raw, i, 1, keepdims=False).reshape(GRID, PATCH), 0, SLOTS)
        for i in (half, 1 - half)
    )

    live = jnp.stack([pad_to(jnp.tile(mine_columns[i], rows_dev), 0, SLOTS) for i in range(2)])
    live = jnp.where(half == 0, live, live[::-1]).astype(F32)[:, :, None]
    unit_embed, unit_patch, unit_class = embed_units(embedding, classifier, vectors, f)

    clip_columns = lax.dynamic_slice(columns, (pair * 2, half, 0), (2, 1, HALF)).reshape(2, HALF)
    slots = jnp.concatenate(
        [
            jnp.broadcast_to(jnp.tile(clip_columns, (1, rows_dev)), (NF, 2, GRID)),
            jnp.broadcast_to(
                ((jnp.arange(NF)[:, None] == 0) & (jnp.arange(2)[None, :] == 0))[:, :, None], (NF, 2, 2)
            ),
            jnp.zeros((NF, 2, SLOTS - GRID - 2), bool),
        ],
        2,
    ).reshape(NF * TOK)
    mask = jnp.where(slots[:, None] | (jnp.arange(128) != HDIM)[None, :], 0.0, -1e30).astype(BF)

    weight_total = jnp.sum(clip_weights).astype(F32)
    if kernels:
        wcol, wdown, vec, xs, fa, gp, qk, pnorm, dx, head, end_rows, small = forward_all(
            times, wide_weights, down_weights, unit_embed, unit_patch, unit_class, live, keep_block, give_block,
            pad_to(labels, 1, D), clip_weights[None], pad_to(class_bias[None], 1, D), mask,
        )
    else:
        wide_all = lax.all_gather(wide_weights.astype(BF), "tm", axis=1, tiled=True)
        wcol = wide_all.reshape(L, D, 2, 4, D).transpose(0, 2, 3, 1, 4)
        wcol = wcol.reshape(2 * L, 2, 2, 4, 2, 96, D)
        wdown = lax.all_gather(down_weights.astype(BF), "tm", axis=1, tiled=True)
        wdown = wdown.reshape(L, 4, 2, 2, 192, D)
        vec = lax.all_gather(unit_embed, "tm", axis=0, tiled=True).T.astype(F32)
        patch = lax.all_gather(unit_patch, "tm", axis=0, tiled=True)
        class_main = lax.all_gather(unit_class, "tm", axis=0, tiled=True)
        pixels = jnp.stack([keep_block, give_block]).astype(F32)
        sums = jnp.stack(
            [jnp.sum(pixels * live), jnp.sum(pixels * pixels * live), jnp.sum(live) * PATCH]
        )
        sums = lax.psum(sums, ("freq", "tm"))
        take_block = lax.ppermute(
            give_block, "tm", [(i, i + 1 - 2 * (i % 2)) for i in range(times)]
        )
        pixels = jnp.concatenate(
            [jnp.where(half == 0, keep_block, take_block), jnp.where(half == 0, take_block, keep_block)], 0
        )
        center = sums[0] / sums[2]
        mel_scale = lax.rsqrt(sums[1] / sums[2] - center * center + 1e-05)
        inside = (jnp.arange(TOK) % SLOTS < GRID)[:, None]
        pnorm = jnp.where(inside, (pixels.astype(F32) - center) * mel_scale, 0.0).astype(BF)
        x = nt(pnorm, patch) + vec[:TOK] + jnp.where(inside, vec[EVEC + GLOB], 0.0)
        xs, fa, gp, qk = [x], [], [], []
        for layer in range(L):
            x, x1, acts, slopes, heads = forward_layer(layer, x, vec, mask, wcol, wdown)
            xs += [x1, x]
            fa.append(acts)
            gp.append(slopes)
            qk.append(heads)
    wcol = wcol.reshape(2 * L, 4, D, D)
    wdown = wdown.reshape(L, 4, D, D)
    if not kernels:
        vec_all = vec[EVEC : EVEC + VROWS]
        class_all = jnp.concatenate([class_main, vec[ECLS : ECLS + CLASSES - CMAIN].T.astype(BF)], 1)

        owner = (f == 0).astype(F32)
        special = xs[2 * L][GRID : GRID + 2]
        normed_end, scale_end = norm_rows(special)
        feature = jnp.mean(normed_end * vec_all[GLOB + 3] + vec_all[GLOB + 4], 0, keepdims=True).astype(BF)
        logits = nn(feature, class_all) + class_bias
        clip = pair * CPD + half
        flags = lax.dynamic_slice_in_dim(labels, clip, 1, 0).astype(F32)
        weight = lax.dynamic_slice_in_dim(clip_weights, clip, 1, 0).astype(F32)[:, None]
        loss_part = owner * jnp.sum(weight * (jax.nn.softplus(logits) - flags * logits))
        dlogits = owner * weight * (jax.nn.sigmoid(logits) - flags) / weight_total
        dlogits_low = dlogits.astype(BF)
        dfinal = jnp.broadcast_to(0.5 * nt(dlogits_low, class_all), (2, D))
        dspecial = norm_back(dfinal * vec_all[GLOB + 3], normed_end, scale_end)
        end_rows = jnp.stack([jnp.sum(dfinal * normed_end, 0), jnp.sum(dfinal, 0)])
        dx = jnp.concatenate(
            [jnp.zeros((GRID, D), F32), dspecial, jnp.zeros((TOK - GRID - 2, D), F32)], 0
        )
        small = jnp.concatenate([dlogits.reshape(-1), loss_part.reshape(1)])
        small = pad_to(small, 0, 1024).reshape(8, 128)
    if kernels:
        gcol, gdown, gpart, scalars = backward_all(
            times, dx, xs, gp, qk, fa, vec, mask, pnorm, head, end_rows, small, wcol, wdown
        )
        small = scalars[0].reshape(-1)
        grad_norm, coef = scalars[1, 0, 0], scalars[2, 0, 0]
        params = (wide_weights, down_weights, embedding, classifier, vectors)
        firsts = (wide_first, down_first, embedding_first, classifier_first, vectors_first)
        seconds = (wide_second, down_second, embedding_second, classifier_second, vectors_second)
        news = update(
            scalars, gcol.reshape(L, 8, shard, D), gdown.reshape(L, FF // times, D),
            gpart.reshape(2, NF, shard, -1), params, firsts, seconds,
        )
        bias = adam(class_bias, bias_first, bias_second, small[:CLASSES] * coef)
        return (
            *news[:5], bias[0], *news[5:10], bias[1], *news[10:15], bias[2], *news[15:],
            grad_norm, small[CLASSES], weight_total,
        )
    else:
        ba = [None] * L
        er = jnp.zeros((EWIDE, D), F32)
        for layer in reversed(range(L)):
            dx, ba[layer], rows = backward_layer(
                layer, dx, xs[2 * layer], xs[2 * layer + 1], gp[layer], qk[layer], vec, mask, wcol, wdown
            )
            er = er + rows
        dgrid = jnp.where(inside, dx, 0.0)
        grad_vectors = er[EVEC : EVEC + GLOB]
        grad_vectors = jnp.concatenate(
            [grad_vectors, jnp.sum(dgrid, 0, keepdims=True), dx[GRID : GRID + 2], end_rows], 0
        )
        wides, downs = [], []
        for l in range(L):
            cols = [tn(fa[l][0], ba[l][i]) for i in range(3)]
            cols += [tn(fa[l][1], ba[l][3])]
            cols += [tn(fa[l][2], ba[l][4 + i]) for i in range(4)]
            wides.append(jnp.concatenate(cols, 1))
            downs.append(jnp.concatenate([tn(fa[l][3 + i], ba[l][8]) for i in range(4)], 0))
        dpos = dgrid.reshape(2, SLOTS, D)[:, :GRID].reshape(2, rows_dev, HALF, D)
        dpos = dpos.transpose(1, 0, 2, 3).reshape(rows_dev * 2 * HALF, D)
        dpos = lax.dynamic_update_slice(jnp.zeros((NGRID, D), F32), dpos, (f * rows_dev * 2 * HALF, 0))
        dembed = jnp.concatenate([dpos, tn(pnorm, dgrid.astype(BF))], 0)
        grads = (
            lax.psum_scatter(jnp.stack(wides), "tm", scatter_dimension=1, tiled=True),
            lax.psum_scatter(jnp.stack(downs), "tm", scatter_dimension=1, tiled=True),
            lax.psum_scatter(dembed, "tm", scatter_dimension=1, tiled=True),
            lax.psum_scatter(tn(feature, dlogits_low), "tm", scatter_dimension=0, tiled=True),
            lax.psum_scatter(grad_vectors, "tm", scatter_dimension=1, tiled=True),
        )
        grads = lax.psum(grads, "freq")
        grad_wide, grad_down, grad_embed, grad_class, grad_vectors = grads
        squares = sum(jnp.sum(v * v) for v in grads)
        square_total, small = lax.psum(
            (jnp.where(f == 0, squares, 0.0), small.reshape(-1)), ("freq", "tm")
        )
    grad_bias = small[:CLASSES]
    loss_sum = small[CLASSES]
    grad_norm = jnp.sqrt(square_total + jnp.sum(grad_bias * grad_bias))
    coef = jnp.minimum(1.0, 1.0 / (grad_norm + 1e-06))

    params = (wide_weights, down_weights, embedding, classifier, vectors, class_bias)
    firsts = (wide_first, down_first, embedding_first, classifier_first, vectors_first, bias_first)
    seconds = (wide_second, down_second, embedding_second, classifier_second, vectors_second, bias_second)
    grads = (grad_wide, grad_down, grad_embed, grad_class, grad_vectors, grad_bias)
    news = [adam(w, m, v, g * coef) for w, m, v, g in zip(params, firsts, seconds, grads)]
    masters = [n[0] for n in news]
    return (
        *masters,
        *[n[1] for n in news],
        *[n[2] for n in news],
        *[m.astype(BF) for m in masters[:4]],
        grad_norm,
        loss_sum,
        weight_total,
    )


def solution(mesh):
    split = (
        P(None, "tm", None), P(None, "tm", None), P(None, "tm"), P("tm", None), P(None, "tm"), P(),
    )
    return jax.shard_map(
        local,
        mesh=mesh,
        in_specs=(P("freq", "tm", None), P(), P(), P()) + split * 3,
        out_specs=split * 3 + split[:4] + (P(), P(), P()),
        check_vma=False,
    )
```
